32 devices in a mesh: strike: 8 (over z, x), dip: 4 (over y, core).
Axes of the slice: x: 2, y: 2, z: 4, core: 2. Of those that a mesh axis runs over, the one named last changes fastest.
Arguments:
- coarse_field: bfloat16 [32, 16, 128], P('strike', 'dip'), may hold values from -6 to 6
- up_weight: bfloat16 [8, 8, 8, 32, 32], replicated, may hold values from -0.375 to 0.375
- first_weight: bfloat16 [3, 3, 3, 32, 32], replicated, may hold values from -0.21875 to 0.21875
- second_weight: bfloat16 [3, 3, 3, 32, 32], replicated, may hold values from -0.21875 to 0.21875
Outputs:
- refined: bfloat16 [128, 64, 512], P('strike', 'dip')
The draws below stay inside these ranges and needn't reach their ends.
All inputs are finite; a program needn't handle non-finite values.
Results may differ from the reference program's by a relative error of at most 0.012.
Values may be sent and summed in bfloat16 or wider, within the bound.
No kernel may reach another device: no remote copies, remote signals or barrier semaphores. Data moves between devices by JAX's collectives and lax.ppermute only.
A program may use at most 192 MiB of HBM per device.

```python
import jax
import jax.numpy as jnp
from jax import lax

C = 32
ZC = 4
NXC = 32
NYC = 16


def block_scale(rng, dims, shards, least, top_value):
    def one(position, shards_of):
        draws = jax.random.uniform(jax.random.fold_in(jax.random.fold_in(rng, 6), position), (shards_of,), jnp.float32, least / len(shards), top_value / len(shards))
        return jnp.repeat(jnp.exp(draws), dims[position] // shards_of).reshape((-1,) + (1,) * (len(dims) - position - 1))

    gain = one(*shards[0])
    for cut in shards[1:]:
        gain = gain * one(*cut)
    return gain


def bell_draw(own_key, dims, deviation, most, shards=(), kind=jnp.bfloat16):
    factor_of = block_scale(own_key, dims, shards, -0.22, 0.18) if shards else 1.0
    result = jax.random.normal(own_key, dims, jnp.float32) * deviation * factor_of
    return jnp.minimum(jnp.maximum(result, -most), most).astype(kind)


def setup_inputs(seed: int = 0) -> dict:
    key_of = jax.random.split(jax.random.key(seed), 5)
    coarse_field = bell_draw(key_of[0], (NXC, NYC, ZC * C), 1.0, 6.0, ((0, 8), (1, 4)))
    up_weight = bell_draw(key_of[1], (8, 8, 8, C, C), (8 * C) ** -0.5, 0.375)
    first_weight = bell_draw(key_of[2], (3, 3, 3, C, C), (27 * C) ** -0.5, 0.21875)
    second_weight = bell_draw(key_of[3], (3, 3, 3, C, C), (27 * C) ** -0.5, 0.21875)
    return {"coarse_field": coarse_field, "up_weight": up_weight, "first_weight": first_weight, "second_weight": second_weight}


HIGHEST = lax.Precision.HIGHEST


def upsample(coarse_field, up_weight):
    size_one, size_two, depth_lanes = coarse_field.shape
    channels = up_weight.shape[3]
    coarse_depth = depth_lanes // channels
    coarse_grid = coarse_field.astype(jnp.float32).reshape(size_one, size_two, coarse_depth, channels)
    padded = jnp.pad(coarse_grid, ((1, 1), (1, 1), (1, 1), (0, 0)))
    weights = up_weight.astype(jnp.float32).reshape(2, 4, 2, 4, 2, 4, channels, channels)

    def one_block(block_index):
        start = (block_index * 8).astype(jnp.int32)
        row_slab = lax.dynamic_slice_in_dim(padded, start, 10, 0)
        summed = jnp.zeros((9, size_two + 1, coarse_depth + 1, 4, 4, 4, channels), jnp.float32)
        for high_one in (0, 1):
            for high_two in (0, 1):
                for high_three in (0, 1):
                    shifted = row_slab[1 - high_one:10 - high_one, 1 - high_two:size_two + 2 - high_two,
                                       1 - high_three:coarse_depth + 2 - high_three]
                    summed = summed + jnp.einsum("abcx,pqrxy->abcpqry", shifted,
                                                 weights[high_one, :, high_two, :, high_three],
                                                 precision=HIGHEST)
        summed = summed.transpose(0, 3, 1, 4, 2, 5, 6)
        summed = summed.reshape(36, 4 * size_two + 4, 4 * coarse_depth + 4, channels)
        return summed[2:34, 2:4 * size_two + 2, 2:4 * coarse_depth + 2]

    blocks = lax.map(one_block, jnp.arange(size_one // 8, dtype=jnp.int32))
    return blocks.reshape(4 * size_one, 4 * size_two, 4 * coarse_depth, channels)


def refine(field_in, weight):
    output = lax.conv_general_dilated(field_in.astype(jnp.float32)[None], weight.astype(jnp.float32),
                                      (1, 1, 1), "SAME", dimension_numbers=("NDHWC", "DHWIO", "NDHWC"),
                                      precision=HIGHEST)
    return output[0]


def reference(coarse_field, up_weight, first_weight, second_weight):
    upsampled = upsample(coarse_field, up_weight)
    base = jax.nn.silu(upsampled).astype(jnp.bfloat16)
    hidden = jax.nn.silu(refine(base, first_weight)).astype(jnp.bfloat16)
    refined = (base.astype(jnp.float32) + refine(hidden, second_weight)).astype(jnp.bfloat16)
    return refined.reshape(refined.shape[0], refined.shape[1], refined.shape[2] * refined.shape[3])
```

```python
import jax
import jax.numpy as jnp
from jax import lax
from jax.experimental import pallas as pl
from jax.experimental.pallas import tpu as pltpu
from jax.sharding import PartitionSpec as P

PITCH = 24
ROWS = 20 * PITCH
BAND = 384


def silu(v):
    half = 0.5 * v
    return half + half * jnp.tanh(half)


def prep_kernel(up_ref, first_ref, second_ref, upmat_ref, band1_ref, band2_ref):
    for h1 in range(2):
        for h2 in range(2):
            for h3 in range(2):
                row = (h1 * 4 + h2 * 2 + (1 - h3)) * 32
                for p1 in range(4):
                    for p2 in range(4):
                        k = ((4 * h1 + p1) * 8 + 4 * h2 + p2) * 8 + 4 * h3
                        parts = [up_ref[pl.ds((k + p3) * 32, 32), :] for p3 in range(4)]
                        upmat_ref[pl.ds(row, 32), pl.ds((p1 * 4 + p2) * 128, 128)] = jnp.concatenate(
                            parts, axis=1
                        )
    ci = lax.broadcasted_iota(jnp.int32, (32, 256), 0)
    lane = lax.broadcasted_iota(jnp.int32, (32, 256), 1)
    group = lane // 32
    copies = (lane % 32 == ci).astype(jnp.bfloat16)

    def spread(w_ref, out_ref, lead, shifts):
        rep = jnp.dot(w_ref[...], copies, preferred_element_type=jnp.float32)
        for tap in range(9):
            taps = [rep[(tap * 3 + d) * 32 : (tap * 3 + d + 1) * 32] for d in range(3)]
            for s, shift in enumerate(shifts):
                for a in range(12):
                    block = jnp.zeros((32, 256), jnp.float32)
                    for d in range(3):
                        b = a + shift - d
                        if 0 <= b < 8:
                            block = jnp.where(group == b, taps[d], block)
                    block = block.astype(jnp.bfloat16)
                    rows = pl.ds(tap * BAND + a * 32, 32)
                    if lead:
                        out_ref[s, rows, :] = block
                    else:
                        out_ref[rows, :] = block

    spread(first_ref, band1_ref, False, (-1,))
    spread(second_ref, band2_ref, True, (1, -3))


def main_kernel(
    own, xm, xp, ym, yp, mm, mp, pm, pp, upmat, band1, band2, out, cells, fine, hidden, b1, b2
):
    strike, dip = lax.axis_index("strike"), lax.axis_index("dip")
    one, zero = jnp.float32(1), jnp.float32(0)
    x_lo = jnp.where(strike == 0, zero, one)
    x_hi = jnp.where(strike == lax.axis_size("strike") - 1, zero, one)
    y_lo = jnp.where(dip == 0, zero, one)
    y_hi = jnp.where(dip == lax.axis_size("dip") - 1, zero, one)

    def put(x0, y0, ref):
        n1, n2 = ref.shape[0], ref.shape[1]
        cells[x0 : x0 + n1, y0 : y0 + n2, :] = ref[...].astype(jnp.float32)

    put(1, 1, own)
    put(0, 1, xm)
    put(5, 1, xp)
    put(1, 0, ym)
    put(1, 5, yp)
    put(0, 0, mm)
    put(0, 5, mp)
    put(5, 0, pm)
    put(5, 5, pp)

    wide = []
    edge = jnp.zeros((40, 32), jnp.float32)
    for h1 in range(2):
        for h2 in range(2):
            window = cells[1 - h1 : 6 - h1, 1 - h2 : 9 - h2, :].reshape(40, 128)
            wide.append(jnp.concatenate([edge, window, edge], axis=1))
    left = jnp.concatenate(
        [
            jnp.concatenate([w[:, 32 * q3 : 32 * q3 + 64] for w in wide], axis=1)
            for q3 in range(5)
        ],
        axis=0,
    ).astype(jnp.bfloat16)

    q2 = lax.broadcasted_iota(jnp.int32, (200, 128), 0) % 8
    q3 = lax.broadcasted_iota(jnp.int32, (200, 128), 0) // 40
    p3 = lax.broadcasted_iota(jnp.int32, (200, 128), 1) // 32
    depth = 4 * q3 + p3
    inside = jnp.where((depth >= 2) & (depth < 18), one, zero)
    low = inside * jnp.where(q2 == 0, y_lo, one)
    high = inside * jnp.where(q2 == 4, y_hi, one)
    for p1 in range(4):
        phase = jnp.dot(left, upmat[:, p1 * 512 : p1 * 512 + 512], preferred_element_type=jnp.float32)
        for p2 in range(4):
            v = silu(phase[:, p2 * 128 : p2 * 128 + 128])
            v = v * (low if p2 < 2 else high)
            v = v.astype(jnp.bfloat16).astype(jnp.float32)
            for c3 in range(5):
                for c1 in range(5):
                    part = v[c3 * 40 + c1 * 8 : c3 * 40 + c1 * 8 + 5]
                    if c1 == 0 and p1 < 2:
                        part = part * x_lo
                    if c1 == 4 and p1 >= 2:
                        part = part * x_hi
                    fine[c3, pl.ds((4 * c1 + p1) * PITCH + p2, 5, stride=4), :] = part

    for dy in range(3):
        for c3 in range(5):
            b1[dy, :, c3 * 128 : c3 * 128 + 128] = fine[c3, pl.ds(dy, ROWS), :].astype(jnp.bfloat16)
    m1 = 18 * PITCH
    row = lax.broadcasted_iota(jnp.int32, (m1, 256), 0)
    i, j = row // PITCH, row % PITCH
    keep = jnp.where(i == 0, x_lo, one) * jnp.where(i == 17, x_hi, one)
    keep = keep * jnp.where(j == 0, y_lo, one) * jnp.where(j == 17, y_hi, one)
    for half in range(2):
        windows = [
            b1[dy, dx * PITCH : dx * PITCH + m1, half * 256 : half * 256 + BAND]
            for dx in range(3)
            for dy in range(3)
        ]
        v = jnp.dot(jnp.concatenate(windows, axis=1), band1[...], preferred_element_type=jnp.float32)
        hidden[:m1, half * 256 : half * 256 + 256] = silu(v) * keep

    for dy in range(3):
        b2[dy] = hidden[pl.ds(dy, m1), :].astype(jnp.bfloat16)
    m2 = 16 * PITCH
    base = jnp.concatenate([fine[c3, pl.ds(2 * PITCH + 2, m2), :] for c3 in range(5)], axis=1)
    for half in range(2):
        windows = [
            b2[dy, dx * PITCH : dx * PITCH + m2, half * 128 : half * 128 + BAND]
            for dx in range(3)
            for dy in range(3)
        ]
        v = jnp.dot(
            jnp.concatenate(windows, axis=1), band2[half], preferred_element_type=jnp.float32
        )
        v = v + base[:, 64 + half * 256 : 320 + half * 256]
        v = v.reshape(16, PITCH, 256)[:, :16].astype(jnp.bfloat16)
        out[:, :, half * 256 : half * 256 + 256] = v


def shifted(block, axes, steps, sizes):
    route = []
    for a in range(sizes[0]):
        for b in range(sizes[1]):
            c, d = a + steps[0], b + steps[1]
            if 0 <= c < sizes[0] and 0 <= d < sizes[1]:
                route.append((a * sizes[1] + b, c * sizes[1] + d))
    return lax.ppermute(block, axes, route)


def body(coarse, up_weight, first_weight, second_weight):
    axes = ("strike", "dip")
    sizes = tuple(lax.axis_size(a) for a in axes)
    vmem = pl.BlockSpec(memory_space=pltpu.VMEM)
    params = pltpu.CompilerParams(vmem_limit_bytes=48 * 1024 * 1024)

    xm = shifted(coarse[3:4], axes, (1, 0), sizes)
    xp = shifted(coarse[:1], axes, (-1, 0), sizes)
    ym = shifted(coarse[:, 3:4], axes, (0, 1), sizes)
    yp = shifted(coarse[:, :1], axes, (0, -1), sizes)
    mm = shifted(coarse[3:4, 3:4], axes, (1, 1), sizes)
    mp = shifted(coarse[3:4, :1], axes, (1, -1), sizes)
    pm = shifted(coarse[:1, 3:4], axes, (-1, 1), sizes)
    pp = shifted(coarse[:1, :1], axes, (-1, -1), sizes)

    bf16 = jnp.bfloat16
    upmat, band1, band2 = pl.pallas_call(
        prep_kernel,
        out_shape=(
            jax.ShapeDtypeStruct((256, 2048), bf16),
            jax.ShapeDtypeStruct((9 * BAND, 256), bf16),
            jax.ShapeDtypeStruct((2, 9 * BAND, 256), bf16),
        ),
        in_specs=[vmem] * 3,
        out_specs=(vmem,) * 3,
        compiler_params=params,
        cost_estimate=pl.CostEstimate(flops=10_000_000, bytes_accessed=12_000_000, transcendentals=0),
        name="arrange_weights",
    )(up_weight.reshape(512 * 32, 32), first_weight.reshape(864, 32), second_weight.reshape(864, 32))
    return pl.pallas_call(
        main_kernel,
        out_shape=jax.ShapeDtypeStruct((16, 16, 512), bf16),
        in_specs=[vmem] * 12,
        out_specs=vmem,
        scratch_shapes=[
            pltpu.VMEM((6, 16, 128), jnp.float32),
            pltpu.VMEM((5, ROWS + 8, 128), jnp.float32),
            pltpu.VMEM((18 * PITCH + 8, 512), jnp.float32),
            pltpu.VMEM((3, ROWS, 640), bf16),
            pltpu.VMEM((3, 18 * PITCH, 512), bf16),
        ],
        compiler_params=params,
        cost_estimate=pl.CostEstimate(
            flops=4_000_000_000, bytes_accessed=8_000_000, transcendentals=800_000
        ),
        name="upsample_refine",
    )(coarse, xm, xp, ym, yp, mm, mp, pm, pp, upmat, band1, band2)


def solution(mesh):
    return jax.shard_map(
        body,
        mesh=mesh,
        in_specs=(P("strike", "dip", None), P(), P(), P()),
        out_specs=P("strike", "dip", None),
        check_vma=False,
    )
```

```python
import jax
import jax.numpy as jnp
from jax import lax
from jax.experimental import pallas as pl
from jax.experimental.pallas import tpu as pltpu
from jax.sharding import PartitionSpec as P

PITCH = 24
ROWS = 20 * PITCH
BAND = 384


def silu(v):
    half = 0.5 * v
    return half + half * jnp.tanh(half)


def prep_kernel(up_ref, first_ref, second_ref, upmat_ref, band1_ref, band2_ref):
    for h1 in range(2):
        for h2 in range(2):
            for h3 in range(2):
                row = (h1 * 4 + h2 * 2 + (1 - h3)) * 32
                for p1 in range(4):
                    for p2 in range(4):
                        k = ((4 * h1 + p1) * 8 + 4 * h2 + p2) * 8 + 4 * h3
                        parts = [up_ref[pl.ds((k + p3) * 32, 32), :] for p3 in range(4)]
                        upmat_ref[pl.ds(row, 32), pl.ds((p1 * 4 + p2) * 128, 128)] = jnp.concatenate(
                            parts, axis=1
                        )
    ci = lax.broadcasted_iota(jnp.int32, (32, 256), 0)
    lane = lax.broadcasted_iota(jnp.int32, (32, 256), 1)
    group = lane // 32
    copies = (lane % 32 == ci).astype(jnp.bfloat16)

    def spread(w_ref, out_ref, lead, shifts):
        rep = jnp.dot(w_ref[...], copies, preferred_element_type=jnp.float32)
        for tap in range(9):
            taps = [rep[(tap * 3 + d) * 32 : (tap * 3 + d + 1) * 32] for d in range(3)]
            for s, shift in enumerate(shifts):
                for a in range(12):
                    block = jnp.zeros((32, 256), jnp.float32)
                    for d in range(3):
                        b = a + shift - d
                        if 0 <= b < 8:
                            block = jnp.where(group == b, taps[d], block)
                    block = block.astype(jnp.bfloat16)
                    rows = pl.ds(tap * BAND + a * 32, 32)
                    if lead:
                        out_ref[s, rows, :] = block
                    else:
                        out_ref[rows, :] = block

    spread(first_ref, band1_ref, False, (-1,))
    spread(second_ref, band2_ref, True, (1, -3))


def main_kernel(
    field, upmat, band1, band2, out, cells, fine, hidden, b1, b2
):
    strike, dip = lax.axis_index("strike"), lax.axis_index("dip")
    one, zero = jnp.float32(1), jnp.float32(0)
    x_lo = jnp.where(strike == 0, zero, one)
    x_hi = jnp.where(strike == lax.axis_size("strike") - 1, zero, one)
    y_lo = jnp.where(dip == 0, zero, one)
    y_hi = jnp.where(dip == lax.axis_size("dip") - 1, zero, one)

    n1, n2 = lax.axis_size("strike"), lax.axis_size("dip")
    spans = (((0, 1), (3, 4)), ((1, 5), (0, 4)), ((5, 6), (0, 1)))
    for s1, ((x0, x1), (u0, u1)) in enumerate(spans):
        for s2, ((y0, y1), (w0, w1)) in enumerate(spans):
            c1 = jnp.clip(strike + (s1 - 1), 0, n1 - 1)
            c2 = jnp.clip(dip + (s2 - 1), 0, n2 - 1)
            scale = (x_lo, one, x_hi)[s1] * (y_lo, one, y_hi)[s2]
            piece = field[c1 * n2 + c2].astype(jnp.float32)[u0:u1, w0:w1]
            cells[x0:x1, y0:y1, :] = piece * scale

    wide = []
    edge = jnp.zeros((40, 32), jnp.float32)
    for h1 in range(2):
        for h2 in range(2):
            window = cells[1 - h1 : 6 - h1, 1 - h2 : 9 - h2, :].reshape(40, 128)
            wide.append(jnp.concatenate([edge, window, edge], axis=1))
    left = jnp.concatenate(
        [
            jnp.concatenate([w[:, 32 * q3 : 32 * q3 + 64] for w in wide], axis=1)
            for q3 in range(5)
        ],
        axis=0,
    ).astype(jnp.bfloat16)

    q2 = lax.broadcasted_iota(jnp.int32, (200, 128), 0) % 8
    q3 = lax.broadcasted_iota(jnp.int32, (200, 128), 0) // 40
    p3 = lax.broadcasted_iota(jnp.int32, (200, 128), 1) // 32
    depth = 4 * q3 + p3
    inside = jnp.where((depth >= 2) & (depth < 18), one, zero)
    low = inside * jnp.where(q2 == 0, y_lo, one)
    high = inside * jnp.where(q2 == 4, y_hi, one)
    for p1 in range(4):
        phase = jnp.dot(left, upmat[:, p1 * 512 : p1 * 512 + 512], preferred_element_type=jnp.float32)
        for p2 in range(4):
            v = silu(phase[:, p2 * 128 : p2 * 128 + 128])
            v = v * (low if p2 < 2 else high)
            v = v.astype(jnp.bfloat16).astype(jnp.float32)
            for c3 in range(5):
                for c1 in range(5):
                    part = v[c3 * 40 + c1 * 8 : c3 * 40 + c1 * 8 + 5]
                    if c1 == 0 and p1 < 2:
                        part = part * x_lo
                    if c1 == 4 and p1 >= 2:
                        part = part * x_hi
                    fine[c3, pl.ds((4 * c1 + p1) * PITCH + p2, 5, stride=4), :] = part

    for dy in range(3):
        for c3 in range(5):
            b1[dy, :, c3 * 128 : c3 * 128 + 128] = fine[c3, pl.ds(dy, ROWS), :].astype(jnp.bfloat16)
    m1 = 18 * PITCH
    row = lax.broadcasted_iota(jnp.int32, (m1, 256), 0)
    i, j = row // PITCH, row % PITCH
    keep = jnp.where(i == 0, x_lo, one) * jnp.where(i == 17, x_hi, one)
    keep = keep * jnp.where(j == 0, y_lo, one) * jnp.where(j == 17, y_hi, one)
    for half in range(2):
        windows = [
            b1[dy, dx * PITCH : dx * PITCH + m1, half * 256 : half * 256 + BAND]
            for dx in range(3)
            for dy in range(3)
        ]
        v = jnp.dot(jnp.concatenate(windows, axis=1), band1[...], preferred_element_type=jnp.float32)
        hidden[:m1, half * 256 : half * 256 + 256] = silu(v) * keep

    for dy in range(3):
        b2[dy] = hidden[pl.ds(dy, m1), :].astype(jnp.bfloat16)
    m2 = 16 * PITCH
    base = jnp.concatenate([fine[c3, pl.ds(2 * PITCH + 2, m2), :] for c3 in range(5)], axis=1)
    for half in range(2):
        windows = [
            b2[dy, dx * PITCH : dx * PITCH + m2, half * 128 : half * 128 + BAND]
            for dx in range(3)
            for dy in range(3)
        ]
        v = jnp.dot(
            jnp.concatenate(windows, axis=1), band2[half], preferred_element_type=jnp.float32
        )
        v = v + base[:, 64 + half * 256 : 320 + half * 256]
        v = v.reshape(16, PITCH, 256)[:, :16].astype(jnp.bfloat16)
        out[:, :, half * 256 : half * 256 + 256] = v


def body(coarse, up_weight, first_weight, second_weight):
    vmem = pl.BlockSpec(memory_space=pltpu.VMEM)
    params = pltpu.CompilerParams(vmem_limit_bytes=48 * 1024 * 1024)

    field = lax.all_gather(coarse, ("strike", "dip"))

    bf16 = jnp.bfloat16
    upmat, band1, band2 = pl.pallas_call(
        prep_kernel,
        out_shape=(
            jax.ShapeDtypeStruct((256, 2048), bf16),
            jax.ShapeDtypeStruct((9 * BAND, 256), bf16),
            jax.ShapeDtypeStruct((2, 9 * BAND, 256), bf16),
        ),
        in_specs=[vmem] * 3,
        out_specs=(vmem,) * 3,
        compiler_params=params,
        cost_estimate=pl.CostEstimate(flops=10_000_000, bytes_accessed=12_000_000, transcendentals=0),
        name="arrange_weights",
    )(up_weight.reshape(512 * 32, 32), first_weight.reshape(864, 32), second_weight.reshape(864, 32))
    return pl.pallas_call(
        main_kernel,
        out_shape=jax.ShapeDtypeStruct((16, 16, 512), bf16),
        in_specs=[vmem] * 4,
        out_specs=vmem,
        scratch_shapes=[
            pltpu.VMEM((6, 16, 128), jnp.float32),
            pltpu.VMEM((5, ROWS + 8, 128), jnp.float32),
            pltpu.VMEM((18 * PITCH + 8, 512), jnp.float32),
            pltpu.VMEM((3, ROWS, 640), bf16),
            pltpu.VMEM((3, 18 * PITCH, 512), bf16),
        ],
        compiler_params=params,
        cost_estimate=pl.CostEstimate(
            flops=4_000_000_000, bytes_accessed=8_000_000, transcendentals=800_000
        ),
        name="upsample_refine",
    )(field, upmat, band1, band2)


def solution(mesh):
    return jax.shard_map(
        body,
        mesh=mesh,
        in_specs=(P("strike", "dip", None), P(), P(), P()),
        out_specs=P("strike", "dip", None),
        check_vma=False,
    )
```

```python
import jax
import jax.numpy as jnp
from jax import lax
from jax.experimental import pallas as pl
from jax.experimental.pallas import tpu as pltpu
from jax.sharding import PartitionSpec as P

PITCH = 24
ROWS = 20 * PITCH
BAND = 384


def silu(v):
    half = 0.5 * v
    return half + half * jnp.tanh(half)


def prep_kernel(
    up_hbm, first_hbm, second_hbm, upmat_ref, band1_ref, band2_ref, up_ref, first_ref, second_ref, sems
):
    fetches = [
        pltpu.make_async_copy(first_hbm, first_ref, sems.at[0]),
        pltpu.make_async_copy(second_hbm, second_ref, sems.at[1]),
    ]
    for part in range(4):
        rows = pl.ds(part * 4096, 4096)
        fetches.append(pltpu.make_async_copy(up_hbm.at[rows], up_ref.at[rows], sems.at[2 + part]))
    for fetch in fetches:
        fetch.start()

    ci = lax.broadcasted_iota(jnp.int32, (32, 256), 0)
    lane = lax.broadcasted_iota(jnp.int32, (32, 256), 1)
    group = lane // 32
    copies = (lane % 32 == ci).astype(jnp.bfloat16)

    def spread(w_ref, out_ref, lead, shifts):
        rep = jnp.dot(w_ref[...], copies, preferred_element_type=jnp.float32)
        for tap in range(9):
            taps = [rep[(tap * 3 + d) * 32 : (tap * 3 + d + 1) * 32] for d in range(3)]
            for s, shift in enumerate(shifts):
                for a in range(12):
                    block = jnp.zeros((32, 256), jnp.float32)
                    for d in range(3):
                        b = a + shift - d
                        if 0 <= b < 8:
                            block = jnp.where(group == b, taps[d], block)
                    block = block.astype(jnp.bfloat16)
                    rows = pl.ds(tap * BAND + a * 32, 32)
                    if lead:
                        out_ref[s, rows, :] = block
                    else:
                        out_ref[rows, :] = block

    fetches[0].wait()
    spread(first_ref, band1_ref, False, (-1,))
    fetches[1].wait()
    spread(second_ref, band2_ref, True, (1, -3))

    for k1 in range(8):
        if k1 % 2 == 0:
            fetches[2 + k1 // 2].wait()
        h1, p1 = divmod(k1, 4)
        for k2 in range(8):
            h2, p2 = divmod(k2, 4)
            for h3 in range(2):
                k = (k1 * 8 + k2) * 8 + 4 * h3
                parts = [up_ref[pl.ds((k + p3) * 32, 32), :] for p3 in range(4)]
                row = (h1 * 4 + h2 * 2 + (1 - h3)) * 32
                upmat_ref[pl.ds(row, 32), pl.ds((p1 * 4 + p2) * 128, 128)] = jnp.concatenate(
                    parts, axis=1
                )


def main_kernel(
    own, strike_a, strike_b, upmat, band1, band2, out, cells, fine, hidden, b1, b2
):
    strike, dip = lax.axis_index("strike"), lax.axis_index("dip")
    one, zero = jnp.float32(1), jnp.float32(0)
    x_lo = jnp.where(strike == 0, zero, one)
    x_hi = jnp.where(strike == lax.axis_size("strike") - 1, zero, one)
    y_lo = jnp.where(dip == 0, zero, one)
    y_hi = jnp.where(dip == lax.axis_size("dip") - 1, zero, one)

    x_even, y_even = strike % 2 == 0, dip % 2 == 0
    below_y, above_y = jnp.where(y_even, 8, 4), jnp.where(y_even, 4, 8)

    def put(x0, x1, block):
        cells[x0:x1, 1:5, :] = block(0)
        cells[x0:x1, 0:1, :] = block(below_y)[:, 3:4]
        cells[x0:x1, 5:6, :] = block(above_y)[:, 0:1]

    def read(ref, first, count):
        return ref[pl.ds(first, count)].astype(jnp.float32)

    put(0, 1, lambda o: jnp.where(x_even, read(strike_b, o + 3, 1), read(strike_a, o + 3, 1)))
    put(1, 5, lambda o: read(own, o, 4))
    put(5, 6, lambda o: jnp.where(x_even, read(strike_a, o, 1), read(strike_b, o, 1)))

    wide = []
    edge = jnp.zeros((40, 32), jnp.float32)
    for h1 in range(2):
        for h2 in range(2):
            window = cells[1 - h1 : 6 - h1, 1 - h2 : 9 - h2, :].reshape(40, 128)
            wide.append(jnp.concatenate([edge, window, edge], axis=1))
    left = jnp.concatenate(
        [
            jnp.concatenate([w[:, 32 * q3 : 32 * q3 + 64] for w in wide], axis=1)
            for q3 in range(5)
        ],
        axis=0,
    ).astype(jnp.bfloat16)

    q2 = lax.broadcasted_iota(jnp.int32, (200, 128), 0) % 8
    q3 = lax.broadcasted_iota(jnp.int32, (200, 128), 0) // 40
    p3 = lax.broadcasted_iota(jnp.int32, (200, 128), 1) // 32
    depth = 4 * q3 + p3
    inside = jnp.where((depth >= 2) & (depth < 18), one, zero)
    low = inside * jnp.where(q2 == 0, y_lo, one)
    high = inside * jnp.where(q2 == 4, y_hi, one)
    for p1 in range(4):
        phase = jnp.dot(left, upmat[:, p1 * 512 : p1 * 512 + 512], preferred_element_type=jnp.float32)
        for p2 in range(4):
            v = silu(phase[:, p2 * 128 : p2 * 128 + 128])
            v = v * (low if p2 < 2 else high)
            v = v.astype(jnp.bfloat16).astype(jnp.float32)
            for c3 in range(5):
                for c1 in range(5):
                    part = v[c3 * 40 + c1 * 8 : c3 * 40 + c1 * 8 + 5]
                    if c1 == 0 and p1 < 2:
                        part = part * x_lo
                    if c1 == 4 and p1 >= 2:
                        part = part * x_hi
                    fine[c3, pl.ds((4 * c1 + p1) * PITCH + p2, 5, stride=4), :] = part

    for dy in range(3):
        for c3 in range(5):
            b1[dy, :, c3 * 128 : c3 * 128 + 128] = fine[c3, pl.ds(dy, ROWS), :].astype(jnp.bfloat16)
    m1 = 18 * PITCH
    row = lax.broadcasted_iota(jnp.int32, (m1, 256), 0)
    i, j = row // PITCH, row % PITCH
    keep = jnp.where(i == 0, x_lo, one) * jnp.where(i == 17, x_hi, one)
    keep = keep * jnp.where(j == 0, y_lo, one) * jnp.where(j == 17, y_hi, one)
    for half in range(2):
        windows = [
            b1[dy, dx * PITCH : dx * PITCH + m1, half * 256 : half * 256 + BAND]
            for dx in range(3)
            for dy in range(3)
        ]
        v = jnp.dot(jnp.concatenate(windows, axis=1), band1[...], preferred_element_type=jnp.float32)
        hidden[:m1, half * 256 : half * 256 + 256] = silu(v) * keep

    for dy in range(3):
        b2[dy] = hidden[pl.ds(dy, m1), :].astype(jnp.bfloat16)
    m2 = 16 * PITCH
    base = jnp.concatenate([fine[c3, pl.ds(2 * PITCH + 2, m2), :] for c3 in range(5)], axis=1)
    for half in range(2):
        windows = [
            b2[dy, dx * PITCH : dx * PITCH + m2, half * 128 : half * 128 + BAND]
            for dx in range(3)
            for dy in range(3)
        ]
        v = jnp.dot(
            jnp.concatenate(windows, axis=1), band2[half], preferred_element_type=jnp.float32
        )
        v = v + base[:, 64 + half * 256 : 320 + half * 256]
        v = v.reshape(16, PITCH, 256)[:, :16].astype(jnp.bfloat16)
        out[:, :, half * 256 : half * 256 + 256] = v


def swapped(block, axis):
    size = lax.axis_size(axis)
    for first in (0, 1):
        pairs = [(i, i + 1) for i in range(first, size - 1, 2)]
        yield lax.ppermute(block, axis, pairs + [(j, i) for i, j in pairs])


def body(coarse, up_weight, first_weight, second_weight):
    vmem = pl.BlockSpec(memory_space=pltpu.VMEM)
    params = pltpu.CompilerParams(vmem_limit_bytes=48 * 1024 * 1024)

    own = jnp.concatenate([coarse, *swapped(coarse, "dip")], axis=0)
    strike_a, strike_b = swapped(own, "strike")

    bf16 = jnp.bfloat16
    upmat, band1, band2 = pl.pallas_call(
        prep_kernel,
        out_shape=(
            jax.ShapeDtypeStruct((256, 2048), bf16),
            jax.ShapeDtypeStruct((9 * BAND, 256), bf16),
            jax.ShapeDtypeStruct((2, 9 * BAND, 256), bf16),
        ),
        in_specs=[pl.BlockSpec(memory_space=pltpu.HBM)] * 3,
        out_specs=(vmem,) * 3,
        scratch_shapes=[
            pltpu.VMEM((512 * 32, 32), bf16),
            pltpu.VMEM((864, 32), bf16),
            pltpu.VMEM((864, 32), bf16),
            pltpu.SemaphoreType.DMA((6,)),
        ],
        compiler_params=params,
        cost_estimate=pl.CostEstimate(flops=10_000_000, bytes_accessed=12_000_000, transcendentals=0),
        name="arrange_weights",
    )(up_weight.reshape(512 * 32, 32), first_weight.reshape(864, 32), second_weight.reshape(864, 32))
    return pl.pallas_call(
        main_kernel,
        out_shape=jax.ShapeDtypeStruct((16, 16, 512), bf16),
        in_specs=[vmem] * 6,
        out_specs=vmem,
        scratch_shapes=[
            pltpu.VMEM((6, 16, 128), jnp.float32),
            pltpu.VMEM((5, ROWS + 8, 128), jnp.float32),
            pltpu.VMEM((18 * PITCH + 8, 512), jnp.float32),
            pltpu.VMEM((3, ROWS, 640), bf16),
            pltpu.VMEM((3, 18 * PITCH, 512), bf16),
        ],
        compiler_params=params,
        cost_estimate=pl.CostEstimate(
            flops=4_000_000_000, bytes_accessed=8_000_000, transcendentals=800_000
        ),
        name="upsample_refine",
    )(own, strike_a, strike_b, upmat, band1, band2)


def solution(mesh):
    return jax.shard_map(
        body,
        mesh=mesh,
        in_specs=(P("strike", "dip", None), P(), P(), P()),
        out_specs=P("strike", "dip", None),
        check_vma=False,
    )
```

```python
import jax
import jax.numpy as jnp
from jax import lax
from jax.experimental import pallas as pl
from jax.experimental.pallas import tpu as pltpu
from jax.sharding import PartitionSpec as P

GROUPS = 4
PAIRS = 10
STEP = GROUPS * PAIRS
ORDER = ((0, 1, 2, 3), (1, 0, 3, 2))
BESIDE = ((0, 4), (1, 4), (1, -1), (0, -1))
WINDOW = 3 * 2 * 384


def silu(v):
    half = 0.5 * v
    return half + half * jnp.tanh(half)


def prep_kernel(
    up_hbm, first_hbm, second_hbm, upmat_ref, band1_ref, band2_ref, up_ref, first_ref, second_ref, sems
):
    fetches = [
        pltpu.make_async_copy(first_hbm, first_ref, sems.at[0]),
        pltpu.make_async_copy(second_hbm, second_ref, sems.at[1]),
    ]
    for part in range(4):
        rows = pl.ds(part * 4096, 4096)
        fetches.append(pltpu.make_async_copy(up_hbm.at[rows], up_ref.at[rows], sems.at[2 + part]))
    for fetch in fetches:
        fetch.start()

    ci = lax.broadcasted_iota(jnp.int32, (32, 128), 0)
    lane = lax.broadcasted_iota(jnp.int32, (32, 128), 1)
    group = lane // 32
    copies = (lane % 32 == ci).astype(jnp.bfloat16)

    def arrange(w_ref, band_ref, out_order):
        rep = jnp.dot(w_ref[...], copies, preferred_element_type=jnp.float32)
        for d1 in range(3):
            for dj in range(2):
                cells = [(0, z) for z in ORDER[0]] + [(1, z) for z in ORDER[1]] + list(BESIDE)
                for n, (side, z_in) in enumerate(cells):
                    row = (d1 * 2 + dj) * 384 + n * 32
                    for o in range(2):
                        block = jnp.zeros((32, 128), jnp.float32)
                        d2 = 2 * dj + side - o
                        for d3 in range(3):
                            z_out = z_in - d3 + 1
                            if 0 <= d2 < 3 and 0 <= z_out < 4:
                                tap = ((d1 * 3 + d2) * 3 + d3) * 32
                                here = group == out_order[o].index(z_out)
                                block = jnp.where(here, rep[tap : tap + 32], block)
                        band_ref[pl.ds(row, 32), pl.ds(o * 128, 128)] = block.astype(jnp.bfloat16)

    fetches[0].wait()
    arrange(first_ref, band1_ref, ORDER)
    fetches[1].wait()
    arrange(second_ref, band2_ref, (ORDER[0], ORDER[0]))
    r = lax.broadcasted_iota(jnp.int32, (256, 256), 0)
    c = lax.broadcasted_iota(jnp.int32, (256, 256), 1)
    swap = jnp.where((r // 32) % 2 == 0, r + 32, r - 32)
    band2_ref[pl.ds(WINDOW, 256), :] = (jnp.where(r < 128, r, swap) == c).astype(jnp.bfloat16)

    for k1 in range(8):
        if k1 % 2 == 0:
            fetches[2 + k1 // 2].wait()
        h1, p1 = divmod(k1, 4)
        for k2 in range(8):
            h2, p2 = divmod(k2, 4)
            for h3 in range(2):
                k = (k1 * 8 + k2) * 8 + 4 * h3
                parts = [up_ref[pl.ds((k + (z + 2) % 4) * 32, 32), :] for z in ORDER[p2 % 2]]
                row = (h1 * 4 + h2 * 2 + (1 - h3)) * 32
                upmat_ref[pl.ds(row, 32), pl.ds((p1 * 4 + p2) * 128, 128)] = jnp.concatenate(
                    parts, axis=1
                )


def main_kernel(
    own, strike_a, strike_b, upmat, band1, band2, out, cells, fine, hidden, b1, b2, result, woven
):
    strike, dip = lax.axis_index("strike"), lax.axis_index("dip")
    one, zero = jnp.float32(1), jnp.float32(0)
    x_lo = jnp.where(strike == 0, zero, one)
    x_hi = jnp.where(strike == lax.axis_size("strike") - 1, zero, one)
    y_lo = jnp.where(dip == 0, zero, one)
    y_hi = jnp.where(dip == lax.axis_size("dip") - 1, zero, one)

    x_even, y_even = strike % 2 == 0, dip % 2 == 0
    below_y, above_y = jnp.where(y_even, 8, 4), jnp.where(y_even, 4, 8)

    def put(x0, x1, block):
        cells[x0:x1, 1:5, :] = block(0)
        cells[x0:x1, 0:1, :] = block(below_y)[:, 3:4]
        cells[x0:x1, 5:6, :] = block(above_y)[:, 0:1]

    def read(ref, first, count):
        return ref[pl.ds(first, count)].astype(jnp.float32)

    put(0, 1, lambda o: jnp.where(x_even, read(strike_b, o + 3, 1), read(strike_a, o + 3, 1)))
    put(1, 5, lambda o: read(own, o, 4))
    put(5, 6, lambda o: jnp.where(x_even, read(strike_a, o, 1), read(strike_b, o, 1)))

    wide = []
    edge = jnp.zeros((40, 32), jnp.float32)
    for h1 in range(2):
        for h2 in range(2):
            window = cells[1 - h1 : 6 - h1, 1 - h2 : 9 - h2, :].reshape(40, 128)
            wide.append(jnp.concatenate([edge, window, edge], axis=1))
    left = jnp.concatenate(
        [
            jnp.concatenate([w[:, 32 * q3 : 32 * q3 + 64] for w in wide], axis=1)
            for q3 in range(5)
        ],
        axis=0,
    ).astype(jnp.bfloat16)

    lane = lax.broadcasted_iota(jnp.int32, (40, 128), 1)
    q2 = lax.broadcasted_iota(jnp.int32, (40, 128), 0) % 8
    outer = (lane < 32) | (lane >= 96)
    front = lane < 64
    low = jnp.where(q2 == 0, y_lo, one)
    high = jnp.where(q2 == 4, y_hi, one)
    none = jnp.zeros((40, 128), jnp.float32)
    for p1 in range(4):
        phase = jnp.dot(left, upmat[:, p1 * 512 : p1 * 512 + 512], preferred_element_type=jnp.float32)
        for pp in range(2):
            tiles = [[], []]
            for side in range(2):
                p2 = 2 * pp + side
                v = phase[:, p2 * 128 : p2 * 128 + 128]
                for g in range(GROUPS):
                    t = jnp.where(front, v[g * 40 : g * 40 + 40], v[g * 40 + 40 : g * 40 + 80])
                    t = silu(t) * (low if pp == 0 else high)
                    tiles[side].append(t.astype(jnp.bfloat16).astype(jnp.float32))
            merged = [jnp.where(outer, tiles[0][g], tiles[1][g]) for g in range(GROUPS)]
            merged = [none] + merged + [none]
            for g in range(GROUPS):
                beside = jnp.where(front, merged[g + 2], merged[g])
                for n, t in enumerate((tiles[0][g], tiles[1][g], beside)):
                    for q1 in range(5):
                        part = t[q1 * 8 : q1 * 8 + 5]
                        if q1 == 0 and p1 < 2:
                            part = part * x_lo
                        if q1 == 4 and p1 >= 2:
                            part = part * x_hi
                        at = (4 * q1 + p1) * STEP + g * PAIRS + pp
                        fine[n, pl.ds(at, 5, stride=2), :] = part

    for dj in range(2):
        for n in range(3):
            b1[dj, :, n * 128 : n * 128 + 128] = fine[n, pl.ds(dj, 20 * STEP), :].astype(jnp.bfloat16)
    m1 = 18 * STEP
    windows = [b1[dj, dx * STEP : dx * STEP + m1, :] for dx in range(3) for dj in range(2)]
    v = silu(
        jnp.dot(jnp.concatenate(windows, axis=1), band1[...], preferred_element_type=jnp.float32)
    )
    row = lax.broadcasted_iota(jnp.int32, (m1, 128), 0)
    lane = lax.broadcasted_iota(jnp.int32, (m1, 128), 1)
    i, g, j = row // STEP, (row // PAIRS) % GROUPS, row % PAIRS
    keep = jnp.where(i == 0, x_lo, one) * jnp.where(i == 17, x_hi, one)
    v0 = v[:, :128] * (keep * jnp.where(j == 0, y_lo, one))
    v1 = v[:, 128:] * (keep * jnp.where(j == 8, y_hi, one))
    hidden[0, 16 : 16 + m1, :] = v0
    hidden[1, 16 : 16 + m1, :] = v1
    hidden[2, 16 : 16 + m1, :] = jnp.where((lane < 32) | (lane >= 96), v0, v1)

    for dj in range(2):
        for n in range(2):
            b2[dj, :, n * 128 : n * 128 + 128] = hidden[n, pl.ds(16 + dj, m1), :].astype(jnp.bfloat16)
        above = jnp.where(g == GROUPS - 1, zero, hidden[2, pl.ds(16 + dj + PAIRS, m1), :])
        below = jnp.where(g == 0, zero, hidden[2, pl.ds(16 + dj - PAIRS, m1), :])
        b2[dj, :, 256:384] = jnp.where(lane < 64, above, below).astype(jnp.bfloat16)
    m2 = 16 * STEP
    windows = [b2[dj, dx * STEP : dx * STEP + m2, :] for dx in range(3) for dj in range(2)]
    windows.append(b1[1, 2 * STEP : 2 * STEP + m2, :256])
    v = jnp.dot(jnp.concatenate(windows, axis=1), band2[...], preferred_element_type=jnp.float32)
    for o in range(2):
        result[o] = v[:, o * 128 : o * 128 + 128]
    for x in range(16):
        for g in range(GROUPS):
            for o in range(2):
                cells8 = result[o, pl.ds(x * STEP + g * PAIRS, 8), :]
                woven[g, pl.ds(x * 16 + o, 8, stride=2), :] = cells8
    for g in range(GROUPS):
        out[:, :, g * 128 : g * 128 + 128] = woven[g].reshape(16, 16, 128).astype(jnp.bfloat16)


def swapped(block, axis):
    size = lax.axis_size(axis)
    for first in (0, 1):
        pairs = [(i, i + 1) for i in range(first, size - 1, 2)]
        yield lax.ppermute(block, axis, pairs + [(j, i) for i, j in pairs])


def body(coarse, up_weight, first_weight, second_weight):
    vmem = pl.BlockSpec(memory_space=pltpu.VMEM)
    params = pltpu.CompilerParams(vmem_limit_bytes=48 * 1024 * 1024)

    own = jnp.concatenate([coarse, *swapped(coarse, "dip")], axis=0)
    strike_a, strike_b = swapped(own, "strike")

    bf16 = jnp.bfloat16
    upmat, band1, band2 = pl.pallas_call(
        prep_kernel,
        out_shape=(
            jax.ShapeDtypeStruct((256, 2048), bf16),
            jax.ShapeDtypeStruct((WINDOW, 256), bf16),
            jax.ShapeDtypeStruct((WINDOW + 256, 256), bf16),
        ),
        in_specs=[pl.BlockSpec(memory_space=pltpu.HBM)] * 3,
        out_specs=(vmem,) * 3,
        scratch_shapes=[
            pltpu.VMEM((512 * 32, 32), bf16),
            pltpu.VMEM((864, 32), bf16),
            pltpu.VMEM((864, 32), bf16),
            pltpu.SemaphoreType.DMA((6,)),
        ],
        compiler_params=params,
        cost_estimate=pl.CostEstimate(flops=10_000_000, bytes_accessed=12_000_000, transcendentals=0),
        name="arrange_weights",
    )(up_weight.reshape(512 * 32, 32), first_weight.reshape(864, 32), second_weight.reshape(864, 32))
    return pl.pallas_call(
        main_kernel,
        out_shape=jax.ShapeDtypeStruct((16, 16, 512), bf16),
        in_specs=[vmem] * 6,
        out_specs=vmem,
        scratch_shapes=[
            pltpu.VMEM((6, 16, 128), jnp.float32),
            pltpu.VMEM((3, 20 * STEP + 8, 128), jnp.float32),
            pltpu.VMEM((3, 18 * STEP + 32, 128), jnp.float32),
            pltpu.VMEM((2, 20 * STEP, 384), bf16),
            pltpu.VMEM((2, 18 * STEP, 384), bf16),
            pltpu.VMEM((2, 16 * STEP, 128), jnp.float32),
            pltpu.VMEM((GROUPS, 256, 128), jnp.float32),
        ],
        compiler_params=params,
        cost_estimate=pl.CostEstimate(
            flops=2_000_000_000, bytes_accessed=8_000_000, transcendentals=800_000
        ),
        name="upsample_refine",
    )(own, strike_a, strike_b, upmat, band1, band2)


def solution(mesh):
    return jax.shard_map(
        body,
        mesh=mesh,
        in_specs=(P("strike", "dip", None), P(), P(), P()),
        out_specs=P("strike", "dip", None),
        check_vma=False,
    )
```

```python
import jax
import jax.numpy as jnp
from jax import lax
from jax.experimental import pallas as pl
from jax.experimental.pallas import tpu as pltpu
from jax.sharding import PartitionSpec as P

GROUPS = 4
PAIRS = 10
STEP = GROUPS * PAIRS
ORDER = ((0, 1, 2, 3), (1, 0, 3, 2))
BESIDE = ((0, 4), (1, 4), (1, -1), (0, -1))
WINDOW = 3 * 2 * 384
LIMIT = 50 * 1024 * 1024


def silu(v):
    half = 0.5 * v
    return half + half * jnp.tanh(half)


def up_kernel(up_hbm, upmat_ref, token_ref, up_ref, sems):
    fetches = []
    for part in range(4):
        rows = pl.ds(part * 4096, 4096)
        fetches.append(pltpu.make_async_copy(up_hbm.at[rows], up_ref.at[rows], sems.at[part]))
    for fetch in fetches:
        fetch.start()
    token_ref[...] = jnp.zeros((8, 128), jnp.float32)

    for k1 in range(8):
        if k1 % 2 == 0:
            fetches[k1 // 2].wait()
        h1, p1 = divmod(k1, 4)
        for k2 in range(8):
            h2, p2 = divmod(k2, 4)
            for h3 in range(2):
                k = (k1 * 8 + k2) * 8 + 4 * h3
                parts = [up_ref[pl.ds((k + (z + 2) % 4) * 32, 32), :] for z in ORDER[p2 % 2]]
                row = (h1 * 4 + h2 * 2 + (1 - h3)) * 32
                upmat_ref[pl.ds(row, 32), pl.ds((p1 * 4 + p2) * 128, 128)] = jnp.concatenate(
                    parts, axis=1
                )


def band_kernel(first_ref, second_ref, band1_ref, band2_ref):
    ci = lax.broadcasted_iota(jnp.int32, (32, 128), 0)
    lane = lax.broadcasted_iota(jnp.int32, (32, 128), 1)
    group = lane // 32
    copies = (lane % 32 == ci).astype(jnp.bfloat16)

    def arrange(w_ref, band_ref, out_order):
        rep = jnp.dot(w_ref[...], copies, preferred_element_type=jnp.float32)
        for d1 in range(3):
            for dj in range(2):
                cells = [(0, z) for z in ORDER[0]] + [(1, z) for z in ORDER[1]] + list(BESIDE)
                for n, (side, z_in) in enumerate(cells):
                    row = (d1 * 2 + dj) * 384 + n * 32
                    for o in range(2):
                        block = jnp.zeros((32, 128), jnp.float32)
                        d2 = 2 * dj + side - o
                        for d3 in range(3):
                            z_out = z_in - d3 + 1
                            if 0 <= d2 < 3 and 0 <= z_out < 4:
                                tap = ((d1 * 3 + d2) * 3 + d3) * 32
                                here = group == out_order[o].index(z_out)
                                block = jnp.where(here, rep[tap : tap + 32], block)
                        band_ref[pl.ds(row, 32), pl.ds(o * 128, 128)] = block.astype(jnp.bfloat16)

    arrange(first_ref, band1_ref, ORDER)
    arrange(second_ref, band2_ref, (ORDER[0], ORDER[0]))
    r = lax.broadcasted_iota(jnp.int32, (256, 256), 0)
    c = lax.broadcasted_iota(jnp.int32, (256, 256), 1)
    swap = jnp.where((r // 32) % 2 == 0, r + 32, r - 32)
    band2_ref[pl.ds(WINDOW, 256), :] = (jnp.where(r < 128, r, swap) == c).astype(jnp.bfloat16)


def pack_kernel(coarse, dip_b, dip_a, token, own):
    own[0:4] = coarse[...]
    own[4:8] = dip_a[...]
    own[8:12] = dip_b[...]


def main_kernel(
    own, strike_a, strike_b, upmat, band1, band2, out, cells, fine, hidden, b1, b2, result, woven
):
    strike, dip = lax.axis_index("strike"), lax.axis_index("dip")
    one, zero = jnp.float32(1), jnp.float32(0)
    x_lo = jnp.where(strike == 0, zero, one)
    x_hi = jnp.where(strike == lax.axis_size("strike") - 1, zero, one)
    y_lo = jnp.where(dip == 0, zero, one)
    y_hi = jnp.where(dip == lax.axis_size("dip") - 1, zero, one)

    x_even, y_even = strike % 2 == 0, dip % 2 == 0
    below_y, above_y = jnp.where(y_even, 8, 4), jnp.where(y_even, 4, 8)

    def put(x0, x1, block):
        cells[x0:x1, 1:5, :] = block(0)
        cells[x0:x1, 0:1, :] = block(below_y)[:, 3:4]
        cells[x0:x1, 5:6, :] = block(above_y)[:, 0:1]

    def read(ref, first, count):
        return ref[pl.ds(first, count)].astype(jnp.float32)

    put(0, 1, lambda o: jnp.where(x_even, read(strike_b, o + 3, 1), read(strike_a, o + 3, 1)))
    put(1, 5, lambda o: read(own, o, 4))
    put(5, 6, lambda o: jnp.where(x_even, read(strike_a, o, 1), read(strike_b, o, 1)))

    wide = []
    edge = jnp.zeros((40, 32), jnp.float32)
    for h1 in range(2):
        for h2 in range(2):
            window = cells[1 - h1 : 6 - h1, 1 - h2 : 9 - h2, :].reshape(40, 128)
            wide.append(jnp.concatenate([edge, window, edge], axis=1))
    left = jnp.concatenate(
        [
            jnp.concatenate([w[:, 32 * q3 : 32 * q3 + 64] for w in wide], axis=1)
            for q3 in range(5)
        ],
        axis=0,
    ).astype(jnp.bfloat16)

    lane = lax.broadcasted_iota(jnp.int32, (40, 128), 1)
    q2 = lax.broadcasted_iota(jnp.int32, (40, 128), 0) % 8
    outer = (lane < 32) | (lane >= 96)
    front = lane < 64
    low = jnp.where(q2 == 0, y_lo, one)
    high = jnp.where(q2 == 4, y_hi, one)
    none = jnp.zeros((40, 128), jnp.float32)
    for p1 in range(4):
        phase = jnp.dot(left, upmat[:, p1 * 512 : p1 * 512 + 512], preferred_element_type=jnp.float32)
        for pp in range(2):
            tiles = [[], []]
            for side in range(2):
                p2 = 2 * pp + side
                v = phase[:, p2 * 128 : p2 * 128 + 128]
                for g in range(GROUPS):
                    t = jnp.where(front, v[g * 40 : g * 40 + 40], v[g * 40 + 40 : g * 40 + 80])
                    t = silu(t) * (low if pp == 0 else high)
                    tiles[side].append(t.astype(jnp.bfloat16).astype(jnp.float32))
            merged = [jnp.where(outer, tiles[0][g], tiles[1][g]) for g in range(GROUPS)]
            merged = [none] + merged + [none]
            for g in range(GROUPS):
                beside = jnp.where(front, merged[g + 2], merged[g])
                for n, t in enumerate((tiles[0][g], tiles[1][g], beside)):
                    for q1 in range(5):
                        part = t[q1 * 8 : q1 * 8 + 5]
                        if q1 == 0 and p1 < 2:
                            part = part * x_lo
                        if q1 == 4 and p1 >= 2:
                            part = part * x_hi
                        at = (4 * q1 + p1) * STEP + g * PAIRS + pp
                        fine[n, pl.ds(at, 5, stride=2), :] = part

    for dj in range(2):
        for n in range(3):
            b1[dj, :, n * 128 : n * 128 + 128] = fine[n, pl.ds(dj, 20 * STEP), :].astype(jnp.bfloat16)
    m1 = 18 * STEP
    windows = [b1[dj, dx * STEP : dx * STEP + m1, :] for dx in range(3) for dj in range(2)]
    v = silu(
        jnp.dot(jnp.concatenate(windows, axis=1), band1[...], preferred_element_type=jnp.float32)
    )
    row = lax.broadcasted_iota(jnp.int32, (m1, 128), 0)
    lane = lax.broadcasted_iota(jnp.int32, (m1, 128), 1)
    i, g, j = row // STEP, (row // PAIRS) % GROUPS, row % PAIRS
    keep = jnp.where(i == 0, x_lo, one) * jnp.where(i == 17, x_hi, one)
    v0 = v[:, :128] * (keep * jnp.where(j == 0, y_lo, one))
    v1 = v[:, 128:] * (keep * jnp.where(j == 8, y_hi, one))
    hidden[0, 16 : 16 + m1, :] = v0
    hidden[1, 16 : 16 + m1, :] = v1
    hidden[2, 16 : 16 + m1, :] = jnp.where((lane < 32) | (lane >= 96), v0, v1)

    for dj in range(2):
        for n in range(2):
            b2[dj, :, n * 128 : n * 128 + 128] = hidden[n, pl.ds(16 + dj, m1), :].astype(jnp.bfloat16)
        above = jnp.where(g == GROUPS - 1, zero, hidden[2, pl.ds(16 + dj + PAIRS, m1), :])
        below = jnp.where(g == 0, zero, hidden[2, pl.ds(16 + dj - PAIRS, m1), :])
        b2[dj, :, 256:384] = jnp.where(lane < 64, above, below).astype(jnp.bfloat16)
    m2 = 16 * STEP
    windows = [b2[dj, dx * STEP : dx * STEP + m2, :] for dx in range(3) for dj in range(2)]
    windows.append(b1[1, 2 * STEP : 2 * STEP + m2, :256])
    v = jnp.dot(jnp.concatenate(windows, axis=1), band2[...], preferred_element_type=jnp.float32)
    for o in range(2):
        result[o] = v[:, o * 128 : o * 128 + 128]
    for x in range(16):
        for g in range(GROUPS):
            for o in range(2):
                cells8 = result[o, pl.ds(x * STEP + g * PAIRS, 8), :]
                woven[g, pl.ds(x * 16 + o, 8, stride=2), :] = cells8
    for g in range(GROUPS):
        out[:, :, g * 128 : g * 128 + 128] = woven[g].reshape(16, 16, 128).astype(jnp.bfloat16)


def swapped(block, axis):
    size = lax.axis_size(axis)
    for first in (0, 1):
        pairs = [(i, i + 1) for i in range(first, size - 1, 2)]
        yield lax.ppermute(block, axis, pairs + [(j, i) for i, j in pairs])


def body(coarse, up_weight, first_weight, second_weight):
    vmem = pl.BlockSpec(memory_space=pltpu.VMEM)
    params = pltpu.CompilerParams(vmem_limit_bytes=32 * 1024 * 1024)

    bf16 = jnp.bfloat16
    shape = jax.ShapeDtypeStruct
    dip_a, dip_b = swapped(coarse, "dip")
    upmat, token = pl.pallas_call(
        up_kernel,
        out_shape=(shape((256, 2048), bf16), shape((8, 128), jnp.float32)),
        in_specs=[pl.BlockSpec(memory_space=pltpu.HBM)],
        out_specs=(vmem, vmem),
        scratch_shapes=[pltpu.VMEM((512 * 32, 32), bf16), pltpu.SemaphoreType.DMA((4,))],
        compiler_params=pltpu.CompilerParams(vmem_limit_bytes=LIMIT),
        cost_estimate=pl.CostEstimate(flops=5_000_000, bytes_accessed=5_000_000, transcendentals=0),
        name="arrange_up",
    )(up_weight.reshape(512 * 32, 32))
    own = pl.pallas_call(
        pack_kernel,
        out_shape=shape((12, 4, 128), bf16),
        in_specs=[vmem] * 4,
        out_specs=vmem,
        name="pack",
    )(coarse, dip_b, dip_a, token)
    strike_a, strike_b = swapped(own, "strike")
    band1, band2 = pl.pallas_call(
        band_kernel,
        out_shape=(shape((WINDOW, 256), bf16), shape((WINDOW + 256, 256), bf16)),
        in_specs=[vmem] * 2,
        out_specs=(vmem, vmem),
        compiler_params=pltpu.CompilerParams(vmem_limit_bytes=16 * 1024 * 1024),
        cost_estimate=pl.CostEstimate(flops=5_000_000, bytes_accessed=5_000_000, transcendentals=0),
        name="arrange_bands",
    )(first_weight.reshape(864, 32), second_weight.reshape(864, 32))
    return pl.pallas_call(
        main_kernel,
        out_shape=jax.ShapeDtypeStruct((16, 16, 512), bf16),
        in_specs=[vmem] * 6,
        out_specs=vmem,
        scratch_shapes=[
            pltpu.VMEM((6, 16, 128), jnp.float32),
            pltpu.VMEM((3, 20 * STEP + 8, 128), jnp.float32),
            pltpu.VMEM((3, 18 * STEP + 32, 128), jnp.float32),
            pltpu.VMEM((2, 20 * STEP, 384), bf16),
            pltpu.VMEM((2, 18 * STEP, 384), bf16),
            pltpu.VMEM((2, 16 * STEP, 128), jnp.float32),
            pltpu.VMEM((GROUPS, 256, 128), jnp.float32),
        ],
        compiler_params=params,
        cost_estimate=pl.CostEstimate(
            flops=2_000_000_000, bytes_accessed=8_000_000, transcendentals=800_000
        ),
        name="upsample_refine",
    )(own, strike_a, strike_b, upmat, band1, band2)


def solution(mesh):
    return jax.shard_map(
        body,
        mesh=mesh,
        in_specs=(P("strike", "dip", None), P(), P(), P()),
        out_specs=P("strike", "dip", None),
        check_vma=False,
    )
```

```python
import jax
import jax.numpy as jnp
from jax import lax
from jax.experimental import pallas as pl
from jax.experimental.pallas import tpu as pltpu
from jax.sharding import PartitionSpec as P

GROUPS = 4
PAIRS = 10
STEP = GROUPS * PAIRS
ORDER = ((0, 1, 2, 3), (1, 0, 3, 2))
BESIDE = ((0, 4), (1, 4), (1, -1), (0, -1))
WINDOW = 3 * 2 * 384
LIMIT = 50 * 1024 * 1024


def silu(v):
    half = 0.5 * v
    return half + half * jnp.tanh(half)


def up_kernel(up_hbm, upmat_ref, token_ref, up_ref, sems):
    fetches = []
    for part in range(4):
        rows = pl.ds(part * 4096, 4096)
        fetches.append(pltpu.make_async_copy(up_hbm.at[rows], up_ref.at[rows], sems.at[part]))
    for fetch in fetches:
        fetch.start()
    token_ref[...] = jnp.zeros((8, 128), jnp.float32)

    for k1 in range(8):
        if k1 % 2 == 0:
            fetches[k1 // 2].wait()
        h1, p1 = divmod(k1, 4)
        for k2 in range(8):
            h2, p2 = divmod(k2, 4)
            for h3 in range(2):
                k = (k1 * 8 + k2) * 8 + 4 * h3
                parts = [up_ref[pl.ds((k + (z + 2) % 4) * 32, 32), :] for z in ORDER[p2 % 2]]
                row = (h1 * 4 + h2 * 2 + (1 - h3)) * 32
                upmat_ref[pl.ds(row, 32), pl.ds((p1 * 4 + p2) * 128, 128)] = jnp.concatenate(
                    parts, axis=1
                )


def band_kernel(first_ref, second_ref, band1_ref, band2_ref):
    ci = lax.broadcasted_iota(jnp.int32, (32, 128), 0)
    lane = lax.broadcasted_iota(jnp.int32, (32, 128), 1)
    group = lane // 32
    copies = (lane % 32 == ci).astype(jnp.bfloat16)

    def arrange(w_ref, band_ref, out_order):
        rep = jnp.dot(w_ref[...], copies, preferred_element_type=jnp.float32)
        for d1 in range(3):
            for dj in range(2):
                cells = [(0, z) for z in ORDER[0]] + [(1, z) for z in ORDER[1]] + list(BESIDE)
                for n, (side, z_in) in enumerate(cells):
                    row = (d1 * 2 + dj) * 384 + n * 32
                    for o in range(2):
                        block = jnp.zeros((32, 128), jnp.float32)
                        d2 = 2 * dj + side - o
                        for d3 in range(3):
                            z_out = z_in - d3 + 1
                            if 0 <= d2 < 3 and 0 <= z_out < 4:
                                tap = ((d1 * 3 + d2) * 3 + d3) * 32
                                here = group == out_order[o].index(z_out)
                                block = jnp.where(here, rep[tap : tap + 32], block)
                        band_ref[pl.ds(row, 32), pl.ds(o * 128, 128)] = block.astype(jnp.bfloat16)

    arrange(first_ref, band1_ref, ORDER)
    arrange(second_ref, band2_ref, (ORDER[0], ORDER[0]))
    r = lax.broadcasted_iota(jnp.int32, (256, 256), 0)
    c = lax.broadcasted_iota(jnp.int32, (256, 256), 1)
    swap = jnp.where((r // 32) % 2 == 0, r + 32, r - 32)
    band2_ref[pl.ds(WINDOW, 256), :] = (jnp.where(r < 128, r, swap) == c).astype(jnp.bfloat16)


def pack_kernel(coarse, dip_a, dip_b, token, own):
    own[0:4] = coarse[...]
    own[4:8] = dip_a[...]
    own[8:12] = dip_b[...]


def main_kernel(
    own, strike_a, strike_b, upmat, band1, band2, out, cells, fine, hidden, b1, b2, result, woven
):
    strike, dip = lax.axis_index("strike"), lax.axis_index("dip")
    one, zero = jnp.float32(1), jnp.float32(0)
    x_lo = jnp.where(strike == 0, zero, one)
    x_hi = jnp.where(strike == lax.axis_size("strike") - 1, zero, one)
    y_lo = jnp.where(dip == 0, zero, one)
    y_hi = jnp.where(dip == lax.axis_size("dip") - 1, zero, one)

    x_even, y_even = strike % 2 == 0, dip % 2 == 0
    below_y, above_y = jnp.where(y_even, 8, 4), jnp.where(y_even, 4, 8)

    def put(x0, x1, block):
        cells[x0:x1, 1:5, :] = block(0)
        cells[x0:x1, 0:1, :] = block(below_y)[:, 3:4]
        cells[x0:x1, 5:6, :] = block(above_y)[:, 0:1]

    def read(ref, first, count):
        return ref[pl.ds(first, count)].astype(jnp.float32)

    put(0, 1, lambda o: jnp.where(x_even, read(strike_b, o + 3, 1), read(strike_a, o + 3, 1)))
    put(1, 5, lambda o: read(own, o, 4))
    put(5, 6, lambda o: jnp.where(x_even, read(strike_a, o, 1), read(strike_b, o, 1)))

    wide = []
    edge = jnp.zeros((40, 32), jnp.float32)
    for h1 in range(2):
        for h2 in range(2):
            window = cells[1 - h1 : 6 - h1, 1 - h2 : 9 - h2, :].reshape(40, 128)
            wide.append(jnp.concatenate([edge, window, edge], axis=1))
    left = jnp.concatenate(
        [
            jnp.concatenate([w[:, 32 * q3 : 32 * q3 + 64] for w in wide], axis=1)
            for q3 in range(5)
        ],
        axis=0,
    ).astype(jnp.bfloat16)

    lane = lax.broadcasted_iota(jnp.int32, (40, 128), 1)
    q2 = lax.broadcasted_iota(jnp.int32, (40, 128), 0) % 8
    outer = (lane < 32) | (lane >= 96)
    front = lane < 64
    low = jnp.where(q2 == 0, y_lo, one)
    high = jnp.where(q2 == 4, y_hi, one)
    none = jnp.zeros((40, 128), jnp.float32)
    for p1 in range(4):
        phase = jnp.dot(left, upmat[:, p1 * 512 : p1 * 512 + 512], preferred_element_type=jnp.float32)
        for pp in range(2):
            tiles = [[], []]
            for side in range(2):
                p2 = 2 * pp + side
                v = phase[:, p2 * 128 : p2 * 128 + 128]
                for g in range(GROUPS):
                    t = jnp.where(front, v[g * 40 : g * 40 + 40], v[g * 40 + 40 : g * 40 + 80])
                    t = silu(t) * (low if pp == 0 else high)
                    tiles[side].append(t.astype(jnp.bfloat16).astype(jnp.float32))
            merged = [jnp.where(outer, tiles[0][g], tiles[1][g]) for g in range(GROUPS)]
            merged = [none] + merged + [none]
            for g in range(GROUPS):
                beside = jnp.where(front, merged[g + 2], merged[g])
                for n, t in enumerate((tiles[0][g], tiles[1][g], beside)):
                    for q1 in range(5):
                        part = t[q1 * 8 : q1 * 8 + 5]
                        if q1 == 0 and p1 < 2:
                            part = part * x_lo
                        if q1 == 4 and p1 >= 2:
                            part = part * x_hi
                        at = (4 * q1 + p1) * STEP + g * PAIRS + pp
                        fine[n, pl.ds(at, 5, stride=2), :] = part

    for dj in range(2):
        for n in range(3):
            b1[dj, :, n * 128 : n * 128 + 128] = fine[n, pl.ds(dj, 20 * STEP), :].astype(jnp.bfloat16)
    m1 = 18 * STEP
    windows = [b1[dj, dx * STEP : dx * STEP + m1, :] for dx in range(3) for dj in range(2)]
    v = silu(
        jnp.dot(jnp.concatenate(windows, axis=1), band1[...], preferred_element_type=jnp.float32)
    )
    row = lax.broadcasted_iota(jnp.int32, (m1, 128), 0)
    lane = lax.broadcasted_iota(jnp.int32, (m1, 128), 1)
    i, g, j = row // STEP, (row // PAIRS) % GROUPS, row % PAIRS
    keep = jnp.where(i == 0, x_lo, one) * jnp.where(i == 17, x_hi, one)
    v0 = v[:, :128] * (keep * jnp.where(j == 0, y_lo, one))
    v1 = v[:, 128:] * (keep * jnp.where(j == 8, y_hi, one))
    hidden[0, 16 : 16 + m1, :] = v0
    hidden[1, 16 : 16 + m1, :] = v1
    hidden[2, 16 : 16 + m1, :] = jnp.where((lane < 32) | (lane >= 96), v0, v1)

    for dj in range(2):
        for n in range(2):
            b2[dj, :, n * 128 : n * 128 + 128] = hidden[n, pl.ds(16 + dj, m1), :].astype(jnp.bfloat16)
        above = jnp.where(g == GROUPS - 1, zero, hidden[2, pl.ds(16 + dj + PAIRS, m1), :])
        below = jnp.where(g == 0, zero, hidden[2, pl.ds(16 + dj - PAIRS, m1), :])
        b2[dj, :, 256:384] = jnp.where(lane < 64, above, below).astype(jnp.bfloat16)
    m2 = 16 * STEP
    windows = [b2[dj, dx * STEP : dx * STEP + m2, :] for dx in range(3) for dj in range(2)]
    windows.append(b1[1, 2 * STEP : 2 * STEP + m2, :256])
    v = jnp.dot(jnp.concatenate(windows, axis=1), band2[...], preferred_element_type=jnp.float32)
    for o in range(2):
        result[o] = v[:, o * 128 : o * 128 + 128]
    for x in range(16):
        for g in range(GROUPS):
            for o in range(2):
                cells8 = result[o, pl.ds(x * STEP + g * PAIRS, 8), :]
                woven[g, pl.ds(x * 16 + o, 8, stride=2), :] = cells8
    for g in range(GROUPS):
        out[:, :, g * 128 : g * 128 + 128] = woven[g].reshape(16, 16, 128).astype(jnp.bfloat16)


def swapped(block, axis):
    size = lax.axis_size(axis)
    for first in (0, 1):
        pairs = [(i, i + 1) for i in range(first, size - 1, 2)]
        yield lax.ppermute(block, axis, pairs + [(j, i) for i, j in pairs])


def body(coarse, up_weight, first_weight, second_weight):
    vmem = pl.BlockSpec(memory_space=pltpu.VMEM)
    params = pltpu.CompilerParams(vmem_limit_bytes=32 * 1024 * 1024)

    bf16 = jnp.bfloat16
    shape = jax.ShapeDtypeStruct
    dip_a, dip_b = swapped(coarse, "dip")
    upmat, token = pl.pallas_call(
        up_kernel,
        out_shape=(shape((256, 2048), bf16), shape((8, 128), jnp.float32)),
        in_specs=[pl.BlockSpec(memory_space=pltpu.HBM)],
        out_specs=(vmem, vmem),
        scratch_shapes=[pltpu.VMEM((512 * 32, 32), bf16), pltpu.SemaphoreType.DMA((4,))],
        compiler_params=pltpu.CompilerParams(vmem_limit_bytes=LIMIT),
        cost_estimate=pl.CostEstimate(flops=5_000_000, bytes_accessed=5_000_000, transcendentals=0),
        name="arrange_up",
    )(up_weight.reshape(512 * 32, 32))
    own = pl.pallas_call(
        pack_kernel,
        out_shape=shape((12, 4, 128), bf16),
        in_specs=[vmem] * 4,
        out_specs=vmem,
        compiler_params=pltpu.CompilerParams(vmem_limit_bytes=1024 * 1024),
        name="pack",
    )(coarse, dip_a, dip_b, token)
    strike_a, strike_b = swapped(own, "strike")
    band1, band2 = pl.pallas_call(
        band_kernel,
        out_shape=(shape((WINDOW, 256), bf16), shape((WINDOW + 256, 256), bf16)),
        in_specs=[vmem] * 2,
        out_specs=(vmem, vmem),
        compiler_params=pltpu.CompilerParams(vmem_limit_bytes=16 * 1024 * 1024),
        cost_estimate=pl.CostEstimate(flops=5_000_000, bytes_accessed=5_000_000, transcendentals=0),
        name="arrange_bands",
    )(first_weight.reshape(864, 32), second_weight.reshape(864, 32))
    return pl.pallas_call(
        main_kernel,
        out_shape=jax.ShapeDtypeStruct((16, 16, 512), bf16),
        in_specs=[vmem] * 6,
        out_specs=vmem,
        scratch_shapes=[
            pltpu.VMEM((6, 16, 128), jnp.float32),
            pltpu.VMEM((3, 20 * STEP + 8, 128), jnp.float32),
            pltpu.VMEM((3, 18 * STEP + 32, 128), jnp.float32),
            pltpu.VMEM((2, 20 * STEP, 384), bf16),
            pltpu.VMEM((2, 18 * STEP, 384), bf16),
            pltpu.VMEM((2, 16 * STEP, 128), jnp.float32),
            pltpu.VMEM((GROUPS, 256, 128), jnp.float32),
        ],
        compiler_params=params,
        cost_estimate=pl.CostEstimate(
            flops=2_000_000_000, bytes_accessed=8_000_000, transcendentals=800_000
        ),
        name="upsample_refine",
    )(own, strike_a, strike_b, upmat, band1, band2)


def solution(mesh):
    return jax.shard_map(
        body,
        mesh=mesh,
        in_specs=(P("strike", "dip", None), P(), P(), P()),
        out_specs=P("strike", "dip", None),
        check_vma=False,
    )
```

```python
import jax
import jax.numpy as jnp
from jax import lax
from jax.experimental import pallas as pl
from jax.experimental.pallas import tpu as pltpu
from jax.sharding import PartitionSpec as P

GROUPS = 4
PAIRS = 10
STEP = GROUPS * PAIRS
ORDER = ((0, 1, 2, 3), (1, 0, 3, 2))
BESIDE = ((0, 4), (1, 4), (1, -1), (0, -1))
WINDOW = 3 * 2 * 384
LIMIT = 50 * 1024 * 1024


def silu(v):
    half = 0.5 * v
    return half + half * jnp.tanh(half)


def arrange_up(up_ref, upmat_ref, k1, p1):
    for h1 in range(2):
        for k2 in range(8):
            h2, p2 = divmod(k2, 4)
            for h3 in range(2):
                k = (k1[h1] * 8 + k2) * 8 + 4 * h3
                parts = [up_ref[pl.ds((k + (z + 2) % 4) * 32, 32), :] for z in ORDER[p2 % 2]]
                row = (h1 * 4 + h2 * 2 + (1 - h3)) * 32
                upmat_ref[pl.ds(row, 32), pl.ds((p1 * 4 + p2) * 128, 128)] = jnp.concatenate(
                    parts, axis=1
                )


SLAB = 64 * 32


def up_kernel(up_hbm, upmat_ref, last_ref, token_ref, up_ref, sems):
    fetches = []
    for p1 in range(4):
        for h1 in range(2):
            source = up_hbm.at[pl.ds((4 * h1 + p1) * SLAB, SLAB)]
            if p1 < 3:
                target = up_ref.at[pl.ds((2 * p1 + h1) * SLAB, SLAB)]
            else:
                target = last_ref.at[pl.ds(h1 * SLAB, SLAB)]
            fetches.append(pltpu.make_async_copy(source, target, sems.at[2 * p1 + h1]))
    for fetch in fetches:
        fetch.start()
    token_ref[...] = jnp.zeros((8, 128), jnp.float32)
    for p1 in range(3):
        fetches[2 * p1].wait()
        fetches[2 * p1 + 1].wait()
        arrange_up(up_ref, upmat_ref, (2 * p1, 2 * p1 + 1), p1)
    fetches[6].wait()
    fetches[7].wait()


def band_kernel(first_ref, second_ref, last_ref, band1_ref, band2_ref, uplast_ref):
    arrange_up(last_ref, uplast_ref, (0, 1), 0)
    ci = lax.broadcasted_iota(jnp.int32, (32, 128), 0)
    lane = lax.broadcasted_iota(jnp.int32, (32, 128), 1)
    group = lane // 32
    copies = (lane % 32 == ci).astype(jnp.bfloat16)

    def arrange(w_ref, band_ref, out_order):
        rep = jnp.dot(w_ref[...], copies, preferred_element_type=jnp.float32)
        for d1 in range(3):
            for dj in range(2):
                cells = [(0, z) for z in ORDER[0]] + [(1, z) for z in ORDER[1]] + list(BESIDE)
                for n, (side, z_in) in enumerate(cells):
                    row = (d1 * 2 + dj) * 384 + n * 32
                    for o in range(2):
                        block = jnp.zeros((32, 128), jnp.float32)
                        d2 = 2 * dj + side - o
                        for d3 in range(3):
                            z_out = z_in - d3 + 1
                            if 0 <= d2 < 3 and 0 <= z_out < 4:
                                tap = ((d1 * 3 + d2) * 3 + d3) * 32
                                here = group == out_order[o].index(z_out)
                                block = jnp.where(here, rep[tap : tap + 32], block)
                        band_ref[pl.ds(row, 32), pl.ds(o * 128, 128)] = block.astype(jnp.bfloat16)

    arrange(first_ref, band1_ref, ORDER)
    arrange(second_ref, band2_ref, (ORDER[0], ORDER[0]))
    r = lax.broadcasted_iota(jnp.int32, (256, 256), 0)
    c = lax.broadcasted_iota(jnp.int32, (256, 256), 1)
    swap = jnp.where((r // 32) % 2 == 0, r + 32, r - 32)
    band2_ref[pl.ds(WINDOW, 256), :] = (jnp.where(r < 128, r, swap) == c).astype(jnp.bfloat16)


def pack_kernel(coarse, dip_a, dip_b, token, own):
    own[0:4] = coarse[...]
    own[4:8] = dip_a[...]
    own[8:12] = dip_b[...]


def main_kernel(
    own, strike_a, strike_b, upmat, uplast, band1, band2, out, cells, fine, hidden, b1, b2, result, woven
):
    strike, dip = lax.axis_index("strike"), lax.axis_index("dip")
    one, zero = jnp.float32(1), jnp.float32(0)
    x_lo = jnp.where(strike == 0, zero, one)
    x_hi = jnp.where(strike == lax.axis_size("strike") - 1, zero, one)
    y_lo = jnp.where(dip == 0, zero, one)
    y_hi = jnp.where(dip == lax.axis_size("dip") - 1, zero, one)

    x_even, y_even = strike % 2 == 0, dip % 2 == 0
    below_y, above_y = jnp.where(y_even, 8, 4), jnp.where(y_even, 4, 8)

    def put(x0, x1, block):
        cells[x0:x1, 1:5, :] = block(0)
        cells[x0:x1, 0:1, :] = block(below_y)[:, 3:4]
        cells[x0:x1, 5:6, :] = block(above_y)[:, 0:1]

    def read(ref, first, count):
        return ref[pl.ds(first, count)].astype(jnp.float32)

    put(0, 1, lambda o: jnp.where(x_even, read(strike_b, o + 3, 1), read(strike_a, o + 3, 1)))
    put(1, 5, lambda o: read(own, o, 4))
    put(5, 6, lambda o: jnp.where(x_even, read(strike_a, o, 1), read(strike_b, o, 1)))

    wide = []
    edge = jnp.zeros((40, 32), jnp.float32)
    for h1 in range(2):
        for h2 in range(2):
            window = cells[1 - h1 : 6 - h1, 1 - h2 : 9 - h2, :].reshape(40, 128)
            wide.append(jnp.concatenate([edge, window, edge], axis=1))
    left = jnp.concatenate(
        [
            jnp.concatenate([w[:, 32 * q3 : 32 * q3 + 64] for w in wide], axis=1)
            for q3 in range(5)
        ],
        axis=0,
    ).astype(jnp.bfloat16)

    lane = lax.broadcasted_iota(jnp.int32, (40, 128), 1)
    q2 = lax.broadcasted_iota(jnp.int32, (40, 128), 0) % 8
    outer = (lane < 32) | (lane >= 96)
    front = lane < 64
    low = jnp.where(q2 == 0, y_lo, one)
    high = jnp.where(q2 == 4, y_hi, one)
    none = jnp.zeros((40, 128), jnp.float32)
    for p1 in range(4):
        taps = upmat[:, p1 * 512 : p1 * 512 + 512] if p1 < 3 else uplast[...]
        phase = jnp.dot(left, taps, preferred_element_type=jnp.float32)
        for pp in range(2):
            tiles = [[], []]
            for side in range(2):
                p2 = 2 * pp + side
                v = phase[:, p2 * 128 : p2 * 128 + 128]
                for g in range(GROUPS):
                    t = jnp.where(front, v[g * 40 : g * 40 + 40], v[g * 40 + 40 : g * 40 + 80])
                    tiles[side].append(silu(t) * (low if pp == 0 else high))
            merged = [jnp.where(outer, tiles[0][g], tiles[1][g]) for g in range(GROUPS)]
            merged = [none] + merged + [none]
            for g in range(GROUPS):
                beside = jnp.where(front, merged[g + 2], merged[g])
                for n, t in enumerate((tiles[0][g], tiles[1][g], beside)):
                    for q1 in range(5):
                        part = t[q1 * 8 : q1 * 8 + 5]
                        if q1 == 0 and p1 < 2:
                            part = part * x_lo
                        if q1 == 4 and p1 >= 2:
                            part = part * x_hi
                        at = (4 * q1 + p1) * STEP + g * PAIRS + pp
                        fine[n, pl.ds(at, 5, stride=2), :] = part

    for dj in range(2):
        for n in range(3):
            b1[dj, :, n * 128 : n * 128 + 128] = fine[n, pl.ds(dj, 20 * STEP), :].astype(jnp.bfloat16)
    m1 = 18 * STEP
    windows = [b1[dj, dx * STEP : dx * STEP + m1, :] for dx in range(3) for dj in range(2)]
    v = silu(
        jnp.dot(jnp.concatenate(windows, axis=1), band1[...], preferred_element_type=jnp.float32)
    )
    row = lax.broadcasted_iota(jnp.int32, (m1, 128), 0)
    lane = lax.broadcasted_iota(jnp.int32, (m1, 128), 1)
    i, g, j = row // STEP, (row // PAIRS) % GROUPS, row % PAIRS
    keep = jnp.where(i == 0, x_lo, one) * jnp.where(i == 17, x_hi, one)
    v0 = v[:, :128] * (keep * jnp.where(j == 0, y_lo, one))
    v1 = v[:, 128:] * (keep * jnp.where(j == 8, y_hi, one))
    hidden[0, 16 : 16 + m1, :] = v0
    hidden[1, 16 : 16 + m1, :] = v1
    hidden[2, 16 : 16 + m1, :] = jnp.where((lane < 32) | (lane >= 96), v0, v1)

    for dj in range(2):
        for n in range(2):
            b2[dj, :, n * 128 : n * 128 + 128] = hidden[n, pl.ds(16 + dj, m1), :].astype(jnp.bfloat16)
        above = jnp.where(g == GROUPS - 1, zero, hidden[2, pl.ds(16 + dj + PAIRS, m1), :])
        below = jnp.where(g == 0, zero, hidden[2, pl.ds(16 + dj - PAIRS, m1), :])
        b2[dj, :, 256:384] = jnp.where(lane < 64, above, below).astype(jnp.bfloat16)
    m2 = 16 * STEP
    windows = [b2[dj, dx * STEP : dx * STEP + m2, :] for dx in range(3) for dj in range(2)]
    windows.append(b1[1, 2 * STEP : 2 * STEP + m2, :256])
    v = jnp.dot(jnp.concatenate(windows, axis=1), band2[...], preferred_element_type=jnp.float32)
    for o in range(2):
        result[o] = v[:, o * 128 : o * 128 + 128]
    for x in range(16):
        for g in range(GROUPS):
            for o in range(2):
                cells8 = result[o, pl.ds(x * STEP + g * PAIRS, 8), :]
                woven[g, pl.ds(x * 16 + o, 8, stride=2), :] = cells8
    for g in range(GROUPS):
        out[:, :, g * 128 : g * 128 + 128] = woven[g].reshape(16, 16, 128).astype(jnp.bfloat16)


def swapped(block, axis):
    size = lax.axis_size(axis)
    for first in (0, 1):
        pairs = [(i, i + 1) for i in range(first, size - 1, 2)]
        yield lax.ppermute(block, axis, pairs + [(j, i) for i, j in pairs])


def body(coarse, up_weight, first_weight, second_weight):
    vmem = pl.BlockSpec(memory_space=pltpu.VMEM)
    params = pltpu.CompilerParams(vmem_limit_bytes=32 * 1024 * 1024)

    bf16 = jnp.bfloat16
    shape = jax.ShapeDtypeStruct
    dip_a, dip_b = swapped(coarse, "dip")
    upmat, last, token = pl.pallas_call(
        up_kernel,
        out_shape=(
            shape((256, 1536), bf16),
            shape((2 * SLAB, 32), bf16),
            shape((8, 128), jnp.float32),
        ),
        in_specs=[pl.BlockSpec(memory_space=pltpu.HBM)],
        out_specs=(vmem,) * 3,
        scratch_shapes=[pltpu.VMEM((6 * SLAB, 32), bf16), pltpu.SemaphoreType.DMA((8,))],
        compiler_params=pltpu.CompilerParams(vmem_limit_bytes=LIMIT),
        cost_estimate=pl.CostEstimate(flops=5_000_000, bytes_accessed=5_000_000, transcendentals=0),
        name="arrange_up",
    )(up_weight.reshape(512 * 32, 32))
    own = pl.pallas_call(
        pack_kernel,
        out_shape=shape((12, 4, 128), bf16),
        in_specs=[vmem] * 4,
        out_specs=vmem,
        compiler_params=pltpu.CompilerParams(vmem_limit_bytes=1024 * 1024),
        name="pack",
    )(coarse, dip_a, dip_b, token)
    strike_a, strike_b = swapped(own, "strike")
    band1, band2, uplast = pl.pallas_call(
        band_kernel,
        out_shape=(
            shape((WINDOW, 256), bf16),
            shape((WINDOW + 256, 256), bf16),
            shape((256, 512), bf16),
        ),
        in_specs=[vmem] * 3,
        out_specs=(vmem,) * 3,
        compiler_params=pltpu.CompilerParams(vmem_limit_bytes=16 * 1024 * 1024),
        cost_estimate=pl.CostEstimate(flops=5_000_000, bytes_accessed=5_000_000, transcendentals=0),
        name="arrange_bands",
    )(first_weight.reshape(864, 32), second_weight.reshape(864, 32), last)
    return pl.pallas_call(
        main_kernel,
        out_shape=jax.ShapeDtypeStruct((16, 16, 512), bf16),
        in_specs=[vmem] * 7,
        out_specs=vmem,
        scratch_shapes=[
            pltpu.VMEM((6, 16, 128), jnp.float32),
            pltpu.VMEM((3, 20 * STEP + 8, 128), jnp.float32),
            pltpu.VMEM((3, 18 * STEP + 32, 128), jnp.float32),
            pltpu.VMEM((2, 20 * STEP, 384), bf16),
            pltpu.VMEM((2, 18 * STEP, 384), bf16),
            pltpu.VMEM((2, 16 * STEP, 128), jnp.float32),
            pltpu.VMEM((GROUPS, 256, 128), jnp.float32),
        ],
        compiler_params=params,
        cost_estimate=pl.CostEstimate(
            flops=2_000_000_000, bytes_accessed=8_000_000, transcendentals=800_000
        ),
        name="upsample_refine",
    )(own, strike_a, strike_b, upmat, uplast, band1, band2)


def solution(mesh):
    return jax.shard_map(
        body,
        mesh=mesh,
        in_specs=(P("strike", "dip", None), P(), P(), P()),
        out_specs=P("strike", "dip", None),
        check_vma=False,
    )
```

```python
import jax
import jax.numpy as jnp
from jax import lax
from jax.experimental import pallas as pl
from jax.experimental.pallas import tpu as pltpu
from jax.sharding import PartitionSpec as P

GROUPS = 4
PAIRS = 10
STEP = GROUPS * PAIRS
ORDER = ((0, 1, 2, 3), (1, 0, 3, 2))
BESIDE = ((0, 4), (1, 4), (1, -1), (0, -1))
WINDOW = 3 * 2 * 384
LIMIT = 50 * 1024 * 1024


def silu(v):
    half = 0.5 * v
    return half + half * jnp.tanh(half)


def up_kernel(up_hbm, upmat_ref, token_ref, up_ref, sems):
    fetches = []
    for part in range(4):
        rows = pl.ds(part * 4096, 4096)
        fetches.append(pltpu.make_async_copy(up_hbm.at[rows], up_ref.at[rows], sems.at[part]))
    for fetch in fetches:
        fetch.start()
    token_ref[...] = jnp.zeros((8, 128), jnp.float32)

    for k1 in range(8):
        if k1 % 2 == 0:
            fetches[k1 // 2].wait()
        h1, p1 = divmod(k1, 4)
        for k2 in range(8):
            h2, p2 = divmod(k2, 4)
            for h3 in range(2):
                k = (k1 * 8 + k2) * 8 + 4 * h3
                parts = [up_ref[pl.ds((k + (z + 2) % 4) * 32, 32), :] for z in ORDER[p2 % 2]]
                row = (h1 * 4 + h2 * 2 + (1 - h3)) * 32
                upmat_ref[pl.ds(row, 32), pl.ds((p1 * 4 + p2) * 128, 128)] = jnp.concatenate(
                    parts, axis=1
                )


def band_kernel(first_ref, second_ref, band1_ref, band2_ref):
    ci = lax.broadcasted_iota(jnp.int32, (32, 128), 0)
    lane = lax.broadcasted_iota(jnp.int32, (32, 128), 1)
    group = lane // 32
    copies = (lane % 32 == ci).astype(jnp.bfloat16)

    def arrange(w_ref, band_ref, out_order):
        rep = jnp.dot(w_ref[...], copies, preferred_element_type=jnp.float32)
        for d1 in range(3):
            for dj in range(2):
                cells = [(0, z) for z in ORDER[0]] + [(1, z) for z in ORDER[1]] + list(BESIDE)
                for n, (side, z_in) in enumerate(cells):
                    row = (d1 * 2 + dj) * 384 + n * 32
                    for o in range(2):
                        block = jnp.zeros((32, 128), jnp.float32)
                        d2 = 2 * dj + side - o
                        for d3 in range(3):
                            z_out = z_in - d3 + 1
                            if 0 <= d2 < 3 and 0 <= z_out < 4:
                                tap = ((d1 * 3 + d2) * 3 + d3) * 32
                                here = group == out_order[o].index(z_out)
                                block = jnp.where(here, rep[tap : tap + 32], block)
                        band_ref[pl.ds(row, 32), pl.ds(o * 128, 128)] = block.astype(jnp.bfloat16)

    arrange(first_ref, band1_ref, ORDER)
    arrange(second_ref, band2_ref, (ORDER[0], ORDER[0]))
    r = lax.broadcasted_iota(jnp.int32, (256, 256), 0)
    c = lax.broadcasted_iota(jnp.int32, (256, 256), 1)
    swap = jnp.where((r // 32) % 2 == 0, r + 32, r - 32)
    band2_ref[pl.ds(WINDOW, 256), :] = (jnp.where(r < 128, r, swap) == c).astype(jnp.bfloat16)


def pack_kernel(coarse, dip_a, dip_b, token, own):
    own[0:4] = coarse[...]
    own[4:8] = dip_a[...]
    own[8:12] = dip_b[...]


def main_kernel(
    own, strike_a, strike_b, upmat, band1, band2, out, cells, fine, hidden, b1, b2, result, woven
):
    strike, dip = lax.axis_index("strike"), lax.axis_index("dip")
    one, zero = jnp.float32(1), jnp.float32(0)
    x_lo = jnp.where(strike == 0, zero, one)
    x_hi = jnp.where(strike == lax.axis_size("strike") - 1, zero, one)
    y_lo = jnp.where(dip == 0, zero, one)
    y_hi = jnp.where(dip == lax.axis_size("dip") - 1, zero, one)

    x_even, y_even = strike % 2 == 0, dip % 2 == 0
    below_y, above_y = jnp.where(y_even, 8, 4), jnp.where(y_even, 4, 8)

    def put(x0, x1, block):
        cells[x0:x1, 1:5, :] = block(0)
        cells[x0:x1, 0:1, :] = block(below_y)[:, 3:4]
        cells[x0:x1, 5:6, :] = block(above_y)[:, 0:1]

    def read(ref, first, count):
        return ref[pl.ds(first, count)].astype(jnp.float32)

    put(0, 1, lambda o: jnp.where(x_even, read(strike_b, o + 3, 1), read(strike_a, o + 3, 1)))
    put(1, 5, lambda o: read(own, o, 4))
    put(5, 6, lambda o: jnp.where(x_even, read(strike_a, o, 1), read(strike_b, o, 1)))

    wide = []
    edge = jnp.zeros((40, 32), jnp.float32)
    for h1 in range(2):
        for h2 in range(2):
            window = cells[1 - h1 : 6 - h1, 1 - h2 : 9 - h2, :].reshape(40, 128)
            wide.append(jnp.concatenate([edge, window, edge], axis=1))
    left = jnp.concatenate(
        [
            jnp.concatenate([w[:, 32 * q3 : 32 * q3 + 64] for w in wide], axis=1)
            for q3 in range(5)
        ],
        axis=0,
    ).astype(jnp.bfloat16)

    lane = lax.broadcasted_iota(jnp.int32, (40, 128), 1)
    q2 = lax.broadcasted_iota(jnp.int32, (40, 128), 0) % 8
    outer = (lane < 32) | (lane >= 96)
    front = lane < 64
    low = jnp.where(q2 == 0, y_lo, one)
    high = jnp.where(q2 == 4, y_hi, one)
    none = jnp.zeros((40, 128), jnp.float32)
    for p1 in range(4):
        phase = jnp.dot(left, upmat[:, p1 * 512 : p1 * 512 + 512], preferred_element_type=jnp.float32)
        for pp in range(2):
            tiles = [[], []]
            for side in range(2):
                p2 = 2 * pp + side
                v = phase[:, p2 * 128 : p2 * 128 + 128]
                for g in range(GROUPS):
                    t = jnp.where(front, v[g * 40 : g * 40 + 40], v[g * 40 + 40 : g * 40 + 80])
                    tiles[side].append(silu(t) * (low if pp == 0 else high))
            merged = [jnp.where(outer, tiles[0][g], tiles[1][g]) for g in range(GROUPS)]
            merged = [none] + merged + [none]
            for g in range(GROUPS):
                beside = jnp.where(front, merged[g + 2], merged[g])
                for n, t in enumerate((tiles[0][g], tiles[1][g], beside)):
                    for q1 in range(5):
                        part = t[q1 * 8 : q1 * 8 + 5]
                        if q1 == 0 and p1 < 2:
                            part = part * x_lo
                        if q1 == 4 and p1 >= 2:
                            part = part * x_hi
                        at = (4 * q1 + p1) * STEP + g * PAIRS + pp
                        fine[n, pl.ds(at, 5, stride=2), :] = part

    for dj in range(2):
        for n in range(3):
            b1[dj, :, n * 128 : n * 128 + 128] = fine[n, pl.ds(dj, 20 * STEP), :].astype(jnp.bfloat16)
    m1 = 18 * STEP
    windows = [b1[dj, dx * STEP : dx * STEP + m1, :] for dx in range(3) for dj in range(2)]
    v = silu(
        jnp.dot(jnp.concatenate(windows, axis=1), band1[...], preferred_element_type=jnp.float32)
    )
    row = lax.broadcasted_iota(jnp.int32, (m1, 128), 0)
    lane = lax.broadcasted_iota(jnp.int32, (m1, 128), 1)
    i, g, j = row // STEP, (row // PAIRS) % GROUPS, row % PAIRS
    keep = jnp.where(i == 0, x_lo, one) * jnp.where(i == 17, x_hi, one)
    v0 = v[:, :128] * (keep * jnp.where(j == 0, y_lo, one))
    v1 = v[:, 128:] * (keep * jnp.where(j == 8, y_hi, one))
    hidden[0, 16 : 16 + m1, :] = v0
    hidden[1, 16 : 16 + m1, :] = v1
    hidden[2, 16 : 16 + m1, :] = jnp.where((lane < 32) | (lane >= 96), v0, v1)

    for dj in range(2):
        for n in range(2):
            b2[dj, :, n * 128 : n * 128 + 128] = hidden[n, pl.ds(16 + dj, m1), :].astype(jnp.bfloat16)
        above = jnp.where(g == GROUPS - 1, zero, hidden[2, pl.ds(16 + dj + PAIRS, m1), :])
        below = jnp.where(g == 0, zero, hidden[2, pl.ds(16 + dj - PAIRS, m1), :])
        b2[dj, :, 256:384] = jnp.where(lane < 64, above, below).astype(jnp.bfloat16)
    m2 = 16 * STEP
    windows = [b2[dj, dx * STEP : dx * STEP + m2, :] for dx in range(3) for dj in range(2)]
    windows.append(b1[1, 2 * STEP : 2 * STEP + m2, :256])
    v = jnp.dot(jnp.concatenate(windows, axis=1), band2[...], preferred_element_type=jnp.float32)
    for o in range(2):
        result[o] = v[:, o * 128 : o * 128 + 128]
    for x in range(16):
        for g in range(GROUPS):
            for o in range(2):
                cells8 = result[o, pl.ds(x * STEP + g * PAIRS, 8), :]
                woven[g, pl.ds(x * 16 + o, 8, stride=2), :] = cells8
    for g in range(GROUPS):
        out[:, :, g * 128 : g * 128 + 128] = woven[g].reshape(16, 16, 128).astype(jnp.bfloat16)


def swapped(block, axis):
    size = lax.axis_size(axis)
    for first in (0, 1):
        pairs = [(i, i + 1) for i in range(first, size - 1, 2)]
        yield lax.ppermute(block, axis, pairs + [(j, i) for i, j in pairs])


def passed_on(block, axis):
    size = lax.axis_size(axis)
    pairs = [(i, i + 1) for i in range(0, size - 1, 2)]
    first = lax.ppermute(block, axis, pairs + [(j, i) for i, j in pairs])
    up = [(i, i + 2) for i in range(0, size - 2, 2)]
    down = [(i, i - 2) for i in range(3, size, 2)]
    return first, lax.ppermute(first, axis, up + down)


def body(coarse, up_weight, first_weight, second_weight):
    vmem = pl.BlockSpec(memory_space=pltpu.VMEM)
    params = pltpu.CompilerParams(vmem_limit_bytes=32 * 1024 * 1024)

    bf16 = jnp.bfloat16
    shape = jax.ShapeDtypeStruct
    dip_a, dip_b = passed_on(coarse, "dip")
    upmat, token = pl.pallas_call(
        up_kernel,
        out_shape=(shape((256, 2048), bf16), shape((8, 128), jnp.float32)),
        in_specs=[pl.BlockSpec(memory_space=pltpu.HBM)],
        out_specs=(vmem, vmem),
        scratch_shapes=[pltpu.VMEM((512 * 32, 32), bf16), pltpu.SemaphoreType.DMA((4,))],
        compiler_params=pltpu.CompilerParams(vmem_limit_bytes=LIMIT),
        cost_estimate=pl.CostEstimate(flops=5_000_000, bytes_accessed=5_000_000, transcendentals=0),
        name="arrange_up",
    )(up_weight.reshape(512 * 32, 32))
    own = pl.pallas_call(
        pack_kernel,
        out_shape=shape((12, 4, 128), bf16),
        in_specs=[vmem] * 4,
        out_specs=vmem,
        compiler_params=pltpu.CompilerParams(vmem_limit_bytes=1024 * 1024),
        name="pack",
    )(coarse, dip_a, dip_b, token)
    strike_a, strike_b = swapped(own, "strike")
    band1, band2 = pl.pallas_call(
        band_kernel,
        out_shape=(shape((WINDOW, 256), bf16), shape((WINDOW + 256, 256), bf16)),
        in_specs=[vmem] * 2,
        out_specs=(vmem, vmem),
        compiler_params=pltpu.CompilerParams(vmem_limit_bytes=16 * 1024 * 1024),
        cost_estimate=pl.CostEstimate(flops=5_000_000, bytes_accessed=5_000_000, transcendentals=0),
        name="arrange_bands",
    )(first_weight.reshape(864, 32), second_weight.reshape(864, 32))
    return pl.pallas_call(
        main_kernel,
        out_shape=jax.ShapeDtypeStruct((16, 16, 512), bf16),
        in_specs=[vmem] * 6,
        out_specs=vmem,
        scratch_shapes=[
            pltpu.VMEM((6, 16, 128), jnp.float32),
            pltpu.VMEM((3, 20 * STEP + 8, 128), jnp.float32),
            pltpu.VMEM((3, 18 * STEP + 32, 128), jnp.float32),
            pltpu.VMEM((2, 20 * STEP, 384), bf16),
            pltpu.VMEM((2, 18 * STEP, 384), bf16),
            pltpu.VMEM((2, 16 * STEP, 128), jnp.float32),
            pltpu.VMEM((GROUPS, 256, 128), jnp.float32),
        ],
        compiler_params=params,
        cost_estimate=pl.CostEstimate(
            flops=2_000_000_000, bytes_accessed=8_000_000, transcendentals=800_000
        ),
        name="upsample_refine",
    )(own, strike_a, strike_b, upmat, band1, band2)


def solution(mesh):
    return jax.shard_map(
        body,
        mesh=mesh,
        in_specs=(P("strike", "dip", None), P(), P(), P()),
        out_specs=P("strike", "dip", None),
        check_vma=False,
    )
```

```python
import jax
import jax.numpy as jnp
from jax import lax
from jax.experimental import pallas as pl
from jax.experimental.pallas import tpu as pltpu
from jax.sharding import PartitionSpec as P

GROUPS = 4
PAIRS = 10
STEP = GROUPS * PAIRS
ORDER = ((0, 1, 2, 3), (1, 0, 3, 2))
BESIDE = ((0, 4), (1, 4), (1, -1), (0, -1))
WINDOW = 3 * 2 * 384
LIMIT = 50 * 1024 * 1024


def silu(v):
    half = 0.5 * v
    return half + half * jnp.tanh(half)


def up_kernel(up_hbm, upmat_ref, token_ref, up_ref, sems):
    fetches = []
    for part in range(4):
        rows = pl.ds(part * 4096, 4096)
        fetches.append(pltpu.make_async_copy(up_hbm.at[rows], up_ref.at[rows], sems.at[part]))
    for fetch in fetches:
        fetch.start()
    token_ref[...] = jnp.zeros((8, 128), jnp.float32)

    for k1 in range(8):
        if k1 % 2 == 0:
            fetches[k1 // 2].wait()
        h1, p1 = divmod(k1, 4)
        for k2 in range(8):
            h2, p2 = divmod(k2, 4)
            for h3 in range(2):
                k = (k1 * 8 + k2) * 8 + 4 * h3
                parts = [up_ref[pl.ds((k + (z + 2) % 4) * 32, 32), :] for z in ORDER[p2 % 2]]
                row = (h1 * 4 + h2 * 2 + (1 - h3)) * 32
                upmat_ref[pl.ds(row, 32), pl.ds((p1 * 4 + p2) * 128, 128)] = jnp.concatenate(
                    parts, axis=1
                )


def band_kernel(first_ref, second_ref, band1_ref, band2_ref):
    ci = lax.broadcasted_iota(jnp.int32, (32, 128), 0)
    lane = lax.broadcasted_iota(jnp.int32, (32, 128), 1)
    group = lane // 32
    copies = (lane % 32 == ci).astype(jnp.bfloat16)

    def arrange(w_ref, band_ref, out_order):
        rep = jnp.dot(w_ref[...], copies, preferred_element_type=jnp.float32)
        for d1 in range(3):
            for dj in range(2):
                cells = [(0, z) for z in ORDER[0]] + [(1, z) for z in ORDER[1]] + list(BESIDE)
                for n, (side, z_in) in enumerate(cells):
                    row = (d1 * 2 + dj) * 384 + n * 32
                    for o in range(2):
                        block = jnp.zeros((32, 128), jnp.float32)
                        d2 = 2 * dj + side - o
                        for d3 in range(3):
                            z_out = z_in - d3 + 1
                            if 0 <= d2 < 3 and 0 <= z_out < 4:
                                tap = ((d1 * 3 + d2) * 3 + d3) * 32
                                here = group == out_order[o].index(z_out)
                                block = jnp.where(here, rep[tap : tap + 32], block)
                        band_ref[pl.ds(row, 32), pl.ds(o * 128, 128)] = block.astype(jnp.bfloat16)

    arrange(first_ref, band1_ref, ORDER)
    arrange(second_ref, band2_ref, (ORDER[0], ORDER[0]))
    r = lax.broadcasted_iota(jnp.int32, (256, 256), 0)
    c = lax.broadcasted_iota(jnp.int32, (256, 256), 1)
    swap = jnp.where((r // 32) % 2 == 0, r + 32, r - 32)
    band2_ref[pl.ds(WINDOW, 256), :] = (jnp.where(r < 128, r, swap) == c).astype(jnp.bfloat16)


def main_kernel(
    field, upmat, band1, band2, out, cells, fine, hidden, b1, b2, result, woven
):
    strike, dip = lax.axis_index("strike"), lax.axis_index("dip")
    one, zero = jnp.float32(1), jnp.float32(0)
    x_lo = jnp.where(strike == 0, zero, one)
    x_hi = jnp.where(strike == lax.axis_size("strike") - 1, zero, one)
    y_lo = jnp.where(dip == 0, zero, one)
    y_hi = jnp.where(dip == lax.axis_size("dip") - 1, zero, one)

    n1, n2 = lax.axis_size("strike"), lax.axis_size("dip")
    spans = (((0, 1), (3, 4)), ((1, 5), (0, 4)), ((5, 6), (0, 1)))
    for s1, ((x0, x1), (u0, u1)) in enumerate(spans):
        for s2, ((y0, y1), (w0, w1)) in enumerate(spans):
            c1 = jnp.clip(strike + (s1 - 1), 0, n1 - 1)
            c2 = jnp.clip(dip + (s2 - 1), 0, n2 - 1)
            scale = (x_lo, one, x_hi)[s1] * (y_lo, one, y_hi)[s2]
            piece = field[c1 * n2 + c2].astype(jnp.float32)[u0:u1, w0:w1]
            cells[x0:x1, y0:y1, :] = piece * scale

    wide = []
    edge = jnp.zeros((40, 32), jnp.float32)
    for h1 in range(2):
        for h2 in range(2):
            window = cells[1 - h1 : 6 - h1, 1 - h2 : 9 - h2, :].reshape(40, 128)
            wide.append(jnp.concatenate([edge, window, edge], axis=1))
    left = jnp.concatenate(
        [
            jnp.concatenate([w[:, 32 * q3 : 32 * q3 + 64] for w in wide], axis=1)
            for q3 in range(5)
        ],
        axis=0,
    ).astype(jnp.bfloat16)

    lane = lax.broadcasted_iota(jnp.int32, (40, 128), 1)
    q2 = lax.broadcasted_iota(jnp.int32, (40, 128), 0) % 8
    outer = (lane < 32) | (lane >= 96)
    front = lane < 64
    low = jnp.where(q2 == 0, y_lo, one)
    high = jnp.where(q2 == 4, y_hi, one)
    none = jnp.zeros((40, 128), jnp.float32)
    for p1 in range(4):
        phase = jnp.dot(left, upmat[:, p1 * 512 : p1 * 512 + 512], preferred_element_type=jnp.float32)
        for pp in range(2):
            tiles = [[], []]
            for side in range(2):
                p2 = 2 * pp + side
                v = phase[:, p2 * 128 : p2 * 128 + 128]
                for g in range(GROUPS):
                    t = jnp.where(front, v[g * 40 : g * 40 + 40], v[g * 40 + 40 : g * 40 + 80])
                    tiles[side].append(silu(t) * (low if pp == 0 else high))
            merged = [jnp.where(outer, tiles[0][g], tiles[1][g]) for g in range(GROUPS)]
            merged = [none] + merged + [none]
            for g in range(GROUPS):
                beside = jnp.where(front, merged[g + 2], merged[g])
                for n, t in enumerate((tiles[0][g], tiles[1][g], beside)):
                    for q1 in range(5):
                        part = t[q1 * 8 : q1 * 8 + 5]
                        if q1 == 0 and p1 < 2:
                            part = part * x_lo
                        if q1 == 4 and p1 >= 2:
                            part = part * x_hi
                        at = (4 * q1 + p1) * STEP + g * PAIRS + pp
                        fine[n, pl.ds(at, 5, stride=2), :] = part

    for dj in range(2):
        for n in range(3):
            b1[dj, :, n * 128 : n * 128 + 128] = fine[n, pl.ds(dj, 20 * STEP), :].astype(jnp.bfloat16)
    m1 = 18 * STEP
    windows = [b1[dj, dx * STEP : dx * STEP + m1, :] for dx in range(3) for dj in range(2)]
    v = silu(
        jnp.dot(jnp.concatenate(windows, axis=1), band1[...], preferred_element_type=jnp.float32)
    )
    row = lax.broadcasted_iota(jnp.int32, (m1, 128), 0)
    lane = lax.broadcasted_iota(jnp.int32, (m1, 128), 1)
    i, g, j = row // STEP, (row // PAIRS) % GROUPS, row % PAIRS
    keep = jnp.where(i == 0, x_lo, one) * jnp.where(i == 17, x_hi, one)
    v0 = v[:, :128] * (keep * jnp.where(j == 0, y_lo, one))
    v1 = v[:, 128:] * (keep * jnp.where(j == 8, y_hi, one))
    hidden[0, 16 : 16 + m1, :] = v0
    hidden[1, 16 : 16 + m1, :] = v1
    hidden[2, 16 : 16 + m1, :] = jnp.where((lane < 32) | (lane >= 96), v0, v1)

    for dj in range(2):
        for n in range(2):
            b2[dj, :, n * 128 : n * 128 + 128] = hidden[n, pl.ds(16 + dj, m1), :].astype(jnp.bfloat16)
        above = jnp.where(g == GROUPS - 1, zero, hidden[2, pl.ds(16 + dj + PAIRS, m1), :])
        below = jnp.where(g == 0, zero, hidden[2, pl.ds(16 + dj - PAIRS, m1), :])
        b2[dj, :, 256:384] = jnp.where(lane < 64, above, below).astype(jnp.bfloat16)
    m2 = 16 * STEP
    windows = [b2[dj, dx * STEP : dx * STEP + m2, :] for dx in range(3) for dj in range(2)]
    windows.append(b1[1, 2 * STEP : 2 * STEP + m2, :256])
    v = jnp.dot(jnp.concatenate(windows, axis=1), band2[...], preferred_element_type=jnp.float32)
    for o in range(2):
        result[o] = v[:, o * 128 : o * 128 + 128]
    for x in range(16):
        for g in range(GROUPS):
            for o in range(2):
                cells8 = result[o, pl.ds(x * STEP + g * PAIRS, 8), :]
                woven[g, pl.ds(x * 16 + o, 8, stride=2), :] = cells8
    for g in range(GROUPS):
        out[:, :, g * 128 : g * 128 + 128] = woven[g].reshape(16, 16, 128).astype(jnp.bfloat16)


def body(coarse, up_weight, first_weight, second_weight):
    vmem = pl.BlockSpec(memory_space=pltpu.VMEM)
    params = pltpu.CompilerParams(vmem_limit_bytes=32 * 1024 * 1024)

    bf16 = jnp.bfloat16
    shape = jax.ShapeDtypeStruct
    count = lax.axis_size("strike") * lax.axis_size("dip")
    field = lax.all_to_all(
        jnp.broadcast_to(coarse, (count, *coarse.shape)), ("strike", "dip"), 0, 0
    )
    upmat, _ = pl.pallas_call(
        up_kernel,
        out_shape=(shape((256, 2048), bf16), shape((8, 128), jnp.float32)),
        in_specs=[pl.BlockSpec(memory_space=pltpu.HBM)],
        out_specs=(vmem, vmem),
        scratch_shapes=[pltpu.VMEM((512 * 32, 32), bf16), pltpu.SemaphoreType.DMA((4,))],
        compiler_params=pltpu.CompilerParams(vmem_limit_bytes=LIMIT),
        cost_estimate=pl.CostEstimate(flops=5_000_000, bytes_accessed=5_000_000, transcendentals=0),
        name="arrange_up",
    )(up_weight.reshape(512 * 32, 32))
    band1, band2 = pl.pallas_call(
        band_kernel,
        out_shape=(shape((WINDOW, 256), bf16), shape((WINDOW + 256, 256), bf16)),
        in_specs=[vmem] * 2,
        out_specs=(vmem, vmem),
        compiler_params=pltpu.CompilerParams(vmem_limit_bytes=16 * 1024 * 1024),
        cost_estimate=pl.CostEstimate(flops=5_000_000, bytes_accessed=5_000_000, transcendentals=0),
        name="arrange_bands",
    )(first_weight.reshape(864, 32), second_weight.reshape(864, 32))
    return pl.pallas_call(
        main_kernel,
        out_shape=jax.ShapeDtypeStruct((16, 16, 512), bf16),
        in_specs=[vmem] * 4,
        out_specs=vmem,
        scratch_shapes=[
            pltpu.VMEM((6, 16, 128), jnp.float32),
            pltpu.VMEM((3, 20 * STEP + 8, 128), jnp.float32),
            pltpu.VMEM((3, 18 * STEP + 32, 128), jnp.float32),
            pltpu.VMEM((2, 20 * STEP, 384), bf16),
            pltpu.VMEM((2, 18 * STEP, 384), bf16),
            pltpu.VMEM((2, 16 * STEP, 128), jnp.float32),
            pltpu.VMEM((GROUPS, 256, 128), jnp.float32),
        ],
        compiler_params=params,
        cost_estimate=pl.CostEstimate(
            flops=2_000_000_000, bytes_accessed=8_000_000, transcendentals=800_000
        ),
        name="upsample_refine",
    )(field, upmat, band1, band2)


def solution(mesh):
    return jax.shard_map(
        body,
        mesh=mesh,
        in_specs=(P("strike", "dip", None), P(), P(), P()),
        out_specs=P("strike", "dip", None),
        check_vma=False,
    )
```

```python
import jax
import jax.numpy as jnp
from jax import lax
from jax.experimental import pallas as pl
from jax.experimental.pallas import tpu as pltpu
from jax.sharding import PartitionSpec as P

GROUPS = 4
PAIRS = 10
STEP = GROUPS * PAIRS
ORDER = ((0, 1, 2, 3), (1, 0, 3, 2))
BESIDE = ((0, 4), (1, 4), (1, -1), (0, -1))
WINDOW = 3 * 2 * 384
LIMIT = 50 * 1024 * 1024


def silu(v):
    half = 0.5 * v
    return half + half * jnp.tanh(half)


def up_kernel(up_hbm, upmat_ref, up_ref, sems):
    fetches = []
    for part in range(4):
        rows = pl.ds(part * 4096, 4096)
        fetches.append(pltpu.make_async_copy(up_hbm.at[rows], up_ref.at[rows], sems.at[part]))
    for fetch in fetches:
        fetch.start()

    for k1 in range(8):
        if k1 % 2 == 0:
            fetches[k1 // 2].wait()
        h1, p1 = divmod(k1, 4)
        for k2 in range(8):
            h2, p2 = divmod(k2, 4)
            for h3 in range(2):
                k = (k1 * 8 + k2) * 8 + 4 * h3
                parts = [up_ref[pl.ds((k + (z + 2) % 4) * 32, 32), :] for z in ORDER[p2 % 2]]
                row = (h1 * 4 + h2 * 2 + (1 - h3)) * 32
                upmat_ref[pl.ds(row, 32), pl.ds((p1 * 4 + p2) * 128, 128)] = jnp.concatenate(
                    parts, axis=1
                )


def band_kernel(first_ref, second_ref, band1_ref, band2_ref):
    ci = lax.broadcasted_iota(jnp.int32, (32, 128), 0)
    lane = lax.broadcasted_iota(jnp.int32, (32, 128), 1)
    group = lane // 32
    copies = (lane % 32 == ci).astype(jnp.bfloat16)

    def arrange(w_ref, band_ref, out_order):
        rep = jnp.dot(w_ref[...], copies, preferred_element_type=jnp.float32)
        for d1 in range(3):
            for dj in range(2):
                cells = [(0, z) for z in ORDER[0]] + [(1, z) for z in ORDER[1]] + list(BESIDE)
                for n, (side, z_in) in enumerate(cells):
                    row = (d1 * 2 + dj) * 384 + n * 32
                    for o in range(2):
                        block = jnp.zeros((32, 128), jnp.float32)
                        d2 = 2 * dj + side - o
                        for d3 in range(3):
                            z_out = z_in - d3 + 1
                            if 0 <= d2 < 3 and 0 <= z_out < 4:
                                tap = ((d1 * 3 + d2) * 3 + d3) * 32
                                here = group == out_order[o].index(z_out)
                                block = jnp.where(here, rep[tap : tap + 32], block)
                        band_ref[pl.ds(row, 32), pl.ds(o * 128, 128)] = block.astype(jnp.bfloat16)

    arrange(first_ref, band1_ref, ORDER)
    arrange(second_ref, band2_ref, (ORDER[0], ORDER[0]))
    r = lax.broadcasted_iota(jnp.int32, (256, 256), 0)
    c = lax.broadcasted_iota(jnp.int32, (256, 256), 1)
    swap = jnp.where((r // 32) % 2 == 0, r + 32, r - 32)
    band2_ref[pl.ds(WINDOW, 256), :] = (jnp.where(r < 128, r, swap) == c).astype(jnp.bfloat16)


def slot_kernel(coarse, slots):
    strike, dip = lax.axis_index("strike"), lax.axis_index("dip")
    n2 = lax.axis_size("dip")
    block = coarse[...].astype(jnp.float32)
    rows = block[0], block[3]
    columns = block[:, 0], block[:, 3]
    for n in range(slots.shape[0]):
        s, d = divmod(n, n2)
        beside = jnp.where(d > dip, columns[1], columns[0])
        slot = jnp.where(s > strike, rows[1], jnp.where(s < strike, rows[0], beside))
        slots[n] = slot.astype(jnp.bfloat16)


def main_kernel(
    coarse, field, upmat, band1, band2, out, cells, fine, hidden, b1, b2, result, woven
):
    strike, dip = lax.axis_index("strike"), lax.axis_index("dip")
    one, zero = jnp.float32(1), jnp.float32(0)
    x_lo = jnp.where(strike == 0, zero, one)
    x_hi = jnp.where(strike == lax.axis_size("strike") - 1, zero, one)
    y_lo = jnp.where(dip == 0, zero, one)
    y_hi = jnp.where(dip == lax.axis_size("dip") - 1, zero, one)

    n1, n2 = lax.axis_size("strike"), lax.axis_size("dip")
    for s1, (x0, x1) in enumerate(((0, 1), (1, 5), (5, 6))):
        for s2, (y0, y1) in enumerate(((0, 1), (1, 5), (5, 6))):
            if s1 == 1 and s2 == 1:
                cells[x0:x1, y0:y1, :] = coarse[...].astype(jnp.float32)
                continue
            c1 = jnp.clip(strike + (s1 - 1), 0, n1 - 1)
            c2 = jnp.clip(dip + (s2 - 1), 0, n2 - 1)
            scale = (x_lo, one, x_hi)[s1] * (y_lo, one, y_hi)[s2]
            slot = field[c1 * n2 + c2].astype(jnp.float32) * scale
            if s1 == 1:
                cells[x0:x1, y0:y1, :] = slot[:, None]
            else:
                cells[x0:x1, y0:y1, :] = slot[(slice(3, 4), slice(0, 4), slice(0, 1))[s2]][None]

    wide = []
    edge = jnp.zeros((40, 32), jnp.float32)
    for h1 in range(2):
        for h2 in range(2):
            window = cells[1 - h1 : 6 - h1, 1 - h2 : 9 - h2, :].reshape(40, 128)
            wide.append(jnp.concatenate([edge, window, edge], axis=1))
    left = jnp.concatenate(
        [
            jnp.concatenate([w[:, 32 * q3 : 32 * q3 + 64] for w in wide], axis=1)
            for q3 in range(5)
        ],
        axis=0,
    ).astype(jnp.bfloat16)

    lane = lax.broadcasted_iota(jnp.int32, (40, 128), 1)
    q2 = lax.broadcasted_iota(jnp.int32, (40, 128), 0) % 8
    outer = (lane < 32) | (lane >= 96)
    front = lane < 64
    low = jnp.where(q2 == 0, y_lo, one)
    high = jnp.where(q2 == 4, y_hi, one)
    none = jnp.zeros((40, 128), jnp.float32)
    for p1 in range(4):
        phase = jnp.dot(left, upmat[:, p1 * 512 : p1 * 512 + 512], preferred_element_type=jnp.float32)
        for pp in range(2):
            tiles = [[], []]
            for side in range(2):
                p2 = 2 * pp + side
                v = phase[:, p2 * 128 : p2 * 128 + 128]
                for g in range(GROUPS):
                    t = jnp.where(front, v[g * 40 : g * 40 + 40], v[g * 40 + 40 : g * 40 + 80])
                    tiles[side].append(silu(t) * (low if pp == 0 else high))
            merged = [jnp.where(outer, tiles[0][g], tiles[1][g]) for g in range(GROUPS)]
            merged = [none] + merged + [none]
            for g in range(GROUPS):
                beside = jnp.where(front, merged[g + 2], merged[g])
                for n, t in enumerate((tiles[0][g], tiles[1][g], beside)):
                    for q1 in range(5):
                        part = t[q1 * 8 : q1 * 8 + 5]
                        if q1 == 0 and p1 < 2:
                            part = part * x_lo
                        if q1 == 4 and p1 >= 2:
                            part = part * x_hi
                        at = (4 * q1 + p1) * STEP + g * PAIRS + pp
                        fine[n, pl.ds(at, 5, stride=2), :] = part

    for dj in range(2):
        for n in range(3):
            b1[dj, :, n * 128 : n * 128 + 128] = fine[n, pl.ds(dj, 20 * STEP), :].astype(jnp.bfloat16)
    m1 = 18 * STEP
    windows = [b1[dj, dx * STEP : dx * STEP + m1, :] for dx in range(3) for dj in range(2)]
    v = silu(
        jnp.dot(jnp.concatenate(windows, axis=1), band1[...], preferred_element_type=jnp.float32)
    )
    row = lax.broadcasted_iota(jnp.int32, (m1, 128), 0)
    lane = lax.broadcasted_iota(jnp.int32, (m1, 128), 1)
    i, g, j = row // STEP, (row // PAIRS) % GROUPS, row % PAIRS
    keep = jnp.where(i == 0, x_lo, one) * jnp.where(i == 17, x_hi, one)
    v0 = v[:, :128] * (keep * jnp.where(j == 0, y_lo, one))
    v1 = v[:, 128:] * (keep * jnp.where(j == 8, y_hi, one))
    hidden[0, 16 : 16 + m1, :] = v0
    hidden[1, 16 : 16 + m1, :] = v1
    hidden[2, 16 : 16 + m1, :] = jnp.where((lane < 32) | (lane >= 96), v0, v1)

    for dj in range(2):
        for n in range(2):
            b2[dj, :, n * 128 : n * 128 + 128] = hidden[n, pl.ds(16 + dj, m1), :].astype(jnp.bfloat16)
        above = jnp.where(g == GROUPS - 1, zero, hidden[2, pl.ds(16 + dj + PAIRS, m1), :])
        below = jnp.where(g == 0, zero, hidden[2, pl.ds(16 + dj - PAIRS, m1), :])
        b2[dj, :, 256:384] = jnp.where(lane < 64, above, below).astype(jnp.bfloat16)
    m2 = 16 * STEP
    windows = [b2[dj, dx * STEP : dx * STEP + m2, :] for dx in range(3) for dj in range(2)]
    windows.append(b1[1, 2 * STEP : 2 * STEP + m2, :256])
    v = jnp.dot(jnp.concatenate(windows, axis=1), band2[...], preferred_element_type=jnp.float32)
    for o in range(2):
        result[o] = v[:, o * 128 : o * 128 + 128]
    for x in range(16):
        for g in range(GROUPS):
            for o in range(2):
                cells8 = result[o, pl.ds(x * STEP + g * PAIRS, 8), :]
                woven[g, pl.ds(x * 16 + o, 8, stride=2), :] = cells8
    for g in range(GROUPS):
        out[:, :, g * 128 : g * 128 + 128] = woven[g].reshape(16, 16, 128).astype(jnp.bfloat16)


def body(coarse, up_weight, first_weight, second_weight):
    vmem = pl.BlockSpec(memory_space=pltpu.VMEM)
    params = pltpu.CompilerParams(vmem_limit_bytes=32 * 1024 * 1024)

    bf16 = jnp.bfloat16
    shape = jax.ShapeDtypeStruct
    count = lax.axis_size("strike") * lax.axis_size("dip")
    slots = pl.pallas_call(
        slot_kernel,
        out_shape=shape((count, 4, 128), bf16),
        in_specs=[vmem],
        out_specs=vmem,
        compiler_params=pltpu.CompilerParams(vmem_limit_bytes=1024 * 1024),
        name="slots",
    )(coarse)
    field = lax.all_to_all(slots, ("strike", "dip"), 0, 0)
    upmat = pl.pallas_call(
        up_kernel,
        out_shape=shape((256, 2048), bf16),
        in_specs=[pl.BlockSpec(memory_space=pltpu.HBM)],
        out_specs=vmem,
        scratch_shapes=[pltpu.VMEM((512 * 32, 32), bf16), pltpu.SemaphoreType.DMA((4,))],
        compiler_params=pltpu.CompilerParams(vmem_limit_bytes=LIMIT),
        cost_estimate=pl.CostEstimate(flops=5_000_000, bytes_accessed=5_000_000, transcendentals=0),
        name="arrange_up",
    )(up_weight.reshape(512 * 32, 32))
    band1, band2 = pl.pallas_call(
        band_kernel,
        out_shape=(shape((WINDOW, 256), bf16), shape((WINDOW + 256, 256), bf16)),
        in_specs=[vmem] * 2,
        out_specs=(vmem, vmem),
        compiler_params=pltpu.CompilerParams(vmem_limit_bytes=16 * 1024 * 1024),
        cost_estimate=pl.CostEstimate(flops=5_000_000, bytes_accessed=5_000_000, transcendentals=0),
        name="arrange_bands",
    )(first_weight.reshape(864, 32), second_weight.reshape(864, 32))
    return pl.pallas_call(
        main_kernel,
        out_shape=jax.ShapeDtypeStruct((16, 16, 512), bf16),
        in_specs=[vmem] * 5,
        out_specs=vmem,
        scratch_shapes=[
            pltpu.VMEM((6, 16, 128), jnp.float32),
            pltpu.VMEM((3, 20 * STEP + 8, 128), jnp.float32),
            pltpu.VMEM((3, 18 * STEP + 32, 128), jnp.float32),
            pltpu.VMEM((2, 20 * STEP, 384), bf16),
            pltpu.VMEM((2, 18 * STEP, 384), bf16),
            pltpu.VMEM((2, 16 * STEP, 128), jnp.float32),
            pltpu.VMEM((GROUPS, 256, 128), jnp.float32),
        ],
        compiler_params=params,
        cost_estimate=pl.CostEstimate(
            flops=2_000_000_000, bytes_accessed=8_000_000, transcendentals=800_000
        ),
        name="upsample_refine",
    )(coarse, field, upmat, band1, band2)


def solution(mesh):
    return jax.shard_map(
        body,
        mesh=mesh,
        in_specs=(P("strike", "dip", None), P(), P(), P()),
        out_specs=P("strike", "dip", None),
        check_vma=False,
    )
```

```python
import jax
import jax.numpy as jnp
from jax import lax
from jax.experimental import pallas as pl
from jax.experimental.pallas import tpu as pltpu
from jax.sharding import PartitionSpec as P

GROUPS = 4
PAIRS = 10
STEP = GROUPS * PAIRS
ORDER = ((0, 1, 2, 3), (1, 0, 3, 2))
BESIDE = ((0, 4), (1, 4), (1, -1), (0, -1))
WINDOW = 3 * 2 * 384
LIMIT = 50 * 1024 * 1024


def silu(v):
    half = 0.5 * v
    return half + half * jnp.tanh(half)


def up_kernel(up_hbm, upmat_ref, token_ref, up_ref, sems):
    fetches = []
    for part in range(4):
        rows = pl.ds(part * 4096, 4096)
        fetches.append(pltpu.make_async_copy(up_hbm.at[rows], up_ref.at[rows], sems.at[part]))
    for fetch in fetches:
        fetch.start()
    token_ref[...] = jnp.zeros((8, 128), jnp.float32)

    for k1 in range(8):
        if k1 % 2 == 0:
            fetches[k1 // 2].wait()
        h1, p1 = divmod(k1, 4)
        for k2 in range(8):
            h2, p2 = divmod(k2, 4)
            for h3 in range(2):
                k = (k1 * 8 + k2) * 8 + 4 * h3
                parts = [up_ref[pl.ds((k + (z + 2) % 4) * 32, 32), :] for z in ORDER[p2 % 2]]
                row = (h1 * 4 + h2 * 2 + (1 - h3)) * 32
                upmat_ref[pl.ds(row, 32), pl.ds((p1 * 4 + p2) * 128, 128)] = jnp.concatenate(
                    parts, axis=1
                )


def band_kernel(first_ref, second_ref, band1_ref, band2_ref):
    ci = lax.broadcasted_iota(jnp.int32, (32, 128), 0)
    lane = lax.broadcasted_iota(jnp.int32, (32, 128), 1)
    group = lane // 32
    copies = (lane % 32 == ci).astype(jnp.bfloat16)

    def arrange(w_ref, band_ref, out_order):
        rep = jnp.dot(w_ref[...], copies, preferred_element_type=jnp.float32)
        for d1 in range(3):
            for dj in range(2):
                cells = [(0, z) for z in ORDER[0]] + [(1, z) for z in ORDER[1]] + list(BESIDE)
                for n, (side, z_in) in enumerate(cells):
                    row = (d1 * 2 + dj) * 384 + n * 32
                    for o in range(2):
                        block = jnp.zeros((32, 128), jnp.float32)
                        d2 = 2 * dj + side - o
                        for d3 in range(3):
                            z_out = z_in - d3 + 1
                            if 0 <= d2 < 3 and 0 <= z_out < 4:
                                tap = ((d1 * 3 + d2) * 3 + d3) * 32
                                here = group == out_order[o].index(z_out)
                                block = jnp.where(here, rep[tap : tap + 32], block)
                        band_ref[pl.ds(row, 32), pl.ds(o * 128, 128)] = block.astype(jnp.bfloat16)

    arrange(first_ref, band1_ref, ORDER)
    arrange(second_ref, band2_ref, (ORDER[0], ORDER[0]))
    r = lax.broadcasted_iota(jnp.int32, (256, 256), 0)
    c = lax.broadcasted_iota(jnp.int32, (256, 256), 1)
    swap = jnp.where((r // 32) % 2 == 0, r + 32, r - 32)
    band2_ref[pl.ds(WINDOW, 256), :] = (jnp.where(r < 128, r, swap) == c).astype(jnp.bfloat16)


def pack_kernel(coarse, dip_a, dip_b, token, own):
    own[0:4] = coarse[...]
    own[4:8] = dip_a[...]
    own[8:12] = dip_b[...]


def main_kernel(
    own, strike_a, strike_b, upmat, band1, band2, out, cells, fine, hidden, b1, b2, result, woven
):
    strike, dip = lax.axis_index("strike"), lax.axis_index("dip")
    one, zero = jnp.float32(1), jnp.float32(0)
    x_lo = jnp.where(strike == 0, zero, one)
    x_hi = jnp.where(strike == lax.axis_size("strike") - 1, zero, one)
    y_lo = jnp.where(dip == 0, zero, one)
    y_hi = jnp.where(dip == lax.axis_size("dip") - 1, zero, one)

    x_even, y_even = strike % 2 == 0, dip % 2 == 0
    below_y, above_y = jnp.where(y_even, 8, 4), jnp.where(y_even, 4, 8)

    def put(x0, x1, block):
        cells[x0:x1, 1:5, :] = block(0)
        cells[x0:x1, 0:1, :] = block(below_y)[:, 3:4]
        cells[x0:x1, 5:6, :] = block(above_y)[:, 0:1]

    def read(ref, first, count):
        return ref[pl.ds(first, count)].astype(jnp.float32)

    put(0, 1, lambda o: jnp.where(x_even, read(strike_b, o + 3, 1), read(strike_a, o + 3, 1)))
    put(1, 5, lambda o: read(own, o, 4))
    put(5, 6, lambda o: jnp.where(x_even, read(strike_a, o, 1), read(strike_b, o, 1)))

    wide = []
    edge = jnp.zeros((40, 32), jnp.float32)
    for h1 in range(2):
        for h2 in range(2):
            window = cells[1 - h1 : 6 - h1, 1 - h2 : 9 - h2, :].reshape(40, 128)
            wide.append(jnp.concatenate([edge, window, edge], axis=1))
    left = jnp.concatenate(
        [
            jnp.concatenate([w[:, 32 * q3 : 32 * q3 + 64] for w in wide], axis=1)
            for q3 in range(5)
        ],
        axis=0,
    ).astype(jnp.bfloat16)

    lane = lax.broadcasted_iota(jnp.int32, (40, 128), 1)
    q2 = lax.broadcasted_iota(jnp.int32, (40, 128), 0) % 8
    outer = (lane < 32) | (lane >= 96)
    front = lane < 64
    low = jnp.where(q2 == 0, y_lo, one)
    high = jnp.where(q2 == 4, y_hi, one)
    none = jnp.zeros((40, 128), jnp.float32)
    for p1 in range(4):
        phase = jnp.dot(left, upmat[:, p1 * 512 : p1 * 512 + 512], preferred_element_type=jnp.float32)
        for pp in range(2):
            tiles = [[], []]
            for side in range(2):
                p2 = 2 * pp + side
                v = phase[:, p2 * 128 : p2 * 128 + 128]
                for g in range(GROUPS):
                    t = jnp.where(front, v[g * 40 : g * 40 + 40], v[g * 40 + 40 : g * 40 + 80])
                    tiles[side].append(silu(t) * (low if pp == 0 else high))
            merged = [jnp.where(outer, tiles[0][g], tiles[1][g]) for g in range(GROUPS)]
            merged = [none] + merged + [none]
            for g in range(GROUPS):
                beside = jnp.where(front, merged[g + 2], merged[g])
                for n, t in enumerate((tiles[0][g], tiles[1][g], beside)):
                    for q1 in range(5):
                        part = t[q1 * 8 : q1 * 8 + 5]
                        if q1 == 0 and p1 < 2:
                            part = part * x_lo
                        if q1 == 4 and p1 >= 2:
                            part = part * x_hi
                        at = (4 * q1 + p1) * STEP + g * PAIRS + pp
                        fine[n, pl.ds(at, 5, stride=2), :] = part

    for dj in range(2):
        for n in range(3):
            b1[dj, :, n * 128 : n * 128 + 128] = fine[n, pl.ds(dj, 20 * STEP), :].astype(jnp.bfloat16)
    m1 = 18 * STEP
    windows = [b1[dj, dx * STEP : dx * STEP + m1, :] for dx in range(3) for dj in range(2)]
    v = silu(
        jnp.dot(jnp.concatenate(windows, axis=1), band1[...], preferred_element_type=jnp.float32)
    )
    row = lax.broadcasted_iota(jnp.int32, (STEP, 128), 0)
    lane = lax.broadcasted_iota(jnp.int32, (STEP, 128), 1)
    starts = [g * PAIRS for g in range(GROUPS)]
    first, last = row == starts[0], row == starts[0] + 8
    for start in starts[1:]:
        first, last = first | (row == start), last | (row == start + 8)
    y_first, y_last = jnp.where(first, y_lo, one), jnp.where(last, y_hi, one)
    outer = (lane < 32) | (lane >= 96)
    front = lane < 64
    inside_above = jnp.where(row < starts[-1], one, zero)
    inside_below = jnp.where(row >= PAIRS, one, zero)
    inside = jnp.where(front, inside_above, inside_below)
    hidden[2, 0:16, :] = jnp.zeros((16, 128), jnp.float32)
    hidden[2, 16 + m1 : 32 + m1, :] = jnp.zeros((16, 128), jnp.float32)
    for x in range(18):
        rows = slice(x * STEP, x * STEP + STEP)
        v0, v1 = v[rows, :128] * y_first, v[rows, 128:] * y_last
        if x in (0, 17):
            edge = x_lo if x == 0 else x_hi
            v0, v1 = v0 * edge, v1 * edge
        hidden[0, 16 + x * STEP : 16 + x * STEP + STEP, :] = v0
        hidden[1, 16 + x * STEP : 16 + x * STEP + STEP, :] = v1
        hidden[2, 16 + x * STEP : 16 + x * STEP + STEP, :] = jnp.where(outer, v0, v1)

    def by_strike(block):
        return block.reshape(18, STEP, 128)

    for dj in range(2):
        for n in range(2):
            b2[dj, :, n * 128 : n * 128 + 128] = hidden[n, pl.ds(16 + dj, m1), :].astype(jnp.bfloat16)
        above = by_strike(hidden[2, pl.ds(16 + dj + PAIRS, m1), :])
        below = by_strike(hidden[2, pl.ds(16 + dj - PAIRS, m1), :])
        beside = jnp.where(front[None], above, below) * inside[None]
        b2[dj, :, 256:384] = beside.reshape(m1, 128).astype(jnp.bfloat16)
    m2 = 16 * STEP
    windows = [b2[dj, dx * STEP : dx * STEP + m2, :] for dx in range(3) for dj in range(2)]
    windows.append(b1[1, 2 * STEP : 2 * STEP + m2, :256])
    v = jnp.dot(jnp.concatenate(windows, axis=1), band2[...], preferred_element_type=jnp.float32)
    for o in range(2):
        result[o] = v[:, o * 128 : o * 128 + 128]
    for x in range(16):
        for g in range(GROUPS):
            for o in range(2):
                cells8 = result[o, pl.ds(x * STEP + g * PAIRS, 8), :]
                woven[g, pl.ds(x * 16 + o, 8, stride=2), :] = cells8
    for g in range(GROUPS):
        out[:, :, g * 128 : g * 128 + 128] = woven[g].reshape(16, 16, 128).astype(jnp.bfloat16)


def swapped(block, axis):
    size = lax.axis_size(axis)
    for first in (0, 1):
        pairs = [(i, i + 1) for i in range(first, size - 1, 2)]
        yield lax.ppermute(block, axis, pairs + [(j, i) for i, j in pairs])


def body(coarse, up_weight, first_weight, second_weight):
    vmem = pl.BlockSpec(memory_space=pltpu.VMEM)
    params = pltpu.CompilerParams(vmem_limit_bytes=32 * 1024 * 1024)

    bf16 = jnp.bfloat16
    shape = jax.ShapeDtypeStruct
    dip_a, dip_b = swapped(coarse, "dip")
    upmat, token = pl.pallas_call(
        up_kernel,
        out_shape=(shape((256, 2048), bf16), shape((8, 128), jnp.float32)),
        in_specs=[pl.BlockSpec(memory_space=pltpu.HBM)],
        out_specs=(vmem, vmem),
        scratch_shapes=[pltpu.VMEM((512 * 32, 32), bf16), pltpu.SemaphoreType.DMA((4,))],
        compiler_params=pltpu.CompilerParams(vmem_limit_bytes=LIMIT),
        cost_estimate=pl.CostEstimate(flops=5_000_000, bytes_accessed=5_000_000, transcendentals=0),
        name="arrange_up",
    )(up_weight.reshape(512 * 32, 32))
    own = pl.pallas_call(
        pack_kernel,
        out_shape=shape((12, 4, 128), bf16),
        in_specs=[vmem] * 4,
        out_specs=vmem,
        compiler_params=pltpu.CompilerParams(vmem_limit_bytes=1024 * 1024),
        name="pack",
    )(coarse, dip_a, dip_b, token)
    strike_a, strike_b = swapped(own, "strike")
    band1, band2 = pl.pallas_call(
        band_kernel,
        out_shape=(shape((WINDOW, 256), bf16), shape((WINDOW + 256, 256), bf16)),
        in_specs=[vmem] * 2,
        out_specs=(vmem, vmem),
        compiler_params=pltpu.CompilerParams(vmem_limit_bytes=16 * 1024 * 1024),
        cost_estimate=pl.CostEstimate(flops=5_000_000, bytes_accessed=5_000_000, transcendentals=0),
        name="arrange_bands",
    )(first_weight.reshape(864, 32), second_weight.reshape(864, 32))
    return pl.pallas_call(
        main_kernel,
        out_shape=jax.ShapeDtypeStruct((16, 16, 512), bf16),
        in_specs=[vmem] * 6,
        out_specs=vmem,
        scratch_shapes=[
            pltpu.VMEM((6, 16, 128), jnp.float32),
            pltpu.VMEM((3, 20 * STEP + 8, 128), jnp.float32),
            pltpu.VMEM((3, 18 * STEP + 32, 128), jnp.float32),
            pltpu.VMEM((2, 20 * STEP, 384), bf16),
            pltpu.VMEM((2, 18 * STEP, 384), bf16),
            pltpu.VMEM((2, 16 * STEP, 128), jnp.float32),
            pltpu.VMEM((GROUPS, 256, 128), jnp.float32),
        ],
        compiler_params=params,
        cost_estimate=pl.CostEstimate(
            flops=2_000_000_000, bytes_accessed=8_000_000, transcendentals=800_000
        ),
        name="upsample_refine",
    )(own, strike_a, strike_b, upmat, band1, band2)


def solution(mesh):
    return jax.shard_map(
        body,
        mesh=mesh,
        in_specs=(P("strike", "dip", None), P(), P(), P()),
        out_specs=P("strike", "dip", None),
        check_vma=False,
    )
```

```python
import jax
import jax.numpy as jnp
from jax import lax
from jax.experimental import pallas as pl
from jax.experimental.pallas import tpu as pltpu
from jax.sharding import PartitionSpec as P

GROUPS = 4
PAIRS = 10
STEP = GROUPS * PAIRS
ORDER = ((0, 1, 2, 3), (1, 0, 3, 2))
BESIDE = ((0, 4), (1, 4), (1, -1), (0, -1))
WINDOW = 3 * 2 * 384
PARTS = 2
LIMIT = 50 * 1024 * 1024


def silu(v):
    half = 0.5 * v
    return half + half * jnp.tanh(half)


def up_kernel(up_hbm, upmat_ref, token_ref, up_ref, sems):
    fetches = []
    for part in range(4):
        rows = pl.ds(part * 4096, 4096)
        fetches.append(pltpu.make_async_copy(up_hbm.at[rows], up_ref.at[rows], sems.at[part]))
    for fetch in fetches:
        fetch.start()
    token_ref[...] = jnp.zeros((8, 128), jnp.float32)

    for k1 in range(8):
        if k1 % 2 == 0:
            fetches[k1 // 2].wait()
        h1, p1 = divmod(k1, 4)
        for k2 in range(8):
            h2, p2 = divmod(k2, 4)
            for h3 in range(2):
                k = (k1 * 8 + k2) * 8 + 4 * h3
                parts = [up_ref[pl.ds((k + (z + 2) % 4) * 32, 32), :] for z in ORDER[p2 % 2]]
                row = (h1 * 4 + h2 * 2 + (1 - h3)) * 32
                upmat_ref[pl.ds(row, 32), pl.ds((p1 * 4 + p2) * 128, 128)] = jnp.concatenate(
                    parts, axis=1
                )


def band_kernel(first_ref, second_ref, band1_ref, band2_ref):
    ci = lax.broadcasted_iota(jnp.int32, (32, 128), 0)
    lane = lax.broadcasted_iota(jnp.int32, (32, 128), 1)
    group = lane // 32
    copies = (lane % 32 == ci).astype(jnp.bfloat16)

    def arrange(w_ref, band_ref, out_order):
        rep = jnp.dot(w_ref[...], copies, preferred_element_type=jnp.float32)
        for d1 in range(3):
            for dj in range(2):
                cells = [(0, z) for z in ORDER[0]] + [(1, z) for z in ORDER[1]] + list(BESIDE)
                for n, (side, z_in) in enumerate(cells):
                    row = (d1 * 2 + dj) * 384 + n * 32
                    for o in range(2):
                        block = jnp.zeros((32, 128), jnp.float32)
                        d2 = 2 * dj + side - o
                        for d3 in range(3):
                            z_out = z_in - d3 + 1
                            if 0 <= d2 < 3 and 0 <= z_out < 4:
                                tap = ((d1 * 3 + d2) * 3 + d3) * 32
                                here = group == out_order[o].index(z_out)
                                block = jnp.where(here, rep[tap : tap + 32], block)
                        band_ref[pl.ds(row, 32), pl.ds(o * 128, 128)] = block.astype(jnp.bfloat16)

    arrange(first_ref, band1_ref, ORDER)
    arrange(second_ref, band2_ref, (ORDER[0], ORDER[0]))
    r = lax.broadcasted_iota(jnp.int32, (256, 256), 0)
    c = lax.broadcasted_iota(jnp.int32, (256, 256), 1)
    swap = jnp.where((r // 32) % 2 == 0, r + 32, r - 32)
    band2_ref[pl.ds(WINDOW, 256), :] = (jnp.where(r < 128, r, swap) == c).astype(jnp.bfloat16)


def pack_kernel(coarse, dip_a, dip_b, token, own):
    own[0:4] = coarse[...]
    own[4:8] = dip_a[...]
    own[8:12] = dip_b[...]


def main_kernel(
    own, strike_a, strike_b, upmat, band1, band2, out, cells, fine, hidden, b1, b2, result, woven, near, sems
):
    strike, dip = lax.axis_index("strike"), lax.axis_index("dip")
    one, zero = jnp.float32(1), jnp.float32(0)
    x_lo = jnp.where(strike == 0, zero, one)
    x_hi = jnp.where(strike == lax.axis_size("strike") - 1, zero, one)
    y_lo = jnp.where(dip == 0, zero, one)
    y_hi = jnp.where(dip == lax.axis_size("dip") - 1, zero, one)

    x_even, y_even = strike % 2 == 0, dip % 2 == 0
    below_y, above_y = jnp.where(y_even, 8, 4), jnp.where(y_even, 4, 8)

    def put(x0, x1, block):
        cells[x0:x1, 1:5, :] = block(0)
        cells[x0:x1, 0:1, :] = block(below_y)[:, 3:4]
        cells[x0:x1, 5:6, :] = block(above_y)[:, 0:1]

    def read(ref, first, count):
        return ref[pl.ds(first, count)].astype(jnp.float32)

    put(0, 1, lambda o: jnp.where(x_even, read(strike_b, o + 3, 1), read(strike_a, o + 3, 1)))
    put(1, 5, lambda o: read(own, o, 4))
    put(5, 6, lambda o: jnp.where(x_even, read(strike_a, o, 1), read(strike_b, o, 1)))

    wide = []
    edge = jnp.zeros((40, 32), jnp.float32)
    for h1 in range(2):
        for h2 in range(2):
            window = cells[1 - h1 : 6 - h1, 1 - h2 : 9 - h2, :].reshape(40, 128)
            wide.append(jnp.concatenate([edge, window, edge], axis=1))
    left = jnp.concatenate(
        [
            jnp.concatenate([w[:, 32 * q3 : 32 * q3 + 64] for w in wide], axis=1)
            for q3 in range(5)
        ],
        axis=0,
    ).astype(jnp.bfloat16)

    lane = lax.broadcasted_iota(jnp.int32, (40, 128), 1)
    q2 = lax.broadcasted_iota(jnp.int32, (40, 128), 0) % 8
    outer = (lane < 32) | (lane >= 96)
    front = lane < 64
    low = jnp.where(q2 == 0, y_lo, one)
    high = jnp.where(q2 == 4, y_hi, one)
    none = jnp.zeros((40, 128), jnp.float32)
    for p1 in range(4):
        phase = jnp.dot(left, upmat[:, p1 * 512 : p1 * 512 + 512], preferred_element_type=jnp.float32)
        for pp in range(2):
            tiles = [[], []]
            for side in range(2):
                p2 = 2 * pp + side
                v = phase[:, p2 * 128 : p2 * 128 + 128]
                for g in range(GROUPS):
                    t = jnp.where(front, v[g * 40 : g * 40 + 40], v[g * 40 + 40 : g * 40 + 80])
                    tiles[side].append(silu(t) * (low if pp == 0 else high))
            merged = [jnp.where(outer, tiles[0][g], tiles[1][g]) for g in range(GROUPS)]
            merged = [none] + merged + [none]
            for g in range(GROUPS):
                beside = jnp.where(front, merged[g + 2], merged[g])
                for n, t in enumerate((tiles[0][g], tiles[1][g], beside)):
                    for q1 in range(5):
                        part = t[q1 * 8 : q1 * 8 + 5]
                        if q1 == 0 and p1 < 2:
                            part = part * x_lo
                        if q1 == 4 and p1 >= 2:
                            part = part * x_hi
                        at = (4 * q1 + p1) * STEP + g * PAIRS + pp
                        fine[n, pl.ds(at, 5, stride=2), :] = part

    for dj in range(2):
        for n in range(3):
            b1[dj, :, n * 128 : n * 128 + 128] = fine[n, pl.ds(dj, 20 * STEP), :].astype(jnp.bfloat16)
    m1 = 18 * STEP
    row = lax.broadcasted_iota(jnp.int32, (STEP, 128), 0)
    lane = lax.broadcasted_iota(jnp.int32, (STEP, 128), 1)
    starts = [g * PAIRS for g in range(GROUPS)]
    first, last = row == starts[0], row == starts[0] + 8
    for start in starts[1:]:
        first, last = first | (row == start), last | (row == start + 8)
    y_first, y_last = jnp.where(first, y_lo, one), jnp.where(last, y_hi, one)
    outer = (lane < 32) | (lane >= 96)
    front = lane < 64
    inside_above = jnp.where(row < starts[-1], one, zero)
    inside_below = jnp.where(row >= PAIRS, one, zero)
    inside = jnp.where(front, inside_above, inside_below)
    hidden[2, 0:16, :] = jnp.zeros((16, 128), jnp.float32)
    hidden[2, 16 + m1 : 32 + m1, :] = jnp.zeros((16, 128), jnp.float32)
    def product(source, first, count, taps, extra=()):
        rows = count * STEP
        windows = [
            source[dj, (first + dx) * STEP : (first + dx) * STEP + rows, :]
            for dx in range(3)
            for dj in range(2)
        ]
        windows += [block[:, :] for block in extra]
        return jnp.dot(
            jnp.concatenate(windows, axis=1), taps[...], preferred_element_type=jnp.float32
        )

    part = 18 // PARTS
    for first in range(0, 18, part):
        v = silu(product(b1, first, part, band1))
        for x in range(first, first + part):
            rows = slice((x - first) * STEP, (x - first) * STEP + STEP)
            v0, v1 = v[rows, :128] * y_first, v[rows, 128:] * y_last
            if x in (0, 17):
                edge = x_lo if x == 0 else x_hi
                v0, v1 = v0 * edge, v1 * edge
            hidden[0, 16 + x * STEP : 16 + x * STEP + STEP, :] = v0
            hidden[1, 16 + x * STEP : 16 + x * STEP + STEP, :] = v1
            hidden[2, 16 + x * STEP : 16 + x * STEP + STEP, :] = jnp.where(outer, v0, v1)

    def by_strike(block):
        return block.reshape(18, STEP, 128)

    for dj in range(2):
        for n in range(2):
            b2[dj, :, n * 128 : n * 128 + 128] = hidden[n, pl.ds(16 + dj, m1), :].astype(jnp.bfloat16)
        above = by_strike(hidden[2, pl.ds(16 + dj + PAIRS, m1), :])
        below = by_strike(hidden[2, pl.ds(16 + dj - PAIRS, m1), :])
        beside = jnp.where(front[None], above, below) * inside[None]
        b2[dj, :, 256:384] = beside.reshape(m1, 128).astype(jnp.bfloat16)
    part = 16 // PARTS
    sends = []
    for n in range(PARTS):
        first = n * part
        base = b1[1, (2 + first) * STEP : (2 + first + part) * STEP, :256]
        v = product(b2, first, part, band2, (base,))
        for o in range(2):
            result[o, first * STEP : (first + part) * STEP] = v[:, o * 128 : o * 128 + 128]
        for x in range(first, first + part):
            for g in range(GROUPS):
                for o in range(2):
                    cells8 = result[o, pl.ds(x * STEP + g * PAIRS, 8), :]
                    woven[g, pl.ds(x * 16 + o, 8, stride=2), :] = cells8
        for g in range(GROUPS):
            near[first : first + part, :, g * 128 : g * 128 + 128] = (
                woven[g, first * 16 : (first + part) * 16].reshape(part, 16, 128).astype(jnp.bfloat16)
            )
        here = pl.ds(first, part)
        sends.append(pltpu.make_async_copy(near.at[here], out.at[here], sems.at[n]))
        sends[-1].start()
    for send in sends:
        send.wait()


def swapped(block, axis):
    size = lax.axis_size(axis)
    for first in (0, 1):
        pairs = [(i, i + 1) for i in range(first, size - 1, 2)]
        yield lax.ppermute(block, axis, pairs + [(j, i) for i, j in pairs])


def body(coarse, up_weight, first_weight, second_weight):
    vmem = pl.BlockSpec(memory_space=pltpu.VMEM)
    params = pltpu.CompilerParams(vmem_limit_bytes=32 * 1024 * 1024)

    bf16 = jnp.bfloat16
    shape = jax.ShapeDtypeStruct
    dip_a, dip_b = swapped(coarse, "dip")
    upmat, token = pl.pallas_call(
        up_kernel,
        out_shape=(shape((256, 2048), bf16), shape((8, 128), jnp.float32)),
        in_specs=[pl.BlockSpec(memory_space=pltpu.HBM)],
        out_specs=(vmem, vmem),
        scratch_shapes=[pltpu.VMEM((512 * 32, 32), bf16), pltpu.SemaphoreType.DMA((4,))],
        compiler_params=pltpu.CompilerParams(vmem_limit_bytes=LIMIT),
        cost_estimate=pl.CostEstimate(flops=5_000_000, bytes_accessed=5_000_000, transcendentals=0),
        name="arrange_up",
    )(up_weight.reshape(512 * 32, 32))
    own = pl.pallas_call(
        pack_kernel,
        out_shape=shape((12, 4, 128), bf16),
        in_specs=[vmem] * 4,
        out_specs=vmem,
        compiler_params=pltpu.CompilerParams(vmem_limit_bytes=1024 * 1024),
        name="pack",
    )(coarse, dip_a, dip_b, token)
    strike_a, strike_b = swapped(own, "strike")
    band1, band2 = pl.pallas_call(
        band_kernel,
        out_shape=(shape((WINDOW, 256), bf16), shape((WINDOW + 256, 256), bf16)),
        in_specs=[vmem] * 2,
        out_specs=(vmem, vmem),
        compiler_params=pltpu.CompilerParams(vmem_limit_bytes=16 * 1024 * 1024),
        cost_estimate=pl.CostEstimate(flops=5_000_000, bytes_accessed=5_000_000, transcendentals=0),
        name="arrange_bands",
    )(first_weight.reshape(864, 32), second_weight.reshape(864, 32))
    return pl.pallas_call(
        main_kernel,
        out_shape=jax.ShapeDtypeStruct((16, 16, 512), bf16),
        in_specs=[vmem] * 6,
        out_specs=pl.BlockSpec(memory_space=pltpu.HBM),
        scratch_shapes=[
            pltpu.VMEM((6, 16, 128), jnp.float32),
            pltpu.VMEM((3, 20 * STEP + 8, 128), jnp.float32),
            pltpu.VMEM((3, 18 * STEP + 32, 128), jnp.float32),
            pltpu.VMEM((2, 20 * STEP, 384), bf16),
            pltpu.VMEM((2, 18 * STEP, 384), bf16),
            pltpu.VMEM((2, 16 * STEP, 128), jnp.float32),
            pltpu.VMEM((GROUPS, 256, 128), jnp.float32),
            pltpu.VMEM((16, 16, 512), bf16),
            pltpu.SemaphoreType.DMA((PARTS,)),
        ],
        compiler_params=params,
        cost_estimate=pl.CostEstimate(
            flops=2_000_000_000, bytes_accessed=8_000_000, transcendentals=800_000
        ),
        name="upsample_refine",
    )(own, strike_a, strike_b, upmat, band1, band2)


def solution(mesh):
    return jax.shard_map(
        body,
        mesh=mesh,
        in_specs=(P("strike", "dip", None), P(), P(), P()),
        out_specs=P("strike", "dip", None),
        check_vma=False,
    )
```

```python
import jax
import jax.numpy as jnp
from jax import lax
from jax.experimental import pallas as pl
from jax.experimental.pallas import tpu as pltpu
from jax.sharding import PartitionSpec as P

GROUPS = 4
PAIRS = 10
STEP = GROUPS * PAIRS
ORDER = ((0, 1, 2, 3), (1, 0, 3, 2))
BESIDE = ((0, 4), (1, 4), (1, -1), (0, -1))
WINDOW = 3 * 2 * 384
FIRST_PARTS, SECOND_PARTS = 3, 4
LIMIT = 50 * 1024 * 1024


def silu(v):
    half = 0.5 * v
    return half + half * jnp.tanh(half)


def up_kernel(up_hbm, upmat_ref, token_ref, up_ref, sems):
    fetches = []
    for part in range(4):
        rows = pl.ds(part * 4096, 4096)
        fetches.append(pltpu.make_async_copy(up_hbm.at[rows], up_ref.at[rows], sems.at[part]))
    for fetch in fetches:
        fetch.start()
    token_ref[...] = jnp.zeros((8, 128), jnp.float32)

    for k1 in range(8):
        if k1 % 2 == 0:
            fetches[k1 // 2].wait()
        h1, p1 = divmod(k1, 4)
        for k2 in range(8):
            h2, p2 = divmod(k2, 4)
            for h3 in range(2):
                k = (k1 * 8 + k2) * 8 + 4 * h3
                parts = [up_ref[pl.ds((k + (z + 2) % 4) * 32, 32), :] for z in ORDER[p2 % 2]]
                row = (h1 * 4 + h2 * 2 + (1 - h3)) * 32
                upmat_ref[pl.ds(row, 32), pl.ds((p1 * 4 + p2) * 128, 128)] = jnp.concatenate(
                    parts, axis=1
                )


def band_kernel(first_ref, second_ref, band1_ref, band2_ref):
    ci = lax.broadcasted_iota(jnp.int32, (32, 128), 0)
    lane = lax.broadcasted_iota(jnp.int32, (32, 128), 1)
    group = lane // 32
    copies = (lane % 32 == ci).astype(jnp.bfloat16)

    def arrange(w_ref, band_ref, out_order):
        rep = jnp.dot(w_ref[...], copies, preferred_element_type=jnp.float32)
        for d1 in range(3):
            for dj in range(2):
                cells = [(0, z) for z in ORDER[0]] + [(1, z) for z in ORDER[1]] + list(BESIDE)
                for n, (side, z_in) in enumerate(cells):
                    row = (d1 * 2 + dj) * 384 + n * 32
                    for o in range(2):
                        block = jnp.zeros((32, 128), jnp.float32)
                        d2 = 2 * dj + side - o
                        for d3 in range(3):
                            z_out = z_in - d3 + 1
                            if 0 <= d2 < 3 and 0 <= z_out < 4:
                                tap = ((d1 * 3 + d2) * 3 + d3) * 32
                                here = group == out_order[o].index(z_out)
                                block = jnp.where(here, rep[tap : tap + 32], block)
                        band_ref[pl.ds(row, 32), pl.ds(o * 128, 128)] = block.astype(jnp.bfloat16)

    arrange(first_ref, band1_ref, ORDER)
    arrange(second_ref, band2_ref, (ORDER[0], ORDER[0]))
    r = lax.broadcasted_iota(jnp.int32, (256, 256), 0)
    c = lax.broadcasted_iota(jnp.int32, (256, 256), 1)
    swap = jnp.where((r // 32) % 2 == 0, r + 32, r - 32)
    band2_ref[pl.ds(WINDOW, 256), :] = (jnp.where(r < 128, r, swap) == c).astype(jnp.bfloat16)


def pack_kernel(coarse, dip_a, dip_b, token, own):
    own[0:4] = coarse[...]
    own[4:8] = dip_a[...]
    own[8:12] = dip_b[...]


def main_kernel(
    own, strike_a, strike_b, upmat, band1, band2, out, cells, fine, hidden, b1, b2, result, woven, near, sems
):
    strike, dip = lax.axis_index("strike"), lax.axis_index("dip")
    one, zero = jnp.float32(1), jnp.float32(0)
    x_lo = jnp.where(strike == 0, zero, one)
    x_hi = jnp.where(strike == lax.axis_size("strike") - 1, zero, one)
    y_lo = jnp.where(dip == 0, zero, one)
    y_hi = jnp.where(dip == lax.axis_size("dip") - 1, zero, one)

    x_even, y_even = strike % 2 == 0, dip % 2 == 0
    below_y, above_y = jnp.where(y_even, 8, 4), jnp.where(y_even, 4, 8)

    def put(x0, x1, block):
        cells[x0:x1, 1:5, :] = block(0)
        cells[x0:x1, 0:1, :] = block(below_y)[:, 3:4]
        cells[x0:x1, 5:6, :] = block(above_y)[:, 0:1]

    def read(ref, first, count):
        return ref[pl.ds(first, count)].astype(jnp.float32)

    put(0, 1, lambda o: jnp.where(x_even, read(strike_b, o + 3, 1), read(strike_a, o + 3, 1)))
    put(1, 5, lambda o: read(own, o, 4))
    put(5, 6, lambda o: jnp.where(x_even, read(strike_a, o, 1), read(strike_b, o, 1)))

    wide = []
    edge = jnp.zeros((40, 32), jnp.float32)
    for h1 in range(2):
        for h2 in range(2):
            window = cells[1 - h1 : 6 - h1, 1 - h2 : 9 - h2, :].reshape(40, 128)
            wide.append(jnp.concatenate([edge, window, edge], axis=1))
    left = jnp.concatenate(
        [
            jnp.concatenate([w[:, 32 * q3 : 32 * q3 + 64] for w in wide], axis=1)
            for q3 in range(5)
        ],
        axis=0,
    ).astype(jnp.bfloat16)

    lane = lax.broadcasted_iota(jnp.int32, (40, 128), 1)
    q2 = lax.broadcasted_iota(jnp.int32, (40, 128), 0) % 8
    outer = (lane < 32) | (lane >= 96)
    front = lane < 64
    low = jnp.where(q2 == 0, y_lo, one)
    high = jnp.where(q2 == 4, y_hi, one)
    none = jnp.zeros((40, 128), jnp.float32)
    for p1 in range(4):
        phase = jnp.dot(left, upmat[:, p1 * 512 : p1 * 512 + 512], preferred_element_type=jnp.float32)
        for pp in range(2):
            tiles = [[], []]
            for side in range(2):
                p2 = 2 * pp + side
                v = phase[:, p2 * 128 : p2 * 128 + 128]
                for g in range(GROUPS):
                    t = jnp.where(front, v[g * 40 : g * 40 + 40], v[g * 40 + 40 : g * 40 + 80])
                    tiles[side].append(silu(t) * (low if pp == 0 else high))
            merged = [jnp.where(outer, tiles[0][g], tiles[1][g]) for g in range(GROUPS)]
            merged = [none] + merged + [none]
            for g in range(GROUPS):
                beside = jnp.where(front, merged[g + 2], merged[g])
                for n, t in enumerate((tiles[0][g], tiles[1][g], beside)):
                    for q1 in range(5):
                        part = t[q1 * 8 : q1 * 8 + 5]
                        if q1 == 0 and p1 < 2:
                            part = part * x_lo
                        if q1 == 4 and p1 >= 2:
                            part = part * x_hi
                        at = (4 * q1 + p1) * STEP + g * PAIRS + pp
                        fine[n, pl.ds(at, 5, stride=2), :] = part

    for dj in range(2):
        for n in range(3):
            b1[dj, :, n * 128 : n * 128 + 128] = fine[n, pl.ds(dj, 20 * STEP), :].astype(jnp.bfloat16)
    m1 = 18 * STEP
    row = lax.broadcasted_iota(jnp.int32, (STEP, 128), 0)
    lane = lax.broadcasted_iota(jnp.int32, (STEP, 128), 1)
    starts = [g * PAIRS for g in range(GROUPS)]
    first, last = row == starts[0], row == starts[0] + 8
    for start in starts[1:]:
        first, last = first | (row == start), last | (row == start + 8)
    y_first, y_last = jnp.where(first, y_lo, one), jnp.where(last, y_hi, one)
    outer = (lane < 32) | (lane >= 96)
    front = lane < 64
    inside_above = jnp.where(row < starts[-1], one, zero)
    inside_below = jnp.where(row >= PAIRS, one, zero)
    inside = jnp.where(front, inside_above, inside_below)
    hidden[2, 0:16, :] = jnp.zeros((16, 128), jnp.float32)
    hidden[2, 16 + m1 : 32 + m1, :] = jnp.zeros((16, 128), jnp.float32)
    def product(source, first, count, taps, extra=()):
        rows = count * STEP
        windows = [
            source[dj, (first + dx) * STEP : (first + dx) * STEP + rows, :]
            for dx in range(3)
            for dj in range(2)
        ]
        windows += [block[:, :] for block in extra]
        return jnp.dot(
            jnp.concatenate(windows, axis=1), taps[...], preferred_element_type=jnp.float32
        )

    part = 18 // FIRST_PARTS
    for first in range(0, 18, part):
        v = silu(product(b1, first, part, band1))
        for x in range(first, first + part):
            rows = slice((x - first) * STEP, (x - first) * STEP + STEP)
            v0, v1 = v[rows, :128] * y_first, v[rows, 128:] * y_last
            if x in (0, 17):
                edge = x_lo if x == 0 else x_hi
                v0, v1 = v0 * edge, v1 * edge
            hidden[0, 16 + x * STEP : 16 + x * STEP + STEP, :] = v0
            hidden[1, 16 + x * STEP : 16 + x * STEP + STEP, :] = v1
            hidden[2, 16 + x * STEP : 16 + x * STEP + STEP, :] = jnp.where(outer, v0, v1)

    def by_strike(block):
        return block.reshape(18, STEP, 128)

    for dj in range(2):
        for n in range(2):
            b2[dj, :, n * 128 : n * 128 + 128] = hidden[n, pl.ds(16 + dj, m1), :].astype(jnp.bfloat16)
        above = by_strike(hidden[2, pl.ds(16 + dj + PAIRS, m1), :])
        below = by_strike(hidden[2, pl.ds(16 + dj - PAIRS, m1), :])
        beside = jnp.where(front[None], above, below) * inside[None]
        b2[dj, :, 256:384] = beside.reshape(m1, 128).astype(jnp.bfloat16)
    part = 16 // SECOND_PARTS
    sends = []
    for n in range(SECOND_PARTS):
        first = n * part
        base = b1[1, (2 + first) * STEP : (2 + first + part) * STEP, :256]
        v = product(b2, first, part, band2, (base,))
        for o in range(2):
            result[o, first * STEP : (first + part) * STEP] = v[:, o * 128 : o * 128 + 128]
        for x in range(first, first + part):
            for g in range(GROUPS):
                for o in range(2):
                    cells8 = result[o, pl.ds(x * STEP + g * PAIRS, 8), :]
                    woven[g, pl.ds(x * 16 + o, 8, stride=2), :] = cells8
        for g in range(GROUPS):
            near[first : first + part, :, g * 128 : g * 128 + 128] = (
                woven[g, first * 16 : (first + part) * 16].reshape(part, 16, 128).astype(jnp.bfloat16)
            )
        here = pl.ds(first, part)
        sends.append(pltpu.make_async_copy(near.at[here], out.at[here], sems.at[n]))
        sends[-1].start()
    for send in sends:
        send.wait()


def swapped(block, axis):
    size = lax.axis_size(axis)
    for first in (0, 1):
        pairs = [(i, i + 1) for i in range(first, size - 1, 2)]
        yield lax.ppermute(block, axis, pairs + [(j, i) for i, j in pairs])


def body(coarse, up_weight, first_weight, second_weight):
    vmem = pl.BlockSpec(memory_space=pltpu.VMEM)
    params = pltpu.CompilerParams(vmem_limit_bytes=32 * 1024 * 1024)

    bf16 = jnp.bfloat16
    shape = jax.ShapeDtypeStruct
    dip_a, dip_b = swapped(coarse, "dip")
    upmat, token = pl.pallas_call(
        up_kernel,
        out_shape=(shape((256, 2048), bf16), shape((8, 128), jnp.float32)),
        in_specs=[pl.BlockSpec(memory_space=pltpu.HBM)],
        out_specs=(vmem, vmem),
        scratch_shapes=[pltpu.VMEM((512 * 32, 32), bf16), pltpu.SemaphoreType.DMA((4,))],
        compiler_params=pltpu.CompilerParams(vmem_limit_bytes=LIMIT),
        cost_estimate=pl.CostEstimate(flops=5_000_000, bytes_accessed=5_000_000, transcendentals=0),
        name="arrange_up",
    )(up_weight.reshape(512 * 32, 32))
    own = pl.pallas_call(
        pack_kernel,
        out_shape=shape((12, 4, 128), bf16),
        in_specs=[vmem] * 4,
        out_specs=vmem,
        compiler_params=pltpu.CompilerParams(vmem_limit_bytes=1024 * 1024),
        name="pack",
    )(coarse, dip_a, dip_b, token)
    strike_a, strike_b = swapped(own, "strike")
    band1, band2 = pl.pallas_call(
        band_kernel,
        out_shape=(shape((WINDOW, 256), bf16), shape((WINDOW + 256, 256), bf16)),
        in_specs=[vmem] * 2,
        out_specs=(vmem, vmem),
        compiler_params=pltpu.CompilerParams(vmem_limit_bytes=16 * 1024 * 1024),
        cost_estimate=pl.CostEstimate(flops=5_000_000, bytes_accessed=5_000_000, transcendentals=0),
        name="arrange_bands",
    )(first_weight.reshape(864, 32), second_weight.reshape(864, 32))
    return pl.pallas_call(
        main_kernel,
        out_shape=jax.ShapeDtypeStruct((16, 16, 512), bf16),
        in_specs=[vmem] * 6,
        out_specs=pl.BlockSpec(memory_space=pltpu.HBM),
        scratch_shapes=[
            pltpu.VMEM((6, 16, 128), jnp.float32),
            pltpu.VMEM((3, 20 * STEP + 8, 128), jnp.float32),
            pltpu.VMEM((3, 18 * STEP + 32, 128), jnp.float32),
            pltpu.VMEM((2, 20 * STEP, 384), bf16),
            pltpu.VMEM((2, 18 * STEP, 384), bf16),
            pltpu.VMEM((2, 16 * STEP, 128), jnp.float32),
            pltpu.VMEM((GROUPS, 256, 128), jnp.float32),
            pltpu.VMEM((16, 16, 512), bf16),
            pltpu.SemaphoreType.DMA((SECOND_PARTS,)),
        ],
        compiler_params=params,
        cost_estimate=pl.CostEstimate(
            flops=2_000_000_000, bytes_accessed=8_000_000, transcendentals=800_000
        ),
        name="upsample_refine",
    )(own, strike_a, strike_b, upmat, band1, band2)


def solution(mesh):
    return jax.shard_map(
        body,
        mesh=mesh,
        in_specs=(P("strike", "dip", None), P(), P(), P()),
        out_specs=P("strike", "dip", None),
        check_vma=False,
    )
```

```python
import jax
import jax.numpy as jnp
from jax import lax
from jax.experimental import pallas as pl
from jax.experimental.pallas import tpu as pltpu
from jax.sharding import PartitionSpec as P

GROUPS = 4
PAIRS = 10
STEP = GROUPS * PAIRS
ORDER = ((0, 1, 2, 3), (1, 0, 3, 2))
BESIDE = ((0, 4), (1, 4), (1, -1), (0, -1))
WINDOW = 3 * 2 * 384
PARTS = 2
LIMIT = 50 * 1024 * 1024


def silu(v):
    half = 0.5 * v
    return half + half * jnp.tanh(half)


def up_kernel(up_hbm, upmat_ref, token_ref, up_ref, sems):
    fetches = []
    for part in range(4):
        rows = pl.ds(part * 4096, 4096)
        fetches.append(pltpu.make_async_copy(up_hbm.at[rows], up_ref.at[rows], sems.at[part]))
    for fetch in fetches:
        fetch.start()
    token_ref[...] = jnp.zeros((8, 128), jnp.float32)

    for k1 in range(8):
        if k1 % 2 == 0:
            fetches[k1 // 2].wait()
        h1, p1 = divmod(k1, 4)
        for k2 in range(8):
            h2, p2 = divmod(k2, 4)
            for h3 in range(2):
                k = (k1 * 8 + k2) * 8 + 4 * h3
                parts = [up_ref[pl.ds((k + (z + 2) % 4) * 32, 32), :] for z in ORDER[p2 % 2]]
                row = (h1 * 4 + h2 * 2 + (1 - h3)) * 32
                upmat_ref[pl.ds(row, 32), pl.ds((p1 * 4 + p2) * 128, 128)] = jnp.concatenate(
                    parts, axis=1
                )


def arrange_bands(first_ref, second_ref, band1_ref, band2_ref):
    ci = lax.broadcasted_iota(jnp.int32, (32, 128), 0)
    lane = lax.broadcasted_iota(jnp.int32, (32, 128), 1)
    group = lane // 32
    copies = (lane % 32 == ci).astype(jnp.bfloat16)

    def arrange(w_ref, band_ref, out_order):
        rep = jnp.dot(w_ref[...], copies, preferred_element_type=jnp.float32)
        for d1 in range(3):
            for dj in range(2):
                cells = [(0, z) for z in ORDER[0]] + [(1, z) for z in ORDER[1]] + list(BESIDE)
                for n, (side, z_in) in enumerate(cells):
                    row = (d1 * 2 + dj) * 384 + n * 32
                    for o in range(2):
                        block = jnp.zeros((32, 128), jnp.float32)
                        d2 = 2 * dj + side - o
                        for d3 in range(3):
                            z_out = z_in - d3 + 1
                            if 0 <= d2 < 3 and 0 <= z_out < 4:
                                tap = ((d1 * 3 + d2) * 3 + d3) * 32
                                here = group == out_order[o].index(z_out)
                                block = jnp.where(here, rep[tap : tap + 32], block)
                        band_ref[pl.ds(row, 32), pl.ds(o * 128, 128)] = block.astype(jnp.bfloat16)

    arrange(first_ref, band1_ref, ORDER)
    arrange(second_ref, band2_ref, (ORDER[0], ORDER[0]))
    r = lax.broadcasted_iota(jnp.int32, (256, 256), 0)
    c = lax.broadcasted_iota(jnp.int32, (256, 256), 1)
    swap = jnp.where((r // 32) % 2 == 0, r + 32, r - 32)
    band2_ref[pl.ds(WINDOW, 256), :] = (jnp.where(r < 128, r, swap) == c).astype(jnp.bfloat16)


def pack_kernel(coarse, dip_a, dip_b, token, own):
    own[0:4] = coarse[...]
    own[4:8] = dip_a[...]
    own[8:12] = dip_b[...]


def edges():
    one, zero = jnp.float32(1), jnp.float32(0)
    strike, dip = lax.axis_index("strike"), lax.axis_index("dip")
    x_lo = jnp.where(strike == 0, zero, one)
    x_hi = jnp.where(strike == lax.axis_size("strike") - 1, zero, one)
    y_lo = jnp.where(dip == 0, zero, one)
    y_hi = jnp.where(dip == lax.axis_size("dip") - 1, zero, one)
    return x_lo, x_hi, y_lo, y_hi


def put(cells, x0, x1, block):
    even = lax.axis_index("dip") % 2 == 0
    below, above = jnp.where(even, 8, 4), jnp.where(even, 4, 8)
    cells[x0:x1, 1:5, :] = block(0)
    cells[x0:x1, 0:1, :] = block(below)[:, 3:4]
    cells[x0:x1, 5:6, :] = block(above)[:, 0:1]


def read(ref, first, count):
    return ref[pl.ds(first, count)].astype(jnp.float32)


def upsample(cells, upmat, fine, q1s, first, sides):
    x_lo, x_hi, y_lo, y_hi = sides
    one = jnp.float32(1)
    count = len(q1s)
    rows = 8 * count
    wide = []
    edge = jnp.zeros((rows, 32), jnp.float32)
    for h1 in range(2):
        for h2 in range(2):
            window = jnp.concatenate(
                [cells[q1 + 1 - h1 : q1 + 2 - h1, 1 - h2 : 9 - h2, :] for q1 in q1s], axis=0
            )
            wide.append(jnp.concatenate([edge, window.reshape(rows, 128), edge], axis=1))
    left = jnp.concatenate(
        [
            jnp.concatenate([w[:, 32 * q3 : 32 * q3 + 64] for w in wide], axis=1)
            for q3 in range(5)
        ],
        axis=0,
    ).astype(jnp.bfloat16)

    lane = lax.broadcasted_iota(jnp.int32, (rows, 128), 1)
    q2 = lax.broadcasted_iota(jnp.int32, (rows, 128), 0) % 8
    outer = (lane < 32) | (lane >= 96)
    front = lane < 64
    low = jnp.where(q2 == 0, y_lo, one)
    high = jnp.where(q2 == 4, y_hi, one)
    none = jnp.zeros((rows, 128), jnp.float32)
    for p1 in range(4):
        phase = jnp.dot(left, upmat[:, p1 * 512 : p1 * 512 + 512], preferred_element_type=jnp.float32)
        for pp in range(2):
            tiles = [[], []]
            for side in range(2):
                p2 = 2 * pp + side
                v = phase[:, p2 * 128 : p2 * 128 + 128]
                for g in range(GROUPS):
                    at = g * rows
                    t = jnp.where(front, v[at : at + rows], v[at + rows : at + 2 * rows])
                    tiles[side].append(silu(t) * (low if pp == 0 else high))
            merged = [jnp.where(outer, tiles[0][g], tiles[1][g]) for g in range(GROUPS)]
            merged = [none] + merged + [none]
            for g in range(GROUPS):
                beside = jnp.where(front, merged[g + 2], merged[g])
                for n, t in enumerate((tiles[0][g], tiles[1][g], beside)):
                    for c, q1 in enumerate(q1s):
                        part = t[c * 8 : c * 8 + 5]
                        if q1 == 0 and p1 < 2:
                            part = part * x_lo
                        if q1 == 4 and p1 >= 2:
                            part = part * x_hi
                        at = (4 * (q1 - first) + p1) * STEP + g * PAIRS + pp
                        fine[n, pl.ds(at, 5, stride=2), :] = part


def windows_of(fine, count, target, first):
    for dj in range(2):
        for n in range(3):
            rows = fine[n, pl.ds(first * STEP + dj, count * STEP), :].astype(jnp.bfloat16)
            target[dj, first * STEP : (first + count) * STEP, n * 128 : n * 128 + 128] = rows


def inner_kernel(own, upmat, first_ref, second_ref, inner, band1_ref, band2_ref, cells, fine):
    arrange_bands(first_ref, second_ref, band1_ref, band2_ref)
    put(cells, 1, 5, lambda o: read(own, o, 4))
    upsample(cells, upmat, fine, (1, 2, 3), 1, edges())
    windows_of(fine, 12, inner, 0)


def main_kernel(
    own, strike_a, strike_b, inner, upmat, band1, band2, out,
    cells, fine, hidden, b1, b2, result, woven, near, sems,
):
    sides = x_lo, x_hi, y_lo, y_hi = edges()
    one, zero = jnp.float32(1), jnp.float32(0)

    even = lax.axis_index("strike") % 2 == 0
    put(cells, 0, 1, lambda o: jnp.where(even, read(strike_b, o + 3, 1), read(strike_a, o + 3, 1)))
    put(cells, 1, 2, lambda o: read(own, o, 1))
    put(cells, 4, 5, lambda o: read(own, o + 3, 1))
    put(cells, 5, 6, lambda o: jnp.where(even, read(strike_a, o, 1), read(strike_b, o, 1)))
    upsample(cells, upmat, fine, (0, 4), 0, sides)
    windows_of(fine, 4, b1, 0)
    b1[:, 4 * STEP : 16 * STEP, :] = inner[...]
    windows_of(fine, 4, b1, 16)

    m1 = 18 * STEP
    row = lax.broadcasted_iota(jnp.int32, (STEP, 128), 0)
    lane = lax.broadcasted_iota(jnp.int32, (STEP, 128), 1)
    starts = [g * PAIRS for g in range(GROUPS)]
    first, last = row == starts[0], row == starts[0] + 8
    for start in starts[1:]:
        first, last = first | (row == start), last | (row == start + 8)
    y_first, y_last = jnp.where(first, y_lo, one), jnp.where(last, y_hi, one)
    outer = (lane < 32) | (lane >= 96)
    front = lane < 64
    inside_above = jnp.where(row < starts[-1], one, zero)
    inside_below = jnp.where(row >= PAIRS, one, zero)
    inside = jnp.where(front, inside_above, inside_below)
    hidden[2, 0:16, :] = jnp.zeros((16, 128), jnp.float32)
    hidden[2, 16 + m1 : 32 + m1, :] = jnp.zeros((16, 128), jnp.float32)
    def product(source, first, count, taps, extra=()):
        rows = count * STEP
        windows = [
            source[dj, (first + dx) * STEP : (first + dx) * STEP + rows, :]
            for dx in range(3)
            for dj in range(2)
        ]
        windows += [block[:, :] for block in extra]
        return jnp.dot(
            jnp.concatenate(windows, axis=1), taps[...], preferred_element_type=jnp.float32
        )

    part = 18 // PARTS
    for first in range(0, 18, part):
        v = silu(product(b1, first, part, band1))
        for x in range(first, first + part):
            rows = slice((x - first) * STEP, (x - first) * STEP + STEP)
            v0, v1 = v[rows, :128] * y_first, v[rows, 128:] * y_last
            if x in (0, 17):
                edge = x_lo if x == 0 else x_hi
                v0, v1 = v0 * edge, v1 * edge
            hidden[0, 16 + x * STEP : 16 + x * STEP + STEP, :] = v0
            hidden[1, 16 + x * STEP : 16 + x * STEP + STEP, :] = v1
            hidden[2, 16 + x * STEP : 16 + x * STEP + STEP, :] = jnp.where(outer, v0, v1)

    def by_strike(block):
        return block.reshape(18, STEP, 128)

    for dj in range(2):
        for n in range(2):
            b2[dj, :, n * 128 : n * 128 + 128] = hidden[n, pl.ds(16 + dj, m1), :].astype(jnp.bfloat16)
        above = by_strike(hidden[2, pl.ds(16 + dj + PAIRS, m1), :])
        below = by_strike(hidden[2, pl.ds(16 + dj - PAIRS, m1), :])
        beside = jnp.where(front[None], above, below) * inside[None]
        b2[dj, :, 256:384] = beside.reshape(m1, 128).astype(jnp.bfloat16)
    part = 16 // PARTS
    sends = []
    for n in range(PARTS):
        first = n * part
        base = b1[1, (2 + first) * STEP : (2 + first + part) * STEP, :256]
        v = product(b2, first, part, band2, (base,))
        for o in range(2):
            result[o, first * STEP : (first + part) * STEP] = v[:, o * 128 : o * 128 + 128]
        for x in range(first, first + part):
            for g in range(GROUPS):
                for o in range(2):
                    cells8 = result[o, pl.ds(x * STEP + g * PAIRS, 8), :]
                    woven[g, pl.ds(x * 16 + o, 8, stride=2), :] = cells8
        for g in range(GROUPS):
            near[first : first + part, :, g * 128 : g * 128 + 128] = (
                woven[g, first * 16 : (first + part) * 16].reshape(part, 16, 128).astype(jnp.bfloat16)
            )
        here = pl.ds(first, part)
        sends.append(pltpu.make_async_copy(near.at[here], out.at[here], sems.at[n]))
        sends[-1].start()
    for send in sends:
        send.wait()


def swapped(block, axis):
    size = lax.axis_size(axis)
    for first in (0, 1):
        pairs = [(i, i + 1) for i in range(first, size - 1, 2)]
        yield lax.ppermute(block, axis, pairs + [(j, i) for i, j in pairs])


def body(coarse, up_weight, first_weight, second_weight):
    vmem = pl.BlockSpec(memory_space=pltpu.VMEM)
    params = pltpu.CompilerParams(vmem_limit_bytes=32 * 1024 * 1024)

    bf16 = jnp.bfloat16
    shape = jax.ShapeDtypeStruct
    dip_a, dip_b = swapped(coarse, "dip")
    upmat, token = pl.pallas_call(
        up_kernel,
        out_shape=(shape((256, 2048), bf16), shape((8, 128), jnp.float32)),
        in_specs=[pl.BlockSpec(memory_space=pltpu.HBM)],
        out_specs=(vmem, vmem),
        scratch_shapes=[pltpu.VMEM((512 * 32, 32), bf16), pltpu.SemaphoreType.DMA((4,))],
        compiler_params=pltpu.CompilerParams(vmem_limit_bytes=LIMIT),
        cost_estimate=pl.CostEstimate(flops=5_000_000, bytes_accessed=5_000_000, transcendentals=0),
        name="arrange_up",
    )(up_weight.reshape(512 * 32, 32))
    own = pl.pallas_call(
        pack_kernel,
        out_shape=shape((12, 4, 128), bf16),
        in_specs=[vmem] * 4,
        out_specs=vmem,
        compiler_params=pltpu.CompilerParams(vmem_limit_bytes=1024 * 1024),
        name="pack",
    )(coarse, dip_a, dip_b, token)
    strike_a, strike_b = swapped(own, "strike")
    inner, band1, band2 = pl.pallas_call(
        inner_kernel,
        out_shape=(
            shape((2, 12 * STEP, 384), bf16),
            shape((WINDOW, 256), bf16),
            shape((WINDOW + 256, 256), bf16),
        ),
        in_specs=[vmem] * 4,
        out_specs=(vmem,) * 3,
        scratch_shapes=[
            pltpu.VMEM((6, 16, 128), jnp.float32),
            pltpu.VMEM((3, 12 * STEP + 8, 128), jnp.float32),
        ],
        compiler_params=pltpu.CompilerParams(vmem_limit_bytes=16 * 1024 * 1024),
        cost_estimate=pl.CostEstimate(
            flops=300_000_000, bytes_accessed=3_000_000, transcendentals=200_000
        ),
        name="upsample_inner",
    )(own, upmat, first_weight.reshape(864, 32), second_weight.reshape(864, 32))
    return pl.pallas_call(
        main_kernel,
        out_shape=jax.ShapeDtypeStruct((16, 16, 512), bf16),
        in_specs=[vmem] * 7,
        out_specs=pl.BlockSpec(memory_space=pltpu.HBM),
        scratch_shapes=[
            pltpu.VMEM((6, 16, 128), jnp.float32),
            pltpu.VMEM((3, 20 * STEP + 8, 128), jnp.float32),
            pltpu.VMEM((3, 18 * STEP + 32, 128), jnp.float32),
            pltpu.VMEM((2, 20 * STEP, 384), bf16),
            pltpu.VMEM((2, 18 * STEP, 384), bf16),
            pltpu.VMEM((2, 16 * STEP, 128), jnp.float32),
            pltpu.VMEM((GROUPS, 256, 128), jnp.float32),
            pltpu.VMEM((16, 16, 512), bf16),
            pltpu.SemaphoreType.DMA((PARTS,)),
        ],
        compiler_params=params,
        cost_estimate=pl.CostEstimate(
            flops=2_000_000_000, bytes_accessed=8_000_000, transcendentals=800_000
        ),
        name="upsample_refine",
    )(own, strike_a, strike_b, inner, upmat, band1, band2)


def solution(mesh):
    return jax.shard_map(
        body,
        mesh=mesh,
        in_specs=(P("strike", "dip", None), P(), P(), P()),
        out_specs=P("strike", "dip", None),
        check_vma=False,
    )
```

```python
import jax
import jax.numpy as jnp
from jax import lax
from jax.experimental import pallas as pl
from jax.experimental.pallas import tpu as pltpu
from jax.sharding import PartitionSpec as P

GROUPS = 4
PAIRS = 10
STEP = GROUPS * PAIRS
ORDER = ((0, 1, 2, 3), (1, 0, 3, 2))
BESIDE = ((0, 4), (1, 4), (1, -1), (0, -1))
WINDOW = 3 * 2 * 384
PARTS = 2
LIMIT = 50 * 1024 * 1024


def silu(v):
    half = 0.5 * v
    return half + half * jnp.tanh(half)


def up_kernel(up_hbm, upmat_ref, token_ref, up_ref, sems):
    fetches = []
    for part in range(16):
        rows = pl.ds(part * 1024, 1024)
        fetches.append(pltpu.make_async_copy(up_hbm.at[rows], up_ref.at[rows], sems.at[part]))
    for fetch in fetches:
        fetch.start()
    token_ref[...] = jnp.zeros((8, 128), jnp.float32)

    for k1 in range(8):
        fetches[2 * k1].wait()
        fetches[2 * k1 + 1].wait()
        h1, p1 = divmod(k1, 4)
        for k2 in range(8):
            h2, p2 = divmod(k2, 4)
            for h3 in range(2):
                k = (k1 * 8 + k2) * 8 + 4 * h3
                parts = [up_ref[pl.ds((k + (z + 2) % 4) * 32, 32), :] for z in ORDER[p2 % 2]]
                row = (h1 * 4 + h2 * 2 + (1 - h3)) * 32
                upmat_ref[pl.ds(row, 32), pl.ds((p1 * 4 + p2) * 128, 128)] = jnp.concatenate(
                    parts, axis=1
                )


def arrange_bands(first_ref, second_ref, band1_ref, band2_ref):
    ci = lax.broadcasted_iota(jnp.int32, (32, 128), 0)
    lane = lax.broadcasted_iota(jnp.int32, (32, 128), 1)
    group = lane // 32
    copies = (lane % 32 == ci).astype(jnp.bfloat16)

    def arrange(w_ref, band_ref, out_order):
        rep = jnp.dot(w_ref[...], copies, preferred_element_type=jnp.float32)
        for d1 in range(3):
            for dj in range(2):
                cells = [(0, z) for z in ORDER[0]] + [(1, z) for z in ORDER[1]] + list(BESIDE)
                for n, (side, z_in) in enumerate(cells):
                    row = (d1 * 2 + dj) * 384 + n * 32
                    for o in range(2):
                        block = jnp.zeros((32, 128), jnp.float32)
                        d2 = 2 * dj + side - o
                        for d3 in range(3):
                            z_out = z_in - d3 + 1
                            if 0 <= d2 < 3 and 0 <= z_out < 4:
                                tap = ((d1 * 3 + d2) * 3 + d3) * 32
                                here = group == out_order[o].index(z_out)
                                block = jnp.where(here, rep[tap : tap + 32], block)
                        band_ref[pl.ds(row, 32), pl.ds(o * 128, 128)] = block.astype(jnp.bfloat16)

    arrange(first_ref, band1_ref, ORDER)
    arrange(second_ref, band2_ref, (ORDER[0], ORDER[0]))
    r = lax.broadcasted_iota(jnp.int32, (256, 256), 0)
    c = lax.broadcasted_iota(jnp.int32, (256, 256), 1)
    swap = jnp.where((r // 32) % 2 == 0, r + 32, r - 32)
    band2_ref[pl.ds(WINDOW, 256), :] = (jnp.where(r < 128, r, swap) == c).astype(jnp.bfloat16)


def pack_kernel(coarse, dip_a, dip_b, token, own):
    own[0:4] = coarse[...]
    own[4:8] = dip_a[...]
    own[8:12] = dip_b[...]


def edges():
    one, zero = jnp.float32(1), jnp.float32(0)
    strike, dip = lax.axis_index("strike"), lax.axis_index("dip")
    x_lo = jnp.where(strike == 0, zero, one)
    x_hi = jnp.where(strike == lax.axis_size("strike") - 1, zero, one)
    y_lo = jnp.where(dip == 0, zero, one)
    y_hi = jnp.where(dip == lax.axis_size("dip") - 1, zero, one)
    return x_lo, x_hi, y_lo, y_hi


def put(cells, x0, x1, block):
    even = lax.axis_index("dip") % 2 == 0
    below, above = jnp.where(even, 8, 4), jnp.where(even, 4, 8)
    cells[x0:x1, 1:5, :] = block(0)
    cells[x0:x1, 0:1, :] = block(below)[:, 3:4]
    cells[x0:x1, 5:6, :] = block(above)[:, 0:1]


def read(ref, first, count):
    return ref[pl.ds(first, count)].astype(jnp.float32)


def upsample(cells, upmat, fine, q1s, first, sides):
    x_lo, x_hi, y_lo, y_hi = sides
    one = jnp.float32(1)
    count = len(q1s)
    rows = 8 * count
    wide = []
    edge = jnp.zeros((rows, 32), jnp.float32)
    for h1 in range(2):
        for h2 in range(2):
            window = jnp.concatenate(
                [cells[q1 + 1 - h1 : q1 + 2 - h1, 1 - h2 : 9 - h2, :] for q1 in q1s], axis=0
            )
            wide.append(jnp.concatenate([edge, window.reshape(rows, 128), edge], axis=1))
    left = jnp.concatenate(
        [
            jnp.concatenate([w[:, 32 * q3 : 32 * q3 + 64] for w in wide], axis=1)
            for q3 in range(5)
        ],
        axis=0,
    ).astype(jnp.bfloat16)

    lane = lax.broadcasted_iota(jnp.int32, (rows, 128), 1)
    q2 = lax.broadcasted_iota(jnp.int32, (rows, 128), 0) % 8
    outer = (lane < 32) | (lane >= 96)
    front = lane < 64
    low = jnp.where(q2 == 0, y_lo, one)
    high = jnp.where(q2 == 4, y_hi, one)
    none = jnp.zeros((rows, 128), jnp.float32)
    for p1 in range(4):
        phase = jnp.dot(left, upmat[:, p1 * 512 : p1 * 512 + 512], preferred_element_type=jnp.float32)
        for pp in range(2):
            tiles = [[], []]
            for side in range(2):
                p2 = 2 * pp + side
                v = phase[:, p2 * 128 : p2 * 128 + 128]
                for g in range(GROUPS):
                    at = g * rows
                    t = jnp.where(front, v[at : at + rows], v[at + rows : at + 2 * rows])
                    tiles[side].append(silu(t) * (low if pp == 0 else high))
            merged = [jnp.where(outer, tiles[0][g], tiles[1][g]) for g in range(GROUPS)]
            merged = [none] + merged + [none]
            for g in range(GROUPS):
                beside = jnp.where(front, merged[g + 2], merged[g])
                for n, t in enumerate((tiles[0][g], tiles[1][g], beside)):
                    for c, q1 in enumerate(q1s):
                        part = t[c * 8 : c * 8 + 5]
                        if q1 == 0 and p1 < 2:
                            part = part * x_lo
                        if q1 == 4 and p1 >= 2:
                            part = part * x_hi
                        at = (4 * (q1 - first) + p1) * STEP + g * PAIRS + pp
                        fine[n, pl.ds(at, 5, stride=2), :] = part


def windows_of(fine, count, target, first):
    for dj in range(2):
        for n in range(3):
            rows = fine[n, pl.ds(first * STEP + dj, count * STEP), :].astype(jnp.bfloat16)
            target[dj, first * STEP : (first + count) * STEP, n * 128 : n * 128 + 128] = rows


def inner_kernel(own, upmat, first_ref, second_ref, inner, band1_ref, band2_ref, cells, fine):
    arrange_bands(first_ref, second_ref, band1_ref, band2_ref)
    put(cells, 1, 5, lambda o: read(own, o, 4))
    upsample(cells, upmat, fine, (1, 2, 3), 1, edges())
    windows_of(fine, 12, inner, 0)


def main_kernel(
    own, strike_a, strike_b, inner, upmat, band1, band2, out,
    cells, fine, hidden, b1, b2, result, woven, near, sems,
):
    sides = x_lo, x_hi, y_lo, y_hi = edges()
    one, zero = jnp.float32(1), jnp.float32(0)

    even = lax.axis_index("strike") % 2 == 0
    put(cells, 0, 1, lambda o: jnp.where(even, read(strike_b, o + 3, 1), read(strike_a, o + 3, 1)))
    put(cells, 1, 2, lambda o: read(own, o, 1))
    put(cells, 4, 5, lambda o: read(own, o + 3, 1))
    put(cells, 5, 6, lambda o: jnp.where(even, read(strike_a, o, 1), read(strike_b, o, 1)))
    upsample(cells, upmat, fine, (0, 4), 0, sides)
    windows_of(fine, 4, b1, 0)
    b1[:, 4 * STEP : 16 * STEP, :] = inner[...]
    windows_of(fine, 4, b1, 16)

    m1 = 18 * STEP
    row = lax.broadcasted_iota(jnp.int32, (STEP, 128), 0)
    lane = lax.broadcasted_iota(jnp.int32, (STEP, 128), 1)
    starts = [g * PAIRS for g in range(GROUPS)]
    first, last = row == starts[0], row == starts[0] + 8
    for start in starts[1:]:
        first, last = first | (row == start), last | (row == start + 8)
    y_first, y_last = jnp.where(first, y_lo, one), jnp.where(last, y_hi, one)
    outer = (lane < 32) | (lane >= 96)
    front = lane < 64
    inside_above = jnp.where(row < starts[-1], one, zero)
    inside_below = jnp.where(row >= PAIRS, one, zero)
    inside = jnp.where(front, inside_above, inside_below)
    hidden[2, 0:16, :] = jnp.zeros((16, 128), jnp.float32)
    hidden[2, 16 + m1 : 32 + m1, :] = jnp.zeros((16, 128), jnp.float32)
    def product(source, first, count, taps, extra=()):
        rows = count * STEP
        windows = [
            source[dj, (first + dx) * STEP : (first + dx) * STEP + rows, :]
            for dx in range(3)
            for dj in range(2)
        ]
        windows += [block[:, :] for block in extra]
        return jnp.dot(
            jnp.concatenate(windows, axis=1), taps[...], preferred_element_type=jnp.float32
        )

    for first, part in ((0, 10), (10, 8)):
        v = silu(product(b1, first, part, band1))
        for x in range(first, first + part):
            rows = slice((x - first) * STEP, (x - first) * STEP + STEP)
            v0, v1 = v[rows, :128] * y_first, v[rows, 128:] * y_last
            if x in (0, 17):
                edge = x_lo if x == 0 else x_hi
                v0, v1 = v0 * edge, v1 * edge
            hidden[0, 16 + x * STEP : 16 + x * STEP + STEP, :] = v0
            hidden[1, 16 + x * STEP : 16 + x * STEP + STEP, :] = v1
            hidden[2, 16 + x * STEP : 16 + x * STEP + STEP, :] = jnp.where(outer, v0, v1)
            if x % 2:
                both = jnp.concatenate([held, jnp.concatenate([v0, v1], axis=1)], axis=0)
                b2[0, (x - 1) * STEP : (x + 1) * STEP, :256] = both.astype(jnp.bfloat16)
            held = jnp.concatenate([v0, v1], axis=1)

    def by_strike(block):
        return block.reshape(18, STEP, 128)

    for dj in range(2):
        for n in range(2 * dj):
            b2[dj, :, n * 128 : n * 128 + 128] = hidden[n, pl.ds(16 + dj, m1), :].astype(jnp.bfloat16)
        above = by_strike(hidden[2, pl.ds(16 + dj + PAIRS, m1), :])
        below = by_strike(hidden[2, pl.ds(16 + dj - PAIRS, m1), :])
        beside = jnp.where(front[None], above, below) * inside[None]
        b2[dj, :, 256:384] = beside.reshape(m1, 128).astype(jnp.bfloat16)
    part = 16 // PARTS
    sends = []
    for n in range(PARTS):
        first = n * part
        base = b1[1, (2 + first) * STEP : (2 + first + part) * STEP, :256]
        v = product(b2, first, part, band2, (base,))
        for o in range(2):
            result[o, first * STEP : (first + part) * STEP] = v[:, o * 128 : o * 128 + 128]
        for x in range(first, first + part):
            for g in range(GROUPS):
                for o in range(2):
                    cells8 = result[o, pl.ds(x * STEP + g * PAIRS, 8), :]
                    woven[g, pl.ds(x * 16 + o, 8, stride=2), :] = cells8
        for g in range(GROUPS):
            near[first : first + part, :, g * 128 : g * 128 + 128] = (
                woven[g, first * 16 : (first + part) * 16].reshape(part, 16, 128).astype(jnp.bfloat16)
            )
        here = pl.ds(first, part)
        sends.append(pltpu.make_async_copy(near.at[here], out.at[here], sems.at[n]))
        sends[-1].start()
    for send in sends:
        send.wait()


def swapped(block, axis):
    size = lax.axis_size(axis)
    for first in (0, 1):
        pairs = [(i, i + 1) for i in range(first, size - 1, 2)]
        yield lax.ppermute(block, axis, pairs + [(j, i) for i, j in pairs])


def body(coarse, up_weight, first_weight, second_weight):
    vmem = pl.BlockSpec(memory_space=pltpu.VMEM)
    params = pltpu.CompilerParams(vmem_limit_bytes=32 * 1024 * 1024)

    bf16 = jnp.bfloat16
    shape = jax.ShapeDtypeStruct
    dip_a, dip_b = swapped(coarse, "dip")
    upmat, token = pl.pallas_call(
        up_kernel,
        out_shape=(shape((256, 2048), bf16), shape((8, 128), jnp.float32)),
        in_specs=[pl.BlockSpec(memory_space=pltpu.HBM)],
        out_specs=(vmem, vmem),
        scratch_shapes=[pltpu.VMEM((512 * 32, 32), bf16), pltpu.SemaphoreType.DMA((16,))],
        compiler_params=pltpu.CompilerParams(vmem_limit_bytes=LIMIT),
        cost_estimate=pl.CostEstimate(flops=5_000_000, bytes_accessed=5_000_000, transcendentals=0),
        name="arrange_up",
    )(up_weight.reshape(512 * 32, 32))
    own = pl.pallas_call(
        pack_kernel,
        out_shape=shape((12, 4, 128), bf16),
        in_specs=[vmem] * 4,
        out_specs=vmem,
        compiler_params=pltpu.CompilerParams(vmem_limit_bytes=1024 * 1024),
        name="pack",
    )(coarse, dip_a, dip_b, token)
    strike_a, strike_b = swapped(own, "strike")
    inner, band1, band2 = pl.pallas_call(
        inner_kernel,
        out_shape=(
            shape((2, 12 * STEP, 384), bf16),
            shape((WINDOW, 256), bf16),
            shape((WINDOW + 256, 256), bf16),
        ),
        in_specs=[vmem] * 4,
        out_specs=(vmem,) * 3,
        scratch_shapes=[
            pltpu.VMEM((6, 16, 128), jnp.float32),
            pltpu.VMEM((3, 12 * STEP + 8, 128), jnp.float32),
        ],
        compiler_params=pltpu.CompilerParams(vmem_limit_bytes=16 * 1024 * 1024),
        cost_estimate=pl.CostEstimate(
            flops=300_000_000, bytes_accessed=3_000_000, transcendentals=200_000
        ),
        name="upsample_inner",
    )(own, upmat, first_weight.reshape(864, 32), second_weight.reshape(864, 32))
    return pl.pallas_call(
        main_kernel,
        out_shape=jax.ShapeDtypeStruct((16, 16, 512), bf16),
        in_specs=[vmem] * 7,
        out_specs=pl.BlockSpec(memory_space=pltpu.HBM),
        scratch_shapes=[
            pltpu.VMEM((6, 16, 128), jnp.float32),
            pltpu.VMEM((3, 20 * STEP + 8, 128), jnp.float32),
            pltpu.VMEM((3, 18 * STEP + 32, 128), jnp.float32),
            pltpu.VMEM((2, 20 * STEP, 384), bf16),
            pltpu.VMEM((2, 18 * STEP, 384), bf16),
            pltpu.VMEM((2, 16 * STEP, 128), jnp.float32),
            pltpu.VMEM((GROUPS, 256, 128), jnp.float32),
            pltpu.VMEM((16, 16, 512), bf16),
            pltpu.SemaphoreType.DMA((PARTS,)),
        ],
        compiler_params=params,
        cost_estimate=pl.CostEstimate(
            flops=2_000_000_000, bytes_accessed=8_000_000, transcendentals=800_000
        ),
        name="upsample_refine",
    )(own, strike_a, strike_b, inner, upmat, band1, band2)


def solution(mesh):
    return jax.shard_map(
        body,
        mesh=mesh,
        in_specs=(P("strike", "dip", None), P(), P(), P()),
        out_specs=P("strike", "dip", None),
        check_vma=False,
    )
```

```python
import jax
import jax.numpy as jnp
from jax import lax
from jax.experimental import pallas as pl
from jax.experimental.pallas import tpu as pltpu
from jax.sharding import PartitionSpec as P

GROUPS = 4
PAIRS = 10
STEP = GROUPS * PAIRS
ORDER = ((0, 1, 2, 3), (1, 0, 3, 2))
BESIDE = ((0, 4), (1, 4), (1, -1), (0, -1))
WINDOW = 3 * 2 * 384
LIMIT = 50 * 1024 * 1024


def silu(v):
    half = 0.5 * v
    return half + half * jnp.tanh(half)


def up_kernel(up_hbm, upmat_ref, token_ref, up_ref, sems):
    fetches = []
    for part in range(4):
        rows = pl.ds(part * 4096, 4096)
        fetches.append(pltpu.make_async_copy(up_hbm.at[rows], up_ref.at[rows], sems.at[part]))
    for fetch in fetches:
        fetch.start()
    token_ref[...] = jnp.zeros((8, 128), jnp.float32)

    for k1 in range(8):
        if k1 % 2 == 0:
            fetches[k1 // 2].wait()
        h1, p1 = divmod(k1, 4)
        for k2 in range(8):
            h2, p2 = divmod(k2, 4)
            for h3 in range(2):
                k = (k1 * 8 + k2) * 8 + 4 * h3
                parts = [up_ref[pl.ds((k + (z + 2) % 4) * 32, 32), :] for z in ORDER[p2 % 2]]
                row = (h1 * 4 + h2 * 2 + (1 - h3)) * 32
                upmat_ref[pl.ds(row, 32), pl.ds((p1 * 4 + p2) * 128, 128)] = jnp.concatenate(
                    parts, axis=1
                )


def arrange_bands(first_ref, second_ref, band1_ref, band2_ref):
    ci = lax.broadcasted_iota(jnp.int32, (32, 128), 0)
    lane = lax.broadcasted_iota(jnp.int32, (32, 128), 1)
    group = lane // 32
    copies = (lane % 32 == ci).astype(jnp.bfloat16)

    def arrange(w_ref, band_ref, out_order):
        rep = jnp.dot(w_ref[...], copies, preferred_element_type=jnp.float32)
        for d1 in range(3):
            for dj in range(2):
                cells = [(0, z) for z in ORDER[0]] + [(1, z) for z in ORDER[1]] + list(BESIDE)
                for n, (side, z_in) in enumerate(cells):
                    row = (d1 * 2 + dj) * 384 + n * 32
                    for o in range(2):
                        block = jnp.zeros((32, 128), jnp.float32)
                        d2 = 2 * dj + side - o
                        for d3 in range(3):
                            z_out = z_in - d3 + 1
                            if 0 <= d2 < 3 and 0 <= z_out < 4:
                                tap = ((d1 * 3 + d2) * 3 + d3) * 32
                                here = group == out_order[o].index(z_out)
                                block = jnp.where(here, rep[tap : tap + 32], block)
                        band_ref[pl.ds(row, 32), pl.ds(o * 128, 128)] = block.astype(jnp.bfloat16)

    arrange(first_ref, band1_ref, ORDER)
    arrange(second_ref, band2_ref, (ORDER[0], ORDER[0]))
    r = lax.broadcasted_iota(jnp.int32, (256, 256), 0)
    c = lax.broadcasted_iota(jnp.int32, (256, 256), 1)
    swap = jnp.where((r // 32) % 2 == 0, r + 32, r - 32)
    band2_ref[pl.ds(WINDOW, 256), :] = (jnp.where(r < 128, r, swap) == c).astype(jnp.bfloat16)


def pack_kernel(coarse, dip_a, dip_b, token, own):
    own[0:4] = coarse[...]
    own[4:8] = dip_a[...]
    own[8:12] = dip_b[...]


def edges():
    one, zero = jnp.float32(1), jnp.float32(0)
    strike, dip = lax.axis_index("strike"), lax.axis_index("dip")
    x_lo = jnp.where(strike == 0, zero, one)
    x_hi = jnp.where(strike == lax.axis_size("strike") - 1, zero, one)
    y_lo = jnp.where(dip == 0, zero, one)
    y_hi = jnp.where(dip == lax.axis_size("dip") - 1, zero, one)
    return x_lo, x_hi, y_lo, y_hi


def put(cells, x0, x1, block):
    even = lax.axis_index("dip") % 2 == 0
    below, above = jnp.where(even, 8, 4), jnp.where(even, 4, 8)
    cells[x0:x1, 1:5, :] = block(0)
    cells[x0:x1, 0:1, :] = block(below)[:, 3:4]
    cells[x0:x1, 5:6, :] = block(above)[:, 0:1]


def read(ref, first, count):
    return ref[pl.ds(first, count)].astype(jnp.float32)


def upsample(cells, upmat, fine, q1s, sides):
    x_lo, x_hi, y_lo, y_hi = sides
    one = jnp.float32(1)
    count = len(q1s)
    rows = 8 * count
    wide = []
    edge = jnp.zeros((rows, 32), jnp.float32)
    for h1 in range(2):
        for h2 in range(2):
            window = jnp.concatenate(
                [cells[q1 + 1 - h1 : q1 + 2 - h1, 1 - h2 : 9 - h2, :] for q1 in q1s], axis=0
            )
            wide.append(jnp.concatenate([edge, window.reshape(rows, 128), edge], axis=1))
    left = jnp.concatenate(
        [
            jnp.concatenate([w[:, 32 * q3 : 32 * q3 + 64] for w in wide], axis=1)
            for q3 in range(5)
        ],
        axis=0,
    ).astype(jnp.bfloat16)

    lane = lax.broadcasted_iota(jnp.int32, (rows, 128), 1)
    q2 = lax.broadcasted_iota(jnp.int32, (rows, 128), 0) % 8
    outer = (lane < 32) | (lane >= 96)
    front = lane < 64
    low = jnp.where(q2 == 0, y_lo, one)
    high = jnp.where(q2 == 4, y_hi, one)
    none = jnp.zeros((rows, 128), jnp.float32)
    for p1 in range(4):
        phase = jnp.dot(left, upmat[:, p1 * 512 : p1 * 512 + 512], preferred_element_type=jnp.float32)
        for pp in range(2):
            tiles = [[], []]
            for side in range(2):
                p2 = 2 * pp + side
                v = phase[:, p2 * 128 : p2 * 128 + 128]
                for g in range(GROUPS):
                    at = g * rows
                    t = jnp.where(front, v[at : at + rows], v[at + rows : at + 2 * rows])
                    tiles[side].append(silu(t) * (low if pp == 0 else high))
            merged = [jnp.where(outer, tiles[0][g], tiles[1][g]) for g in range(GROUPS)]
            merged = [none] + merged + [none]
            for g in range(GROUPS):
                beside = jnp.where(front, merged[g + 2], merged[g])
                for n, t in enumerate((tiles[0][g], tiles[1][g], beside)):
                    for c, q1 in enumerate(q1s):
                        part = t[c * 8 : c * 8 + 5]
                        if q1 == 0 and p1 < 2:
                            part = part * x_lo
                        if q1 == 4 and p1 >= 2:
                            part = part * x_hi
                        at = (4 * c + p1) * STEP + g * PAIRS + pp
                        fine[n, pl.ds(at, 5, stride=2), :] = part


def windows_of(fine, first, count, target, at):
    for dj in range(2):
        for n in range(3):
            rows = fine[n, pl.ds(first * STEP + dj, count * STEP), :].astype(jnp.bfloat16)
            target[dj, at * STEP : (at + count) * STEP, n * 128 : n * 128 + 128] = rows


def inner_kernel(own, upmat, first_ref, second_ref, inner, band1_ref, band2_ref, cells, fine):
    arrange_bands(first_ref, second_ref, band1_ref, band2_ref)
    put(cells, 1, 5, lambda o: read(own, o, 4))
    upsample(cells, upmat, fine, (1, 2, 3), edges())
    windows_of(fine, 0, 12, inner, 0)


def product(source, strips, taps, base=None):
    columns = []
    for dx in range(3):
        for dj in range(2):
            columns.append(
                jnp.concatenate(
                    [source[dj, (at + dx) * STEP : (at + dx + n) * STEP, :] for at, n in strips], axis=0
                )
            )
    if base is not None:
        columns.append(base)
    return jnp.dot(jnp.concatenate(columns, axis=1), taps[...], preferred_element_type=jnp.float32)


def main_kernel(
    own, strike_a, strike_b, inner, upmat, band1, band2, out,
    cells, fine, hidden, b1, b2, result, woven, near, sems,
):
    sides = x_lo, x_hi, y_lo, y_hi = edges()
    one, zero = jnp.float32(1), jnp.float32(0)

    v_inner = product(inner, ((0, 10),), band1)

    even = lax.axis_index("strike") % 2 == 0
    put(cells, 0, 1, lambda o: jnp.where(even, read(strike_b, o + 3, 1), read(strike_a, o + 3, 1)))
    put(cells, 1, 2, lambda o: read(own, o, 1))
    put(cells, 4, 5, lambda o: read(own, o + 3, 1))
    put(cells, 5, 6, lambda o: jnp.where(even, read(strike_a, o, 1), read(strike_b, o, 1)))
    upsample(cells, upmat, fine, (0, 4), sides)
    windows_of(fine, 0, 4, b1, 0)
    b1[:, 4 * STEP : 6 * STEP, :] = inner[:, : 2 * STEP, :]
    b1[:, 6 * STEP : 8 * STEP, :] = inner[:, 10 * STEP : 12 * STEP, :]
    windows_of(fine, 4, 4, b1, 8)

    v_outer = product(b1, ((0, 4), (6, 4)), band1)

    row = lax.broadcasted_iota(jnp.int32, (STEP, 128), 0)
    lane = lax.broadcasted_iota(jnp.int32, (STEP, 128), 1)
    starts = [g * PAIRS for g in range(GROUPS)]
    first, last = row == starts[0], row == starts[0] + 8
    for start in starts[1:]:
        first, last = first | (row == start), last | (row == start + 8)
    y_first, y_last = jnp.where(first, y_lo, one), jnp.where(last, y_hi, one)
    outer = (lane < 32) | (lane >= 96)
    front = lane < 64
    inside_above = jnp.where(row < starts[-1], one, zero)
    inside_below = jnp.where(row >= PAIRS, one, zero)
    inside = jnp.where(front, inside_above, inside_below)

    def clear(at):
        hidden[2, at : at + 16, :] = jnp.zeros((16, 128), jnp.float32)

    def keep(v, at, count):
        v = silu(v)
        for n in range(count):
            x = at + n
            rows = slice(n * STEP, n * STEP + STEP)
            v0, v1 = v[rows, :128] * y_first, v[rows, 128:] * y_last
            if x in (0, 17):
                edge = x_lo if x == 0 else x_hi
                v0, v1 = v0 * edge, v1 * edge
            here = slice(16 + x * STEP, 16 + x * STEP + STEP)
            hidden[0, here, :] = v0
            hidden[1, here, :] = v1
            hidden[2, here, :] = jnp.where(outer, v0, v1)
        rows = count * STEP
        start = 16 + at * STEP
        here = slice(at * STEP, at * STEP + rows)
        for dj in range(2):
            for n in range(2):
                b2[dj, here, n * 128 : n * 128 + 128] = hidden[n, pl.ds(start + dj, rows), :].astype(
                    jnp.bfloat16
                )
            above = hidden[2, pl.ds(start + dj + PAIRS, rows), :].reshape(count, STEP, 128)
            below = hidden[2, pl.ds(start + dj - PAIRS, rows), :].reshape(count, STEP, 128)
            beside = jnp.where(front[None], above, below) * inside[None]
            b2[dj, here, 256:384] = beside.reshape(rows, 128).astype(jnp.bfloat16)

    def finish(v, strips, chain):
        sends = []
        for o in range(2):
            result[2 * chain + o] = v[:, o * 128 : o * 128 + 128]
        row = 0
        for k, (at, count) in enumerate(strips):
            for x in range(at, at + count):
                for g in range(GROUPS):
                    for o in range(2):
                        cells8 = result[2 * chain + o, pl.ds(row + g * PAIRS, 8), :]
                        woven[g, pl.ds(x * 16 + o, 8, stride=2), :] = cells8
                row += STEP
            for g in range(GROUPS):
                near[at : at + count, :, g * 128 : g * 128 + 128] = (
                    woven[g, at * 16 : (at + count) * 16].reshape(count, 16, 128).astype(jnp.bfloat16)
                )
            here = pl.ds(at, count)
            sends.append(pltpu.make_async_copy(near.at[here], out.at[here], sems.at[chain + k]))
            sends[-1].start()
        return sends

    clear(4 * STEP)
    clear(16 + 14 * STEP)
    keep(v_inner, 4, 10)
    base = inner[1, 2 * STEP : 10 * STEP, :256]
    v_inner = product(b2, ((4, 8),), band2, base)

    clear(0)
    clear(16 + 18 * STEP)
    keep(v_outer[: 4 * STEP], 0, 4)
    keep(v_outer[4 * STEP :], 14, 4)
    base = jnp.concatenate(
        [b1[1, 2 * STEP : 6 * STEP, :256], b1[1, 6 * STEP : 10 * STEP, :256]], axis=0
    )
    v_outer = product(b2, ((0, 4), (12, 4)), band2, base)

    sends = finish(v_inner, ((4, 8),), 0)
    sends += finish(v_outer, ((0, 4), (12, 4)), 1)
    for send in sends:
        send.wait()


def swapped(block, axis):
    size = lax.axis_size(axis)
    for first in (0, 1):
        pairs = [(i, i + 1) for i in range(first, size - 1, 2)]
        yield lax.ppermute(block, axis, pairs + [(j, i) for i, j in pairs])


def body(coarse, up_weight, first_weight, second_weight):
    vmem = pl.BlockSpec(memory_space=pltpu.VMEM)
    params = pltpu.CompilerParams(vmem_limit_bytes=32 * 1024 * 1024)

    bf16 = jnp.bfloat16
    shape = jax.ShapeDtypeStruct
    dip_a, dip_b = swapped(coarse, "dip")
    upmat, token = pl.pallas_call(
        up_kernel,
        out_shape=(shape((256, 2048), bf16), shape((8, 128), jnp.float32)),
        in_specs=[pl.BlockSpec(memory_space=pltpu.HBM)],
        out_specs=(vmem, vmem),
        scratch_shapes=[pltpu.VMEM((512 * 32, 32), bf16), pltpu.SemaphoreType.DMA((4,))],
        compiler_params=pltpu.CompilerParams(vmem_limit_bytes=LIMIT),
        cost_estimate=pl.CostEstimate(flops=5_000_000, bytes_accessed=5_000_000, transcendentals=0),
        name="arrange_up",
    )(up_weight.reshape(512 * 32, 32))
    own = pl.pallas_call(
        pack_kernel,
        out_shape=shape((12, 4, 128), bf16),
        in_specs=[vmem] * 4,
        out_specs=vmem,
        compiler_params=pltpu.CompilerParams(vmem_limit_bytes=1024 * 1024),
        name="pack",
    )(coarse, dip_a, dip_b, token)
    strike_a, strike_b = swapped(own, "strike")
    inner, band1, band2 = pl.pallas_call(
        inner_kernel,
        out_shape=(
            shape((2, 12 * STEP, 384), bf16),
            shape((WINDOW, 256), bf16),
            shape((WINDOW + 256, 256), bf16),
        ),
        in_specs=[vmem] * 4,
        out_specs=(vmem,) * 3,
        scratch_shapes=[
            pltpu.VMEM((6, 16, 128), jnp.float32),
            pltpu.VMEM((3, 12 * STEP + 8, 128), jnp.float32),
        ],
        compiler_params=pltpu.CompilerParams(vmem_limit_bytes=16 * 1024 * 1024),
        cost_estimate=pl.CostEstimate(
            flops=300_000_000, bytes_accessed=3_000_000, transcendentals=200_000
        ),
        name="upsample_inner",
    )(own, upmat, first_weight.reshape(864, 32), second_weight.reshape(864, 32))
    return pl.pallas_call(
        main_kernel,
        out_shape=jax.ShapeDtypeStruct((16, 16, 512), bf16),
        in_specs=[vmem] * 7,
        out_specs=pl.BlockSpec(memory_space=pltpu.HBM),
        scratch_shapes=[
            pltpu.VMEM((6, 16, 128), jnp.float32),
            pltpu.VMEM((3, 8 * STEP + 8, 128), jnp.float32),
            pltpu.VMEM((3, 18 * STEP + 32, 128), jnp.float32),
            pltpu.VMEM((2, 12 * STEP, 384), bf16),
            pltpu.VMEM((2, 18 * STEP, 384), bf16),
            pltpu.VMEM((4, 8 * STEP, 128), jnp.float32),
            pltpu.VMEM((GROUPS, 256, 128), jnp.float32),
            pltpu.VMEM((16, 16, 512), bf16),
            pltpu.SemaphoreType.DMA((3,)),
        ],
        compiler_params=params,
        cost_estimate=pl.CostEstimate(
            flops=2_000_000_000, bytes_accessed=8_000_000, transcendentals=800_000
        ),
        name="upsample_refine",
    )(own, strike_a, strike_b, inner, upmat, band1, band2)


def solution(mesh):
    return jax.shard_map(
        body,
        mesh=mesh,
        in_specs=(P("strike", "dip", None), P(), P(), P()),
        out_specs=P("strike", "dip", None),
        check_vma=False,
    )
```

```python
import jax
import jax.numpy as jnp
from jax import lax
from jax.experimental import pallas as pl
from jax.experimental.pallas import tpu as pltpu
from jax.sharding import PartitionSpec as P

GROUPS = 4
PAIRS = 10
STEP = GROUPS * PAIRS
ORDER = ((0, 1, 2, 3), (1, 0, 3, 2))
BESIDE = ((0, 4), (1, 4), (1, -1), (0, -1))
WINDOW = 3 * 2 * 384
LIMIT = 50 * 1024 * 1024


def silu(v):
    half = 0.5 * v
    return half + half * jnp.tanh(half)


def up_kernel(up_hbm, upmat_ref, token_ref, up_ref, sems):
    slab = 64 * 32

    def fetch(k1):
        rows = pl.ds(pl.multiple_of(k1 * slab, slab), slab)
        return pltpu.make_async_copy(up_hbm.at[rows], up_ref.at[rows], sems.at[k1])

    for k1 in range(8):
        fetch(k1).start()
    token_ref[...] = jnp.zeros((8, 128), jnp.float32)

    @pl.loop(0, 8)
    def _(k1):
        fetch(k1).wait()
        h1, p1 = k1 // 4, k1 % 4
        for k2 in range(8):
            h2, p2 = divmod(k2, 4)
            for h3 in range(2):
                parts = []
                for z in ORDER[p2 % 2]:
                    at = k1 * slab + (k2 * 8 + 4 * h3 + (z + 2) % 4) * 32
                    parts.append(up_ref[pl.ds(pl.multiple_of(at, 32), 32), :])
                row = pl.multiple_of(h1 * 128 + h2 * 64 + (1 - h3) * 32, 32)
                column = pl.multiple_of(p1 * 512 + p2 * 128, 128)
                upmat_ref[pl.ds(row, 32), pl.ds(column, 128)] = jnp.concatenate(parts, axis=1)


def arrange_bands(first_ref, second_ref, band1_ref, band2_ref):
    ci = lax.broadcasted_iota(jnp.int32, (32, 128), 0)
    lane = lax.broadcasted_iota(jnp.int32, (32, 128), 1)
    group = lane // 32
    copies = (lane % 32 == ci).astype(jnp.bfloat16)

    def arrange(w_ref, band_ref, out_order):
        rep = jnp.dot(w_ref[...], copies, preferred_element_type=jnp.float32)
        for d1 in range(3):
            for dj in range(2):
                cells = [(0, z) for z in ORDER[0]] + [(1, z) for z in ORDER[1]] + list(BESIDE)
                for n, (side, z_in) in enumerate(cells):
                    row = (d1 * 2 + dj) * 384 + n * 32
                    for o in range(2):
                        block = jnp.zeros((32, 128), jnp.float32)
                        d2 = 2 * dj + side - o
                        for d3 in range(3):
                            z_out = z_in - d3 + 1
                            if 0 <= d2 < 3 and 0 <= z_out < 4:
                                tap = ((d1 * 3 + d2) * 3 + d3) * 32
                                here = group == out_order[o].index(z_out)
                                block = jnp.where(here, rep[tap : tap + 32], block)
                        band_ref[pl.ds(row, 32), pl.ds(o * 128, 128)] = block.astype(jnp.bfloat16)

    arrange(first_ref, band1_ref, ORDER)
    arrange(second_ref, band2_ref, (ORDER[0], ORDER[0]))
    r = lax.broadcasted_iota(jnp.int32, (256, 256), 0)
    c = lax.broadcasted_iota(jnp.int32, (256, 256), 1)
    swap = jnp.where((r // 32) % 2 == 0, r + 32, r - 32)
    band2_ref[pl.ds(WINDOW, 256), :] = (jnp.where(r < 128, r, swap) == c).astype(jnp.bfloat16)


def pack_kernel(coarse, dip_a, dip_b, token, own):
    own[0:4] = coarse[...]
    own[4:8] = dip_a[...]
    own[8:12] = dip_b[...]


def edges():
    one, zero = jnp.float32(1), jnp.float32(0)
    strike, dip = lax.axis_index("strike"), lax.axis_index("dip")
    x_lo = jnp.where(strike == 0, zero, one)
    x_hi = jnp.where(strike == lax.axis_size("strike") - 1, zero, one)
    y_lo = jnp.where(dip == 0, zero, one)
    y_hi = jnp.where(dip == lax.axis_size("dip") - 1, zero, one)
    return x_lo, x_hi, y_lo, y_hi


def put(cells, x0, x1, block):
    even = lax.axis_index("dip") % 2 == 0
    below, above = jnp.where(even, 8, 4), jnp.where(even, 4, 8)
    cells[x0:x1, 1:5, :] = block(0)
    cells[x0:x1, 0:1, :] = block(below)[:, 3:4]
    cells[x0:x1, 5:6, :] = block(above)[:, 0:1]


def read(ref, first, count):
    return ref[pl.ds(first, count)].astype(jnp.float32)


def upsample(cells, upmat, fine, q1s, sides):
    x_lo, x_hi, y_lo, y_hi = sides
    one = jnp.float32(1)
    count = len(q1s)
    rows = 8 * count
    wide = []
    edge = jnp.zeros((rows, 32), jnp.float32)
    for h1 in range(2):
        for h2 in range(2):
            window = jnp.concatenate(
                [cells[q1 + 1 - h1 : q1 + 2 - h1, 1 - h2 : 9 - h2, :] for q1 in q1s], axis=0
            )
            wide.append(jnp.concatenate([edge, window.reshape(rows, 128), edge], axis=1))
    left = jnp.concatenate(
        [
            jnp.concatenate([w[:, 32 * q3 : 32 * q3 + 64] for w in wide], axis=1)
            for q3 in range(5)
        ],
        axis=0,
    ).astype(jnp.bfloat16)

    lane = lax.broadcasted_iota(jnp.int32, (rows, 128), 1)
    q2 = lax.broadcasted_iota(jnp.int32, (rows, 128), 0) % 8
    outer = (lane < 32) | (lane >= 96)
    front = lane < 64
    low = jnp.where(q2 == 0, y_lo, one)
    high = jnp.where(q2 == 4, y_hi, one)
    none = jnp.zeros((rows, 128), jnp.float32)

    @pl.loop(0, 4)
    def _(p1):
        taps = upmat[:, pl.ds(pl.multiple_of(p1 * 512, 512), 512)]
        phase = jnp.dot(left, taps, preferred_element_type=jnp.float32)
        below = jnp.where(p1 < 2, x_lo, one)
        above = jnp.where(p1 < 2, one, x_hi)
        for pp in range(2):
            tiles = [[], []]
            for side in range(2):
                p2 = 2 * pp + side
                v = phase[:, p2 * 128 : p2 * 128 + 128]
                for g in range(GROUPS):
                    at = g * rows
                    t = jnp.where(front, v[at : at + rows], v[at + rows : at + 2 * rows])
                    tiles[side].append(silu(t) * (low if pp == 0 else high))
            merged = [jnp.where(outer, tiles[0][g], tiles[1][g]) for g in range(GROUPS)]
            merged = [none] + merged + [none]
            for g in range(GROUPS):
                beside = jnp.where(front, merged[g + 2], merged[g])
                for n, t in enumerate((tiles[0][g], tiles[1][g], beside)):
                    for c, q1 in enumerate(q1s):
                        part = t[c * 8 : c * 8 + 5]
                        if q1 == 0:
                            part = part * below
                        if q1 == 4:
                            part = part * above
                        at = p1 * STEP + (4 * c * STEP + g * PAIRS + pp)
                        fine[n, pl.ds(at, 5, stride=2), :] = part


def windows_of(fine, first, count, target, at):
    for dj in range(2):
        for n in range(3):
            rows = fine[n, pl.ds(first * STEP + dj, count * STEP), :].astype(jnp.bfloat16)
            target[dj, at * STEP : (at + count) * STEP, n * 128 : n * 128 + 128] = rows


def inner_kernel(own, upmat, first_ref, second_ref, inner, band1_ref, band2_ref, cells, fine):
    arrange_bands(first_ref, second_ref, band1_ref, band2_ref)
    put(cells, 1, 5, lambda o: read(own, o, 4))
    upsample(cells, upmat, fine, (1, 2, 3), edges())
    windows_of(fine, 0, 12, inner, 0)


def product(source, strips, taps, base=None):
    columns = []
    for dx in range(3):
        for dj in range(2):
            columns.append(
                jnp.concatenate(
                    [source[dj, (at + dx) * STEP : (at + dx + n) * STEP, :] for at, n in strips], axis=0
                )
            )
    if base is not None:
        columns.append(base)
    return jnp.dot(jnp.concatenate(columns, axis=1), taps[...], preferred_element_type=jnp.float32)


def main_kernel(
    own, strike_a, strike_b, inner, upmat, band1, band2, out,
    cells, fine, hidden, b1, b2, result, woven, near, sems,
):
    sides = x_lo, x_hi, y_lo, y_hi = edges()
    one, zero = jnp.float32(1), jnp.float32(0)

    v_inner = product(inner, ((0, 10),), band1)

    even = lax.axis_index("strike") % 2 == 0
    put(cells, 0, 1, lambda o: jnp.where(even, read(strike_b, o + 3, 1), read(strike_a, o + 3, 1)))
    put(cells, 1, 2, lambda o: read(own, o, 1))
    put(cells, 4, 5, lambda o: read(own, o + 3, 1))
    put(cells, 5, 6, lambda o: jnp.where(even, read(strike_a, o, 1), read(strike_b, o, 1)))
    upsample(cells, upmat, fine, (0, 4), sides)
    windows_of(fine, 0, 4, b1, 0)
    b1[:, 4 * STEP : 6 * STEP, :] = inner[:, : 2 * STEP, :]
    b1[:, 6 * STEP : 8 * STEP, :] = inner[:, 10 * STEP : 12 * STEP, :]
    windows_of(fine, 4, 4, b1, 8)

    v_outer = product(b1, ((0, 4), (6, 4)), band1)

    row = lax.broadcasted_iota(jnp.int32, (STEP, 128), 0)
    lane = lax.broadcasted_iota(jnp.int32, (STEP, 128), 1)
    starts = [g * PAIRS for g in range(GROUPS)]
    first, last = row == starts[0], row == starts[0] + 8
    for start in starts[1:]:
        first, last = first | (row == start), last | (row == start + 8)
    y_first, y_last = jnp.where(first, y_lo, one), jnp.where(last, y_hi, one)
    outer = (lane < 32) | (lane >= 96)
    front = lane < 64
    inside_above = jnp.where(row < starts[-1], one, zero)
    inside_below = jnp.where(row >= PAIRS, one, zero)
    inside = jnp.where(front, inside_above, inside_below)

    def clear(at):
        hidden[2, at : at + 16, :] = jnp.zeros((16, 128), jnp.float32)

    def keep(v, at, count):
        v = silu(v)
        for n in range(count):
            x = at + n
            rows = slice(n * STEP, n * STEP + STEP)
            v0, v1 = v[rows, :128] * y_first, v[rows, 128:] * y_last
            if x in (0, 17):
                edge = x_lo if x == 0 else x_hi
                v0, v1 = v0 * edge, v1 * edge
            here = slice(16 + x * STEP, 16 + x * STEP + STEP)
            hidden[0, here, :] = v0
            hidden[1, here, :] = v1
            hidden[2, here, :] = jnp.where(outer, v0, v1)
        rows = count * STEP
        start = 16 + at * STEP
        here = slice(at * STEP, at * STEP + rows)
        for dj in range(2):
            for n in range(2):
                b2[dj, here, n * 128 : n * 128 + 128] = hidden[n, pl.ds(start + dj, rows), :].astype(
                    jnp.bfloat16
                )
            above = hidden[2, pl.ds(start + dj + PAIRS, rows), :].reshape(count, STEP, 128)
            below = hidden[2, pl.ds(start + dj - PAIRS, rows), :].reshape(count, STEP, 128)
            beside = jnp.where(front[None], above, below) * inside[None]
            b2[dj, here, 256:384] = beside.reshape(rows, 128).astype(jnp.bfloat16)

    def finish(v, strips, chain):
        sends = []
        for o in range(2):
            result[2 * chain + o] = v[:, o * 128 : o * 128 + 128]
        row = 0
        for k, (at, count) in enumerate(strips):
            for x in range(at, at + count):
                for g in range(GROUPS):
                    for o in range(2):
                        cells8 = result[2 * chain + o, pl.ds(row + g * PAIRS, 8), :]
                        woven[g, pl.ds(x * 16 + o, 8, stride=2), :] = cells8
                row += STEP
            for g in range(GROUPS):
                near[at : at + count, :, g * 128 : g * 128 + 128] = (
                    woven[g, at * 16 : (at + count) * 16].reshape(count, 16, 128).astype(jnp.bfloat16)
                )
            here = pl.ds(at, count)
            sends.append(pltpu.make_async_copy(near.at[here], out.at[here], sems.at[chain + k]))
            sends[-1].start()
        return sends

    clear(4 * STEP)
    clear(16 + 14 * STEP)
    keep(v_inner, 4, 10)
    base = inner[1, 2 * STEP : 10 * STEP, :256]
    v_inner = product(b2, ((4, 8),), band2, base)

    clear(0)
    clear(16 + 18 * STEP)
    keep(v_outer[: 4 * STEP], 0, 4)
    keep(v_outer[4 * STEP :], 14, 4)
    base = jnp.concatenate(
        [b1[1, 2 * STEP : 6 * STEP, :256], b1[1, 6 * STEP : 10 * STEP, :256]], axis=0
    )
    v_outer = product(b2, ((0, 4), (12, 4)), band2, base)

    sends = finish(v_inner, ((4, 8),), 0)
    sends += finish(v_outer, ((0, 4), (12, 4)), 1)
    for send in sends:
        send.wait()


def swapped(block, axis):
    size = lax.axis_size(axis)
    for first in (0, 1):
        pairs = [(i, i + 1) for i in range(first, size - 1, 2)]
        yield lax.ppermute(block, axis, pairs + [(j, i) for i, j in pairs])


def body(coarse, up_weight, first_weight, second_weight):
    vmem = pl.BlockSpec(memory_space=pltpu.VMEM)
    params = pltpu.CompilerParams(vmem_limit_bytes=32 * 1024 * 1024)

    bf16 = jnp.bfloat16
    shape = jax.ShapeDtypeStruct
    dip_a, dip_b = swapped(coarse, "dip")
    upmat, token = pl.pallas_call(
        up_kernel,
        out_shape=(shape((256, 2048), bf16), shape((8, 128), jnp.float32)),
        in_specs=[pl.BlockSpec(memory_space=pltpu.HBM)],
        out_specs=(vmem, vmem),
        scratch_shapes=[pltpu.VMEM((512 * 32, 32), bf16), pltpu.SemaphoreType.DMA((8,))],
        compiler_params=pltpu.CompilerParams(vmem_limit_bytes=LIMIT),
        cost_estimate=pl.CostEstimate(flops=5_000_000, bytes_accessed=5_000_000, transcendentals=0),
        name="arrange_up",
    )(up_weight.reshape(512 * 32, 32))
    own = pl.pallas_call(
        pack_kernel,
        out_shape=shape((12, 4, 128), bf16),
        in_specs=[vmem] * 4,
        out_specs=vmem,
        compiler_params=pltpu.CompilerParams(vmem_limit_bytes=1024 * 1024),
        name="pack",
    )(coarse, dip_a, dip_b, token)
    strike_a, strike_b = swapped(own, "strike")
    inner, band1, band2 = pl.pallas_call(
        inner_kernel,
        out_shape=(
            shape((2, 12 * STEP, 384), bf16),
            shape((WINDOW, 256), bf16),
            shape((WINDOW + 256, 256), bf16),
        ),
        in_specs=[vmem] * 4,
        out_specs=(vmem,) * 3,
        scratch_shapes=[
            pltpu.VMEM((6, 16, 128), jnp.float32),
            pltpu.VMEM((3, 12 * STEP + 8, 128), jnp.float32),
        ],
        compiler_params=pltpu.CompilerParams(vmem_limit_bytes=16 * 1024 * 1024),
        cost_estimate=pl.CostEstimate(
            flops=300_000_000, bytes_accessed=3_000_000, transcendentals=200_000
        ),
        name="upsample_inner",
    )(own, upmat, first_weight.reshape(864, 32), second_weight.reshape(864, 32))
    return pl.pallas_call(
        main_kernel,
        out_shape=jax.ShapeDtypeStruct((16, 16, 512), bf16),
        in_specs=[vmem] * 7,
        out_specs=pl.BlockSpec(memory_space=pltpu.HBM),
        scratch_shapes=[
            pltpu.VMEM((6, 16, 128), jnp.float32),
            pltpu.VMEM((3, 8 * STEP + 8, 128), jnp.float32),
            pltpu.VMEM((3, 18 * STEP + 32, 128), jnp.float32),
            pltpu.VMEM((2, 12 * STEP, 384), bf16),
            pltpu.VMEM((2, 18 * STEP, 384), bf16),
            pltpu.VMEM((4, 8 * STEP, 128), jnp.float32),
            pltpu.VMEM((GROUPS, 256, 128), jnp.float32),
            pltpu.VMEM((16, 16, 512), bf16),
            pltpu.SemaphoreType.DMA((3,)),
        ],
        compiler_params=params,
        cost_estimate=pl.CostEstimate(
            flops=2_000_000_000, bytes_accessed=8_000_000, transcendentals=800_000
        ),
        name="upsample_refine",
    )(own, strike_a, strike_b, inner, upmat, band1, band2)


def solution(mesh):
    return jax.shard_map(
        body,
        mesh=mesh,
        in_specs=(P("strike", "dip", None), P(), P(), P()),
        out_specs=P("strike", "dip", None),
        check_vma=False,
    )
```

```python
import jax
import jax.numpy as jnp
from jax import lax
from jax.experimental import pallas as pl
from jax.experimental.pallas import tpu as pltpu
from jax.sharding import PartitionSpec as P

GROUPS = 4
PAIRS = 10
STEP = GROUPS * PAIRS
ORDER = ((0, 1, 2, 3), (1, 0, 3, 2))
BESIDE = ((0, 4), (1, 4), (1, -1), (0, -1))
WINDOW = 3 * 2 * 384
TIGHT = GROUPS * 8
AHEAD = 3
LIMIT = 50 * 1024 * 1024


def silu(v):
    half = 0.5 * v
    return half + half * jnp.tanh(half)


def up_kernel(up_hbm, upmat_ref, token_ref, up_ref, sems):
    fetches = []
    for k1 in range(8):
        rows = pl.ds(k1 * 2048, 2048)
        fetches.append(pltpu.make_async_copy(up_hbm.at[rows], up_ref.at[rows], sems.at[k1]))
    for fetch in fetches[:AHEAD]:
        fetch.start()
    token_ref[...] = jnp.zeros((8, 128), jnp.float32)

    for k1 in range(8):
        fetches[k1].wait()
        if k1 + AHEAD < 8:
            fetches[k1 + AHEAD].start()
        h1, p1 = divmod(k1, 4)
        for k2 in range(8):
            h2, p2 = divmod(k2, 4)
            for h3 in range(2):
                k = (k1 * 8 + k2) * 8 + 4 * h3
                parts = [up_ref[pl.ds((k + (z + 2) % 4) * 32, 32), :] for z in ORDER[p2 % 2]]
                row = (h1 * 4 + h2 * 2 + (1 - h3)) * 32
                upmat_ref[pl.ds(row, 32), pl.ds((p1 * 4 + p2) * 128, 128)] = jnp.concatenate(
                    parts, axis=1
                )


def arrange_bands(first_ref, second_ref, band1_ref, band2_ref):
    ci = lax.broadcasted_iota(jnp.int32, (32, 128), 0)
    lane = lax.broadcasted_iota(jnp.int32, (32, 128), 1)
    group = lane // 32
    copies = (lane % 32 == ci).astype(jnp.bfloat16)

    def arrange(w_ref, band_ref, out_order):
        rep = jnp.dot(w_ref[...], copies, preferred_element_type=jnp.float32)
        for d1 in range(3):
            for dj in range(2):
                cells = [(0, z) for z in ORDER[0]] + [(1, z) for z in ORDER[1]] + list(BESIDE)
                for n, (side, z_in) in enumerate(cells):
                    row = (d1 * 2 + dj) * 384 + n * 32
                    for o in range(2):
                        block = jnp.zeros((32, 128), jnp.float32)
                        d2 = 2 * dj + side - o
                        for d3 in range(3):
                            z_out = z_in - d3 + 1
                            if 0 <= d2 < 3 and 0 <= z_out < 4:
                                tap = ((d1 * 3 + d2) * 3 + d3) * 32
                                here = group == out_order[o].index(z_out)
                                block = jnp.where(here, rep[tap : tap + 32], block)
                        band_ref[pl.ds(row, 32), pl.ds(o * 128, 128)] = block.astype(jnp.bfloat16)

    arrange(first_ref, band1_ref, ORDER)
    arrange(second_ref, band2_ref, (ORDER[0], ORDER[0]))
    r = lax.broadcasted_iota(jnp.int32, (256, 256), 0)
    c = lax.broadcasted_iota(jnp.int32, (256, 256), 1)
    swap = jnp.where((r // 32) % 2 == 0, r + 32, r - 32)
    band2_ref[pl.ds(WINDOW, 256), :] = (jnp.where(r < 128, r, swap) == c).astype(jnp.bfloat16)


def pack_kernel(coarse, dip_a, dip_b, token, own):
    own[0:4] = coarse[...]
    own[4:8] = dip_a[...]
    own[8:12] = dip_b[...]


def edges():
    one, zero = jnp.float32(1), jnp.float32(0)
    strike, dip = lax.axis_index("strike"), lax.axis_index("dip")
    x_lo = jnp.where(strike == 0, zero, one)
    x_hi = jnp.where(strike == lax.axis_size("strike") - 1, zero, one)
    y_lo = jnp.where(dip == 0, zero, one)
    y_hi = jnp.where(dip == lax.axis_size("dip") - 1, zero, one)
    return x_lo, x_hi, y_lo, y_hi


def put(cells, x0, x1, block):
    even = lax.axis_index("dip") % 2 == 0
    below, above = jnp.where(even, 8, 4), jnp.where(even, 4, 8)
    cells[x0:x1, 1:5, :] = block(0)
    cells[x0:x1, 0:1, :] = block(below)[:, 3:4]
    cells[x0:x1, 5:6, :] = block(above)[:, 0:1]


def read(ref, first, count):
    return ref[pl.ds(first, count)].astype(jnp.float32)


def upsample(cells, upmat, fine, q1s, sides):
    x_lo, x_hi, y_lo, y_hi = sides
    one = jnp.float32(1)
    count = len(q1s)
    rows = 8 * count
    wide = []
    edge = jnp.zeros((rows, 32), jnp.float32)
    for h1 in range(2):
        for h2 in range(2):
            window = jnp.concatenate(
                [cells[q1 + 1 - h1 : q1 + 2 - h1, 1 - h2 : 9 - h2, :] for q1 in q1s], axis=0
            )
            wide.append(jnp.concatenate([edge, window.reshape(rows, 128), edge], axis=1))
    left = jnp.concatenate(
        [
            jnp.concatenate([w[:, 32 * q3 : 32 * q3 + 64] for w in wide], axis=1)
            for q3 in range(5)
        ],
        axis=0,
    ).astype(jnp.bfloat16)

    lane = lax.broadcasted_iota(jnp.int32, (rows, 128), 1)
    q2 = lax.broadcasted_iota(jnp.int32, (rows, 128), 0) % 8
    outer = (lane < 32) | (lane >= 96)
    front = lane < 64
    low = jnp.where(q2 == 0, y_lo, one)
    high = jnp.where(q2 == 4, y_hi, one)
    none = jnp.zeros((rows, 128), jnp.float32)
    for p1 in range(4):
        phase = jnp.dot(left, upmat[:, p1 * 512 : p1 * 512 + 512], preferred_element_type=jnp.float32)
        for pp in range(2):
            tiles = [[], []]
            for side in range(2):
                p2 = 2 * pp + side
                v = phase[:, p2 * 128 : p2 * 128 + 128]
                for g in range(GROUPS):
                    at = g * rows
                    t = jnp.where(front, v[at : at + rows], v[at + rows : at + 2 * rows])
                    tiles[side].append(silu(t) * (low if pp == 0 else high))
            merged = [jnp.where(outer, tiles[0][g], tiles[1][g]) for g in range(GROUPS)]
            merged = [none] + merged + [none]
            for g in range(GROUPS):
                beside = jnp.where(front, merged[g + 2], merged[g])
                for n, t in enumerate((tiles[0][g], tiles[1][g], beside)):
                    for c, q1 in enumerate(q1s):
                        part = t[c * 8 : c * 8 + 5]
                        if q1 == 0 and p1 < 2:
                            part = part * x_lo
                        if q1 == 4 and p1 >= 2:
                            part = part * x_hi
                        at = (4 * c + p1) * STEP + g * PAIRS + pp
                        fine[n, pl.ds(at, 5, stride=2), :] = part


def windows_of(fine, first, count, target, at):
    for dj in range(2):
        for n in range(3):
            rows = fine[n, pl.ds(first * STEP + dj, count * STEP), :].astype(jnp.bfloat16)
            target[dj, at * STEP : (at + count) * STEP, n * 128 : n * 128 + 128] = rows


def tight(block, at):
    return jnp.concatenate([block[pl.ds(at + g * PAIRS, 8), :] for g in range(GROUPS)], axis=0)


def centre_of(fine, first, count, target, at):
    for n in range(count):
        here = slice((at + n) * TIGHT, (at + n + 1) * TIGHT)
        for o in range(2):
            rows = tight(fine.at[o], (first + n) * STEP + 1)
            target[here, o * 128 : o * 128 + 128] = rows.astype(jnp.bfloat16)


def inner_kernel(
    own, upmat, first_ref, second_ref, inner, centre, band1_ref, band2_ref, cells, fine
):
    arrange_bands(first_ref, second_ref, band1_ref, band2_ref)
    put(cells, 1, 5, lambda o: read(own, o, 4))
    upsample(cells, upmat, fine, (1, 2, 3), edges())
    windows_of(fine, 0, 12, inner, 0)
    centre_of(fine, 0, 12, centre, 0)


def product(source, strips, step, taps, base=None):
    columns = []
    for dx in range(3):
        for dj in range(2):
            columns.append(
                jnp.concatenate(
                    [source[dj, (at + dx) * step : (at + dx + n) * step, :] for at, n in strips], axis=0
                )
            )
    if base is not None:
        columns.append(base)
    return jnp.dot(jnp.concatenate(columns, axis=1), taps[...], preferred_element_type=jnp.float32)


def main_kernel(
    own, strike_a, strike_b, inner, centre, upmat, band1, band2, out,
    cells, fine, hidden, b1, b2, ends, woven, near, sems,
):
    sides = x_lo, x_hi, y_lo, y_hi = edges()
    one, zero = jnp.float32(1), jnp.float32(0)

    v_inner = product(inner, ((0, 10),), STEP, band1)

    even = lax.axis_index("strike") % 2 == 0
    put(cells, 0, 1, lambda o: jnp.where(even, read(strike_b, o + 3, 1), read(strike_a, o + 3, 1)))
    put(cells, 1, 2, lambda o: read(own, o, 1))
    put(cells, 4, 5, lambda o: read(own, o + 3, 1))
    put(cells, 5, 6, lambda o: jnp.where(even, read(strike_a, o, 1), read(strike_b, o, 1)))
    upsample(cells, upmat, fine, (0, 4), sides)
    windows_of(fine, 0, 4, b1, 0)
    b1[:, 4 * STEP : 6 * STEP, :] = inner[:, : 2 * STEP, :]
    b1[:, 6 * STEP : 8 * STEP, :] = inner[:, 10 * STEP : 12 * STEP, :]
    windows_of(fine, 4, 4, b1, 8)
    centre_of(fine, 2, 2, ends, 0)
    ends[2 * TIGHT : 4 * TIGHT, :] = centre[0 : 2 * TIGHT, :]
    ends[4 * TIGHT : 6 * TIGHT, :] = centre[10 * TIGHT : 12 * TIGHT, :]
    centre_of(fine, 4, 2, ends, 6)

    v_outer = product(b1, ((0, 4), (6, 4)), STEP, band1)

    row = lax.broadcasted_iota(jnp.int32, (STEP, 128), 0)
    lane = lax.broadcasted_iota(jnp.int32, (STEP, 128), 1)
    starts = [g * PAIRS for g in range(GROUPS)]
    first, last = row == starts[0], row == starts[0] + 8
    for start in starts[1:]:
        first, last = first | (row == start), last | (row == start + 8)
    y_first, y_last = jnp.where(first, y_lo, one), jnp.where(last, y_hi, one)
    outer = (lane < 32) | (lane >= 96)
    row = lax.broadcasted_iota(jnp.int32, (TIGHT, 128), 0)
    lane = lax.broadcasted_iota(jnp.int32, (TIGHT, 128), 1)
    front = lane < 64
    inside_above = jnp.where(row < TIGHT - 8, one, zero)
    inside_below = jnp.where(row >= 8, one, zero)
    inside = jnp.where(front, inside_above, inside_below)

    def clear(at):
        hidden[2, at : at + 16, :] = jnp.zeros((16, 128), jnp.float32)

    def keep(v, at, count):
        v = silu(v)
        for n in range(count):
            x = at + n
            rows = slice(n * STEP, n * STEP + STEP)
            v0, v1 = v[rows, :128] * y_first, v[rows, 128:] * y_last
            if x in (0, 17):
                edge = x_lo if x == 0 else x_hi
                v0, v1 = v0 * edge, v1 * edge
            here = slice(16 + x * STEP, 16 + x * STEP + STEP)
            hidden[0, here, :] = v0
            hidden[1, here, :] = v1
            hidden[2, here, :] = jnp.where(outer, v0, v1)
        for x in range(at, at + count):
            here = slice(x * TIGHT, (x + 1) * TIGHT)
            for dj in range(2):
                start = 16 + x * STEP + dj
                for n in range(2):
                    rows = tight(hidden.at[n], start)
                    b2[dj, here, n * 128 : n * 128 + 128] = rows.astype(jnp.bfloat16)
                above = tight(hidden.at[2], start + PAIRS)
                below = tight(hidden.at[2], start - PAIRS)
                beside = jnp.where(front, above, below) * inside
                b2[dj, here, 256:384] = beside.astype(jnp.bfloat16)

    def finish(v, strips, chain):
        sends = []
        row = 0
        for k, (at, count) in enumerate(strips):
            for x in range(at, at + count):
                for g in range(GROUPS):
                    for o in range(2):
                        cells8 = v[row : row + 8, o * 128 : o * 128 + 128]
                        woven[g, pl.ds(x * 16 + o, 8, stride=2), :] = cells8
                    row += 8
            for g in range(GROUPS):
                near[at : at + count, :, g * 128 : g * 128 + 128] = (
                    woven[g, at * 16 : (at + count) * 16].reshape(count, 16, 128).astype(jnp.bfloat16)
                )
            here = pl.ds(at, count)
            sends.append(pltpu.make_async_copy(near.at[here], out.at[here], sems.at[chain + k]))
            sends[-1].start()
        return sends

    clear(4 * STEP)
    clear(16 + 14 * STEP)
    keep(v_inner, 4, 10)
    v_inner = product(b2, ((4, 8),), TIGHT, band2, centre[2 * TIGHT : 10 * TIGHT, :])

    clear(0)
    clear(16 + 18 * STEP)
    keep(v_outer[: 4 * STEP], 0, 4)
    keep(v_outer[4 * STEP :], 14, 4)
    v_outer = product(b2, ((0, 4), (12, 4)), TIGHT, band2, ends[...])

    sends = finish(v_inner, ((4, 8),), 0)
    sends += finish(v_outer, ((0, 4), (12, 4)), 1)
    for send in sends:
        send.wait()


def swapped(block, axis):
    size = lax.axis_size(axis)
    for first in (0, 1):
        pairs = [(i, i + 1) for i in range(first, size - 1, 2)]
        yield lax.ppermute(block, axis, pairs + [(j, i) for i, j in pairs])


def body(coarse, up_weight, first_weight, second_weight):
    vmem = pl.BlockSpec(memory_space=pltpu.VMEM)
    params = pltpu.CompilerParams(vmem_limit_bytes=32 * 1024 * 1024)

    bf16 = jnp.bfloat16
    shape = jax.ShapeDtypeStruct
    dip_a, dip_b = swapped(coarse, "dip")
    upmat, token = pl.pallas_call(
        up_kernel,
        out_shape=(shape((256, 2048), bf16), shape((8, 128), jnp.float32)),
        in_specs=[pl.BlockSpec(memory_space=pltpu.HBM)],
        out_specs=(vmem, vmem),
        scratch_shapes=[pltpu.VMEM((512 * 32, 32), bf16), pltpu.SemaphoreType.DMA((8,))],
        compiler_params=pltpu.CompilerParams(vmem_limit_bytes=LIMIT),
        cost_estimate=pl.CostEstimate(flops=5_000_000, bytes_accessed=5_000_000, transcendentals=0),
        name="arrange_up",
    )(up_weight.reshape(512 * 32, 32))
    own = pl.pallas_call(
        pack_kernel,
        out_shape=shape((12, 4, 128), bf16),
        in_specs=[vmem] * 4,
        out_specs=vmem,
        compiler_params=pltpu.CompilerParams(vmem_limit_bytes=1024 * 1024),
        name="pack",
    )(coarse, dip_a, dip_b, token)
    strike_a, strike_b = swapped(own, "strike")
    inner, centre, band1, band2 = pl.pallas_call(
        inner_kernel,
        out_shape=(
            shape((2, 12 * STEP, 384), bf16),
            shape((12 * TIGHT, 256), bf16),
            shape((WINDOW, 256), bf16),
            shape((WINDOW + 256, 256), bf16),
        ),
        in_specs=[vmem] * 4,
        out_specs=(vmem,) * 4,
        scratch_shapes=[
            pltpu.VMEM((6, 16, 128), jnp.float32),
            pltpu.VMEM((3, 12 * STEP + 8, 128), jnp.float32),
        ],
        compiler_params=pltpu.CompilerParams(vmem_limit_bytes=16 * 1024 * 1024),
        cost_estimate=pl.CostEstimate(
            flops=300_000_000, bytes_accessed=3_000_000, transcendentals=200_000
        ),
        name="upsample_inner",
    )(own, upmat, first_weight.reshape(864, 32), second_weight.reshape(864, 32))
    return pl.pallas_call(
        main_kernel,
        out_shape=jax.ShapeDtypeStruct((16, 16, 512), bf16),
        in_specs=[vmem] * 8,
        out_specs=pl.BlockSpec(memory_space=pltpu.HBM),
        scratch_shapes=[
            pltpu.VMEM((6, 16, 128), jnp.float32),
            pltpu.VMEM((3, 8 * STEP + 8, 128), jnp.float32),
            pltpu.VMEM((3, 18 * STEP + 32, 128), jnp.float32),
            pltpu.VMEM((2, 12 * STEP, 384), bf16),
            pltpu.VMEM((2, 18 * TIGHT, 384), bf16),
            pltpu.VMEM((8 * TIGHT, 256), bf16),
            pltpu.VMEM((GROUPS, 256, 128), jnp.float32),
            pltpu.VMEM((16, 16, 512), bf16),
            pltpu.SemaphoreType.DMA((3,)),
        ],
        compiler_params=params,
        cost_estimate=pl.CostEstimate(
            flops=2_000_000_000, bytes_accessed=8_000_000, transcendentals=800_000
        ),
        name="upsample_refine",
    )(own, strike_a, strike_b, inner, centre, upmat, band1, band2)


def solution(mesh):
    return jax.shard_map(
        body,
        mesh=mesh,
        in_specs=(P("strike", "dip", None), P(), P(), P()),
        out_specs=P("strike", "dip", None),
        check_vma=False,
    )
```

```python
import jax
import jax.numpy as jnp
from jax import lax
from jax.experimental import pallas as pl
from jax.experimental.pallas import tpu as pltpu
from jax.sharding import PartitionSpec as P

GROUPS = 4
PAIRS = 10
STEP = GROUPS * PAIRS
ORDER = ((0, 1, 2, 3), (1, 0, 3, 2))
BESIDE = ((0, 4), (1, 4), (1, -1), (0, -1))
WINDOW = 3 * 2 * 384
TIGHT = GROUPS * 8
AHEAD = 8
LIMIT = 50 * 1024 * 1024


def silu(v):
    half = 0.5 * v
    return half + half * jnp.tanh(half)


def up_kernel(up_hbm, upmat_ref, token_ref, up_ref, sems):
    fetches = []
    for k1 in range(8):
        rows = pl.ds(k1 * 2048, 2048)
        fetches.append(pltpu.make_async_copy(up_hbm.at[rows], up_ref.at[rows], sems.at[k1]))
    for fetch in fetches[:AHEAD]:
        fetch.start()
    token_ref[...] = jnp.zeros((8, 128), jnp.float32)

    for k1 in range(8):
        fetches[k1].wait()
        if k1 + AHEAD < 8:
            fetches[k1 + AHEAD].start()
        h1, p1 = divmod(k1, 4)
        for k2 in range(8):
            h2, p2 = divmod(k2, 4)
            for h3 in range(2):
                k = (k1 * 8 + k2) * 8 + 4 * h3
                parts = [up_ref[pl.ds((k + (z + 2) % 4) * 32, 32), :] for z in ORDER[p2 % 2]]
                row = (h1 * 4 + h2 * 2 + (1 - h3)) * 32
                upmat_ref[pl.ds(row, 32), pl.ds((p1 * 4 + p2) * 128, 128)] = jnp.concatenate(
                    parts, axis=1
                )


def arrange_bands(first_ref, second_ref, band1_ref, band2_ref):
    ci = lax.broadcasted_iota(jnp.int32, (32, 128), 0)
    lane = lax.broadcasted_iota(jnp.int32, (32, 128), 1)
    group = lane // 32
    copies = (lane % 32 == ci).astype(jnp.bfloat16)

    def arrange(w_ref, band_ref, out_order):
        rep = jnp.dot(w_ref[...], copies, preferred_element_type=jnp.float32)
        for d1 in range(3):
            for dj in range(2):
                cells = [(0, z) for z in ORDER[0]] + [(1, z) for z in ORDER[1]] + list(BESIDE)
                for n, (side, z_in) in enumerate(cells):
                    row = (d1 * 2 + dj) * 384 + n * 32
                    for o in range(2):
                        block = jnp.zeros((32, 128), jnp.float32)
                        d2 = 2 * dj + side - o
                        for d3 in range(3):
                            z_out = z_in - d3 + 1
                            if 0 <= d2 < 3 and 0 <= z_out < 4:
                                tap = ((d1 * 3 + d2) * 3 + d3) * 32
                                here = group == out_order[o].index(z_out)
                                block = jnp.where(here, rep[tap : tap + 32], block)
                        band_ref[pl.ds(row, 32), pl.ds(o * 128, 128)] = block.astype(jnp.bfloat16)

    arrange(first_ref, band1_ref, ORDER)
    arrange(second_ref, band2_ref, (ORDER[0], ORDER[0]))
    r = lax.broadcasted_iota(jnp.int32, (256, 256), 0)
    c = lax.broadcasted_iota(jnp.int32, (256, 256), 1)
    swap = jnp.where((r // 32) % 2 == 0, r + 32, r - 32)
    band2_ref[pl.ds(WINDOW, 256), :] = (jnp.where(r < 128, r, swap) == c).astype(jnp.bfloat16)


def pack_kernel(coarse, dip_a, dip_b, token, own):
    own[0:4] = coarse[...]
    own[4:8] = dip_a[...]
    own[8:12] = dip_b[...]


def edges():
    one, zero = jnp.float32(1), jnp.float32(0)
    strike, dip = lax.axis_index("strike"), lax.axis_index("dip")
    x_lo = jnp.where(strike == 0, zero, one)
    x_hi = jnp.where(strike == lax.axis_size("strike") - 1, zero, one)
    y_lo = jnp.where(dip == 0, zero, one)
    y_hi = jnp.where(dip == lax.axis_size("dip") - 1, zero, one)
    return x_lo, x_hi, y_lo, y_hi


def put(cells, x0, x1, block):
    even = lax.axis_index("dip") % 2 == 0
    below, above = jnp.where(even, 8, 4), jnp.where(even, 4, 8)
    cells[x0:x1, 1:5, :] = block(0)
    cells[x0:x1, 0:1, :] = block(below)[:, 3:4]
    cells[x0:x1, 5:6, :] = block(above)[:, 0:1]


def read(ref, first, count):
    return ref[pl.ds(first, count)].astype(jnp.float32)


def upsample(cells, upmat, fine, q1s, sides):
    x_lo, x_hi, y_lo, y_hi = sides
    one = jnp.float32(1)
    count = len(q1s)
    rows = 8 * count
    wide = []
    edge = jnp.zeros((rows, 32), jnp.float32)
    for h1 in range(2):
        for h2 in range(2):
            window = jnp.concatenate(
                [cells[q1 + 1 - h1 : q1 + 2 - h1, 1 - h2 : 9 - h2, :] for q1 in q1s], axis=0
            )
            wide.append(jnp.concatenate([edge, window.reshape(rows, 128), edge], axis=1))
    left = jnp.concatenate(
        [
            jnp.concatenate([w[:, 32 * q3 : 32 * q3 + 64] for w in wide], axis=1)
            for q3 in range(5)
        ],
        axis=0,
    ).astype(jnp.bfloat16)

    lane = lax.broadcasted_iota(jnp.int32, (rows, 128), 1)
    q2 = lax.broadcasted_iota(jnp.int32, (rows, 128), 0) % 8
    outer = (lane < 32) | (lane >= 96)
    front = lane < 64
    low = jnp.where(q2 == 0, y_lo, one)
    high = jnp.where(q2 == 4, y_hi, one)
    none = jnp.zeros((rows, 128), jnp.float32)
    for p1 in range(4):
        phase = jnp.dot(left, upmat[:, p1 * 512 : p1 * 512 + 512], preferred_element_type=jnp.float32)
        for pp in range(2):
            tiles = [[], []]
            for side in range(2):
                p2 = 2 * pp + side
                v = phase[:, p2 * 128 : p2 * 128 + 128]
                for g in range(GROUPS):
                    at = g * rows
                    t = jnp.where(front, v[at : at + rows], v[at + rows : at + 2 * rows])
                    tiles[side].append(silu(t) * (low if pp == 0 else high))
            merged = [jnp.where(outer, tiles[0][g], tiles[1][g]) for g in range(GROUPS)]
            merged = [none] + merged + [none]
            for g in range(GROUPS):
                beside = jnp.where(front, merged[g + 2], merged[g])
                for n, t in enumerate((tiles[0][g], tiles[1][g], beside)):
                    for c, q1 in enumerate(q1s):
                        part = t[c * 8 : c * 8 + 5]
                        if q1 == 0 and p1 < 2:
                            part = part * x_lo
                        if q1 == 4 and p1 >= 2:
                            part = part * x_hi
                        at = (4 * c + p1) * STEP + g * PAIRS + pp
                        fine[n, pl.ds(at, 5, stride=2), :] = part


def windows_of(fine, first, count, target, at):
    for dj in range(2):
        for n in range(3):
            rows = fine[n, pl.ds(first * STEP + dj, count * STEP), :].astype(jnp.bfloat16)
            target[dj, at * STEP : (at + count) * STEP, n * 128 : n * 128 + 128] = rows


def tight(block, at):
    return jnp.concatenate([block[pl.ds(at + g * PAIRS, 8), :] for g in range(GROUPS)], axis=0)


def centre_of(fine, first, count, target, at):
    for n in range(count):
        here = slice((at + n) * TIGHT, (at + n + 1) * TIGHT)
        for o in range(2):
            rows = tight(fine.at[o], (first + n) * STEP + 1)
            target[here, o * 128 : o * 128 + 128] = rows.astype(jnp.bfloat16)


def inner_kernel(
    own, upmat, first_ref, second_ref, inner, centre, band1_ref, band2_ref, cells, fine
):
    arrange_bands(first_ref, second_ref, band1_ref, band2_ref)
    put(cells, 1, 5, lambda o: read(own, o, 4))
    upsample(cells, upmat, fine, (1, 2, 3), edges())
    windows_of(fine, 0, 12, inner, 0)
    centre_of(fine, 0, 12, centre, 0)


def product(source, strips, step, taps, base=None):
    results = []
    row = 0
    for at, n in strips:
        columns = [
            source[dj, (at + dx) * step : (at + dx + n) * step, :] for dx in range(3) for dj in range(2)
        ]
        if base is not None:
            columns.append(base[row : row + n * step, :])
        row += n * step
        results.append(
            jnp.dot(jnp.concatenate(columns, axis=1), taps[...], preferred_element_type=jnp.float32)
        )
    return jnp.concatenate(results, axis=0)


def main_kernel(
    own, strike_a, strike_b, inner, centre, upmat, band1, band2, out,
    cells, fine, hidden, b1, b2, ends, woven, near, sems,
):
    sides = x_lo, x_hi, y_lo, y_hi = edges()
    one, zero = jnp.float32(1), jnp.float32(0)

    v_inner = product(inner, ((0, 6), (6, 4)), STEP, band1)

    even = lax.axis_index("strike") % 2 == 0
    put(cells, 0, 1, lambda o: jnp.where(even, read(strike_b, o + 3, 1), read(strike_a, o + 3, 1)))
    put(cells, 1, 2, lambda o: read(own, o, 1))
    put(cells, 4, 5, lambda o: read(own, o + 3, 1))
    put(cells, 5, 6, lambda o: jnp.where(even, read(strike_a, o, 1), read(strike_b, o, 1)))
    upsample(cells, upmat, fine, (0, 4), sides)
    windows_of(fine, 0, 4, b1, 0)
    b1[:, 4 * STEP : 6 * STEP, :] = inner[:, : 2 * STEP, :]
    b1[:, 6 * STEP : 8 * STEP, :] = inner[:, 10 * STEP : 12 * STEP, :]
    windows_of(fine, 4, 4, b1, 8)
    centre_of(fine, 2, 2, ends, 0)
    ends[2 * TIGHT : 4 * TIGHT, :] = centre[0 : 2 * TIGHT, :]
    ends[4 * TIGHT : 6 * TIGHT, :] = centre[10 * TIGHT : 12 * TIGHT, :]
    centre_of(fine, 4, 2, ends, 6)

    v_outer = product(b1, ((0, 4), (6, 4)), STEP, band1)

    row = lax.broadcasted_iota(jnp.int32, (STEP, 128), 0)
    lane = lax.broadcasted_iota(jnp.int32, (STEP, 128), 1)
    starts = [g * PAIRS for g in range(GROUPS)]
    first, last = row == starts[0], row == starts[0] + 8
    for start in starts[1:]:
        first, last = first | (row == start), last | (row == start + 8)
    y_first, y_last = jnp.where(first, y_lo, one), jnp.where(last, y_hi, one)
    outer = (lane < 32) | (lane >= 96)
    row = lax.broadcasted_iota(jnp.int32, (TIGHT, 128), 0)
    lane = lax.broadcasted_iota(jnp.int32, (TIGHT, 128), 1)
    front = lane < 64
    inside_above = jnp.where(row < TIGHT - 8, one, zero)
    inside_below = jnp.where(row >= 8, one, zero)
    inside = jnp.where(front, inside_above, inside_below)

    def clear(at):
        hidden[2, at : at + 16, :] = jnp.zeros((16, 128), jnp.float32)

    def keep(v, at, count):
        v = silu(v)
        for n in range(count):
            x = at + n
            rows = slice(n * STEP, n * STEP + STEP)
            v0, v1 = v[rows, :128] * y_first, v[rows, 128:] * y_last
            if x in (0, 17):
                edge = x_lo if x == 0 else x_hi
                v0, v1 = v0 * edge, v1 * edge
            here = slice(16 + x * STEP, 16 + x * STEP + STEP)
            hidden[0, here, :] = v0
            hidden[1, here, :] = v1
            hidden[2, here, :] = jnp.where(outer, v0, v1)
        for x in range(at, at + count):
            here = slice(x * TIGHT, (x + 1) * TIGHT)
            for dj in range(2):
                start = 16 + x * STEP + dj
                for n in range(2):
                    rows = tight(hidden.at[n], start)
                    b2[dj, here, n * 128 : n * 128 + 128] = rows.astype(jnp.bfloat16)
                above = tight(hidden.at[2], start + PAIRS)
                below = tight(hidden.at[2], start - PAIRS)
                beside = jnp.where(front, above, below) * inside
                b2[dj, here, 256:384] = beside.astype(jnp.bfloat16)

    def finish(v, strips, chain):
        sends = []
        row = 0
        for k, (at, count) in enumerate(strips):
            for x in range(at, at + count):
                for g in range(GROUPS):
                    for o in range(2):
                        cells8 = v[row : row + 8, o * 128 : o * 128 + 128]
                        woven[g, pl.ds(x * 16 + o, 8, stride=2), :] = cells8
                    row += 8
            for g in range(GROUPS):
                near[at : at + count, :, g * 128 : g * 128 + 128] = (
                    woven[g, at * 16 : (at + count) * 16].reshape(count, 16, 128).astype(jnp.bfloat16)
                )
            here = pl.ds(at, count)
            sends.append(pltpu.make_async_copy(near.at[here], out.at[here], sems.at[chain + k]))
            sends[-1].start()
        return sends

    clear(4 * STEP)
    clear(16 + 14 * STEP)
    keep(v_inner, 4, 10)
    v_inner = product(b2, ((4, 4), (8, 4)), TIGHT, band2, centre[2 * TIGHT : 10 * TIGHT, :])

    clear(0)
    clear(16 + 18 * STEP)
    keep(v_outer[: 4 * STEP], 0, 4)
    keep(v_outer[4 * STEP :], 14, 4)
    v_outer = product(b2, ((0, 4), (12, 4)), TIGHT, band2, ends[...])

    sends = finish(v_inner, ((4, 8),), 0)
    sends += finish(v_outer, ((0, 4), (12, 4)), 1)
    for send in sends:
        send.wait()


def swapped(block, axis):
    size = lax.axis_size(axis)
    for first in (0, 1):
        pairs = [(i, i + 1) for i in range(first, size - 1, 2)]
        yield lax.ppermute(block, axis, pairs + [(j, i) for i, j in pairs])


def body(coarse, up_weight, first_weight, second_weight):
    vmem = pl.BlockSpec(memory_space=pltpu.VMEM)
    params = pltpu.CompilerParams(vmem_limit_bytes=32 * 1024 * 1024)

    bf16 = jnp.bfloat16
    shape = jax.ShapeDtypeStruct
    dip_a, dip_b = swapped(coarse, "dip")
    upmat, token = pl.pallas_call(
        up_kernel,
        out_shape=(shape((256, 2048), bf16), shape((8, 128), jnp.float32)),
        in_specs=[pl.BlockSpec(memory_space=pltpu.HBM)],
        out_specs=(vmem, vmem),
        scratch_shapes=[pltpu.VMEM((512 * 32, 32), bf16), pltpu.SemaphoreType.DMA((8,))],
        compiler_params=pltpu.CompilerParams(vmem_limit_bytes=LIMIT),
        cost_estimate=pl.CostEstimate(flops=5_000_000, bytes_accessed=5_000_000, transcendentals=0),
        name="arrange_up",
    )(up_weight.reshape(512 * 32, 32))
    own = pl.pallas_call(
        pack_kernel,
        out_shape=shape((12, 4, 128), bf16),
        in_specs=[vmem] * 4,
        out_specs=vmem,
        compiler_params=pltpu.CompilerParams(vmem_limit_bytes=1024 * 1024),
        name="pack",
    )(coarse, dip_a, dip_b, token)
    strike_a, strike_b = swapped(own, "strike")
    inner, centre, band1, band2 = pl.pallas_call(
        inner_kernel,
        out_shape=(
            shape((2, 12 * STEP, 384), bf16),
            shape((12 * TIGHT, 256), bf16),
            shape((WINDOW, 256), bf16),
            shape((WINDOW + 256, 256), bf16),
        ),
        in_specs=[vmem] * 4,
        out_specs=(vmem,) * 4,
        scratch_shapes=[
            pltpu.VMEM((6, 16, 128), jnp.float32),
            pltpu.VMEM((3, 12 * STEP + 8, 128), jnp.float32),
        ],
        compiler_params=pltpu.CompilerParams(vmem_limit_bytes=16 * 1024 * 1024),
        cost_estimate=pl.CostEstimate(
            flops=300_000_000, bytes_accessed=3_000_000, transcendentals=200_000
        ),
        name="upsample_inner",
    )(own, upmat, first_weight.reshape(864, 32), second_weight.reshape(864, 32))
    return pl.pallas_call(
        main_kernel,
        out_shape=jax.ShapeDtypeStruct((16, 16, 512), bf16),
        in_specs=[vmem] * 8,
        out_specs=pl.BlockSpec(memory_space=pltpu.HBM),
        scratch_shapes=[
            pltpu.VMEM((6, 16, 128), jnp.float32),
            pltpu.VMEM((3, 8 * STEP + 8, 128), jnp.float32),
            pltpu.VMEM((3, 18 * STEP + 32, 128), jnp.float32),
            pltpu.VMEM((2, 12 * STEP, 384), bf16),
            pltpu.VMEM((2, 18 * TIGHT, 384), bf16),
            pltpu.VMEM((8 * TIGHT, 256), bf16),
            pltpu.VMEM((GROUPS, 256, 128), jnp.float32),
            pltpu.VMEM((16, 16, 512), bf16),
            pltpu.SemaphoreType.DMA((3,)),
        ],
        compiler_params=params,
        cost_estimate=pl.CostEstimate(
            flops=2_000_000_000, bytes_accessed=8_000_000, transcendentals=800_000
        ),
        name="upsample_refine",
    )(own, strike_a, strike_b, inner, centre, upmat, band1, band2)


def solution(mesh):
    return jax.shard_map(
        body,
        mesh=mesh,
        in_specs=(P("strike", "dip", None), P(), P(), P()),
        out_specs=P("strike", "dip", None),
        check_vma=False,
    )
```

```python
import jax
import jax.numpy as jnp
from jax import lax
from jax.experimental import pallas as pl
from jax.experimental.pallas import tpu as pltpu
from jax.sharding import PartitionSpec as P

GROUPS = 4
PAIRS = 10
STEP = GROUPS * PAIRS
ORDER = ((0, 1, 2, 3), (1, 0, 3, 2))
BESIDE = ((0, 4), (1, 4), (1, -1), (0, -1))
WINDOW = 3 * 2 * 384
TIGHT = GROUPS * 8
PIECES = (16, 16, 8, 8, 4, 4, 1, 1)
LIMIT = 50 * 1024 * 1024


def silu(v):
    half = 0.5 * v
    return half + half * jnp.tanh(half)


def up_kernel(up_hbm, upmat_ref, token_ref, up_ref, sems):
    slab = 64 * 32
    fetches = []
    for k1, pieces in enumerate(PIECES):
        rows = pl.ds(k1 * slab, slab)
        fetches.append(pltpu.make_async_copy(up_hbm.at[rows], up_ref.at[rows], sems.at[k1]))
        size = slab // pieces
        for piece in range(pieces):
            rows = pl.ds(k1 * slab + piece * size, size)
            pltpu.make_async_copy(up_hbm.at[rows], up_ref.at[rows], sems.at[k1]).start()
    token_ref[...] = jnp.zeros((8, 128), jnp.float32)

    for k1 in range(8):
        fetches[k1].wait()
        h1, p1 = divmod(k1, 4)
        for k2 in range(8):
            h2, p2 = divmod(k2, 4)
            for h3 in range(2):
                k = (k1 * 8 + k2) * 8 + 4 * h3
                parts = [up_ref[pl.ds((k + (z + 2) % 4) * 32, 32), :] for z in ORDER[p2 % 2]]
                row = (h1 * 4 + h2 * 2 + (1 - h3)) * 32
                upmat_ref[pl.ds(row, 32), pl.ds((p1 * 4 + p2) * 128, 128)] = jnp.concatenate(
                    parts, axis=1
                )


def arrange_bands(first_ref, second_ref, band1_ref, band2_ref):
    ci = lax.broadcasted_iota(jnp.int32, (32, 128), 0)
    lane = lax.broadcasted_iota(jnp.int32, (32, 128), 1)
    group = lane // 32
    copies = (lane % 32 == ci).astype(jnp.bfloat16)

    def arrange(w_ref, band_ref, out_order):
        rep = jnp.dot(w_ref[...], copies, preferred_element_type=jnp.float32)
        for d1 in range(3):
            for dj in range(2):
                cells = [(0, z) for z in ORDER[0]] + [(1, z) for z in ORDER[1]] + list(BESIDE)
                for n, (side, z_in) in enumerate(cells):
                    row = (d1 * 2 + dj) * 384 + n * 32
                    for o in range(2):
                        block = jnp.zeros((32, 128), jnp.float32)
                        d2 = 2 * dj + side - o
                        for d3 in range(3):
                            z_out = z_in - d3 + 1
                            if 0 <= d2 < 3 and 0 <= z_out < 4:
                                tap = ((d1 * 3 + d2) * 3 + d3) * 32
                                here = group == out_order[o].index(z_out)
                                block = jnp.where(here, rep[tap : tap + 32], block)
                        band_ref[pl.ds(row, 32), pl.ds(o * 128, 128)] = block.astype(jnp.bfloat16)

    arrange(first_ref, band1_ref, ORDER)
    arrange(second_ref, band2_ref, (ORDER[0], ORDER[0]))
    r = lax.broadcasted_iota(jnp.int32, (256, 256), 0)
    c = lax.broadcasted_iota(jnp.int32, (256, 256), 1)
    swap = jnp.where((r // 32) % 2 == 0, r + 32, r - 32)
    band2_ref[pl.ds(WINDOW, 256), :] = (jnp.where(r < 128, r, swap) == c).astype(jnp.bfloat16)


def pack_kernel(coarse, dip_a, dip_b, token, own):
    own[0:4] = coarse[...]
    own[4:8] = dip_a[...]
    own[8:12] = dip_b[...]


def edges():
    one, zero = jnp.float32(1), jnp.float32(0)
    strike, dip = lax.axis_index("strike"), lax.axis_index("dip")
    x_lo = jnp.where(strike == 0, zero, one)
    x_hi = jnp.where(strike == lax.axis_size("strike") - 1, zero, one)
    y_lo = jnp.where(dip == 0, zero, one)
    y_hi = jnp.where(dip == lax.axis_size("dip") - 1, zero, one)
    return x_lo, x_hi, y_lo, y_hi


def put(cells, x0, x1, block):
    even = lax.axis_index("dip") % 2 == 0
    below, above = jnp.where(even, 8, 4), jnp.where(even, 4, 8)
    cells[x0:x1, 1:5, :] = block(0)
    cells[x0:x1, 0:1, :] = block(below)[:, 3:4]
    cells[x0:x1, 5:6, :] = block(above)[:, 0:1]


def read(ref, first, count):
    return ref[pl.ds(first, count)].astype(jnp.float32)


def upsample(cells, upmat, fine, q1s, sides):
    x_lo, x_hi, y_lo, y_hi = sides
    one = jnp.float32(1)
    count = len(q1s)
    rows = 8 * count
    wide = []
    edge = jnp.zeros((rows, 32), jnp.float32)
    for h1 in range(2):
        for h2 in range(2):
            window = jnp.concatenate(
                [cells[q1 + 1 - h1 : q1 + 2 - h1, 1 - h2 : 9 - h2, :] for q1 in q1s], axis=0
            )
            wide.append(jnp.concatenate([edge, window.reshape(rows, 128), edge], axis=1))
    left = jnp.concatenate(
        [
            jnp.concatenate([w[:, 32 * q3 : 32 * q3 + 64] for w in wide], axis=1)
            for q3 in range(5)
        ],
        axis=0,
    ).astype(jnp.bfloat16)

    lane = lax.broadcasted_iota(jnp.int32, (rows, 128), 1)
    q2 = lax.broadcasted_iota(jnp.int32, (rows, 128), 0) % 8
    outer = (lane < 32) | (lane >= 96)
    front = lane < 64
    low = jnp.where(q2 == 0, y_lo, one)
    high = jnp.where(q2 == 4, y_hi, one)
    none = jnp.zeros((rows, 128), jnp.float32)
    for p1 in range(4):
        phase = jnp.dot(left, upmat[:, p1 * 512 : p1 * 512 + 512], preferred_element_type=jnp.float32)
        for pp in range(2):
            tiles = [[], []]
            for side in range(2):
                p2 = 2 * pp + side
                v = phase[:, p2 * 128 : p2 * 128 + 128]
                for g in range(GROUPS):
                    at = g * rows
                    t = jnp.where(front, v[at : at + rows], v[at + rows : at + 2 * rows])
                    tiles[side].append(silu(t) * (low if pp == 0 else high))
            merged = [jnp.where(outer, tiles[0][g], tiles[1][g]) for g in range(GROUPS)]
            merged = [none] + merged + [none]
            for g in range(GROUPS):
                beside = jnp.where(front, merged[g + 2], merged[g])
                for n, t in enumerate((tiles[0][g], tiles[1][g], beside)):
                    for c, q1 in enumerate(q1s):
                        part = t[c * 8 : c * 8 + 5]
                        if q1 == 0 and p1 < 2:
                            part = part * x_lo
                        if q1 == 4 and p1 >= 2:
                            part = part * x_hi
                        at = (4 * c + p1) * STEP + g * PAIRS + pp
                        fine[n, pl.ds(at, 5, stride=2), :] = part


def windows_of(fine, first, count, target, at):
    for dj in range(2):
        for n in range(3):
            rows = fine[n, pl.ds(first * STEP + dj, count * STEP), :].astype(jnp.bfloat16)
            target[dj, at * STEP : (at + count) * STEP, n * 128 : n * 128 + 128] = rows


def tight(block, at):
    return jnp.concatenate([block[pl.ds(at + g * PAIRS, 8), :] for g in range(GROUPS)], axis=0)


def centre_of(fine, first, count, target, at):
    for n in range(count):
        here = slice((at + n) * TIGHT, (at + n + 1) * TIGHT)
        for o in range(2):
            rows = tight(fine.at[o], (first + n) * STEP + 1)
            target[here, o * 128 : o * 128 + 128] = rows.astype(jnp.bfloat16)


def inner_kernel(
    own, upmat, first_ref, second_ref, inner, centre, band1_ref, band2_ref, cells, fine
):
    arrange_bands(first_ref, second_ref, band1_ref, band2_ref)
    put(cells, 1, 5, lambda o: read(own, o, 4))
    upsample(cells, upmat, fine, (1, 2, 3), edges())
    windows_of(fine, 0, 12, inner, 0)
    centre_of(fine, 0, 12, centre, 0)


def product(source, strips, step, taps, base=None):
    results = []
    row = 0
    for at, n in strips:
        columns = [
            source[dj, (at + dx) * step : (at + dx + n) * step, :] for dx in range(3) for dj in range(2)
        ]
        if base is not None:
            columns.append(base[row : row + n * step, :])
        row += n * step
        results.append(
            jnp.dot(jnp.concatenate(columns, axis=1), taps[...], preferred_element_type=jnp.float32)
        )
    return jnp.concatenate(results, axis=0)


def main_kernel(
    own, strike_a, strike_b, inner, centre, upmat, band1, band2, out,
    cells, fine, hidden, b1, b2, ends, woven, near, sems,
):
    sides = x_lo, x_hi, y_lo, y_hi = edges()
    one, zero = jnp.float32(1), jnp.float32(0)

    v_inner = product(inner, ((0, 6), (6, 4)), STEP, band1)

    even = lax.axis_index("strike") % 2 == 0
    put(cells, 0, 1, lambda o: jnp.where(even, read(strike_b, o + 3, 1), read(strike_a, o + 3, 1)))
    put(cells, 1, 2, lambda o: read(own, o, 1))
    put(cells, 4, 5, lambda o: read(own, o + 3, 1))
    put(cells, 5, 6, lambda o: jnp.where(even, read(strike_a, o, 1), read(strike_b, o, 1)))
    upsample(cells, upmat, fine, (0, 4), sides)
    windows_of(fine, 0, 4, b1, 0)
    b1[:, 4 * STEP : 6 * STEP, :] = inner[:, : 2 * STEP, :]
    b1[:, 6 * STEP : 8 * STEP, :] = inner[:, 10 * STEP : 12 * STEP, :]
    windows_of(fine, 4, 4, b1, 8)
    centre_of(fine, 2, 2, ends, 0)
    ends[2 * TIGHT : 4 * TIGHT, :] = centre[0 : 2 * TIGHT, :]
    ends[4 * TIGHT : 6 * TIGHT, :] = centre[10 * TIGHT : 12 * TIGHT, :]
    centre_of(fine, 4, 2, ends, 6)

    v_outer = product(b1, ((0, 4), (6, 4)), STEP, band1)

    row = lax.broadcasted_iota(jnp.int32, (STEP, 128), 0)
    lane = lax.broadcasted_iota(jnp.int32, (STEP, 128), 1)
    starts = [g * PAIRS for g in range(GROUPS)]
    first, last = row == starts[0], row == starts[0] + 8
    for start in starts[1:]:
        first, last = first | (row == start), last | (row == start + 8)
    y_first, y_last = jnp.where(first, y_lo, one), jnp.where(last, y_hi, one)
    outer = (lane < 32) | (lane >= 96)
    row = lax.broadcasted_iota(jnp.int32, (TIGHT, 128), 0)
    lane = lax.broadcasted_iota(jnp.int32, (TIGHT, 128), 1)
    front = lane < 64
    inside_above = jnp.where(row < TIGHT - 8, one, zero)
    inside_below = jnp.where(row >= 8, one, zero)
    inside = jnp.where(front, inside_above, inside_below)

    def clear(at):
        hidden[2, at : at + 16, :] = jnp.zeros((16, 128), jnp.float32)

    def keep(v, at, count):
        v = silu(v)
        for n in range(count):
            x = at + n
            rows = slice(n * STEP, n * STEP + STEP)
            v0, v1 = v[rows, :128] * y_first, v[rows, 128:] * y_last
            if x in (0, 17):
                edge = x_lo if x == 0 else x_hi
                v0, v1 = v0 * edge, v1 * edge
            here = slice(16 + x * STEP, 16 + x * STEP + STEP)
            hidden[0, here, :] = v0
            hidden[1, here, :] = v1
            hidden[2, here, :] = jnp.where(outer, v0, v1)
        for x in range(at, at + count):
            here = slice(x * TIGHT, (x + 1) * TIGHT)
            for dj in range(2):
                start = 16 + x * STEP + dj
                for n in range(2):
                    rows = tight(hidden.at[n], start)
                    b2[dj, here, n * 128 : n * 128 + 128] = rows.astype(jnp.bfloat16)
                above = tight(hidden.at[2], start + PAIRS)
                below = tight(hidden.at[2], start - PAIRS)
                beside = jnp.where(front, above, below) * inside
                b2[dj, here, 256:384] = beside.astype(jnp.bfloat16)

    def finish(v, strips, chain):
        sends = []
        row = 0
        for k, (at, count) in enumerate(strips):
            for x in range(at, at + count):
                for g in range(GROUPS):
                    for o in range(2):
                        cells8 = v[row : row + 8, o * 128 : o * 128 + 128]
                        woven[g, pl.ds(x * 16 + o, 8, stride=2), :] = cells8
                    row += 8
            for g in range(GROUPS):
                near[at : at + count, :, g * 128 : g * 128 + 128] = (
                    woven[g, at * 16 : (at + count) * 16].reshape(count, 16, 128).astype(jnp.bfloat16)
                )
            here = pl.ds(at, count)
            sends.append(pltpu.make_async_copy(near.at[here], out.at[here], sems.at[chain + k]))
            sends[-1].start()
        return sends

    clear(4 * STEP)
    clear(16 + 14 * STEP)
    keep(v_inner, 4, 10)
    v_inner = product(b2, ((4, 4), (8, 4)), TIGHT, band2, centre[2 * TIGHT : 10 * TIGHT, :])

    clear(0)
    clear(16 + 18 * STEP)
    keep(v_outer[: 4 * STEP], 0, 4)
    keep(v_outer[4 * STEP :], 14, 4)
    v_outer = product(b2, ((0, 4), (12, 4)), TIGHT, band2, ends[...])

    sends = finish(v_inner, ((4, 8),), 0)
    sends += finish(v_outer, ((0, 4), (12, 4)), 1)
    for send in sends:
        send.wait()


def swapped(block, axis):
    size = lax.axis_size(axis)
    for first in (0, 1):
        pairs = [(i, i + 1) for i in range(first, size - 1, 2)]
        yield lax.ppermute(block, axis, pairs + [(j, i) for i, j in pairs])


def body(coarse, up_weight, first_weight, second_weight):
    vmem = pl.BlockSpec(memory_space=pltpu.VMEM)
    params = pltpu.CompilerParams(vmem_limit_bytes=32 * 1024 * 1024)

    bf16 = jnp.bfloat16
    shape = jax.ShapeDtypeStruct
    dip_a, dip_b = swapped(coarse, "dip")
    upmat, token = pl.pallas_call(
        up_kernel,
        out_shape=(shape((256, 2048), bf16), shape((8, 128), jnp.float32)),
        in_specs=[pl.BlockSpec(memory_space=pltpu.HBM)],
        out_specs=(vmem, vmem),
        scratch_shapes=[pltpu.VMEM((512 * 32, 32), bf16), pltpu.SemaphoreType.DMA((8,))],
        compiler_params=pltpu.CompilerParams(vmem_limit_bytes=LIMIT),
        cost_estimate=pl.CostEstimate(flops=5_000_000, bytes_accessed=5_000_000, transcendentals=0),
        name="arrange_up",
    )(up_weight.reshape(512 * 32, 32))
    own = pl.pallas_call(
        pack_kernel,
        out_shape=shape((12, 4, 128), bf16),
        in_specs=[vmem] * 4,
        out_specs=vmem,
        compiler_params=pltpu.CompilerParams(vmem_limit_bytes=1024 * 1024),
        name="pack",
    )(coarse, dip_a, dip_b, token)
    strike_a, strike_b = swapped(own, "strike")
    inner, centre, band1, band2 = pl.pallas_call(
        inner_kernel,
        out_shape=(
            shape((2, 12 * STEP, 384), bf16),
            shape((12 * TIGHT, 256), bf16),
            shape((WINDOW, 256), bf16),
            shape((WINDOW + 256, 256), bf16),
        ),
        in_specs=[vmem] * 4,
        out_specs=(vmem,) * 4,
        scratch_shapes=[
            pltpu.VMEM((6, 16, 128), jnp.float32),
            pltpu.VMEM((3, 12 * STEP + 8, 128), jnp.float32),
        ],
        compiler_params=pltpu.CompilerParams(vmem_limit_bytes=16 * 1024 * 1024),
        cost_estimate=pl.CostEstimate(
            flops=300_000_000, bytes_accessed=3_000_000, transcendentals=200_000
        ),
        name="upsample_inner",
    )(own, upmat, first_weight.reshape(864, 32), second_weight.reshape(864, 32))
    return pl.pallas_call(
        main_kernel,
        out_shape=jax.ShapeDtypeStruct((16, 16, 512), bf16),
        in_specs=[vmem] * 8,
        out_specs=pl.BlockSpec(memory_space=pltpu.HBM),
        scratch_shapes=[
            pltpu.VMEM((6, 16, 128), jnp.float32),
            pltpu.VMEM((3, 8 * STEP + 8, 128), jnp.float32),
            pltpu.VMEM((3, 18 * STEP + 32, 128), jnp.float32),
            pltpu.VMEM((2, 12 * STEP, 384), bf16),
            pltpu.VMEM((2, 18 * TIGHT, 384), bf16),
            pltpu.VMEM((8 * TIGHT, 256), bf16),
            pltpu.VMEM((GROUPS, 256, 128), jnp.float32),
            pltpu.VMEM((16, 16, 512), bf16),
            pltpu.SemaphoreType.DMA((3,)),
        ],
        compiler_params=params,
        cost_estimate=pl.CostEstimate(
            flops=2_000_000_000, bytes_accessed=8_000_000, transcendentals=800_000
        ),
        name="upsample_refine",
    )(own, strike_a, strike_b, inner, centre, upmat, band1, band2)


def solution(mesh):
    return jax.shard_map(
        body,
        mesh=mesh,
        in_specs=(P("strike", "dip", None), P(), P(), P()),
        out_specs=P("strike", "dip", None),
        check_vma=False,
    )
```

```python
import jax
import jax.numpy as jnp
from jax import lax
from jax.experimental import pallas as pl
from jax.experimental.pallas import tpu as pltpu
from jax.sharding import PartitionSpec as P

GROUPS = 4
PAIRS = 10
STEP = GROUPS * PAIRS
ORDER = ((0, 1, 2, 3), (1, 0, 3, 2))
BESIDE = ((0, 4), (1, 4), (1, -1), (0, -1))
WINDOW = 3 * 2 * 384
TIGHT = GROUPS * 8
AHEAD = 8
LIMIT = 50 * 1024 * 1024


def silu(v):
    half = 0.5 * v
    return half + half * jnp.tanh(half)


def up_kernel(up_hbm, upmat_ref, token_ref, up_ref, sems):
    fetches = []
    for k1 in range(8):
        rows = pl.ds(k1 * 2048, 2048)
        fetches.append(pltpu.make_async_copy(up_hbm.at[rows], up_ref.at[rows], sems.at[k1]))
    for fetch in fetches[:AHEAD]:
        fetch.start()
    token_ref[...] = jnp.zeros((8, 128), jnp.float32)

    for k1 in range(8):
        fetches[k1].wait()
        if k1 + AHEAD < 8:
            fetches[k1 + AHEAD].start()
        h1, p1 = divmod(k1, 4)
        for k2 in range(8):
            h2, p2 = divmod(k2, 4)
            for h3 in range(2):
                k = (k1 * 8 + k2) * 8 + 4 * h3
                parts = [up_ref[pl.ds((k + (z + 2) % 4) * 32, 32), :] for z in ORDER[p2 % 2]]
                row = (h1 * 4 + h2 * 2 + (1 - h3)) * 32
                upmat_ref[pl.ds(row, 32), pl.ds((p1 * 4 + p2) * 128, 128)] = jnp.concatenate(
                    parts, axis=1
                )


def arrange_bands(first_ref, second_ref, band1_ref, band2_ref):
    ci = lax.broadcasted_iota(jnp.int32, (32, 128), 0)
    lane = lax.broadcasted_iota(jnp.int32, (32, 128), 1)
    group = lane // 32
    copies = (lane % 32 == ci).astype(jnp.bfloat16)

    masks = [(group == n).astype(jnp.float32).astype(jnp.bfloat16) for n in range(4)]

    def arrange(w_ref, band_ref, out_order):
        rep = jnp.dot(w_ref[...], copies, preferred_element_type=jnp.float32).astype(jnp.bfloat16)
        placed = {}

        def place(tap, n):
            if (tap, n) not in placed:
                placed[tap, n] = rep[tap * 32 : tap * 32 + 32] * masks[n]
            return placed[tap, n]

        blocks = {}
        for d1 in range(3):
            for dj in range(2):
                cells = [(0, z) for z in ORDER[0]] + [(1, z) for z in ORDER[1]] + list(BESIDE)
                for n, (side, z_in) in enumerate(cells):
                    row = (d1 * 2 + dj) * 384 + n * 32
                    for o in range(2):
                        d2 = 2 * dj + side - o
                        parts = []
                        for d3 in range(3):
                            z_out = z_in - d3 + 1
                            if 0 <= d2 < 3 and 0 <= z_out < 4:
                                parts.append(((d1 * 3 + d2) * 3 + d3, out_order[o].index(z_out)))
                        key = tuple(parts)
                        if key not in blocks:
                            block = jnp.zeros((32, 128), jnp.bfloat16)
                            for k, part in enumerate(parts):
                                block = place(*part) if k == 0 else block + place(*part)
                            blocks[key] = block
                        band_ref[pl.ds(row, 32), pl.ds(o * 128, 128)] = blocks[key]

    arrange(first_ref, band1_ref, ORDER)
    arrange(second_ref, band2_ref, (ORDER[0], ORDER[0]))
    r = lax.broadcasted_iota(jnp.int32, (256, 256), 0)
    c = lax.broadcasted_iota(jnp.int32, (256, 256), 1)
    swap = jnp.where((r // 32) % 2 == 0, r + 32, r - 32)
    band2_ref[pl.ds(WINDOW, 256), :] = (jnp.where(r < 128, r, swap) == c).astype(jnp.bfloat16)


def pack_kernel(coarse, dip_a, dip_b, token, own):
    own[0:4] = coarse[...]
    own[4:8] = dip_a[...]
    own[8:12] = dip_b[...]


def edges():
    one, zero = jnp.float32(1), jnp.float32(0)
    strike, dip = lax.axis_index("strike"), lax.axis_index("dip")
    x_lo = jnp.where(strike == 0, zero, one)
    x_hi = jnp.where(strike == lax.axis_size("strike") - 1, zero, one)
    y_lo = jnp.where(dip == 0, zero, one)
    y_hi = jnp.where(dip == lax.axis_size("dip") - 1, zero, one)
    return x_lo, x_hi, y_lo, y_hi


def put(cells, x0, x1, block):
    even = lax.axis_index("dip") % 2 == 0
    below, above = jnp.where(even, 8, 4), jnp.where(even, 4, 8)
    cells[x0:x1, 1:5, :] = block(0)
    cells[x0:x1, 0:1, :] = block(below)[:, 3:4]
    cells[x0:x1, 5:6, :] = block(above)[:, 0:1]


def read(ref, first, count):
    return ref[pl.ds(first, count)].astype(jnp.float32)


def upsample(cells, upmat, fine, q1s, sides):
    x_lo, x_hi, y_lo, y_hi = sides
    one = jnp.float32(1)
    count = len(q1s)
    rows = 8 * count
    wide = []
    edge = jnp.zeros((rows, 32), jnp.float32)
    for h1 in range(2):
        for h2 in range(2):
            window = jnp.concatenate(
                [cells[q1 + 1 - h1 : q1 + 2 - h1, 1 - h2 : 9 - h2, :] for q1 in q1s], axis=0
            )
            wide.append(jnp.concatenate([edge, window.reshape(rows, 128), edge], axis=1))
    left = jnp.concatenate(
        [
            jnp.concatenate([w[:, 32 * q3 : 32 * q3 + 64] for w in wide], axis=1)
            for q3 in range(5)
        ],
        axis=0,
    ).astype(jnp.bfloat16)

    lane = lax.broadcasted_iota(jnp.int32, (rows, 128), 1)
    q2 = lax.broadcasted_iota(jnp.int32, (rows, 128), 0) % 8
    outer = (lane < 32) | (lane >= 96)
    front = lane < 64
    low = jnp.where(q2 == 0, y_lo, one)
    high = jnp.where(q2 == 4, y_hi, one)
    none = jnp.zeros((rows, 128), jnp.float32)
    for p1 in range(4):
        phase = jnp.dot(left, upmat[:, p1 * 512 : p1 * 512 + 512], preferred_element_type=jnp.float32)
        for pp in range(2):
            tiles = [[], []]
            for side in range(2):
                p2 = 2 * pp + side
                v = phase[:, p2 * 128 : p2 * 128 + 128]
                for g in range(GROUPS):
                    at = g * rows
                    t = jnp.where(front, v[at : at + rows], v[at + rows : at + 2 * rows])
                    tiles[side].append(silu(t) * (low if pp == 0 else high))
            merged = [jnp.where(outer, tiles[0][g], tiles[1][g]) for g in range(GROUPS)]
            merged = [none] + merged + [none]
            for g in range(GROUPS):
                beside = jnp.where(front, merged[g + 2], merged[g])
                for n, t in enumerate((tiles[0][g], tiles[1][g], beside)):
                    for c, q1 in enumerate(q1s):
                        part = t[c * 8 : c * 8 + 5]
                        if q1 == 0 and p1 < 2:
                            part = part * x_lo
                        if q1 == 4 and p1 >= 2:
                            part = part * x_hi
                        at = (4 * c + p1) * STEP + g * PAIRS + pp
                        fine[n, pl.ds(at, 5, stride=2), :] = part


def windows_of(fine, first, count, target, at):
    for dj in range(2):
        for n in range(3):
            rows = fine[n, pl.ds(first * STEP + dj, count * STEP), :].astype(jnp.bfloat16)
            target[dj, at * STEP : (at + count) * STEP, n * 128 : n * 128 + 128] = rows


def tight(block, at):
    return jnp.concatenate([block[pl.ds(at + g * PAIRS, 8), :] for g in range(GROUPS)], axis=0)


def centre_of(fine, first, count, target, at):
    for n in range(count):
        here = slice((at + n) * TIGHT, (at + n + 1) * TIGHT)
        for o in range(2):
            rows = tight(fine.at[o], (first + n) * STEP + 1)
            target[here, o * 128 : o * 128 + 128] = rows.astype(jnp.bfloat16)


def inner_kernel(
    own, upmat, first_ref, second_ref, inner, centre, band1_ref, band2_ref, cells, fine
):
    arrange_bands(first_ref, second_ref, band1_ref, band2_ref)
    put(cells, 1, 5, lambda o: read(own, o, 4))
    upsample(cells, upmat, fine, (1, 2, 3), edges())
    windows_of(fine, 0, 12, inner, 0)
    centre_of(fine, 0, 12, centre, 0)


def product(source, strips, step, taps, base=None):
    results = []
    row = 0
    for at, n in strips:
        columns = [
            source[dj, (at + dx) * step : (at + dx + n) * step, :] for dx in range(3) for dj in range(2)
        ]
        if base is not None:
            columns.append(base[row : row + n * step, :])
        row += n * step
        results.append(
            jnp.dot(jnp.concatenate(columns, axis=1), taps[...], preferred_element_type=jnp.float32)
        )
    return jnp.concatenate(results, axis=0)


def main_kernel(
    own, strike_a, strike_b, inner, centre, upmat, band1, band2, out,
    cells, fine, hidden, b1, b2, ends, woven, near, sems,
):
    sides = x_lo, x_hi, y_lo, y_hi = edges()
    one, zero = jnp.float32(1), jnp.float32(0)

    v_inner = product(inner, ((0, 6), (6, 4)), STEP, band1)

    even = lax.axis_index("strike") % 2 == 0
    put(cells, 0, 1, lambda o: jnp.where(even, read(strike_b, o + 3, 1), read(strike_a, o + 3, 1)))
    put(cells, 1, 2, lambda o: read(own, o, 1))
    put(cells, 4, 5, lambda o: read(own, o + 3, 1))
    put(cells, 5, 6, lambda o: jnp.where(even, read(strike_a, o, 1), read(strike_b, o, 1)))
    upsample(cells, upmat, fine, (0, 4), sides)
    windows_of(fine, 0, 4, b1, 0)
    b1[:, 4 * STEP : 6 * STEP, :] = inner[:, : 2 * STEP, :]
    b1[:, 6 * STEP : 8 * STEP, :] = inner[:, 10 * STEP : 12 * STEP, :]
    windows_of(fine, 4, 4, b1, 8)
    centre_of(fine, 2, 2, ends, 0)
    ends[2 * TIGHT : 4 * TIGHT, :] = centre[0 : 2 * TIGHT, :]
    ends[4 * TIGHT : 6 * TIGHT, :] = centre[10 * TIGHT : 12 * TIGHT, :]
    centre_of(fine, 4, 2, ends, 6)

    v_outer = product(b1, ((0, 4), (6, 4)), STEP, band1)

    row = lax.broadcasted_iota(jnp.int32, (STEP, 128), 0)
    lane = lax.broadcasted_iota(jnp.int32, (STEP, 128), 1)
    starts = [g * PAIRS for g in range(GROUPS)]
    first, last = row == starts[0], row == starts[0] + 8
    for start in starts[1:]:
        first, last = first | (row == start), last | (row == start + 8)
    y_first, y_last = jnp.where(first, y_lo, one), jnp.where(last, y_hi, one)
    outer = (lane < 32) | (lane >= 96)
    row = lax.broadcasted_iota(jnp.int32, (TIGHT, 128), 0)
    lane = lax.broadcasted_iota(jnp.int32, (TIGHT, 128), 1)
    front = lane < 64
    inside_above = jnp.where(row < TIGHT - 8, one, zero)
    inside_below = jnp.where(row >= 8, one, zero)
    inside = jnp.where(front, inside_above, inside_below)

    def clear(at):
        hidden[2, at : at + 16, :] = jnp.zeros((16, 128), jnp.float32)

    def keep(v, at, count):
        v = silu(v)
        for n in range(count):
            x = at + n
            rows = slice(n * STEP, n * STEP + STEP)
            v0, v1 = v[rows, :128] * y_first, v[rows, 128:] * y_last
            if x in (0, 17):
                edge = x_lo if x == 0 else x_hi
                v0, v1 = v0 * edge, v1 * edge
            here = slice(16 + x * STEP, 16 + x * STEP + STEP)
            hidden[0, here, :] = v0
            hidden[1, here, :] = v1
            hidden[2, here, :] = jnp.where(outer, v0, v1)
        for x in range(at, at + count):
            here = slice(x * TIGHT, (x + 1) * TIGHT)
            for dj in range(2):
                start = 16 + x * STEP + dj
                for n in range(2):
                    rows = tight(hidden.at[n], start)
                    b2[dj, here, n * 128 : n * 128 + 128] = rows.astype(jnp.bfloat16)
                above = tight(hidden.at[2], start + PAIRS)
                below = tight(hidden.at[2], start - PAIRS)
                beside = jnp.where(front, above, below) * inside
                b2[dj, here, 256:384] = beside.astype(jnp.bfloat16)

    def finish(v, strips, chain):
        sends = []
        row = 0
        for k, (at, count) in enumerate(strips):
            for x in range(at, at + count):
                for g in range(GROUPS):
                    for o in range(2):
                        cells8 = v[row : row + 8, o * 128 : o * 128 + 128]
                        woven[g, pl.ds(x * 16 + o, 8, stride=2), :] = cells8
                    row += 8
            for g in range(GROUPS):
                near[at : at + count, :, g * 128 : g * 128 + 128] = (
                    woven[g, at * 16 : (at + count) * 16].reshape(count, 16, 128).astype(jnp.bfloat16)
                )
            here = pl.ds(at, count)
            sends.append(pltpu.make_async_copy(near.at[here], out.at[here], sems.at[chain + k]))
            sends[-1].start()
        return sends

    clear(4 * STEP)
    clear(16 + 14 * STEP)
    keep(v_inner, 4, 10)
    v_inner = product(b2, ((4, 4), (8, 4)), TIGHT, band2, centre[2 * TIGHT : 10 * TIGHT, :])

    clear(0)
    clear(16 + 18 * STEP)
    keep(v_outer[: 4 * STEP], 0, 4)
    keep(v_outer[4 * STEP :], 14, 4)
    v_outer = product(b2, ((0, 4), (12, 4)), TIGHT, band2, ends[...])

    sends = finish(v_inner, ((4, 8),), 0)
    sends += finish(v_outer, ((0, 4), (12, 4)), 1)
    for send in sends:
        send.wait()


def swapped(block, axis):
    size = lax.axis_size(axis)
    for first in (0, 1):
        pairs = [(i, i + 1) for i in range(first, size - 1, 2)]
        yield lax.ppermute(block, axis, pairs + [(j, i) for i, j in pairs])


def body(coarse, up_weight, first_weight, second_weight):
    vmem = pl.BlockSpec(memory_space=pltpu.VMEM)
    params = pltpu.CompilerParams(vmem_limit_bytes=32 * 1024 * 1024)

    bf16 = jnp.bfloat16
    shape = jax.ShapeDtypeStruct
    dip_a, dip_b = swapped(coarse, "dip")
    upmat, token = pl.pallas_call(
        up_kernel,
        out_shape=(shape((256, 2048), bf16), shape((8, 128), jnp.float32)),
        in_specs=[pl.BlockSpec(memory_space=pltpu.HBM)],
        out_specs=(vmem, vmem),
        scratch_shapes=[pltpu.VMEM((512 * 32, 32), bf16), pltpu.SemaphoreType.DMA((8,))],
        compiler_params=pltpu.CompilerParams(vmem_limit_bytes=LIMIT),
        cost_estimate=pl.CostEstimate(flops=5_000_000, bytes_accessed=5_000_000, transcendentals=0),
        name="arrange_up",
    )(up_weight.reshape(512 * 32, 32))
    own = pl.pallas_call(
        pack_kernel,
        out_shape=shape((12, 4, 128), bf16),
        in_specs=[vmem] * 4,
        out_specs=vmem,
        compiler_params=pltpu.CompilerParams(vmem_limit_bytes=1024 * 1024),
        name="pack",
    )(coarse, dip_a, dip_b, token)
    strike_a, strike_b = swapped(own, "strike")
    inner, centre, band1, band2 = pl.pallas_call(
        inner_kernel,
        out_shape=(
            shape((2, 12 * STEP, 384), bf16),
            shape((12 * TIGHT, 256), bf16),
            shape((WINDOW, 256), bf16),
            shape((WINDOW + 256, 256), bf16),
        ),
        in_specs=[vmem] * 4,
        out_specs=(vmem,) * 4,
        scratch_shapes=[
            pltpu.VMEM((6, 16, 128), jnp.float32),
            pltpu.VMEM((3, 12 * STEP + 8, 128), jnp.float32),
        ],
        compiler_params=pltpu.CompilerParams(vmem_limit_bytes=16 * 1024 * 1024),
        cost_estimate=pl.CostEstimate(
            flops=300_000_000, bytes_accessed=3_000_000, transcendentals=200_000
        ),
        name="upsample_inner",
    )(own, upmat, first_weight.reshape(864, 32), second_weight.reshape(864, 32))
    return pl.pallas_call(
        main_kernel,
        out_shape=jax.ShapeDtypeStruct((16, 16, 512), bf16),
        in_specs=[vmem] * 8,
        out_specs=pl.BlockSpec(memory_space=pltpu.HBM),
        scratch_shapes=[
            pltpu.VMEM((6, 16, 128), jnp.float32),
            pltpu.VMEM((3, 8 * STEP + 8, 128), jnp.float32),
            pltpu.VMEM((3, 18 * STEP + 32, 128), jnp.float32),
            pltpu.VMEM((2, 12 * STEP, 384), bf16),
            pltpu.VMEM((2, 18 * TIGHT, 384), bf16),
            pltpu.VMEM((8 * TIGHT, 256), bf16),
            pltpu.VMEM((GROUPS, 256, 128), jnp.float32),
            pltpu.VMEM((16, 16, 512), bf16),
            pltpu.SemaphoreType.DMA((3,)),
        ],
        compiler_params=params,
        cost_estimate=pl.CostEstimate(
            flops=2_000_000_000, bytes_accessed=8_000_000, transcendentals=800_000
        ),
        name="upsample_refine",
    )(own, strike_a, strike_b, inner, centre, upmat, band1, band2)


def solution(mesh):
    return jax.shard_map(
        body,
        mesh=mesh,
        in_specs=(P("strike", "dip", None), P(), P(), P()),
        out_specs=P("strike", "dip", None),
        check_vma=False,
    )
```

```python
import jax
import jax.numpy as jnp
from jax import lax
from jax.experimental import pallas as pl
from jax.experimental.pallas import tpu as pltpu
from jax.sharding import PartitionSpec as P

GROUPS = 4
PAIRS = 10
STEP = GROUPS * PAIRS
ORDER = ((0, 1, 2, 3), (1, 0, 3, 2))
BESIDE = ((0, 4), (1, 4), (1, -1), (0, -1))
WINDOW = 3 * 2 * 384
TIGHT = GROUPS * 8
AHEAD = 8
LIMIT = 50 * 1024 * 1024


def silu(v):
    half = 0.5 * v
    return half + half * jnp.tanh(half)


def up_kernel(up_hbm, upmat_ref, token_ref, up_ref, sems):
    fetches = []
    for k1 in range(8):
        rows = pl.ds(k1 * 2048, 2048)
        fetches.append(pltpu.make_async_copy(up_hbm.at[rows], up_ref.at[rows], sems.at[k1]))
    for fetch in fetches[:AHEAD]:
        fetch.start()
    token_ref[...] = jnp.zeros((8, 128), jnp.float32)

    for k1 in range(8):
        fetches[k1].wait()
        if k1 + AHEAD < 8:
            fetches[k1 + AHEAD].start()
        h1, p1 = divmod(k1, 4)
        for k2 in range(8):
            h2, p2 = divmod(k2, 4)
            for h3 in range(2):
                k = (k1 * 8 + k2) * 8 + 4 * h3
                parts = [up_ref[pl.ds((k + (z + 2) % 4) * 32, 32), :] for z in ORDER[p2 % 2]]
                row = (h1 * 4 + h2 * 2 + (1 - h3)) * 32
                upmat_ref[pl.ds(row, 32), pl.ds((p1 * 4 + p2) * 128, 128)] = jnp.concatenate(
                    parts, axis=1
                )


def arrange_bands(first_ref, second_ref, band1_ref, band2_ref):
    ci = lax.broadcasted_iota(jnp.int32, (32, 128), 0)
    lane = lax.broadcasted_iota(jnp.int32, (32, 128), 1)
    group = lane // 32
    copies = (lane % 32 == ci).astype(jnp.bfloat16)

    masks = [(group == n).astype(jnp.float32).astype(jnp.bfloat16) for n in range(4)]

    def arrange(w_ref, band_ref, out_order):
        rep = jnp.dot(w_ref[...], copies, preferred_element_type=jnp.float32).astype(jnp.bfloat16)
        placed = {}

        def place(tap, n):
            if (tap, n) not in placed:
                placed[tap, n] = rep[tap * 32 : tap * 32 + 32] * masks[n]
            return placed[tap, n]

        blocks = {}
        for d1 in range(3):
            for dj in range(2):
                cells = [(0, z) for z in ORDER[0]] + [(1, z) for z in ORDER[1]] + list(BESIDE)
                for n, (side, z_in) in enumerate(cells):
                    row = (d1 * 2 + dj) * 384 + n * 32
                    for o in range(2):
                        d2 = 2 * dj + side - o
                        parts = []
                        for d3 in range(3):
                            z_out = z_in - d3 + 1
                            if 0 <= d2 < 3 and 0 <= z_out < 4:
                                parts.append(((d1 * 3 + d2) * 3 + d3, out_order[o].index(z_out)))
                        key = tuple(parts)
                        if key not in blocks:
                            block = jnp.zeros((32, 128), jnp.bfloat16)
                            for k, part in enumerate(parts):
                                block = place(*part) if k == 0 else block + place(*part)
                            blocks[key] = block
                        band_ref[pl.ds(row, 32), pl.ds(o * 128, 128)] = blocks[key]

    arrange(first_ref, band1_ref, ORDER)
    arrange(second_ref, band2_ref, (ORDER[0], ORDER[0]))
    r = lax.broadcasted_iota(jnp.int32, (256, 256), 0)
    c = lax.broadcasted_iota(jnp.int32, (256, 256), 1)
    swap = jnp.where((r // 32) % 2 == 0, r + 32, r - 32)
    band2_ref[pl.ds(WINDOW, 256), :] = (jnp.where(r < 128, r, swap) == c).astype(jnp.bfloat16)


def pack_kernel(coarse, dip_a, dip_b, token, own):
    own[0:4] = coarse[...]
    own[4:8] = dip_a[...]
    own[8:12] = dip_b[...]


def edges():
    one, zero = jnp.float32(1), jnp.float32(0)
    strike, dip = lax.axis_index("strike"), lax.axis_index("dip")
    x_lo = jnp.where(strike == 0, zero, one)
    x_hi = jnp.where(strike == lax.axis_size("strike") - 1, zero, one)
    y_lo = jnp.where(dip == 0, zero, one)
    y_hi = jnp.where(dip == lax.axis_size("dip") - 1, zero, one)
    return x_lo, x_hi, y_lo, y_hi


def put(cells, x0, x1, block):
    even = lax.axis_index("dip") % 2 == 0
    below, above = jnp.where(even, 8, 4), jnp.where(even, 4, 8)
    cells[x0:x1, 1:5, :] = block(0)
    cells[x0:x1, 0:1, :] = block(below)[:, 3:4]
    cells[x0:x1, 5:6, :] = block(above)[:, 0:1]


def read(ref, first, count):
    return ref[pl.ds(first, count)].astype(jnp.float32)


def upsample(cells, upmat, fine, q1s, sides, beside_it=None):
    x_lo, x_hi, y_lo, y_hi = sides
    one = jnp.float32(1)
    count = len(q1s)
    rows = 8 * count
    wide = []
    edge = jnp.zeros((rows, 32), jnp.float32)
    for h1 in range(2):
        for h2 in range(2):
            window = jnp.concatenate(
                [cells[q1 + 1 - h1 : q1 + 2 - h1, 1 - h2 : 9 - h2, :] for q1 in q1s], axis=0
            )
            wide.append(jnp.concatenate([edge, window.reshape(rows, 128), edge], axis=1))
    left = jnp.concatenate(
        [
            jnp.concatenate([w[:, 32 * q3 : 32 * q3 + 64] for w in wide], axis=1)
            for q3 in range(5)
        ],
        axis=0,
    ).astype(jnp.bfloat16)

    phases = [
        jnp.dot(left, upmat[:, p1 * 512 : p1 * 512 + 512], preferred_element_type=jnp.float32)
        for p1 in range(4)
    ]
    other = beside_it() if beside_it else None

    lane = lax.broadcasted_iota(jnp.int32, (rows, 128), 1)
    q2 = lax.broadcasted_iota(jnp.int32, (rows, 128), 0) % 8
    outer = (lane < 32) | (lane >= 96)
    front = lane < 64
    low = jnp.where(q2 == 0, y_lo, one)
    high = jnp.where(q2 == 4, y_hi, one)
    none = jnp.zeros((rows, 128), jnp.float32)
    for p1 in range(4):
        phase = phases[p1]
        for pp in range(2):
            tiles = [[], []]
            for side in range(2):
                p2 = 2 * pp + side
                v = phase[:, p2 * 128 : p2 * 128 + 128]
                for g in range(GROUPS):
                    at = g * rows
                    t = jnp.where(front, v[at : at + rows], v[at + rows : at + 2 * rows])
                    tiles[side].append(silu(t) * (low if pp == 0 else high))
            merged = [jnp.where(outer, tiles[0][g], tiles[1][g]) for g in range(GROUPS)]
            merged = [none] + merged + [none]
            for g in range(GROUPS):
                beside = jnp.where(front, merged[g + 2], merged[g])
                for n, t in enumerate((tiles[0][g], tiles[1][g], beside)):
                    for c, q1 in enumerate(q1s):
                        part = t[c * 8 : c * 8 + 5]
                        if q1 == 0 and p1 < 2:
                            part = part * x_lo
                        if q1 == 4 and p1 >= 2:
                            part = part * x_hi
                        at = (4 * c + p1) * STEP + g * PAIRS + pp
                        fine[n, pl.ds(at, 5, stride=2), :] = part
    return other


def windows_of(fine, first, count, target, at):
    for dj in range(2):
        for n in range(3):
            rows = fine[n, pl.ds(first * STEP + dj, count * STEP), :].astype(jnp.bfloat16)
            target[dj, at * STEP : (at + count) * STEP, n * 128 : n * 128 + 128] = rows


def tight(block, at):
    return jnp.concatenate([block[pl.ds(at + g * PAIRS, 8), :] for g in range(GROUPS)], axis=0)


def centre_of(fine, first, count, target, at):
    for n in range(count):
        here = slice((at + n) * TIGHT, (at + n + 1) * TIGHT)
        for o in range(2):
            rows = tight(fine.at[o], (first + n) * STEP + 1)
            target[here, o * 128 : o * 128 + 128] = rows.astype(jnp.bfloat16)


def inner_kernel(
    own, upmat, first_ref, second_ref, inner, centre, band1_ref, band2_ref, cells, fine
):
    arrange_bands(first_ref, second_ref, band1_ref, band2_ref)
    put(cells, 1, 5, lambda o: read(own, o, 4))
    upsample(cells, upmat, fine, (1, 2, 3), edges())
    windows_of(fine, 0, 12, inner, 0)
    centre_of(fine, 0, 12, centre, 0)


def product(source, strips, step, taps, base=None):
    results = []
    row = 0
    for at, n in strips:
        columns = [
            source[dj, (at + dx) * step : (at + dx + n) * step, :] for dx in range(3) for dj in range(2)
        ]
        if base is not None:
            columns.append(base[row : row + n * step, :])
        row += n * step
        results.append(
            jnp.dot(jnp.concatenate(columns, axis=1), taps[...], preferred_element_type=jnp.float32)
        )
    return jnp.concatenate(results, axis=0)


def main_kernel(
    own, strike_a, strike_b, inner, centre, upmat, band1, band2, out,
    cells, fine, hidden, b1, b2, ends, woven, near, sems,
):
    sides = x_lo, x_hi, y_lo, y_hi = edges()
    one, zero = jnp.float32(1), jnp.float32(0)

    even = lax.axis_index("strike") % 2 == 0
    put(cells, 0, 1, lambda o: jnp.where(even, read(strike_b, o + 3, 1), read(strike_a, o + 3, 1)))
    put(cells, 1, 2, lambda o: read(own, o, 1))
    put(cells, 4, 5, lambda o: read(own, o + 3, 1))
    put(cells, 5, 6, lambda o: jnp.where(even, read(strike_a, o, 1), read(strike_b, o, 1)))
    v_inner = upsample(
        cells, upmat, fine, (0, 4), sides, lambda: product(inner, ((0, 6), (6, 4)), STEP, band1)
    )
    windows_of(fine, 0, 4, b1, 0)
    b1[:, 4 * STEP : 6 * STEP, :] = inner[:, : 2 * STEP, :]
    b1[:, 6 * STEP : 8 * STEP, :] = inner[:, 10 * STEP : 12 * STEP, :]
    windows_of(fine, 4, 4, b1, 8)
    centre_of(fine, 2, 2, ends, 0)
    ends[2 * TIGHT : 4 * TIGHT, :] = centre[0 : 2 * TIGHT, :]
    ends[4 * TIGHT : 6 * TIGHT, :] = centre[10 * TIGHT : 12 * TIGHT, :]
    centre_of(fine, 4, 2, ends, 6)

    v_outer = product(b1, ((0, 4), (6, 4)), STEP, band1)

    row = lax.broadcasted_iota(jnp.int32, (STEP, 128), 0)
    lane = lax.broadcasted_iota(jnp.int32, (STEP, 128), 1)
    starts = [g * PAIRS for g in range(GROUPS)]
    first, last = row == starts[0], row == starts[0] + 8
    for start in starts[1:]:
        first, last = first | (row == start), last | (row == start + 8)
    y_first, y_last = jnp.where(first, y_lo, one), jnp.where(last, y_hi, one)
    outer = (lane < 32) | (lane >= 96)
    row = lax.broadcasted_iota(jnp.int32, (TIGHT, 128), 0)
    lane = lax.broadcasted_iota(jnp.int32, (TIGHT, 128), 1)
    front = lane < 64
    inside_above = jnp.where(row < TIGHT - 8, one, zero)
    inside_below = jnp.where(row >= 8, one, zero)
    inside = jnp.where(front, inside_above, inside_below)

    def clear(at):
        hidden[2, at : at + 16, :] = jnp.zeros((16, 128), jnp.float32)

    def keep(v, at, count):
        v = silu(v)
        for n in range(count):
            x = at + n
            rows = slice(n * STEP, n * STEP + STEP)
            v0, v1 = v[rows, :128] * y_first, v[rows, 128:] * y_last
            if x in (0, 17):
                edge = x_lo if x == 0 else x_hi
                v0, v1 = v0 * edge, v1 * edge
            here = slice(16 + x * STEP, 16 + x * STEP + STEP)
            hidden[0, here, :] = v0
            hidden[1, here, :] = v1
            hidden[2, here, :] = jnp.where(outer, v0, v1)
        for x in range(at, at + count):
            here = slice(x * TIGHT, (x + 1) * TIGHT)
            for dj in range(2):
                start = 16 + x * STEP + dj
                for n in range(2):
                    rows = tight(hidden.at[n], start)
                    b2[dj, here, n * 128 : n * 128 + 128] = rows.astype(jnp.bfloat16)
                above = tight(hidden.at[2], start + PAIRS)
                below = tight(hidden.at[2], start - PAIRS)
                beside = jnp.where(front, above, below) * inside
                b2[dj, here, 256:384] = beside.astype(jnp.bfloat16)

    def finish(v, strips, chain):
        sends = []
        row = 0
        for k, (at, count) in enumerate(strips):
            for x in range(at, at + count):
                for g in range(GROUPS):
                    for o in range(2):
                        cells8 = v[row : row + 8, o * 128 : o * 128 + 128]
                        woven[g, pl.ds(x * 16 + o, 8, stride=2), :] = cells8
                    row += 8
            for g in range(GROUPS):
                near[at : at + count, :, g * 128 : g * 128 + 128] = (
                    woven[g, at * 16 : (at + count) * 16].reshape(count, 16, 128).astype(jnp.bfloat16)
                )
            here = pl.ds(at, count)
            sends.append(pltpu.make_async_copy(near.at[here], out.at[here], sems.at[chain + k]))
            sends[-1].start()
        return sends

    clear(4 * STEP)
    clear(16 + 14 * STEP)
    keep(v_inner, 4, 10)
    v_inner = product(b2, ((4, 4), (8, 4)), TIGHT, band2, centre[2 * TIGHT : 10 * TIGHT, :])

    clear(0)
    clear(16 + 18 * STEP)
    keep(v_outer[: 4 * STEP], 0, 4)
    keep(v_outer[4 * STEP :], 14, 4)
    v_outer = product(b2, ((0, 4), (12, 4)), TIGHT, band2, ends[...])

    sends = finish(v_inner, ((4, 8),), 0)
    sends += finish(v_outer, ((0, 4), (12, 4)), 1)
    for send in sends:
        send.wait()


def swapped(block, axis):
    size = lax.axis_size(axis)
    for first in (0, 1):
        pairs = [(i, i + 1) for i in range(first, size - 1, 2)]
        yield lax.ppermute(block, axis, pairs + [(j, i) for i, j in pairs])


def body(coarse, up_weight, first_weight, second_weight):
    vmem = pl.BlockSpec(memory_space=pltpu.VMEM)
    params = pltpu.CompilerParams(vmem_limit_bytes=32 * 1024 * 1024)

    bf16 = jnp.bfloat16
    shape = jax.ShapeDtypeStruct
    dip_a, dip_b = swapped(coarse, "dip")
    upmat, token = pl.pallas_call(
        up_kernel,
        out_shape=(shape((256, 2048), bf16), shape((8, 128), jnp.float32)),
        in_specs=[pl.BlockSpec(memory_space=pltpu.HBM)],
        out_specs=(vmem, vmem),
        scratch_shapes=[pltpu.VMEM((512 * 32, 32), bf16), pltpu.SemaphoreType.DMA((8,))],
        compiler_params=pltpu.CompilerParams(vmem_limit_bytes=LIMIT),
        cost_estimate=pl.CostEstimate(flops=5_000_000, bytes_accessed=5_000_000, transcendentals=0),
        name="arrange_up",
    )(up_weight.reshape(512 * 32, 32))
    own = pl.pallas_call(
        pack_kernel,
        out_shape=shape((12, 4, 128), bf16),
        in_specs=[vmem] * 4,
        out_specs=vmem,
        compiler_params=pltpu.CompilerParams(vmem_limit_bytes=1024 * 1024),
        name="pack",
    )(coarse, dip_a, dip_b, token)
    strike_a, strike_b = swapped(own, "strike")
    inner, centre, band1, band2 = pl.pallas_call(
        inner_kernel,
        out_shape=(
            shape((2, 12 * STEP, 384), bf16),
            shape((12 * TIGHT, 256), bf16),
            shape((WINDOW, 256), bf16),
            shape((WINDOW + 256, 256), bf16),
        ),
        in_specs=[vmem] * 4,
        out_specs=(vmem,) * 4,
        scratch_shapes=[
            pltpu.VMEM((6, 16, 128), jnp.float32),
            pltpu.VMEM((3, 12 * STEP + 8, 128), jnp.float32),
        ],
        compiler_params=pltpu.CompilerParams(vmem_limit_bytes=16 * 1024 * 1024),
        cost_estimate=pl.CostEstimate(
            flops=300_000_000, bytes_accessed=3_000_000, transcendentals=200_000
        ),
        name="upsample_inner",
    )(own, upmat, first_weight.reshape(864, 32), second_weight.reshape(864, 32))
    return pl.pallas_call(
        main_kernel,
        out_shape=jax.ShapeDtypeStruct((16, 16, 512), bf16),
        in_specs=[vmem] * 8,
        out_specs=pl.BlockSpec(memory_space=pltpu.HBM),
        scratch_shapes=[
            pltpu.VMEM((6, 16, 128), jnp.float32),
            pltpu.VMEM((3, 8 * STEP + 8, 128), jnp.float32),
            pltpu.VMEM((3, 18 * STEP + 32, 128), jnp.float32),
            pltpu.VMEM((2, 12 * STEP, 384), bf16),
            pltpu.VMEM((2, 18 * TIGHT, 384), bf16),
            pltpu.VMEM((8 * TIGHT, 256), bf16),
            pltpu.VMEM((GROUPS, 256, 128), jnp.float32),
            pltpu.VMEM((16, 16, 512), bf16),
            pltpu.SemaphoreType.DMA((3,)),
        ],
        compiler_params=params,
        cost_estimate=pl.CostEstimate(
            flops=2_000_000_000, bytes_accessed=8_000_000, transcendentals=800_000
        ),
        name="upsample_refine",
    )(own, strike_a, strike_b, inner, centre, upmat, band1, band2)


def solution(mesh):
    return jax.shard_map(
        body,
        mesh=mesh,
        in_specs=(P("strike", "dip", None), P(), P(), P()),
        out_specs=P("strike", "dip", None),
        check_vma=False,
    )
```

```python
import jax
import jax.numpy as jnp
from jax import lax
from jax.experimental import pallas as pl
from jax.experimental.pallas import tpu as pltpu
from jax.sharding import PartitionSpec as P

GROUPS = 4
PAIRS = 10
STEP = GROUPS * PAIRS
ORDER = ((0, 1, 2, 3), (1, 0, 3, 2))
BESIDE = ((0, 4), (1, 4), (1, -1), (0, -1))
WINDOW = 3 * 2 * 384
TIGHT = GROUPS * 8
AHEAD = 8
LIMIT = 50 * 1024 * 1024


def silu(v):
    half = 0.5 * v
    return half + half * jnp.tanh(half)


def up_kernel(up_hbm, upmat_ref, up_ref, sems):
    fetches = []
    for k1 in range(8):
        rows = pl.ds(k1 * 2048, 2048)
        fetches.append(pltpu.make_async_copy(up_hbm.at[rows], up_ref.at[rows], sems.at[k1]))
    for fetch in fetches[:AHEAD]:
        fetch.start()

    for k1 in range(8):
        fetches[k1].wait()
        if k1 + AHEAD < 8:
            fetches[k1 + AHEAD].start()
        h1, p1 = divmod(k1, 4)
        for k2 in range(8):
            h2, p2 = divmod(k2, 4)
            for h3 in range(2):
                k = (k1 * 8 + k2) * 8 + 4 * h3
                parts = [up_ref[pl.ds((k + (z + 2) % 4) * 32, 32), :] for z in ORDER[p2 % 2]]
                row = (h1 * 4 + h2 * 2 + (1 - h3)) * 32
                upmat_ref[pl.ds(row, 32), pl.ds((p1 * 4 + p2) * 128, 128)] = jnp.concatenate(
                    parts, axis=1
                )


def arrange_bands(first_ref, second_ref, band1_ref, band2_ref):
    ci = lax.broadcasted_iota(jnp.int32, (32, 128), 0)
    lane = lax.broadcasted_iota(jnp.int32, (32, 128), 1)
    group = lane // 32
    copies = (lane % 32 == ci).astype(jnp.bfloat16)

    masks = [(group == n).astype(jnp.float32).astype(jnp.bfloat16) for n in range(4)]

    def arrange(w_ref, band_ref, out_order):
        rep = jnp.dot(w_ref[...], copies, preferred_element_type=jnp.float32).astype(jnp.bfloat16)
        placed = {}

        def place(tap, n):
            if (tap, n) not in placed:
                placed[tap, n] = rep[tap * 32 : tap * 32 + 32] * masks[n]
            return placed[tap, n]

        blocks = {}
        for d1 in range(3):
            for dj in range(2):
                cells = [(0, z) for z in ORDER[0]] + [(1, z) for z in ORDER[1]] + list(BESIDE)
                for n, (side, z_in) in enumerate(cells):
                    row = (d1 * 2 + dj) * 384 + n * 32
                    for o in range(2):
                        d2 = 2 * dj + side - o
                        parts = []
                        for d3 in range(3):
                            z_out = z_in - d3 + 1
                            if 0 <= d2 < 3 and 0 <= z_out < 4:
                                parts.append(((d1 * 3 + d2) * 3 + d3, out_order[o].index(z_out)))
                        key = tuple(parts)
                        if key not in blocks:
                            block = jnp.zeros((32, 128), jnp.bfloat16)
                            for k, part in enumerate(parts):
                                block = place(*part) if k == 0 else block + place(*part)
                            blocks[key] = block
                        band_ref[pl.ds(row, 32), pl.ds(o * 128, 128)] = blocks[key]

    arrange(first_ref, band1_ref, ORDER)
    arrange(second_ref, band2_ref, (ORDER[0], ORDER[0]))
    r = lax.broadcasted_iota(jnp.int32, (256, 256), 0)
    c = lax.broadcasted_iota(jnp.int32, (256, 256), 1)
    swap = jnp.where((r // 32) % 2 == 0, r + 32, r - 32)
    band2_ref[pl.ds(WINDOW, 256), :] = (jnp.where(r < 128, r, swap) == c).astype(jnp.bfloat16)


def edges():
    one, zero = jnp.float32(1), jnp.float32(0)
    strike, dip = lax.axis_index("strike"), lax.axis_index("dip")
    x_lo = jnp.where(strike == 0, zero, one)
    x_hi = jnp.where(strike == lax.axis_size("strike") - 1, zero, one)
    y_lo = jnp.where(dip == 0, zero, one)
    y_hi = jnp.where(dip == lax.axis_size("dip") - 1, zero, one)
    return x_lo, x_hi, y_lo, y_hi


def put(cells, x0, x1, block):
    even = lax.axis_index("dip") % 2 == 0
    below, above = jnp.where(even, 8, 4), jnp.where(even, 4, 8)
    cells[x0:x1, 1:5, :] = block(0)
    cells[x0:x1, 0:1, :] = block(below)[:, 3:4]
    cells[x0:x1, 5:6, :] = block(above)[:, 0:1]


def read(ref, first, count):
    return ref[pl.ds(first, count)].astype(jnp.float32)


def upsample(cells, upmat, fine, q1s, sides):
    x_lo, x_hi, y_lo, y_hi = sides
    one = jnp.float32(1)
    count = len(q1s)
    rows = 8 * count
    wide = []
    edge = jnp.zeros((rows, 32), jnp.float32)
    for h1 in range(2):
        for h2 in range(2):
            window = jnp.concatenate(
                [cells[q1 + 1 - h1 : q1 + 2 - h1, 1 - h2 : 9 - h2, :] for q1 in q1s], axis=0
            )
            wide.append(jnp.concatenate([edge, window.reshape(rows, 128), edge], axis=1))
    left = jnp.concatenate(
        [
            jnp.concatenate([w[:, 32 * q3 : 32 * q3 + 64] for w in wide], axis=1)
            for q3 in range(5)
        ],
        axis=0,
    ).astype(jnp.bfloat16)

    lane = lax.broadcasted_iota(jnp.int32, (rows, 128), 1)
    q2 = lax.broadcasted_iota(jnp.int32, (rows, 128), 0) % 8
    outer = (lane < 32) | (lane >= 96)
    front = lane < 64
    low = jnp.where(q2 == 0, y_lo, one)
    high = jnp.where(q2 == 4, y_hi, one)
    none = jnp.zeros((rows, 128), jnp.float32)
    for p1 in range(4):
        phase = jnp.dot(left, upmat[:, p1 * 512 : p1 * 512 + 512], preferred_element_type=jnp.float32)
        for pp in range(2):
            tiles = [[], []]
            for side in range(2):
                p2 = 2 * pp + side
                v = phase[:, p2 * 128 : p2 * 128 + 128]
                for g in range(GROUPS):
                    at = g * rows
                    t = jnp.where(front, v[at : at + rows], v[at + rows : at + 2 * rows])
                    tiles[side].append(silu(t) * (low if pp == 0 else high))
            merged = [jnp.where(outer, tiles[0][g], tiles[1][g]) for g in range(GROUPS)]
            merged = [none] + merged + [none]
            for g in range(GROUPS):
                beside = jnp.where(front, merged[g + 2], merged[g])
                for n, t in enumerate((tiles[0][g], tiles[1][g], beside)):
                    for c, q1 in enumerate(q1s):
                        part = t[c * 8 : c * 8 + 5]
                        if q1 == 0 and p1 < 2:
                            part = part * x_lo
                        if q1 == 4 and p1 >= 2:
                            part = part * x_hi
                        at = (4 * c + p1) * STEP + g * PAIRS + pp
                        fine[n, pl.ds(at, 5, stride=2), :] = part


def windows_of(fine, first, count, target, at):
    for dj in range(2):
        for n in range(3):
            rows = fine[n, pl.ds(first * STEP + dj, count * STEP), :].astype(jnp.bfloat16)
            target[dj, at * STEP : (at + count) * STEP, n * 128 : n * 128 + 128] = rows


def tight(block, at):
    return jnp.concatenate([block[pl.ds(at + g * PAIRS, 8), :] for g in range(GROUPS)], axis=0)


def centre_of(fine, first, count, target, at):
    for n in range(count):
        here = slice((at + n) * TIGHT, (at + n + 1) * TIGHT)
        for o in range(2):
            rows = tight(fine.at[o], (first + n) * STEP + 1)
            target[here, o * 128 : o * 128 + 128] = rows.astype(jnp.bfloat16)


def inner_work(own, upmat, first_ref, second_ref, inner, centre, band1_ref, band2_ref, cells, fine):
    arrange_bands(first_ref, second_ref, band1_ref, band2_ref)
    put(cells, 1, 5, lambda o: read(own, o, 4))
    upsample(cells, upmat, fine, (1, 2, 3), edges())
    windows_of(fine, 0, 12, inner, 0)
    centre_of(fine, 0, 12, centre, 0)


def pack_kernel(
    coarse, dip_a, dip_b, upmat, first_ref, second_ref,
    own, inner, centre, band1_ref, band2_ref, cells, fine,
):
    own[0:4] = coarse[...]
    own[4:8] = dip_a[...]
    own[8:12] = dip_b[...]

    @pl.when(lax.axis_index("strike") == 0)
    def _():
        inner_work(own, upmat, first_ref, second_ref, inner, centre, band1_ref, band2_ref, cells, fine)


def inner_kernel(
    own, upmat, first_ref, second_ref, _inner, _centre, _band1, _band2,
    inner, centre, band1_ref, band2_ref, cells, fine,
):
    @pl.when(lax.axis_index("strike") != 0)
    def _():
        inner_work(own, upmat, first_ref, second_ref, inner, centre, band1_ref, band2_ref, cells, fine)


def product(source, strips, step, taps, base=None):
    results = []
    row = 0
    for at, n in strips:
        columns = [
            source[dj, (at + dx) * step : (at + dx + n) * step, :] for dx in range(3) for dj in range(2)
        ]
        if base is not None:
            columns.append(base[row : row + n * step, :])
        row += n * step
        results.append(
            jnp.dot(jnp.concatenate(columns, axis=1), taps[...], preferred_element_type=jnp.float32)
        )
    return jnp.concatenate(results, axis=0)


def main_kernel(
    own, strike_a, strike_b, inner, centre, upmat, band1, band2, out,
    cells, fine, hidden, b1, b2, ends, woven, near, sems,
):
    sides = x_lo, x_hi, y_lo, y_hi = edges()
    one, zero = jnp.float32(1), jnp.float32(0)

    v_inner = product(inner, ((0, 6), (6, 4)), STEP, band1)

    even = lax.axis_index("strike") % 2 == 0
    put(cells, 0, 1, lambda o: jnp.where(even, read(strike_b, o + 3, 1), read(strike_a, o + 3, 1)))
    put(cells, 1, 2, lambda o: read(own, o, 1))
    put(cells, 4, 5, lambda o: read(own, o + 3, 1))
    put(cells, 5, 6, lambda o: jnp.where(even, read(strike_a, o, 1), read(strike_b, o, 1)))
    upsample(cells, upmat, fine, (0, 4), sides)
    windows_of(fine, 0, 4, b1, 0)
    b1[:, 4 * STEP : 6 * STEP, :] = inner[:, : 2 * STEP, :]
    b1[:, 6 * STEP : 8 * STEP, :] = inner[:, 10 * STEP : 12 * STEP, :]
    windows_of(fine, 4, 4, b1, 8)
    centre_of(fine, 2, 2, ends, 0)
    ends[2 * TIGHT : 4 * TIGHT, :] = centre[0 : 2 * TIGHT, :]
    ends[4 * TIGHT : 6 * TIGHT, :] = centre[10 * TIGHT : 12 * TIGHT, :]
    centre_of(fine, 4, 2, ends, 6)

    v_outer = product(b1, ((0, 4), (6, 4)), STEP, band1)

    row = lax.broadcasted_iota(jnp.int32, (STEP, 128), 0)
    lane = lax.broadcasted_iota(jnp.int32, (STEP, 128), 1)
    starts = [g * PAIRS for g in range(GROUPS)]
    first, last = row == starts[0], row == starts[0] + 8
    for start in starts[1:]:
        first, last = first | (row == start), last | (row == start + 8)
    y_first, y_last = jnp.where(first, y_lo, one), jnp.where(last, y_hi, one)
    outer = (lane < 32) | (lane >= 96)
    row = lax.broadcasted_iota(jnp.int32, (TIGHT, 128), 0)
    lane = lax.broadcasted_iota(jnp.int32, (TIGHT, 128), 1)
    front = lane < 64
    inside_above = jnp.where(row < TIGHT - 8, one, zero)
    inside_below = jnp.where(row >= 8, one, zero)
    inside = jnp.where(front, inside_above, inside_below)

    def clear(at):
        hidden[2, at : at + 16, :] = jnp.zeros((16, 128), jnp.float32)

    def keep(v, at, count):
        v = silu(v)
        for n in range(count):
            x = at + n
            rows = slice(n * STEP, n * STEP + STEP)
            v0, v1 = v[rows, :128] * y_first, v[rows, 128:] * y_last
            if x in (0, 17):
                edge = x_lo if x == 0 else x_hi
                v0, v1 = v0 * edge, v1 * edge
            here = slice(16 + x * STEP, 16 + x * STEP + STEP)
            hidden[0, here, :] = v0
            hidden[1, here, :] = v1
            hidden[2, here, :] = jnp.where(outer, v0, v1)
        for x in range(at, at + count):
            here = slice(x * TIGHT, (x + 1) * TIGHT)
            for dj in range(2):
                start = 16 + x * STEP + dj
                for n in range(2):
                    rows = tight(hidden.at[n], start)
                    b2[dj, here, n * 128 : n * 128 + 128] = rows.astype(jnp.bfloat16)
                above = tight(hidden.at[2], start + PAIRS)
                below = tight(hidden.at[2], start - PAIRS)
                beside = jnp.where(front, above, below) * inside
                b2[dj, here, 256:384] = beside.astype(jnp.bfloat16)

    def finish(v, strips, chain):
        sends = []
        row = 0
        for k, (at, count) in enumerate(strips):
            for x in range(at, at + count):
                for g in range(GROUPS):
                    for o in range(2):
                        cells8 = v[row : row + 8, o * 128 : o * 128 + 128]
                        woven[g, pl.ds(x * 16 + o, 8, stride=2), :] = cells8
                    row += 8
            for g in range(GROUPS):
                near[at : at + count, :, g * 128 : g * 128 + 128] = (
                    woven[g, at * 16 : (at + count) * 16].reshape(count, 16, 128).astype(jnp.bfloat16)
                )
            here = pl.ds(at, count)
            sends.append(pltpu.make_async_copy(near.at[here], out.at[here], sems.at[chain + k]))
            sends[-1].start()
        return sends

    clear(4 * STEP)
    clear(16 + 14 * STEP)
    keep(v_inner, 4, 10)
    v_inner = product(b2, ((4, 4), (8, 4)), TIGHT, band2, centre[2 * TIGHT : 10 * TIGHT, :])

    clear(0)
    clear(16 + 18 * STEP)
    keep(v_outer[: 4 * STEP], 0, 4)
    keep(v_outer[4 * STEP :], 14, 4)
    v_outer = product(b2, ((0, 4), (12, 4)), TIGHT, band2, ends[...])

    sends = finish(v_inner, ((4, 8),), 0)
    sends += finish(v_outer, ((0, 4), (12, 4)), 1)
    for send in sends:
        send.wait()


def swapped(block, axis):
    size = lax.axis_size(axis)
    for first in (0, 1):
        pairs = [(i, i + 1) for i in range(first, size - 1, 2)]
        yield lax.ppermute(block, axis, pairs + [(j, i) for i, j in pairs])


def body(coarse, up_weight, first_weight, second_weight):
    vmem = pl.BlockSpec(memory_space=pltpu.VMEM)
    params = pltpu.CompilerParams(vmem_limit_bytes=32 * 1024 * 1024)

    bf16 = jnp.bfloat16
    shape = jax.ShapeDtypeStruct
    dip_a, dip_b = swapped(coarse, "dip")
    upmat = pl.pallas_call(
        up_kernel,
        out_shape=shape((256, 2048), bf16),
        in_specs=[pl.BlockSpec(memory_space=pltpu.HBM)],
        out_specs=vmem,
        scratch_shapes=[pltpu.VMEM((512 * 32, 32), bf16), pltpu.SemaphoreType.DMA((8,))],
        compiler_params=pltpu.CompilerParams(vmem_limit_bytes=LIMIT),
        cost_estimate=pl.CostEstimate(flops=5_000_000, bytes_accessed=5_000_000, transcendentals=0),
        name="arrange_up",
    )(up_weight.reshape(512 * 32, 32))
    first, second = first_weight.reshape(864, 32), second_weight.reshape(864, 32)
    inner_shapes = (
        shape((2, 12 * STEP, 384), bf16),
        shape((12 * TIGHT, 256), bf16),
        shape((WINDOW, 256), bf16),
        shape((WINDOW + 256, 256), bf16),
    )
    inner_scratch = [
        pltpu.VMEM((6, 16, 128), jnp.float32),
        pltpu.VMEM((3, 12 * STEP + 8, 128), jnp.float32),
    ]
    inner_params = pltpu.CompilerParams(vmem_limit_bytes=16 * 1024 * 1024)
    own, *early = pl.pallas_call(
        pack_kernel,
        out_shape=(shape((12, 4, 128), bf16), *inner_shapes),
        in_specs=[vmem] * 6,
        out_specs=(vmem,) * 5,
        scratch_shapes=inner_scratch,
        compiler_params=inner_params,
        name="pack",
    )(coarse, dip_a, dip_b, upmat, first, second)
    strike_a, strike_b = swapped(own, "strike")
    inner, centre, band1, band2 = pl.pallas_call(
        inner_kernel,
        out_shape=inner_shapes,
        in_specs=[vmem] * 8,
        out_specs=(vmem,) * 4,
        scratch_shapes=inner_scratch,
        input_output_aliases={4: 0, 5: 1, 6: 2, 7: 3},
        compiler_params=inner_params,
        cost_estimate=pl.CostEstimate(
            flops=300_000_000, bytes_accessed=3_000_000, transcendentals=200_000
        ),
        name="upsample_inner",
    )(own, upmat, first, second, *early)
    return pl.pallas_call(
        main_kernel,
        out_shape=jax.ShapeDtypeStruct((16, 16, 512), bf16),
        in_specs=[vmem] * 8,
        out_specs=pl.BlockSpec(memory_space=pltpu.HBM),
        scratch_shapes=[
            pltpu.VMEM((6, 16, 128), jnp.float32),
            pltpu.VMEM((3, 8 * STEP + 8, 128), jnp.float32),
            pltpu.VMEM((3, 18 * STEP + 32, 128), jnp.float32),
            pltpu.VMEM((2, 12 * STEP, 384), bf16),
            pltpu.VMEM((2, 18 * TIGHT, 384), bf16),
            pltpu.VMEM((8 * TIGHT, 256), bf16),
            pltpu.VMEM((GROUPS, 256, 128), jnp.float32),
            pltpu.VMEM((16, 16, 512), bf16),
            pltpu.SemaphoreType.DMA((3,)),
        ],
        compiler_params=params,
        cost_estimate=pl.CostEstimate(
            flops=2_000_000_000, bytes_accessed=8_000_000, transcendentals=800_000
        ),
        name="upsample_refine",
    )(own, strike_a, strike_b, inner, centre, upmat, band1, band2)


def solution(mesh):
    return jax.shard_map(
        body,
        mesh=mesh,
        in_specs=(P("strike", "dip", None), P(), P(), P()),
        out_specs=P("strike", "dip", None),
        check_vma=False,
    )
```

```python
import jax
import jax.numpy as jnp
from jax import lax
from jax.experimental import pallas as pl
from jax.experimental.pallas import tpu as pltpu
from jax.sharding import PartitionSpec as P

GROUPS = 4
PAIRS = 10
STEP = GROUPS * PAIRS
ORDER = ((0, 1, 2, 3), (1, 0, 3, 2))
BESIDE = ((0, 4), (1, 4), (1, -1), (0, -1))
WINDOW = 3 * 2 * 384
TIGHT = GROUPS * 8
AHEAD = 8
LIMIT = 50 * 1024 * 1024


def silu(v):
    half = 0.5 * v
    return half + half * jnp.tanh(half)


def up_kernel(up_hbm, upmat_ref, up_ref, sems):
    fetches = []
    for k1 in range(8):
        rows = pl.ds(k1 * 2048, 2048)
        fetches.append(pltpu.make_async_copy(up_hbm.at[rows], up_ref.at[rows], sems.at[k1]))
    for fetch in fetches[:AHEAD]:
        fetch.start()

    for k1 in range(8):
        fetches[k1].wait()
        if k1 + AHEAD < 8:
            fetches[k1 + AHEAD].start()
        h1, p1 = divmod(k1, 4)
        for k2 in range(8):
            h2, p2 = divmod(k2, 4)
            for h3 in range(2):
                k = (k1 * 8 + k2) * 8 + 4 * h3
                parts = [up_ref[pl.ds((k + (z + 2) % 4) * 32, 32), :] for z in ORDER[p2 % 2]]
                row = (h1 * 4 + h2 * 2 + (1 - h3)) * 32
                upmat_ref[pl.ds(row, 32), pl.ds((p1 * 4 + p2) * 128, 128)] = jnp.concatenate(
                    parts, axis=1
                )


def arrange_bands(first_ref, second_ref, band1_ref, band2_ref):
    ci = lax.broadcasted_iota(jnp.int32, (32, 128), 0)
    lane = lax.broadcasted_iota(jnp.int32, (32, 128), 1)
    group = lane // 32
    copies = (lane % 32 == ci).astype(jnp.bfloat16)

    masks = [(group == n).astype(jnp.float32).astype(jnp.bfloat16) for n in range(4)]

    def arrange(w_ref, band_ref, out_order):
        rep = jnp.dot(w_ref[...], copies, preferred_element_type=jnp.float32).astype(jnp.bfloat16)
        placed = {}

        def place(tap, n):
            if (tap, n) not in placed:
                placed[tap, n] = rep[tap * 32 : tap * 32 + 32] * masks[n]
            return placed[tap, n]

        blocks = {}
        for d1 in range(3):
            for dj in range(2):
                cells = [(0, z) for z in ORDER[0]] + [(1, z) for z in ORDER[1]] + list(BESIDE)
                for n, (side, z_in) in enumerate(cells):
                    row = (d1 * 2 + dj) * 384 + n * 32
                    for o in range(2):
                        d2 = 2 * dj + side - o
                        parts = []
                        for d3 in range(3):
                            z_out = z_in - d3 + 1
                            if 0 <= d2 < 3 and 0 <= z_out < 4:
                                parts.append(((d1 * 3 + d2) * 3 + d3, out_order[o].index(z_out)))
                        key = tuple(parts)
                        if key not in blocks:
                            block = jnp.zeros((32, 128), jnp.bfloat16)
                            for k, part in enumerate(parts):
                                block = place(*part) if k == 0 else block + place(*part)
                            blocks[key] = block
                        band_ref[pl.ds(row, 32), pl.ds(o * 128, 128)] = blocks[key]

    arrange(first_ref, band1_ref, ORDER)
    arrange(second_ref, band2_ref, (ORDER[0], ORDER[0]))
    r = lax.broadcasted_iota(jnp.int32, (256, 256), 0)
    c = lax.broadcasted_iota(jnp.int32, (256, 256), 1)
    swap = jnp.where((r // 32) % 2 == 0, r + 32, r - 32)
    band2_ref[pl.ds(WINDOW, 256), :] = (jnp.where(r < 128, r, swap) == c).astype(jnp.bfloat16)


def edges():
    one, zero = jnp.float32(1), jnp.float32(0)
    strike, dip = lax.axis_index("strike"), lax.axis_index("dip")
    x_lo = jnp.where(strike == 0, zero, one)
    x_hi = jnp.where(strike == lax.axis_size("strike") - 1, zero, one)
    y_lo = jnp.where(dip == 0, zero, one)
    y_hi = jnp.where(dip == lax.axis_size("dip") - 1, zero, one)
    return x_lo, x_hi, y_lo, y_hi


def put(cells, x0, x1, block):
    even = lax.axis_index("dip") % 2 == 0
    below, above = jnp.where(even, 8, 4), jnp.where(even, 4, 8)
    cells[x0:x1, 1:5, :] = block(0)
    cells[x0:x1, 0:1, :] = block(below)[:, 3:4]
    cells[x0:x1, 5:6, :] = block(above)[:, 0:1]


def read(ref, first, count):
    return ref[pl.ds(first, count)].astype(jnp.float32)


def upsample(cells, upmat, fine, q1s, sides):
    x_lo, x_hi, y_lo, y_hi = sides
    one = jnp.float32(1)
    count = len(q1s)
    rows = 8 * count
    wide = []
    edge = jnp.zeros((rows, 32), jnp.float32)
    for h1 in range(2):
        for h2 in range(2):
            window = jnp.concatenate(
                [cells[q1 + 1 - h1 : q1 + 2 - h1, 1 - h2 : 9 - h2, :] for q1 in q1s], axis=0
            )
            wide.append(jnp.concatenate([edge, window.reshape(rows, 128), edge], axis=1))
    left = jnp.concatenate(
        [
            jnp.concatenate([w[:, 32 * q3 : 32 * q3 + 64] for w in wide], axis=1)
            for q3 in range(5)
        ],
        axis=0,
    ).astype(jnp.bfloat16)

    lane = lax.broadcasted_iota(jnp.int32, (rows, 128), 1)
    q2 = lax.broadcasted_iota(jnp.int32, (rows, 128), 0) % 8
    outer = (lane < 32) | (lane >= 96)
    front = lane < 64
    low = jnp.where(q2 == 0, y_lo, one)
    high = jnp.where(q2 == 4, y_hi, one)
    none = jnp.zeros((rows, 128), jnp.float32)
    for p1 in range(4):
        phase = jnp.dot(left, upmat[:, p1 * 512 : p1 * 512 + 512], preferred_element_type=jnp.float32)
        for pp in range(2):
            tiles = [[], []]
            for side in range(2):
                p2 = 2 * pp + side
                v = phase[:, p2 * 128 : p2 * 128 + 128]
                for g in range(GROUPS):
                    at = g * rows
                    t = jnp.where(front, v[at : at + rows], v[at + rows : at + 2 * rows])
                    tiles[side].append(silu(t) * (low if pp == 0 else high))
            merged = [jnp.where(outer, tiles[0][g], tiles[1][g]) for g in range(GROUPS)]
            merged = [none] + merged + [none]
            for g in range(GROUPS):
                beside = jnp.where(front, merged[g + 2], merged[g])
                for n, t in enumerate((tiles[0][g], tiles[1][g], beside)):
                    for c, q1 in enumerate(q1s):
                        part = t[c * 8 : c * 8 + 5]
                        if q1 == 0 and p1 < 2:
                            part = part * x_lo
                        if q1 == 4 and p1 >= 2:
                            part = part * x_hi
                        at = (4 * c + p1) * STEP + g * PAIRS + pp
                        fine[n, pl.ds(at, 5, stride=2), :] = part


def windows_of(fine, first, count, target, at):
    for dj in range(2):
        for n in range(3):
            rows = fine[n, pl.ds(first * STEP + dj, count * STEP), :].astype(jnp.bfloat16)
            target[dj, at * STEP : (at + count) * STEP, n * 128 : n * 128 + 128] = rows


def tight(block, at):
    return jnp.concatenate([block[pl.ds(at + g * PAIRS, 8), :] for g in range(GROUPS)], axis=0)


def centre_of(fine, first, count, target, at):
    for n in range(count):
        here = slice((at + n) * TIGHT, (at + n + 1) * TIGHT)
        for o in range(2):
            rows = tight(fine.at[o], (first + n) * STEP + 1)
            target[here, o * 128 : o * 128 + 128] = rows.astype(jnp.bfloat16)


def clear(block, at):
    block[2, at : at + 16, :] = jnp.zeros((16, 128), jnp.float32)


def keep(v, at, count, hidden, shift, target, target_at, sides):
    x_lo, x_hi, y_lo, y_hi = sides
    one, zero = jnp.float32(1), jnp.float32(0)
    row = lax.broadcasted_iota(jnp.int32, (STEP, 128), 0)
    lane = lax.broadcasted_iota(jnp.int32, (STEP, 128), 1)
    starts = [g * PAIRS for g in range(GROUPS)]
    first, last = row == starts[0], row == starts[0] + 8
    for start in starts[1:]:
        first, last = first | (row == start), last | (row == start + 8)
    y_first, y_last = jnp.where(first, y_lo, one), jnp.where(last, y_hi, one)
    outer = (lane < 32) | (lane >= 96)
    row = lax.broadcasted_iota(jnp.int32, (TIGHT, 128), 0)
    lane = lax.broadcasted_iota(jnp.int32, (TIGHT, 128), 1)
    front = lane < 64
    inside_above = jnp.where(row < TIGHT - 8, one, zero)
    inside_below = jnp.where(row >= 8, one, zero)
    inside = jnp.where(front, inside_above, inside_below)

    v = silu(v)
    for n in range(count):
        x = at + n
        rows = slice(n * STEP, n * STEP + STEP)
        v0, v1 = v[rows, :128] * y_first, v[rows, 128:] * y_last
        if x in (0, 17):
            edge = x_lo if x == 0 else x_hi
            v0, v1 = v0 * edge, v1 * edge
        here = slice(16 + (x - shift) * STEP, 16 + (x - shift) * STEP + STEP)
        hidden[0, here, :] = v0
        hidden[1, here, :] = v1
        hidden[2, here, :] = jnp.where(outer, v0, v1)
    for n in range(count):
        here = slice((target_at + n) * TIGHT, (target_at + n + 1) * TIGHT)
        for dj in range(2):
            start = 16 + (at + n - shift) * STEP + dj
            for o in range(2):
                rows = tight(hidden.at[o], start)
                target[dj, here, o * 128 : o * 128 + 128] = rows.astype(jnp.bfloat16)
            above = tight(hidden.at[2], start + PAIRS)
            below = tight(hidden.at[2], start - PAIRS)
            beside = jnp.where(front, above, below) * inside
            target[dj, here, 256:384] = beside.astype(jnp.bfloat16)


def inner_work(
    own, upmat, first_ref, second_ref, inner, centre, band1_ref, band2_ref, ready, cells, fine, hidden
):
    arrange_bands(first_ref, second_ref, band1_ref, band2_ref)
    sides = edges()
    put(cells, 1, 5, lambda o: read(own, o, 4))
    upsample(cells, upmat, fine, (1, 2, 3), sides)
    windows_of(fine, 0, 12, inner, 0)
    centre_of(fine, 0, 12, centre, 0)
    v = product(inner, ((0, 6), (6, 4)), STEP, band1_ref)
    clear(hidden, 0)
    clear(hidden, 16 + 10 * STEP)
    keep(v, 4, 10, hidden, 4, ready, 0, sides)


def pack_kernel(
    coarse, dip_a, dip_b, upmat, first_ref, second_ref,
    own, inner, centre, band1_ref, band2_ref, ready, cells, fine, hidden,
):
    own[0:4] = coarse[...]
    own[4:8] = dip_a[...]
    own[8:12] = dip_b[...]

    @pl.when(lax.axis_index("strike") == 0)
    def _():
        inner_work(own, upmat, first_ref, second_ref, inner, centre, band1_ref, band2_ref, ready, cells, fine, hidden)


def inner_kernel(
    own, upmat, first_ref, second_ref, _inner, _centre, _band1, _band2, _ready,
    inner, centre, band1_ref, band2_ref, ready, cells, fine, hidden,
):
    @pl.when(lax.axis_index("strike") != 0)
    def _():
        inner_work(own, upmat, first_ref, second_ref, inner, centre, band1_ref, band2_ref, ready, cells, fine, hidden)


def product(source, strips, step, taps, base=None):
    results = []
    row = 0
    for at, n in strips:
        columns = [
            source[dj, (at + dx) * step : (at + dx + n) * step, :] for dx in range(3) for dj in range(2)
        ]
        if base is not None:
            columns.append(base[row : row + n * step, :])
        row += n * step
        results.append(
            jnp.dot(jnp.concatenate(columns, axis=1), taps[...], preferred_element_type=jnp.float32)
        )
    return jnp.concatenate(results, axis=0)


def main_kernel(
    own, strike_a, strike_b, inner, centre, upmat, band1, band2, ready, out,
    cells, fine, hidden, b1, b2, ends, woven, near, sems,
):
    sides = x_lo, x_hi, y_lo, y_hi = edges()
    one, zero = jnp.float32(1), jnp.float32(0)

    v_inner = product(ready, ((0, 4), (4, 4)), TIGHT, band2, centre[2 * TIGHT : 10 * TIGHT, :])

    even = lax.axis_index("strike") % 2 == 0
    put(cells, 0, 1, lambda o: jnp.where(even, read(strike_b, o + 3, 1), read(strike_a, o + 3, 1)))
    put(cells, 1, 2, lambda o: read(own, o, 1))
    put(cells, 4, 5, lambda o: read(own, o + 3, 1))
    put(cells, 5, 6, lambda o: jnp.where(even, read(strike_a, o, 1), read(strike_b, o, 1)))
    upsample(cells, upmat, fine, (0, 4), sides)
    windows_of(fine, 0, 4, b1, 0)
    b1[:, 4 * STEP : 6 * STEP, :] = inner[:, : 2 * STEP, :]
    b1[:, 6 * STEP : 8 * STEP, :] = inner[:, 10 * STEP : 12 * STEP, :]
    windows_of(fine, 4, 4, b1, 8)
    centre_of(fine, 2, 2, ends, 0)
    ends[2 * TIGHT : 4 * TIGHT, :] = centre[0 : 2 * TIGHT, :]
    ends[4 * TIGHT : 6 * TIGHT, :] = centre[10 * TIGHT : 12 * TIGHT, :]
    centre_of(fine, 4, 2, ends, 6)

    v_outer = product(b1, ((0, 4), (6, 4)), STEP, band1)

    def finish(v, strips, chain):
        sends = []
        row = 0
        for k, (at, count) in enumerate(strips):
            for x in range(at, at + count):
                for g in range(GROUPS):
                    for o in range(2):
                        cells8 = v[row : row + 8, o * 128 : o * 128 + 128]
                        woven[g, pl.ds(x * 16 + o, 8, stride=2), :] = cells8
                    row += 8
            for g in range(GROUPS):
                near[at : at + count, :, g * 128 : g * 128 + 128] = (
                    woven[g, at * 16 : (at + count) * 16].reshape(count, 16, 128).astype(jnp.bfloat16)
                )
            here = pl.ds(at, count)
            sends.append(pltpu.make_async_copy(near.at[here], out.at[here], sems.at[chain + k]))
            sends[-1].start()
        return sends

    clear(hidden, 0)
    clear(hidden, 16 + 4 * STEP)
    clear(hidden, 14 * STEP)
    clear(hidden, 16 + 18 * STEP)
    keep(v_outer[: 4 * STEP], 0, 4, hidden, 0, b2, 0, sides)
    keep(v_outer[4 * STEP :], 14, 4, hidden, 0, b2, 14, sides)
    b2[:, 4 * TIGHT : 6 * TIGHT, :] = ready[:, : 2 * TIGHT, :]
    b2[:, 12 * TIGHT : 14 * TIGHT, :] = ready[:, 8 * TIGHT : 10 * TIGHT, :]
    v_outer = product(b2, ((0, 4), (12, 4)), TIGHT, band2, ends[...])

    sends = finish(v_inner, ((4, 8),), 0)
    sends += finish(v_outer, ((0, 4), (12, 4)), 1)
    for send in sends:
        send.wait()


def swapped(block, axis):
    size = lax.axis_size(axis)
    for first in (0, 1):
        pairs = [(i, i + 1) for i in range(first, size - 1, 2)]
        yield lax.ppermute(block, axis, pairs + [(j, i) for i, j in pairs])


def body(coarse, up_weight, first_weight, second_weight):
    vmem = pl.BlockSpec(memory_space=pltpu.VMEM)
    params = pltpu.CompilerParams(vmem_limit_bytes=32 * 1024 * 1024)

    bf16 = jnp.bfloat16
    shape = jax.ShapeDtypeStruct
    dip_a, dip_b = swapped(coarse, "dip")
    upmat = pl.pallas_call(
        up_kernel,
        out_shape=shape((256, 2048), bf16),
        in_specs=[pl.BlockSpec(memory_space=pltpu.HBM)],
        out_specs=vmem,
        scratch_shapes=[pltpu.VMEM((512 * 32, 32), bf16), pltpu.SemaphoreType.DMA((8,))],
        compiler_params=pltpu.CompilerParams(vmem_limit_bytes=LIMIT),
        cost_estimate=pl.CostEstimate(flops=5_000_000, bytes_accessed=5_000_000, transcendentals=0),
        name="arrange_up",
    )(up_weight.reshape(512 * 32, 32))
    first, second = first_weight.reshape(864, 32), second_weight.reshape(864, 32)
    inner_shapes = (
        shape((2, 12 * STEP, 384), bf16),
        shape((12 * TIGHT, 256), bf16),
        shape((WINDOW, 256), bf16),
        shape((WINDOW + 256, 256), bf16),
        shape((2, 10 * TIGHT, 384), bf16),
    )
    inner_scratch = [
        pltpu.VMEM((6, 16, 128), jnp.float32),
        pltpu.VMEM((3, 12 * STEP + 8, 128), jnp.float32),
        pltpu.VMEM((3, 10 * STEP + 32, 128), jnp.float32),
    ]
    inner_params = pltpu.CompilerParams(vmem_limit_bytes=16 * 1024 * 1024)
    own, *early = pl.pallas_call(
        pack_kernel,
        out_shape=(shape((12, 4, 128), bf16), *inner_shapes),
        in_specs=[vmem] * 6,
        out_specs=(vmem,) * 6,
        scratch_shapes=inner_scratch,
        compiler_params=inner_params,
        name="pack",
    )(coarse, dip_a, dip_b, upmat, first, second)
    strike_a, strike_b = swapped(own, "strike")
    inner, centre, band1, band2, ready = pl.pallas_call(
        inner_kernel,
        out_shape=inner_shapes,
        in_specs=[vmem] * 9,
        out_specs=(vmem,) * 5,
        scratch_shapes=inner_scratch,
        input_output_aliases={4: 0, 5: 1, 6: 2, 7: 3, 8: 4},
        compiler_params=inner_params,
        cost_estimate=pl.CostEstimate(
            flops=300_000_000, bytes_accessed=3_000_000, transcendentals=200_000
        ),
        name="upsample_inner",
    )(own, upmat, first, second, *early)
    return pl.pallas_call(
        main_kernel,
        out_shape=jax.ShapeDtypeStruct((16, 16, 512), bf16),
        in_specs=[vmem] * 9,
        out_specs=pl.BlockSpec(memory_space=pltpu.HBM),
        scratch_shapes=[
            pltpu.VMEM((6, 16, 128), jnp.float32),
            pltpu.VMEM((3, 8 * STEP + 8, 128), jnp.float32),
            pltpu.VMEM((3, 18 * STEP + 32, 128), jnp.float32),
            pltpu.VMEM((2, 12 * STEP, 384), bf16),
            pltpu.VMEM((2, 18 * TIGHT, 384), bf16),
            pltpu.VMEM((8 * TIGHT, 256), bf16),
            pltpu.VMEM((GROUPS, 256, 128), jnp.float32),
            pltpu.VMEM((16, 16, 512), bf16),
            pltpu.SemaphoreType.DMA((3,)),
        ],
        compiler_params=params,
        cost_estimate=pl.CostEstimate(
            flops=2_000_000_000, bytes_accessed=8_000_000, transcendentals=800_000
        ),
        name="upsample_refine",
    )(own, strike_a, strike_b, inner, centre, upmat, band1, band2, ready)


def solution(mesh):
    return jax.shard_map(
        body,
        mesh=mesh,
        in_specs=(P("strike", "dip", None), P(), P(), P()),
        out_specs=P("strike", "dip", None),
        check_vma=False,
    )
```

```python
import jax
import jax.numpy as jnp
from jax import lax
from jax.experimental import pallas as pl
from jax.experimental.pallas import tpu as pltpu
from jax.sharding import PartitionSpec as P

GROUPS = 4
PAIRS = 10
STEP = GROUPS * PAIRS
ORDER = ((0, 1, 2, 3), (1, 0, 3, 2))
BESIDE = ((0, 4), (1, 4), (1, -1), (0, -1))
WINDOW = 3 * 2 * 384
TIGHT = GROUPS * 8
AHEAD = 8
LIMIT = 50 * 1024 * 1024


def silu(v):
    half = 0.5 * v
    return half + half * jnp.tanh(half)


def up_kernel(up_hbm, upmat_ref, up_ref, sems):
    fetches = []
    for k1 in range(8):
        rows = pl.ds(k1 * 2048, 2048)
        fetches.append(pltpu.make_async_copy(up_hbm.at[rows], up_ref.at[rows], sems.at[k1]))
    for fetch in fetches[:AHEAD]:
        fetch.start()

    for k1 in range(8):
        fetches[k1].wait()
        if k1 + AHEAD < 8:
            fetches[k1 + AHEAD].start()
        h1, p1 = divmod(k1, 4)
        for k2 in range(8):
            h2, p2 = divmod(k2, 4)
            for h3 in range(2):
                k = (k1 * 8 + k2) * 8 + 4 * h3
                parts = [up_ref[pl.ds((k + (z + 2) % 4) * 32, 32), :] for z in ORDER[p2 % 2]]
                row = (h1 * 4 + h2 * 2 + (1 - h3)) * 32
                upmat_ref[pl.ds(row, 32), pl.ds((p1 * 4 + p2) * 128, 128)] = jnp.concatenate(
                    parts, axis=1
                )


def arrange_bands(first_ref, second_ref, band1_ref, band2_ref):
    ci = lax.broadcasted_iota(jnp.int32, (32, 128), 0)
    lane = lax.broadcasted_iota(jnp.int32, (32, 128), 1)
    group = lane // 32
    copies = (lane % 32 == ci).astype(jnp.bfloat16)

    masks = [(group == n).astype(jnp.float32).astype(jnp.bfloat16) for n in range(4)]

    def arrange(w_ref, band_ref, out_order):
        rep = jnp.dot(w_ref[...], copies, preferred_element_type=jnp.float32).astype(jnp.bfloat16)
        placed = {}

        def place(tap, n):
            if (tap, n) not in placed:
                placed[tap, n] = rep[tap * 32 : tap * 32 + 32] * masks[n]
            return placed[tap, n]

        blocks = {}
        for d1 in range(3):
            for dj in range(2):
                cells = [(0, z) for z in ORDER[0]] + [(1, z) for z in ORDER[1]] + list(BESIDE)
                for n, (side, z_in) in enumerate(cells):
                    row = (d1 * 2 + dj) * 384 + n * 32
                    for o in range(2):
                        d2 = 2 * dj + side - o
                        parts = []
                        for d3 in range(3):
                            z_out = z_in - d3 + 1
                            if 0 <= d2 < 3 and 0 <= z_out < 4:
                                parts.append(((d1 * 3 + d2) * 3 + d3, out_order[o].index(z_out)))
                        key = tuple(parts)
                        if key not in blocks:
                            block = jnp.zeros((32, 128), jnp.bfloat16)
                            for k, part in enumerate(parts):
                                block = place(*part) if k == 0 else block + place(*part)
                            blocks[key] = block
                        band_ref[pl.ds(row, 32), pl.ds(o * 128, 128)] = blocks[key]

    arrange(first_ref, band1_ref, ORDER)
    arrange(second_ref, band2_ref, (ORDER[0], ORDER[0]))
    r = lax.broadcasted_iota(jnp.int32, (256, 256), 0)
    c = lax.broadcasted_iota(jnp.int32, (256, 256), 1)
    swap = jnp.where((r // 32) % 2 == 0, r + 32, r - 32)
    band2_ref[pl.ds(WINDOW, 256), :] = (jnp.where(r < 128, r, swap) == c).astype(jnp.bfloat16)


def edges():
    one, zero = jnp.float32(1), jnp.float32(0)
    strike, dip = lax.axis_index("strike"), lax.axis_index("dip")
    x_lo = jnp.where(strike == 0, zero, one)
    x_hi = jnp.where(strike == lax.axis_size("strike") - 1, zero, one)
    y_lo = jnp.where(dip == 0, zero, one)
    y_hi = jnp.where(dip == lax.axis_size("dip") - 1, zero, one)
    return x_lo, x_hi, y_lo, y_hi


def put(cells, x0, x1, block):
    even = lax.axis_index("dip") % 2 == 0
    below, above = jnp.where(even, 8, 4), jnp.where(even, 4, 8)
    cells[x0:x1, 1:5, :] = block(0)
    cells[x0:x1, 0:1, :] = block(below)[:, 3:4]
    cells[x0:x1, 5:6, :] = block(above)[:, 0:1]


def read(ref, first, count):
    return ref[pl.ds(first, count)].astype(jnp.float32)


def upsample(cells, upmat, fine, q1s, sides):
    x_lo, x_hi, y_lo, y_hi = sides
    one = jnp.float32(1)
    count = len(q1s)
    rows = 8 * count
    wide = []
    edge = jnp.zeros((rows, 32), jnp.float32)
    for h1 in range(2):
        for h2 in range(2):
            window = jnp.concatenate(
                [cells[q1 + 1 - h1 : q1 + 2 - h1, 1 - h2 : 9 - h2, :] for q1 in q1s], axis=0
            )
            wide.append(jnp.concatenate([edge, window.reshape(rows, 128), edge], axis=1))
    left = jnp.concatenate(
        [
            jnp.concatenate([w[:, 32 * q3 : 32 * q3 + 64] for w in wide], axis=1)
            for q3 in range(5)
        ],
        axis=0,
    ).astype(jnp.bfloat16)

    lane = lax.broadcasted_iota(jnp.int32, (rows, 128), 1)
    q2 = lax.broadcasted_iota(jnp.int32, (rows, 128), 0) % 8
    outer = (lane < 32) | (lane >= 96)
    front = lane < 64
    low = jnp.where(q2 == 0, y_lo, one)
    high = jnp.where(q2 == 4, y_hi, one)
    none = jnp.zeros((rows, 128), jnp.float32)
    for p1 in range(4):
        phase = jnp.dot(left, upmat[:, p1 * 512 : p1 * 512 + 512], preferred_element_type=jnp.float32)
        for pp in range(2):
            tiles = [[], []]
            for side in range(2):
                p2 = 2 * pp + side
                v = phase[:, p2 * 128 : p2 * 128 + 128]
                for g in range(GROUPS):
                    at = g * rows
                    t = jnp.where(front, v[at : at + rows], v[at + rows : at + 2 * rows])
                    tiles[side].append(silu(t) * (low if pp == 0 else high))
            merged = [jnp.where(outer, tiles[0][g], tiles[1][g]) for g in range(GROUPS)]
            merged = [none] + merged + [none]
            for g in range(GROUPS):
                beside = jnp.where(front, merged[g + 2], merged[g])
                for n, t in enumerate((tiles[0][g], tiles[1][g], beside)):
                    for c, q1 in enumerate(q1s):
                        part = t[c * 8 : c * 8 + 5]
                        if q1 == 0 and p1 < 2:
                            part = part * x_lo
                        if q1 == 4 and p1 >= 2:
                            part = part * x_hi
                        at = (4 * c + p1) * STEP + g * PAIRS + pp
                        fine[n, pl.ds(at, 5, stride=2), :] = part


def windows_of(fine, first, count, target, at):
    for dj in range(2):
        for n in range(3):
            rows = fine[n, pl.ds(first * STEP + dj, count * STEP), :].astype(jnp.bfloat16)
            target[dj, at * STEP : (at + count) * STEP, n * 128 : n * 128 + 128] = rows


def tight(block, at):
    return jnp.concatenate([block[pl.ds(at + g * PAIRS, 8), :] for g in range(GROUPS)], axis=0)


def centre_of(fine, first, count, target, at):
    for n in range(count):
        here = slice((at + n) * TIGHT, (at + n + 1) * TIGHT)
        for o in range(2):
            rows = tight(fine.at[o], (first + n) * STEP + 1)
            target[here, o * 128 : o * 128 + 128] = rows.astype(jnp.bfloat16)


def clear(block, at):
    block[2, at : at + 16, :] = jnp.zeros((16, 128), jnp.float32)


def keep(v, at, count, hidden, shift, target, target_at, sides):
    x_lo, x_hi, y_lo, y_hi = sides
    one, zero = jnp.float32(1), jnp.float32(0)
    row = lax.broadcasted_iota(jnp.int32, (STEP, 128), 0)
    lane = lax.broadcasted_iota(jnp.int32, (STEP, 128), 1)
    starts = [g * PAIRS for g in range(GROUPS)]
    first, last = row == starts[0], row == starts[0] + 8
    for start in starts[1:]:
        first, last = first | (row == start), last | (row == start + 8)
    y_first, y_last = jnp.where(first, y_lo, one), jnp.where(last, y_hi, one)
    outer = (lane < 32) | (lane >= 96)
    row = lax.broadcasted_iota(jnp.int32, (TIGHT, 128), 0)
    lane = lax.broadcasted_iota(jnp.int32, (TIGHT, 128), 1)
    front = lane < 64
    inside_above = jnp.where(row < TIGHT - 8, one, zero)
    inside_below = jnp.where(row >= 8, one, zero)
    inside = jnp.where(front, inside_above, inside_below)

    v = silu(v)
    for n in range(count):
        x = at + n
        rows = slice(n * STEP, n * STEP + STEP)
        v0, v1 = v[rows, :128] * y_first, v[rows, 128:] * y_last
        if x in (0, 17):
            edge = x_lo if x == 0 else x_hi
            v0, v1 = v0 * edge, v1 * edge
        here = slice(16 + (x - shift) * STEP, 16 + (x - shift) * STEP + STEP)
        hidden[0, here, :] = v0
        hidden[1, here, :] = v1
        hidden[2, here, :] = jnp.where(outer, v0, v1)
    for n in range(count):
        here = slice((target_at + n) * TIGHT, (target_at + n + 1) * TIGHT)
        for dj in range(2):
            start = 16 + (at + n - shift) * STEP + dj
            for o in range(2):
                rows = tight(hidden.at[o], start)
                target[dj, here, o * 128 : o * 128 + 128] = rows.astype(jnp.bfloat16)
            above = tight(hidden.at[2], start + PAIRS)
            below = tight(hidden.at[2], start - PAIRS)
            beside = jnp.where(front, above, below) * inside
            target[dj, here, 256:384] = beside.astype(jnp.bfloat16)


def weave(v, row, woven, near, at, count):
    for x in range(at, at + count):
        for g in range(GROUPS):
            for o in range(2):
                cells8 = v[row : row + 8, o * 128 : o * 128 + 128]
                woven[g, pl.ds(x * 16 + o, 8, stride=2), :] = cells8
            row += 8
    for g in range(GROUPS):
        near[at : at + count, :, g * 128 : g * 128 + 128] = (
            woven[g, at * 16 : (at + count) * 16].reshape(count, 16, 128).astype(jnp.bfloat16)
        )


def inner_work(
    own, upmat, first_ref, second_ref, inner, centre, band1_ref, band2_ref, ready, middle,
    cells, fine, hidden, woven,
):
    arrange_bands(first_ref, second_ref, band1_ref, band2_ref)
    sides = edges()
    put(cells, 1, 5, lambda o: read(own, o, 4))
    upsample(cells, upmat, fine, (1, 2, 3), sides)
    windows_of(fine, 0, 12, inner, 0)
    centre_of(fine, 0, 12, centre, 0)
    v = product(inner, ((0, 6), (6, 4)), STEP, band1_ref)
    clear(hidden, 0)
    clear(hidden, 16 + 10 * STEP)
    keep(v, 4, 10, hidden, 4, ready, 0, sides)
    v = product(ready, ((0, 4), (4, 4)), TIGHT, band2_ref, centre[2 * TIGHT : 10 * TIGHT, :])
    weave(v, 0, woven, middle, 0, 8)


def pack_kernel(
    coarse, dip_a, dip_b, upmat, first_ref, second_ref,
    own, inner, centre, band1_ref, band2_ref, ready, middle, cells, fine, hidden, woven,
):
    own[0:4] = coarse[...]
    own[4:8] = dip_a[...]
    own[8:12] = dip_b[...]

    @pl.when(lax.axis_index("strike") == 0)
    def _():
        inner_work(
            own, upmat, first_ref, second_ref, inner, centre, band1_ref, band2_ref, ready, middle,
            cells, fine, hidden, woven,
        )


def inner_kernel(
    own, upmat, first_ref, second_ref, _inner, _centre, _band1, _band2, _ready, _middle,
    inner, centre, band1_ref, band2_ref, ready, middle, cells, fine, hidden, woven,
):
    @pl.when(lax.axis_index("strike") != 0)
    def _():
        inner_work(
            own, upmat, first_ref, second_ref, inner, centre, band1_ref, band2_ref, ready, middle,
            cells, fine, hidden, woven,
        )


def product(source, strips, step, taps, base=None):
    results = []
    row = 0
    for at, n in strips:
        columns = [
            source[dj, (at + dx) * step : (at + dx + n) * step, :] for dx in range(3) for dj in range(2)
        ]
        if base is not None:
            columns.append(base[row : row + n * step, :])
        row += n * step
        results.append(
            jnp.dot(jnp.concatenate(columns, axis=1), taps[...], preferred_element_type=jnp.float32)
        )
    return jnp.concatenate(results, axis=0)


def main_kernel(
    own, strike_a, strike_b, inner, centre, upmat, band1, band2, ready, middle, out,
    cells, fine, hidden, b1, b2, ends, woven, near, sems,
):
    sends = [pltpu.make_async_copy(middle, out.at[pl.ds(4, 8)], sems.at[0])]
    sends[0].start()
    sides = edges()

    even = lax.axis_index("strike") % 2 == 0
    put(cells, 0, 1, lambda o: jnp.where(even, read(strike_b, o + 3, 1), read(strike_a, o + 3, 1)))
    put(cells, 1, 2, lambda o: read(own, o, 1))
    put(cells, 4, 5, lambda o: read(own, o + 3, 1))
    put(cells, 5, 6, lambda o: jnp.where(even, read(strike_a, o, 1), read(strike_b, o, 1)))
    upsample(cells, upmat, fine, (0, 4), sides)
    windows_of(fine, 0, 4, b1, 0)
    b1[:, 4 * STEP : 6 * STEP, :] = inner[:, : 2 * STEP, :]
    b1[:, 6 * STEP : 8 * STEP, :] = inner[:, 10 * STEP : 12 * STEP, :]
    windows_of(fine, 4, 4, b1, 8)
    centre_of(fine, 2, 2, ends, 0)
    ends[2 * TIGHT : 4 * TIGHT, :] = centre[0 : 2 * TIGHT, :]
    ends[4 * TIGHT : 6 * TIGHT, :] = centre[10 * TIGHT : 12 * TIGHT, :]
    centre_of(fine, 4, 2, ends, 6)

    v_outer = product(b1, ((0, 4), (6, 4)), STEP, band1)

    clear(hidden, 0)
    clear(hidden, 16 + 4 * STEP)
    clear(hidden, 14 * STEP)
    clear(hidden, 16 + 18 * STEP)
    keep(v_outer[: 4 * STEP], 0, 4, hidden, 0, b2, 0, sides)
    keep(v_outer[4 * STEP :], 14, 4, hidden, 0, b2, 14, sides)
    b2[:, 4 * TIGHT : 6 * TIGHT, :] = ready[:, : 2 * TIGHT, :]
    b2[:, 12 * TIGHT : 14 * TIGHT, :] = ready[:, 8 * TIGHT : 10 * TIGHT, :]
    v_outer = product(b2, ((0, 4), (12, 4)), TIGHT, band2, ends[...])

    for n, at in enumerate((0, 12)):
        weave(v_outer, n * 4 * TIGHT, woven, near, at, 4)
        here = pl.ds(at, 4)
        sends.append(pltpu.make_async_copy(near.at[here], out.at[here], sems.at[n + 1]))
        sends[-1].start()
    for send in sends:
        send.wait()


def swapped(block, axis):
    size = lax.axis_size(axis)
    for first in (0, 1):
        pairs = [(i, i + 1) for i in range(first, size - 1, 2)]
        yield lax.ppermute(block, axis, pairs + [(j, i) for i, j in pairs])


def body(coarse, up_weight, first_weight, second_weight):
    vmem = pl.BlockSpec(memory_space=pltpu.VMEM)
    params = pltpu.CompilerParams(vmem_limit_bytes=32 * 1024 * 1024)

    bf16 = jnp.bfloat16
    shape = jax.ShapeDtypeStruct
    dip_a, dip_b = swapped(coarse, "dip")
    upmat = pl.pallas_call(
        up_kernel,
        out_shape=shape((256, 2048), bf16),
        in_specs=[pl.BlockSpec(memory_space=pltpu.HBM)],
        out_specs=vmem,
        scratch_shapes=[pltpu.VMEM((512 * 32, 32), bf16), pltpu.SemaphoreType.DMA((8,))],
        compiler_params=pltpu.CompilerParams(vmem_limit_bytes=LIMIT),
        cost_estimate=pl.CostEstimate(flops=5_000_000, bytes_accessed=5_000_000, transcendentals=0),
        name="arrange_up",
    )(up_weight.reshape(512 * 32, 32))
    first, second = first_weight.reshape(864, 32), second_weight.reshape(864, 32)
    inner_shapes = (
        shape((2, 12 * STEP, 384), bf16),
        shape((12 * TIGHT, 256), bf16),
        shape((WINDOW, 256), bf16),
        shape((WINDOW + 256, 256), bf16),
        shape((2, 10 * TIGHT, 384), bf16),
        shape((8, 16, 512), bf16),
    )
    inner_scratch = [
        pltpu.VMEM((6, 16, 128), jnp.float32),
        pltpu.VMEM((3, 12 * STEP + 8, 128), jnp.float32),
        pltpu.VMEM((3, 10 * STEP + 32, 128), jnp.float32),
        pltpu.VMEM((GROUPS, 128, 128), jnp.float32),
    ]
    inner_params = pltpu.CompilerParams(vmem_limit_bytes=16 * 1024 * 1024)
    own, *early = pl.pallas_call(
        pack_kernel,
        out_shape=(shape((12, 4, 128), bf16), *inner_shapes),
        in_specs=[vmem] * 6,
        out_specs=(vmem,) * 7,
        scratch_shapes=inner_scratch,
        compiler_params=inner_params,
        name="pack",
    )(coarse, dip_a, dip_b, upmat, first, second)
    strike_a, strike_b = swapped(own, "strike")
    inner, centre, band1, band2, ready, middle = pl.pallas_call(
        inner_kernel,
        out_shape=inner_shapes,
        in_specs=[vmem] * 10,
        out_specs=(vmem,) * 6,
        scratch_shapes=inner_scratch,
        input_output_aliases={4: 0, 5: 1, 6: 2, 7: 3, 8: 4, 9: 5},
        compiler_params=inner_params,
        cost_estimate=pl.CostEstimate(
            flops=300_000_000, bytes_accessed=3_000_000, transcendentals=200_000
        ),
        name="upsample_inner",
    )(own, upmat, first, second, *early)
    return pl.pallas_call(
        main_kernel,
        out_shape=jax.ShapeDtypeStruct((16, 16, 512), bf16),
        in_specs=[vmem] * 10,
        out_specs=pl.BlockSpec(memory_space=pltpu.HBM),
        scratch_shapes=[
            pltpu.VMEM((6, 16, 128), jnp.float32),
            pltpu.VMEM((3, 8 * STEP + 8, 128), jnp.float32),
            pltpu.VMEM((3, 18 * STEP + 32, 128), jnp.float32),
            pltpu.VMEM((2, 12 * STEP, 384), bf16),
            pltpu.VMEM((2, 18 * TIGHT, 384), bf16),
            pltpu.VMEM((8 * TIGHT, 256), bf16),
            pltpu.VMEM((GROUPS, 256, 128), jnp.float32),
            pltpu.VMEM((16, 16, 512), bf16),
            pltpu.SemaphoreType.DMA((3,)),
        ],
        compiler_params=params,
        cost_estimate=pl.CostEstimate(
            flops=2_000_000_000, bytes_accessed=8_000_000, transcendentals=800_000
        ),
        name="upsample_refine",
    )(own, strike_a, strike_b, inner, centre, upmat, band1, band2, ready, middle)


def solution(mesh):
    return jax.shard_map(
        body,
        mesh=mesh,
        in_specs=(P("strike", "dip", None), P(), P(), P()),
        out_specs=P("strike", "dip", None),
        check_vma=False,
    )
```

```python
import jax
import jax.numpy as jnp
from jax import lax
from jax.experimental import pallas as pl
from jax.experimental.pallas import tpu as pltpu
from jax.sharding import PartitionSpec as P

GROUPS = 4
PAIRS = 10
STEP = GROUPS * PAIRS
ORDER = ((0, 1, 2, 3), (1, 0, 3, 2))
BESIDE = ((0, 4), (1, 4), (1, -1), (0, -1))
WINDOW = 3 * 2 * 384
TIGHT = GROUPS * 8
AHEAD = 8
LIMIT = 50 * 1024 * 1024


def silu(v):
    half = 0.5 * v
    return half + half * jnp.tanh(half)


def up_kernel(up_hbm, upmat_ref, up_ref, sems):
    fetches = []
    for k1 in range(8):
        rows = pl.ds(k1 * 2048, 2048)
        fetches.append(pltpu.make_async_copy(up_hbm.at[rows], up_ref.at[rows], sems.at[k1]))
    for fetch in fetches[:AHEAD]:
        fetch.start()

    for k1 in range(8):
        fetches[k1].wait()
        if k1 + AHEAD < 8:
            fetches[k1 + AHEAD].start()
        h1, p1 = divmod(k1, 4)
        for k2 in range(8):
            h2, p2 = divmod(k2, 4)
            for h3 in range(2):
                k = (k1 * 8 + k2) * 8 + 4 * h3
                parts = [up_ref[pl.ds((k + (z + 2) % 4) * 32, 32), :] for z in ORDER[p2 % 2]]
                row = (h1 * 4 + h2 * 2 + (1 - h3)) * 32
                upmat_ref[pl.ds(row, 32), pl.ds((p1 * 4 + p2) * 128, 128)] = jnp.concatenate(
                    parts, axis=1
                )


def arrange_band(weight_ref, target_ref, order, residual):
    ci = lax.broadcasted_iota(jnp.int32, (32, 128), 0)
    lane = lax.broadcasted_iota(jnp.int32, (32, 128), 1)
    group = lane // 32
    copies = (lane % 32 == ci).astype(jnp.bfloat16)

    masks = [(group == n).astype(jnp.float32).astype(jnp.bfloat16) for n in range(4)]

    def arrange(w_ref, band_ref, out_order):
        rep = jnp.dot(w_ref[...], copies, preferred_element_type=jnp.float32).astype(jnp.bfloat16)
        placed = {}

        def place(tap, n):
            if (tap, n) not in placed:
                placed[tap, n] = rep[tap * 32 : tap * 32 + 32] * masks[n]
            return placed[tap, n]

        blocks = {}
        for d1 in range(3):
            for dj in range(2):
                cells = [(0, z) for z in ORDER[0]] + [(1, z) for z in ORDER[1]] + list(BESIDE)
                for n, (side, z_in) in enumerate(cells):
                    row = (d1 * 2 + dj) * 384 + n * 32
                    for o in range(2):
                        d2 = 2 * dj + side - o
                        parts = []
                        for d3 in range(3):
                            z_out = z_in - d3 + 1
                            if 0 <= d2 < 3 and 0 <= z_out < 4:
                                parts.append(((d1 * 3 + d2) * 3 + d3, out_order[o].index(z_out)))
                        key = tuple(parts)
                        if key not in blocks:
                            block = jnp.zeros((32, 128), jnp.bfloat16)
                            for k, part in enumerate(parts):
                                block = place(*part) if k == 0 else block + place(*part)
                            blocks[key] = block
                        band_ref[pl.ds(row, 32), pl.ds(o * 128, 128)] = blocks[key]

    arrange(weight_ref, target_ref, order)
    if not residual:
        return
    r = lax.broadcasted_iota(jnp.int32, (256, 256), 0)
    c = lax.broadcasted_iota(jnp.int32, (256, 256), 1)
    swap = jnp.where((r // 32) % 2 == 0, r + 32, r - 32)
    target_ref[pl.ds(WINDOW, 256), :] = (jnp.where(r < 128, r, swap) == c).astype(jnp.bfloat16)


def edges():
    one, zero = jnp.float32(1), jnp.float32(0)
    strike, dip = lax.axis_index("strike"), lax.axis_index("dip")
    x_lo = jnp.where(strike == 0, zero, one)
    x_hi = jnp.where(strike == lax.axis_size("strike") - 1, zero, one)
    y_lo = jnp.where(dip == 0, zero, one)
    y_hi = jnp.where(dip == lax.axis_size("dip") - 1, zero, one)
    return x_lo, x_hi, y_lo, y_hi


def put(cells, x0, x1, block):
    even = lax.axis_index("dip") % 2 == 0
    below, above = jnp.where(even, 8, 4), jnp.where(even, 4, 8)
    cells[x0:x1, 1:5, :] = block(0)
    cells[x0:x1, 0:1, :] = block(below)[:, 3:4]
    cells[x0:x1, 5:6, :] = block(above)[:, 0:1]


def read(ref, first, count):
    return ref[pl.ds(first, count)].astype(jnp.float32)


def upsample(cells, upmat, fine, q1s, sides):
    x_lo, x_hi, y_lo, y_hi = sides
    one = jnp.float32(1)
    count = len(q1s)
    rows = 8 * count
    wide = []
    edge = jnp.zeros((rows, 32), jnp.float32)
    for h1 in range(2):
        for h2 in range(2):
            window = jnp.concatenate(
                [cells[q1 + 1 - h1 : q1 + 2 - h1, 1 - h2 : 9 - h2, :] for q1 in q1s], axis=0
            )
            wide.append(jnp.concatenate([edge, window.reshape(rows, 128), edge], axis=1))
    left = jnp.concatenate(
        [
            jnp.concatenate([w[:, 32 * q3 : 32 * q3 + 64] for w in wide], axis=1)
            for q3 in range(5)
        ],
        axis=0,
    ).astype(jnp.bfloat16)

    lane = lax.broadcasted_iota(jnp.int32, (rows, 128), 1)
    q2 = lax.broadcasted_iota(jnp.int32, (rows, 128), 0) % 8
    outer = (lane < 32) | (lane >= 96)
    front = lane < 64
    low = jnp.where(q2 == 0, y_lo, one)
    high = jnp.where(q2 == 4, y_hi, one)
    none = jnp.zeros((rows, 128), jnp.float32)
    for p1 in range(4):
        phase = jnp.dot(left, upmat[:, p1 * 512 : p1 * 512 + 512], preferred_element_type=jnp.float32)
        for pp in range(2):
            tiles = [[], []]
            for side in range(2):
                p2 = 2 * pp + side
                v = phase[:, p2 * 128 : p2 * 128 + 128]
                for g in range(GROUPS):
                    at = g * rows
                    t = jnp.where(front, v[at : at + rows], v[at + rows : at + 2 * rows])
                    tiles[side].append(silu(t) * (low if pp == 0 else high))
            merged = [jnp.where(outer, tiles[0][g], tiles[1][g]) for g in range(GROUPS)]
            merged = [none] + merged + [none]
            for g in range(GROUPS):
                beside = jnp.where(front, merged[g + 2], merged[g])
                for n, t in enumerate((tiles[0][g], tiles[1][g], beside)):
                    for c, q1 in enumerate(q1s):
                        part = t[c * 8 : c * 8 + 5]
                        if q1 == 0 and p1 < 2:
                            part = part * x_lo
                        if q1 == 4 and p1 >= 2:
                            part = part * x_hi
                        at = (4 * c + p1) * STEP + g * PAIRS + pp
                        fine[n, pl.ds(at, 5, stride=2), :] = part


def windows_of(fine, first, count, target, at):
    for dj in range(2):
        for n in range(3):
            rows = fine[n, pl.ds(first * STEP + dj, count * STEP), :].astype(jnp.bfloat16)
            target[dj, at * STEP : (at + count) * STEP, n * 128 : n * 128 + 128] = rows


def tight(block, at):
    return jnp.concatenate([block[pl.ds(at + g * PAIRS, 8), :] for g in range(GROUPS)], axis=0)


def centre_of(fine, first, count, target, at):
    for n in range(count):
        here = slice((at + n) * TIGHT, (at + n + 1) * TIGHT)
        for o in range(2):
            rows = tight(fine.at[o], (first + n) * STEP + 1)
            target[here, o * 128 : o * 128 + 128] = rows.astype(jnp.bfloat16)


def clear(block, at):
    block[2, at : at + 16, :] = jnp.zeros((16, 128), jnp.float32)


def keep(v, at, count, hidden, shift, target, target_at, sides):
    x_lo, x_hi, y_lo, y_hi = sides
    one, zero = jnp.float32(1), jnp.float32(0)
    row = lax.broadcasted_iota(jnp.int32, (STEP, 128), 0)
    lane = lax.broadcasted_iota(jnp.int32, (STEP, 128), 1)
    starts = [g * PAIRS for g in range(GROUPS)]
    first, last = row == starts[0], row == starts[0] + 8
    for start in starts[1:]:
        first, last = first | (row == start), last | (row == start + 8)
    y_first, y_last = jnp.where(first, y_lo, one), jnp.where(last, y_hi, one)
    outer = (lane < 32) | (lane >= 96)
    row = lax.broadcasted_iota(jnp.int32, (TIGHT, 128), 0)
    lane = lax.broadcasted_iota(jnp.int32, (TIGHT, 128), 1)
    front = lane < 64
    inside_above = jnp.where(row < TIGHT - 8, one, zero)
    inside_below = jnp.where(row >= 8, one, zero)
    inside = jnp.where(front, inside_above, inside_below)

    v = silu(v)
    for n in range(count):
        x = at + n
        rows = slice(n * STEP, n * STEP + STEP)
        v0, v1 = v[rows, :128] * y_first, v[rows, 128:] * y_last
        if x in (0, 17):
            edge = x_lo if x == 0 else x_hi
            v0, v1 = v0 * edge, v1 * edge
        here = slice(16 + (x - shift) * STEP, 16 + (x - shift) * STEP + STEP)
        hidden[0, here, :] = v0
        hidden[1, here, :] = v1
        hidden[2, here, :] = jnp.where(outer, v0, v1)
    for n in range(count):
        here = slice((target_at + n) * TIGHT, (target_at + n + 1) * TIGHT)
        for dj in range(2):
            start = 16 + (at + n - shift) * STEP + dj
            for o in range(2):
                rows = tight(hidden.at[o], start)
                target[dj, here, o * 128 : o * 128 + 128] = rows.astype(jnp.bfloat16)
            above = tight(hidden.at[2], start + PAIRS)
            below = tight(hidden.at[2], start - PAIRS)
            beside = jnp.where(front, above, below) * inside
            target[dj, here, 256:384] = beside.astype(jnp.bfloat16)


def weave(v, row, woven, near, at, count):
    for x in range(at, at + count):
        for g in range(GROUPS):
            for o in range(2):
                cells8 = v[row : row + 8, o * 128 : o * 128 + 128]
                woven[g, pl.ds(x * 16 + o, 8, stride=2), :] = cells8
            row += 8
    for g in range(GROUPS):
        near[at : at + count, :, g * 128 : g * 128 + 128] = (
            woven[g, at * 16 : (at + count) * 16].reshape(count, 16, 128).astype(jnp.bfloat16)
        )


def inner_work(
    own, upmat, first_ref, second_ref, inner, centre, band1_ref, band2_ref, ready, middle,
    cells, fine, hidden, woven,
):
    arrange_band(first_ref, band1_ref, ORDER, False)
    sides = edges()
    put(cells, 1, 5, lambda o: read(own, o, 4))
    upsample(cells, upmat, fine, (1, 2, 3), sides)
    windows_of(fine, 0, 12, inner, 0)
    centre_of(fine, 0, 12, centre, 0)
    v = product(inner, ((0, 6), (6, 4)), STEP, band1_ref)
    arrange_band(second_ref, band2_ref, (ORDER[0], ORDER[0]), True)
    clear(hidden, 0)
    clear(hidden, 16 + 10 * STEP)
    keep(v, 4, 10, hidden, 4, ready, 0, sides)
    v = product(ready, ((0, 4), (4, 4)), TIGHT, band2_ref, centre[2 * TIGHT : 10 * TIGHT, :])
    weave(v, 0, woven, middle, 0, 8)


def pack_kernel(
    coarse, dip_a, dip_b, upmat, first_ref, second_ref,
    own, inner, centre, band1_ref, band2_ref, ready, middle, cells, fine, hidden, woven,
):
    own[0:4] = coarse[...]
    own[4:8] = dip_a[...]
    own[8:12] = dip_b[...]

    @pl.when(lax.axis_index("strike") == 0)
    def _():
        inner_work(
            own, upmat, first_ref, second_ref, inner, centre, band1_ref, band2_ref, ready, middle,
            cells, fine, hidden, woven,
        )


def inner_kernel(
    own, upmat, first_ref, second_ref, _inner, _centre, _band1, _band2, _ready, _middle,
    inner, centre, band1_ref, band2_ref, ready, middle, cells, fine, hidden, woven,
):
    @pl.when(lax.axis_index("strike") != 0)
    def _():
        inner_work(
            own, upmat, first_ref, second_ref, inner, centre, band1_ref, band2_ref, ready, middle,
            cells, fine, hidden, woven,
        )


def product(source, strips, step, taps, base=None):
    results = []
    row = 0
    for at, n in strips:
        columns = [
            source[dj, (at + dx) * step : (at + dx + n) * step, :] for dx in range(3) for dj in range(2)
        ]
        if base is not None:
            columns.append(base[row : row + n * step, :])
        row += n * step
        results.append(
            jnp.dot(jnp.concatenate(columns, axis=1), taps[...], preferred_element_type=jnp.float32)
        )
    return jnp.concatenate(results, axis=0)


def main_kernel(
    own, strike_a, strike_b, inner, centre, upmat, band1, band2, ready, middle, out,
    cells, fine, hidden, b1, b2, ends, woven, near, sems,
):
    sends = [pltpu.make_async_copy(middle, out.at[pl.ds(4, 8)], sems.at[0])]
    sends[0].start()
    sides = edges()

    even = lax.axis_index("strike") % 2 == 0
    put(cells, 0, 1, lambda o: jnp.where(even, read(strike_b, o + 3, 1), read(strike_a, o + 3, 1)))
    put(cells, 1, 2, lambda o: read(own, o, 1))
    put(cells, 4, 5, lambda o: read(own, o + 3, 1))
    put(cells, 5, 6, lambda o: jnp.where(even, read(strike_a, o, 1), read(strike_b, o, 1)))
    upsample(cells, upmat, fine, (0, 4), sides)
    windows_of(fine, 0, 4, b1, 0)
    b1[:, 4 * STEP : 6 * STEP, :] = inner[:, : 2 * STEP, :]
    b1[:, 6 * STEP : 8 * STEP, :] = inner[:, 10 * STEP : 12 * STEP, :]
    windows_of(fine, 4, 4, b1, 8)
    centre_of(fine, 2, 2, ends, 0)
    ends[2 * TIGHT : 4 * TIGHT, :] = centre[0 : 2 * TIGHT, :]
    ends[4 * TIGHT : 6 * TIGHT, :] = centre[10 * TIGHT : 12 * TIGHT, :]
    centre_of(fine, 4, 2, ends, 6)

    v_outer = product(b1, ((0, 4), (6, 4)), STEP, band1)

    clear(hidden, 0)
    clear(hidden, 16 + 4 * STEP)
    clear(hidden, 14 * STEP)
    clear(hidden, 16 + 18 * STEP)
    keep(v_outer[: 4 * STEP], 0, 4, hidden, 0, b2, 0, sides)
    keep(v_outer[4 * STEP :], 14, 4, hidden, 0, b2, 14, sides)
    b2[:, 4 * TIGHT : 6 * TIGHT, :] = ready[:, : 2 * TIGHT, :]
    b2[:, 12 * TIGHT : 14 * TIGHT, :] = ready[:, 8 * TIGHT : 10 * TIGHT, :]
    v_outer = product(b2, ((0, 4), (12, 4)), TIGHT, band2, ends[...])

    for n, at in enumerate((0, 12)):
        weave(v_outer, n * 4 * TIGHT, woven, near, at, 4)
        here = pl.ds(at, 4)
        sends.append(pltpu.make_async_copy(near.at[here], out.at[here], sems.at[n + 1]))
        sends[-1].start()
    for send in sends:
        send.wait()


def swapped(block, axis):
    size = lax.axis_size(axis)
    for first in (0, 1):
        pairs = [(i, i + 1) for i in range(first, size - 1, 2)]
        yield lax.ppermute(block, axis, pairs + [(j, i) for i, j in pairs])


def body(coarse, up_weight, first_weight, second_weight):
    vmem = pl.BlockSpec(memory_space=pltpu.VMEM)
    params = pltpu.CompilerParams(vmem_limit_bytes=32 * 1024 * 1024)

    bf16 = jnp.bfloat16
    shape = jax.ShapeDtypeStruct
    dip_a, dip_b = swapped(coarse, "dip")
    upmat = pl.pallas_call(
        up_kernel,
        out_shape=shape((256, 2048), bf16),
        in_specs=[pl.BlockSpec(memory_space=pltpu.HBM)],
        out_specs=vmem,
        scratch_shapes=[pltpu.VMEM((512 * 32, 32), bf16), pltpu.SemaphoreType.DMA((8,))],
        compiler_params=pltpu.CompilerParams(vmem_limit_bytes=LIMIT),
        cost_estimate=pl.CostEstimate(flops=5_000_000, bytes_accessed=5_000_000, transcendentals=0),
        name="arrange_up",
    )(up_weight.reshape(512 * 32, 32))
    first, second = first_weight.reshape(864, 32), second_weight.reshape(864, 32)
    inner_shapes = (
        shape((2, 12 * STEP, 384), bf16),
        shape((12 * TIGHT, 256), bf16),
        shape((WINDOW, 256), bf16),
        shape((WINDOW + 256, 256), bf16),
        shape((2, 10 * TIGHT, 384), bf16),
        shape((8, 16, 512), bf16),
    )
    inner_scratch = [
        pltpu.VMEM((6, 16, 128), jnp.float32),
        pltpu.VMEM((3, 12 * STEP + 8, 128), jnp.float32),
        pltpu.VMEM((3, 10 * STEP + 32, 128), jnp.float32),
        pltpu.VMEM((GROUPS, 128, 128), jnp.float32),
    ]
    inner_params = pltpu.CompilerParams(vmem_limit_bytes=16 * 1024 * 1024)
    own, *early = pl.pallas_call(
        pack_kernel,
        out_shape=(shape((12, 4, 128), bf16), *inner_shapes),
        in_specs=[vmem] * 6,
        out_specs=(vmem,) * 7,
        scratch_shapes=inner_scratch,
        compiler_params=inner_params,
        name="pack",
    )(coarse, dip_a, dip_b, upmat, first, second)
    strike_a, strike_b = swapped(own, "strike")
    inner, centre, band1, band2, ready, middle = pl.pallas_call(
        inner_kernel,
        out_shape=inner_shapes,
        in_specs=[vmem] * 10,
        out_specs=(vmem,) * 6,
        scratch_shapes=inner_scratch,
        input_output_aliases={4: 0, 5: 1, 6: 2, 7: 3, 8: 4, 9: 5},
        compiler_params=inner_params,
        cost_estimate=pl.CostEstimate(
            flops=300_000_000, bytes_accessed=3_000_000, transcendentals=200_000
        ),
        name="upsample_inner",
    )(own, upmat, first, second, *early)
    return pl.pallas_call(
        main_kernel,
        out_shape=jax.ShapeDtypeStruct((16, 16, 512), bf16),
        in_specs=[vmem] * 10,
        out_specs=pl.BlockSpec(memory_space=pltpu.HBM),
        scratch_shapes=[
            pltpu.VMEM((6, 16, 128), jnp.float32),
            pltpu.VMEM((3, 8 * STEP + 8, 128), jnp.float32),
            pltpu.VMEM((3, 18 * STEP + 32, 128), jnp.float32),
            pltpu.VMEM((2, 12 * STEP, 384), bf16),
            pltpu.VMEM((2, 18 * TIGHT, 384), bf16),
            pltpu.VMEM((8 * TIGHT, 256), bf16),
            pltpu.VMEM((GROUPS, 256, 128), jnp.float32),
            pltpu.VMEM((16, 16, 512), bf16),
            pltpu.SemaphoreType.DMA((3,)),
        ],
        compiler_params=params,
        cost_estimate=pl.CostEstimate(
            flops=2_000_000_000, bytes_accessed=8_000_000, transcendentals=800_000
        ),
        name="upsample_refine",
    )(own, strike_a, strike_b, inner, centre, upmat, band1, band2, ready, middle)


def solution(mesh):
    return jax.shard_map(
        body,
        mesh=mesh,
        in_specs=(P("strike", "dip", None), P(), P(), P()),
        out_specs=P("strike", "dip", None),
        check_vma=False,
    )
```

```python
import jax
import jax.numpy as jnp
from jax import lax
from jax.experimental import pallas as pl
from jax.experimental.pallas import tpu as pltpu
from jax.sharding import PartitionSpec as P

GROUPS = 4
PAIRS = 10
STEP = GROUPS * PAIRS
ORDER = ((0, 1, 2, 3), (1, 0, 3, 2))
BESIDE = ((0, 4), (1, 4), (1, -1), (0, -1))
WINDOW = 3 * 2 * 384
TIGHT = GROUPS * 8
AHEAD = 8
LIMIT = 50 * 1024 * 1024


def silu(v):
    half = 0.5 * v
    return half + half * jnp.tanh(half)


def up_kernel(up_hbm, upmat_ref, up_ref, sems):
    fetches = []
    for k1 in range(8):
        rows = pl.ds(k1 * 2048, 2048)
        fetches.append(pltpu.make_async_copy(up_hbm.at[rows], up_ref.at[rows], sems.at[k1]))
    for fetch in fetches[:AHEAD]:
        fetch.start()

    for k1 in range(8):
        fetches[k1].wait()
        if k1 + AHEAD < 8:
            fetches[k1 + AHEAD].start()
        h1, p1 = divmod(k1, 4)
        for k2 in range(8):
            h2, p2 = divmod(k2, 4)
            for h3 in range(2):
                k = (k1 * 8 + k2) * 8 + 4 * h3
                parts = [up_ref[pl.ds((k + (z + 2) % 4) * 32, 32), :] for z in ORDER[p2 % 2]]
                row = (h1 * 4 + h2 * 2 + (1 - h3)) * 32
                upmat_ref[pl.ds(row, 32), pl.ds((p1 * 4 + p2) * 128, 128)] = jnp.concatenate(
                    parts, axis=1
                )


def arrange_bands(first_ref, second_ref, band1_ref, band2_ref):
    ci = lax.broadcasted_iota(jnp.int32, (32, 128), 0)
    lane = lax.broadcasted_iota(jnp.int32, (32, 128), 1)
    group = lane // 32
    copies = (lane % 32 == ci).astype(jnp.bfloat16)

    masks = [(group == n).astype(jnp.float32).astype(jnp.bfloat16) for n in range(4)]

    def arrange(w_ref, band_ref, out_order):
        rep = jnp.dot(w_ref[...], copies, preferred_element_type=jnp.float32).astype(jnp.bfloat16)
        placed = {}

        def place(tap, n):
            if (tap, n) not in placed:
                placed[tap, n] = rep[tap * 32 : tap * 32 + 32] * masks[n]
            return placed[tap, n]

        blocks = {}
        for d1 in range(3):
            for dj in range(2):
                cells = [(0, z) for z in ORDER[0]] + [(1, z) for z in ORDER[1]] + list(BESIDE)
                for n, (side, z_in) in enumerate(cells):
                    row = (d1 * 2 + dj) * 384 + n * 32
                    for o in range(2):
                        d2 = 2 * dj + side - o
                        parts = []
                        for d3 in range(3):
                            z_out = z_in - d3 + 1
                            if 0 <= d2 < 3 and 0 <= z_out < 4:
                                parts.append(((d1 * 3 + d2) * 3 + d3, out_order[o].index(z_out)))
                        key = tuple(parts)
                        if key not in blocks:
                            block = jnp.zeros((32, 128), jnp.bfloat16)
                            for k, part in enumerate(parts):
                                block = place(*part) if k == 0 else block + place(*part)
                            blocks[key] = block
                        band_ref[pl.ds(row, 32), pl.ds(o * 128, 128)] = blocks[key]

    arrange(first_ref, band1_ref, ORDER)
    arrange(second_ref, band2_ref, (ORDER[0], ORDER[0]))
    r = lax.broadcasted_iota(jnp.int32, (256, 256), 0)
    c = lax.broadcasted_iota(jnp.int32, (256, 256), 1)
    swap = jnp.where((r // 32) % 2 == 0, r + 32, r - 32)
    band2_ref[pl.ds(WINDOW, 256), :] = (jnp.where(r < 128, r, swap) == c).astype(jnp.bfloat16)


def edges():
    one, zero = jnp.float32(1), jnp.float32(0)
    strike, dip = lax.axis_index("strike"), lax.axis_index("dip")
    x_lo = jnp.where(strike == 0, zero, one)
    x_hi = jnp.where(strike == lax.axis_size("strike") - 1, zero, one)
    y_lo = jnp.where(dip == 0, zero, one)
    y_hi = jnp.where(dip == lax.axis_size("dip") - 1, zero, one)
    return x_lo, x_hi, y_lo, y_hi


def put(cells, x0, x1, block):
    even = lax.axis_index("dip") % 2 == 0
    below, above = jnp.where(even, 8, 4), jnp.where(even, 4, 8)
    cells[x0:x1, 1:5, :] = block(0)
    cells[x0:x1, 0:1, :] = block(below)[:, 3:4]
    cells[x0:x1, 5:6, :] = block(above)[:, 0:1]


def read(ref, first, count):
    return ref[pl.ds(first, count)].astype(jnp.float32)


def upsample(cells, upmat, fine, q1s, sides):
    x_lo, x_hi, y_lo, y_hi = sides
    one = jnp.float32(1)
    count = len(q1s)
    rows = 8 * count
    wide = []
    edge = jnp.zeros((rows, 32), jnp.float32)
    for h1 in range(2):
        for h2 in range(2):
            window = jnp.concatenate(
                [cells[q1 + 1 - h1 : q1 + 2 - h1, 1 - h2 : 9 - h2, :] for q1 in q1s], axis=0
            )
            wide.append(jnp.concatenate([edge, window.reshape(rows, 128), edge], axis=1))
    left = jnp.concatenate(
        [
            jnp.concatenate([w[:, 32 * q3 : 32 * q3 + 64] for w in wide], axis=1)
            for q3 in range(5)
        ],
        axis=0,
    ).astype(jnp.bfloat16)

    lane = lax.broadcasted_iota(jnp.int32, (rows, 128), 1)
    q2 = lax.broadcasted_iota(jnp.int32, (rows, 128), 0) % 8
    outer = (lane < 32) | (lane >= 96)
    front = lane < 64
    low = jnp.where(q2 == 0, y_lo, one)
    high = jnp.where(q2 == 4, y_hi, one)
    none = jnp.zeros((rows, 128), jnp.float32)
    for p1 in range(4):
        phase = jnp.dot(left, upmat[:, p1 * 512 : p1 * 512 + 512], preferred_element_type=jnp.float32)
        for pp in range(2):
            tiles = [[], []]
            for side in range(2):
                p2 = 2 * pp + side
                v = phase[:, p2 * 128 : p2 * 128 + 128]
                for g in range(GROUPS):
                    at = g * rows
                    t = jnp.where(front, v[at : at + rows], v[at + rows : at + 2 * rows])
                    tiles[side].append(silu(t) * (low if pp == 0 else high))
            merged = [jnp.where(outer, tiles[0][g], tiles[1][g]) for g in range(GROUPS)]
            merged = [none] + merged + [none]
            for g in range(GROUPS):
                beside = jnp.where(front, merged[g + 2], merged[g])
                for n, t in enumerate((tiles[0][g], tiles[1][g], beside)):
                    for c, q1 in enumerate(q1s):
                        part = t[c * 8 : c * 8 + 5]
                        if q1 == 0 and p1 < 2:
                            part = part * x_lo
                        if q1 == 4 and p1 >= 2:
                            part = part * x_hi
                        at = (4 * c + p1) * STEP + g * PAIRS + pp
                        fine[n, pl.ds(at, 5, stride=2), :] = part


def windows_of(fine, first, count, target, at):
    for dj in range(2):
        for n in range(3):
            rows = fine[n, pl.ds(first * STEP + dj, count * STEP), :].astype(jnp.bfloat16)
            target[dj, at * STEP : (at + count) * STEP, n * 128 : n * 128 + 128] = rows


def tight(block, at):
    return jnp.concatenate([block[pl.ds(at + g * PAIRS, 8), :] for g in range(GROUPS)], axis=0)


def centre_of(fine, first, count, target, at):
    for n in range(count):
        here = slice((at + n) * TIGHT, (at + n + 1) * TIGHT)
        for o in range(2):
            rows = tight(fine.at[o], (first + n) * STEP + 1)
            target[here, o * 128 : o * 128 + 128] = rows.astype(jnp.bfloat16)


def clear(block, at):
    block[2, at : at + 16, :] = jnp.zeros((16, 128), jnp.float32)


def keep(v, at, count, hidden, shift, target, target_at, sides):
    x_lo, x_hi, y_lo, y_hi = sides
    one, zero = jnp.float32(1), jnp.float32(0)
    row = lax.broadcasted_iota(jnp.int32, (STEP, 128), 0)
    lane = lax.broadcasted_iota(jnp.int32, (STEP, 128), 1)
    starts = [g * PAIRS for g in range(GROUPS)]
    first, last = row == starts[0], row == starts[0] + 8
    for start in starts[1:]:
        first, last = first | (row == start), last | (row == start + 8)
    y_first, y_last = jnp.where(first, y_lo, one), jnp.where(last, y_hi, one)
    outer = (lane < 32) | (lane >= 96)
    row = lax.broadcasted_iota(jnp.int32, (TIGHT, 128), 0)
    lane = lax.broadcasted_iota(jnp.int32, (TIGHT, 128), 1)
    front = lane < 64
    inside_above = jnp.where(row < TIGHT - 8, one, zero)
    inside_below = jnp.where(row >= 8, one, zero)
    inside = jnp.where(front, inside_above, inside_below)

    v = silu(v)
    for n in range(count):
        x = at + n
        rows = slice(n * STEP, n * STEP + STEP)
        v0, v1 = v[rows, :128] * y_first, v[rows, 128:] * y_last
        if x in (0, 17):
            edge = x_lo if x == 0 else x_hi
            v0, v1 = v0 * edge, v1 * edge
        here = slice(16 + (x - shift) * STEP, 16 + (x - shift) * STEP + STEP)
        hidden[0, here, :] = v0
        hidden[1, here, :] = v1
        hidden[2, here, :] = jnp.where(outer, v0, v1)
    for n in range(count):
        here = slice((target_at + n) * TIGHT, (target_at + n + 1) * TIGHT)
        for dj in range(2):
            start = 16 + (at + n - shift) * STEP + dj
            for o in range(2):
                rows = tight(hidden.at[o], start)
                target[dj, here, o * 128 : o * 128 + 128] = rows.astype(jnp.bfloat16)
            above = tight(hidden.at[2], start + PAIRS)
            below = tight(hidden.at[2], start - PAIRS)
            beside = jnp.where(front, above, below) * inside
            target[dj, here, 256:384] = beside.astype(jnp.bfloat16)


def weave(v, row, woven, near, at, count):
    for x in range(at, at + count):
        for g in range(GROUPS):
            for o in range(2):
                cells8 = v[row : row + 8, o * 128 : o * 128 + 128]
                woven[g, pl.ds(x * 16 + o, 8, stride=2), :] = cells8
            row += 8
    for g in range(GROUPS):
        near[at : at + count, :, g * 128 : g * 128 + 128] = (
            woven[g, at * 16 : (at + count) * 16].reshape(count, 16, 128).astype(jnp.bfloat16)
        )


def inner_work(
    own, upmat, first_ref, second_ref, inner, centre, band1_ref, band2_ref, ready, middle,
    cells, fine, hidden, woven,
):
    arrange_bands(first_ref, second_ref, band1_ref, band2_ref)
    sides = edges()
    put(cells, 1, 5, lambda o: read(own, o, 4))
    upsample(cells, upmat, fine, (1, 2, 3), sides)
    windows_of(fine, 0, 12, inner, 0)
    centre_of(fine, 0, 12, centre, 0)
    v = product(inner, ((0, 5), (5, 5)), STEP, band1_ref)
    clear(hidden, 0)
    clear(hidden, 16 + 10 * STEP)
    keep(v, 4, 10, hidden, 4, ready, 0, sides)
    v = product(ready, ((0, 4), (4, 4)), TIGHT, band2_ref, centre[2 * TIGHT : 10 * TIGHT, :])
    weave(v, 0, woven, middle, 0, 8)


def pack_kernel(
    coarse, dip_a, dip_b, upmat, first_ref, second_ref,
    own, inner, centre, band1_ref, band2_ref, ready, middle, cells, fine, hidden, woven,
):
    own[0:4] = coarse[...]
    own[4:8] = dip_a[...]
    own[8:12] = dip_b[...]

    @pl.when(lax.axis_index("strike") == 0)
    def _():
        inner_work(
            own, upmat, first_ref, second_ref, inner, centre, band1_ref, band2_ref, ready, middle,
            cells, fine, hidden, woven,
        )


def inner_kernel(
    own, upmat, first_ref, second_ref, _inner, _centre, _band1, _band2, _ready, _middle,
    inner, centre, band1_ref, band2_ref, ready, middle, cells, fine, hidden, woven,
):
    @pl.when(lax.axis_index("strike") != 0)
    def _():
        inner_work(
            own, upmat, first_ref, second_ref, inner, centre, band1_ref, band2_ref, ready, middle,
            cells, fine, hidden, woven,
        )


def product(source, strips, step, taps, base=None):
    results = []
    row = 0
    for at, n in strips:
        columns = [
            source[dj, (at + dx) * step : (at + dx + n) * step, :] for dx in range(3) for dj in range(2)
        ]
        if base is not None:
            columns.append(base[row : row + n * step, :])
        row += n * step
        results.append(
            jnp.dot(jnp.concatenate(columns, axis=1), taps[...], preferred_element_type=jnp.float32)
        )
    return jnp.concatenate(results, axis=0)


def main_kernel(
    own, strike_a, strike_b, inner, centre, upmat, band1, band2, ready, middle, out,
    cells, fine, hidden, b1, b2, ends, woven, near, sems,
):
    sends = [pltpu.make_async_copy(middle, out.at[pl.ds(4, 8)], sems.at[0])]
    sends[0].start()
    sides = edges()

    even = lax.axis_index("strike") % 2 == 0
    put(cells, 0, 1, lambda o: jnp.where(even, read(strike_b, o + 3, 1), read(strike_a, o + 3, 1)))
    put(cells, 1, 2, lambda o: read(own, o, 1))
    put(cells, 4, 5, lambda o: read(own, o + 3, 1))
    put(cells, 5, 6, lambda o: jnp.where(even, read(strike_a, o, 1), read(strike_b, o, 1)))
    upsample(cells, upmat, fine, (0, 4), sides)
    windows_of(fine, 0, 4, b1, 0)
    b1[:, 4 * STEP : 6 * STEP, :] = inner[:, : 2 * STEP, :]
    b1[:, 6 * STEP : 8 * STEP, :] = inner[:, 10 * STEP : 12 * STEP, :]
    windows_of(fine, 4, 4, b1, 8)
    centre_of(fine, 2, 2, ends, 0)
    ends[2 * TIGHT : 4 * TIGHT, :] = centre[0 : 2 * TIGHT, :]
    ends[4 * TIGHT : 6 * TIGHT, :] = centre[10 * TIGHT : 12 * TIGHT, :]
    centre_of(fine, 4, 2, ends, 6)

    v_outer = product(b1, ((0, 4), (6, 4)), STEP, band1)

    clear(hidden, 0)
    clear(hidden, 16 + 4 * STEP)
    clear(hidden, 14 * STEP)
    clear(hidden, 16 + 18 * STEP)
    keep(v_outer[: 4 * STEP], 0, 4, hidden, 0, b2, 0, sides)
    keep(v_outer[4 * STEP :], 14, 4, hidden, 0, b2, 14, sides)
    b2[:, 4 * TIGHT : 6 * TIGHT, :] = ready[:, : 2 * TIGHT, :]
    b2[:, 12 * TIGHT : 14 * TIGHT, :] = ready[:, 8 * TIGHT : 10 * TIGHT, :]
    v_outer = product(b2, ((0, 4), (12, 4)), TIGHT, band2, ends[...])

    for n, at in enumerate((0, 12)):
        weave(v_outer, n * 4 * TIGHT, woven, near, at, 4)
        here = pl.ds(at, 4)
        sends.append(pltpu.make_async_copy(near.at[here], out.at[here], sems.at[n + 1]))
        sends[-1].start()
    for send in sends:
        send.wait()


def swapped(block, axis):
    size = lax.axis_size(axis)
    for first in (0, 1):
        pairs = [(i, i + 1) for i in range(first, size - 1, 2)]
        yield lax.ppermute(block, axis, pairs + [(j, i) for i, j in pairs])


def body(coarse, up_weight, first_weight, second_weight):
    vmem = pl.BlockSpec(memory_space=pltpu.VMEM)
    params = pltpu.CompilerParams(vmem_limit_bytes=32 * 1024 * 1024)

    bf16 = jnp.bfloat16
    shape = jax.ShapeDtypeStruct
    dip_a, dip_b = swapped(coarse, "dip")
    upmat = pl.pallas_call(
        up_kernel,
        out_shape=shape((256, 2048), bf16),
        in_specs=[pl.BlockSpec(memory_space=pltpu.HBM)],
        out_specs=vmem,
        scratch_shapes=[pltpu.VMEM((512 * 32, 32), bf16), pltpu.SemaphoreType.DMA((8,))],
        compiler_params=pltpu.CompilerParams(vmem_limit_bytes=LIMIT),
        cost_estimate=pl.CostEstimate(flops=5_000_000, bytes_accessed=5_000_000, transcendentals=0),
        name="arrange_up",
    )(up_weight.reshape(512 * 32, 32))
    first, second = first_weight.reshape(864, 32), second_weight.reshape(864, 32)
    inner_shapes = (
        shape((2, 12 * STEP, 384), bf16),
        shape((12 * TIGHT, 256), bf16),
        shape((WINDOW, 256), bf16),
        shape((WINDOW + 256, 256), bf16),
        shape((2, 10 * TIGHT, 384), bf16),
        shape((8, 16, 512), bf16),
    )
    inner_scratch = [
        pltpu.VMEM((6, 16, 128), jnp.float32),
        pltpu.VMEM((3, 12 * STEP + 8, 128), jnp.float32),
        pltpu.VMEM((3, 10 * STEP + 32, 128), jnp.float32),
        pltpu.VMEM((GROUPS, 128, 128), jnp.float32),
    ]
    inner_params = pltpu.CompilerParams(vmem_limit_bytes=16 * 1024 * 1024)
    own, *early = pl.pallas_call(
        pack_kernel,
        out_shape=(shape((12, 4, 128), bf16), *inner_shapes),
        in_specs=[vmem] * 6,
        out_specs=(vmem,) * 7,
        scratch_shapes=inner_scratch,
        compiler_params=inner_params,
        name="pack",
    )(coarse, dip_a, dip_b, upmat, first, second)
    strike_a, strike_b = swapped(own, "strike")
    inner, centre, band1, band2, ready, middle = pl.pallas_call(
        inner_kernel,
        out_shape=inner_shapes,
        in_specs=[vmem] * 10,
        out_specs=(vmem,) * 6,
        scratch_shapes=inner_scratch,
        input_output_aliases={4: 0, 5: 1, 6: 2, 7: 3, 8: 4, 9: 5},
        compiler_params=inner_params,
        cost_estimate=pl.CostEstimate(
            flops=300_000_000, bytes_accessed=3_000_000, transcendentals=200_000
        ),
        name="upsample_inner",
    )(own, upmat, first, second, *early)
    return pl.pallas_call(
        main_kernel,
        out_shape=jax.ShapeDtypeStruct((16, 16, 512), bf16),
        in_specs=[vmem] * 10,
        out_specs=pl.BlockSpec(memory_space=pltpu.HBM),
        scratch_shapes=[
            pltpu.VMEM((6, 16, 128), jnp.float32),
            pltpu.VMEM((3, 8 * STEP + 8, 128), jnp.float32),
            pltpu.VMEM((3, 18 * STEP + 32, 128), jnp.float32),
            pltpu.VMEM((2, 12 * STEP, 384), bf16),
            pltpu.VMEM((2, 18 * TIGHT, 384), bf16),
            pltpu.VMEM((8 * TIGHT, 256), bf16),
            pltpu.VMEM((GROUPS, 256, 128), jnp.float32),
            pltpu.VMEM((16, 16, 512), bf16),
            pltpu.SemaphoreType.DMA((3,)),
        ],
        compiler_params=params,
        cost_estimate=pl.CostEstimate(
            flops=2_000_000_000, bytes_accessed=8_000_000, transcendentals=800_000
        ),
        name="upsample_refine",
    )(own, strike_a, strike_b, inner, centre, upmat, band1, band2, ready, middle)


def solution(mesh):
    return jax.shard_map(
        body,
        mesh=mesh,
        in_specs=(P("strike", "dip", None), P(), P(), P()),
        out_specs=P("strike", "dip", None),
        check_vma=False,
    )
```
